32 devices in a mesh: dp: 4 (over y, x), mp: 8 (over z, core).
Axes of the slice: x: 2, y: 2, z: 4, core: 2. Of those that a mesh axis runs over, the one named last changes fastest.
Arguments:
- inputs: bfloat16 [3, 2048, 2, 2048], P(None, ('dp', 'mp')), may hold values from -6 to 6
- cotangent: bfloat16 [3, 2048, 2, 2048], P(None, ('dp', 'mp')), may hold values from -6 to 6
- doc_ids: int32 [3, 2, 2048], replicated, may hold values from 0 to 7, as said below
- gain_attn: float32 [2048], replicated, may hold values from 0.5 to 1.5
- w_query: bfloat16 [2048, 2048], P('dp', 'mp'), may hold values from -0.1875 to 0.1875
- w_key: bfloat16 [2048, 2048], P('dp', 'mp'), may hold values from -0.125 to 0.125
- w_value: bfloat16 [2048, 2048], P('dp', 'mp'), may hold values from -0.125 to 0.125
- w_out: bfloat16 [2048, 2048], P('mp', 'dp'), may hold values from -3 to 3
- gain_ffn: float32 [2048], replicated, may hold values from 0.5 to 1.5
- w_gate: bfloat16 [2048, 8192], P('dp', 'mp'), may hold values from -0.125 to 0.125
- w_up: bfloat16 [2048, 8192], P('dp', 'mp'), may hold values from -0.125 to 0.125
- w_down: bfloat16 [8192, 2048], P('mp', 'dp'), may hold values from -0.0625 to 0.0625
Outputs:
- outputs: bfloat16 [3, 2048, 2, 2048], P(None, ('dp', 'mp'))
- input_grad: float32 [3, 2048, 2, 2048], P(None, ('dp', 'mp'))
- grad_gain_attn: float32 [2048], replicated
- grad_query: float32 [2048, 2048], P('dp', 'mp')
- grad_key: float32 [2048, 2048], P('dp', 'mp')
- grad_value: float32 [2048, 2048], P('dp', 'mp')
- grad_out: float32 [2048, 2048], P('mp', 'dp')
- grad_gain_ffn: float32 [2048], replicated
- grad_gate: float32 [2048, 8192], P('dp', 'mp')
- grad_up: float32 [2048, 8192], P('dp', 'mp')
- grad_down: float32 [8192, 2048], P('mp', 'dp')
The draws below stay inside these ranges and needn't reach their ends.
Inputs may be any that keep to these rules, and one draw needn't show every extreme that they name: `doc_ids`: in each sequence the numbers never fall along the tokens, start at 0 and take every value up to 7; one document begins within the first 512 tokens and ends within the last 512.
All inputs are finite; a program needn't handle non-finite values.
Results may differ from the reference program's by a relative error of at most 0.018.
Values may be sent and summed in bfloat16 or wider, within the bound.
A program may use at most 168 MiB of HBM per device.

```python
import math
import jax
import jax.numpy as jnp
from jax import lax

D = 2048
HEADS = 16
HEAD = 128
FF = 8192
SLICE_TOK = 512
MICRO = 3
SEQS = 2
DOCS = 8
TOKENS = 2048


def draw_doc_ids(key, part):
    key = jax.random.fold_in(key, 7)

    def one_row(row_key):
        head_key, tail_key = jax.random.split(row_key)
        head_bounds = jax.random.permutation(head_key, SLICE_TOK - 1)[:3].astype(jnp.int32) + 1
        tail_bounds = jax.random.permutation(tail_key, SLICE_TOK - 1)[:DOCS - 4].astype(jnp.int32) + (TOKENS - SLICE_TOK + 1)
        bounds = jnp.concatenate([head_bounds, tail_bounds])
        positions = jnp.arange(TOKENS, dtype=jnp.int32)
        return jnp.sum((positions[:, None] >= bounds[None, :]).astype(jnp.int32), axis=1).astype(jnp.int32)
    rows = jax.vmap(one_row)(jax.random.split(key, MICRO * SEQS))
    return rows.reshape(MICRO, SEQS, TOKENS)


def raised(array, rng, source, target, parts, factor):
    def block_of(axis_at):
        return (jnp.arange(array.shape[axis_at]) // (array.shape[axis_at] // parts)).reshape((-1,) + (1,) * (array.ndim - 1 - axis_at))

    near = jax.random.permutation(rng, parts)[block_of(target)]
    other_side = (block_of(target) + parts // 2) % parts
    return jnp.where((block_of(source) == near) | (block_of(source) == other_side), factor * array, array)


def levels(stream_key, extent, cuts, smallest, high):
    loudness = 1.0
    for axis_at, blocks in cuts:
        steps = jax.random.uniform(jax.random.fold_in(jax.random.fold_in(stream_key, 6), axis_at), (blocks,), jnp.float32, smallest / len(cuts), high / len(cuts))
        loudness = loudness * jnp.repeat(jnp.exp(steps), extent[axis_at] // blocks).reshape((-1,) + (1,) * (len(extent) - 1 - axis_at))
    return loudness


def gaussian(key, extent, spread, most, pieces=(), kind=jnp.bfloat16):
    array = spread * jax.random.normal(key, extent, jnp.float32)
    if pieces:
        array = array * levels(key, extent, pieces, -0.22, 0.18)
    return jnp.clip(array, -most, most).astype(kind)


def noise_with(rng, shape, spread, most, cuts, heavy, held_as=jnp.bfloat16):
    array = spread * jax.random.normal(rng, shape, jnp.float32)
    if cuts:
        array = array * levels(rng, shape, cuts, -0.22, 0.18)
    return jnp.clip(raised(array, jax.random.fold_in(rng, 3), *heavy), -most, most).astype(held_as)


def setup_inputs(seed: int = 0) -> dict:
    arg_keys = jax.random.split(jax.random.key(seed), 13)
    inputs = gaussian(arg_keys[0], (MICRO, TOKENS, SEQS, D), 1.0, 6.0, ((1, 32),))
    cotangent = noise_with(arg_keys[1], (MICRO, TOKENS, SEQS, D), 1.0, 6.0, ((1, 32),), (1, 3, 32, 2.75))
    doc_ids = draw_doc_ids(jax.random.fold_in(arg_keys[12], 71), 0)
    gain_attn = jnp.clip(1.0 + 0.1 * jax.random.normal(arg_keys[3], (D,), jnp.float32), 0.5, 1.5)
    w_query = gaussian(arg_keys[4], (D, D), (D // 2) ** -0.5, 0.1875, ((0, 4), (1, 8)))
    w_key = gaussian(arg_keys[5], (D, D), D ** -0.5, 0.125, ((0, 4), (1, 8)))
    w_value = gaussian(arg_keys[6], (D, D), D ** -0.5, 0.125, ((0, 4), (1, 8)))
    w_out = gaussian(arg_keys[7], (D, D), (max(1, TOKENS // 512)) ** -0.5, 3.0, ((0, 8), (1, 4)))
    gain_ffn = jnp.clip(1.0 + 0.1 * jax.random.normal(arg_keys[8], (D,), jnp.float32), 0.5, 1.5)
    w_gate = gaussian(arg_keys[9], (D, FF), D ** -0.5, 0.125, ((0, 4), (1, 8)))
    w_up = gaussian(arg_keys[10], (D, FF), D ** -0.5, 0.125, ((0, 4), (1, 8)))
    w_down = gaussian(arg_keys[11], (FF, D), FF ** -0.5, 0.0625, ((0, 8), (1, 4)))
    return dict(inputs=inputs, cotangent=cotangent, doc_ids=doc_ids, gain_attn=gain_attn, w_query=w_query, w_key=w_key, w_value=w_value, w_out=w_out, gain_ffn=gain_ffn, w_gate=w_gate, w_up=w_up, w_down=w_down)


@jax.custom_vjp
def low(v):
    return lax.optimization_barrier(v.astype(jnp.bfloat16)).astype(jnp.float32)

@jax.custom_vjp
def low_back(v):
    return v

def low_keep(v):
    return (low(v), None)

def low_pass(kept, grad):
    return (grad,)

def back_keep(v):
    return (v, None)

def back_low(kept, grad):
    return (low(grad),)
low.defvjp(low_keep, low_pass)
low_back.defvjp(back_keep, back_low)
epsilon = 1e-05
rope_base = 10000.0
highest = lax.Precision.HIGHEST

def matmul(left, right):
    return jnp.dot(left, right, precision=highest, preferred_element_type=jnp.float32)

def normed(values, gain):
    return values * lax.rsqrt(lax.optimization_barrier(jnp.mean(values * values, axis=-1, keepdims=True)) + epsilon) * gain

def rope_tables(positions, head_size):
    half_size = head_size // 2
    inverse = jnp.power(rope_base, -(jnp.arange(half_size, dtype=jnp.float32) * 2.0 / head_size))
    angles = positions.astype(jnp.float32)[:, None] * inverse[None, :]
    return (jnp.cos(angles)[:, None, :], jnp.sin(angles)[:, None, :])

def rotate(values, cosine_table, sine_table):
    half_size = values.shape[-1] // 2
    first_half = values[..., :half_size]
    second_half = values[..., half_size:]
    return jnp.concatenate([first_half * cosine_table - second_half * sine_table, second_half * cosine_table + first_half * sine_table], axis=-1)

def layer(hidden, gain_attn, w_query, w_key, w_value, w_out, gain_ffn, w_gate, w_up, w_down, visible, cosine_table, sine_table, score_shift):
    length = hidden.shape[0]
    score_scale = HEAD ** (-0.5)
    normed_one = low(normed(hidden, gain_attn))
    query_pre = low_back(matmul(normed_one, w_query)).reshape(length, HEADS, HEAD)
    key_pre = low_back(matmul(normed_one, w_key)).reshape(length, HEADS, HEAD)
    values = low(low_back(matmul(normed_one, w_value))).reshape(length, HEADS, HEAD)
    queries = low(rotate(query_pre, cosine_table, sine_table))
    keys_rot = low(rotate(key_pre, cosine_table, sine_table))

    def one_head(triple):
        head_query, head_key, head_value = triple
        scores = low_back(matmul(head_query, head_key.T) * score_scale - score_shift)
        weights = low(jnp.where(visible, jax.nn.sigmoid(scores), 0.0))
        return matmul(weights, head_value)
    per_head = lax.map(jax.checkpoint(one_head), (jnp.swapaxes(queries, 0, 1), jnp.swapaxes(keys_rot, 0, 1), jnp.swapaxes(values, 0, 1)))
    mixture = low(low_back(jnp.swapaxes(per_head, 0, 1).reshape(length, HEADS * HEAD)))
    middle = hidden + low_back(matmul(mixture, w_out))
    normed_two = low(normed(middle, gain_ffn))
    gate_value = low_back(matmul(normed_two, w_gate))
    up_value = low_back(matmul(normed_two, w_up))
    activated = low(jax.nn.silu(gate_value) * up_value)
    return middle + low_back(matmul(activated, w_down))

def reference(inputs, cotangent, doc_ids, gain_attn, w_query, w_key, w_value, w_out, gain_ffn, w_gate, w_up, w_down):
    params = tuple((tensor.astype(jnp.float32) for tensor in (gain_attn, w_query, w_key, w_value, w_out, gain_ffn, w_gate, w_up, w_down)))
    positions = jnp.arange(TOKENS, dtype=jnp.int32)
    cosine_table, sine_table = rope_tables(positions, HEAD)
    score_shift = math.log(TOKENS)
    causal = positions[:, None] >= positions[None, :]
    totals = [jnp.zeros_like(tensor) for tensor in params]
    results = []
    input_grads = []
    for micro_index in range(MICRO):
        seq_results = []
        seq_grads = []
        for seq_index in range(SEQS):
            doc_row = doc_ids[micro_index, seq_index]
            visible = causal & (doc_row[:, None] == doc_row[None, :])

            def forward(hidden, *weights):
                return layer(hidden, *weights, visible, cosine_table, sine_table, score_shift)
            result, pullback = jax.vjp(forward, inputs[micro_index, :, seq_index].astype(jnp.float32), *params)
            grads = pullback(cotangent[micro_index, :, seq_index].astype(jnp.float32))
            seq_results.append(result.astype(jnp.bfloat16))
            seq_grads.append(grads[0])
            totals = [running + update for running, update in zip(totals, grads[1:])]
        results.append(jnp.stack(seq_results, axis=1))
        input_grads.append(jnp.stack(seq_grads, axis=1))
    return (jnp.stack(results), jnp.stack(input_grads), totals[0], totals[1], totals[2], totals[3], totals[4], totals[5], totals[6], totals[7], totals[8])
```

```python
import functools
import math

import jax
import jax.numpy as jnp
from jax import lax
from jax.experimental import pallas as pl
from jax.experimental.pallas import tpu as pltpu
from jax.sharding import PartitionSpec as P

HEAD = 128
epsilon = 1e-05
rope_base = 10000.0
F32 = jnp.float32
BF16 = jnp.bfloat16


def rope_tables(positions):
    half_size = HEAD // 2
    inverse = jnp.power(rope_base, -(jnp.arange(half_size, dtype=F32) * 2.0 / HEAD))
    angles = positions.astype(F32)[:, None] * inverse[None, :]
    return (jnp.cos(angles), jnp.sin(angles))


def full_tables(positions):
    cosine, sine = rope_tables(positions)
    return (
        jnp.concatenate([cosine, cosine], axis=-1),
        jnp.concatenate([-sine, sine], axis=-1),
    )


def swap_halves(values):
    half_size = HEAD // 2
    return jnp.concatenate([values[..., half_size:], values[..., :half_size]], axis=-1)


def dot(left, right):
    return jnp.dot(left, right, preferred_element_type=F32)


def dot_tn(left, right):
    return lax.dot_general(left, right, (((0,), (0,)), ((), ())), preferred_element_type=F32)


def dot_nt(left, right):
    return lax.dot_general(left, right, (((1,), (1,)), ((), ())), preferred_element_type=F32)


def norm_factor(values):
    return lax.rsqrt(jnp.mean(values * values, axis=-1, keepdims=True) + epsilon)


def norm_back(values, factor, gain, incoming):
    scaled = incoming * gain
    gain_term = jnp.sum(incoming * values * factor, axis=0)
    input_term = factor * scaled - values * factor**3 * jnp.mean(
        scaled * values, axis=-1, keepdims=True
    )
    return (input_term, gain_term)


def sigmoid_of(raw, scale, shift):
    return 1.0 / (1.0 + jnp.exp(shift - raw * scale))


def attend_kernel(block, scale, shift, qkv_ref, first_ref, out_ref):
    total = qkv_ref.shape[0]
    for i in range(total // block):
        rows = pl.ds(i * block, block)
        queries = qkv_ref[rows, 0:HEAD]
        first = first_ref[rows, :]
        row_at = lax.broadcasted_iota(jnp.int32, (block, block), 0) + i * block
        acc = jnp.zeros((block, HEAD), F32)
        for j in range(i + 1):
            cols = pl.ds(j * block, block)
            raw = dot_nt(queries, qkv_ref[cols, HEAD : 2 * HEAD])
            sig = sigmoid_of(raw, scale, shift)
            col_at = lax.broadcasted_iota(jnp.int32, (block, block), 1) + j * block
            visible = col_at >= first
            if j == i:
                visible = visible & (col_at <= row_at)
            weights = jnp.where(visible, sig, 0.0).astype(BF16)
            acc += dot(weights, qkv_ref[cols, 2 * HEAD :])
        out_ref[rows, :] = acc.astype(BF16)


def attend_back_kernel(block, scale, shift, qkv_ref, grad_ref, first_ref, cos_ref, sin_ref, out_ref, dq_ref):
    total = qkv_ref.shape[0]
    count = total // block

    def unrotate(values, rows):
        swapped = pltpu.roll(values, HEAD // 2, 1)
        return (values * cos_ref[rows, :] - swapped * sin_ref[rows, :]).astype(BF16)

    for j in range(count):
        cols = pl.ds(j * block, block)
        keys = qkv_ref[cols, HEAD : 2 * HEAD]
        values = qkv_ref[cols, 2 * HEAD :]
        keys_t = keys.T
        col_at = lax.broadcasted_iota(jnp.int32, (block, block), 0) + j * block
        dk = jnp.zeros((block, HEAD), F32)
        dv = jnp.zeros((block, HEAD), F32)
        for i in range(j, count):
            rows = pl.ds(i * block, block)
            queries = qkv_ref[rows, 0:HEAD]
            grads = grad_ref[rows, :]
            sig = sigmoid_of(dot_nt(keys, queries), scale, shift)
            visible = col_at >= first_ref[:, rows]
            if j == i:
                row_at = lax.broadcasted_iota(jnp.int32, (block, block), 1) + i * block
                visible = visible & (col_at <= row_at)
            sig = jnp.where(visible, sig, 0.0)
            prob_grad = dot_nt(values, grads)
            score_grad = (prob_grad * sig * (1.0 - sig)).astype(BF16)
            dv += dot(sig.astype(BF16), grads)
            dk += dot(score_grad, queries)
            part = dot(keys_t, score_grad)
            if j == 0:
                dq_ref[:, rows] = part
            else:
                dq_ref[:, rows] += part
        out_ref[cols, HEAD : 2 * HEAD] = unrotate(dk * scale, cols)
        out_ref[cols, 2 * HEAD :] = dv.astype(BF16)
    for i in range(count):
        rows = pl.ds(i * block, block)
        out_ref[rows, 0:HEAD] = unrotate(dq_ref[:, rows].T * scale, rows)


def attend(qkv, first_col, scale, shift):
    total = qkv.shape[0]
    pairs = total * total // 2
    return pl.pallas_call(
        functools.partial(attend_kernel, min(512, total), scale, shift),
        out_shape=jax.ShapeDtypeStruct((total, HEAD), BF16),
        compiler_params=pltpu.CompilerParams(vmem_limit_bytes=40 * 2**20),
        cost_estimate=pl.CostEstimate(
            flops=4 * pairs * HEAD, bytes_accessed=total * HEAD * 8, transcendentals=2 * pairs
        ),
        name="attend",
    )(qkv, first_col)


def attend_back(qkv, grads, first_row, cos_full, sin_full, scale, shift):
    total = qkv.shape[0]
    pairs = total * total // 2
    return pl.pallas_call(
        functools.partial(attend_back_kernel, min(512, total), scale, shift),
        out_shape=jax.ShapeDtypeStruct((total, 3 * HEAD), BF16),
        scratch_shapes=[pltpu.VMEM((HEAD, total), F32)],
        compiler_params=pltpu.CompilerParams(vmem_limit_bytes=40 * 2**20),
        cost_estimate=pl.CostEstimate(
            flops=10 * pairs * HEAD, bytes_accessed=total * HEAD * 20, transcendentals=2 * pairs
        ),
        name="attend_back",
    )(qkv, grads, first_row, cos_full, sin_full)


def first_visible(ids):
    at = jnp.arange(ids.shape[-1], dtype=jnp.int32)
    starts = jnp.concatenate([jnp.ones_like(ids[..., :1], jnp.bool_), ids[..., 1:] != ids[..., :-1]], axis=-1)
    return lax.cummax(jnp.where(starts, at, 0), axis=ids.ndim - 1)


def exchange(blocks):
    return lax.all_to_all(blocks, "dp", split_axis=0, concat_axis=0, tiled=True)


def sliced_scores(qkv, kv_all, first, positions, scale, shift):
    raw = jnp.einsum("pqd,pkd->pqk", qkv[..., :HEAD], kv_all[..., :HEAD], preferred_element_type=F32)
    at = jnp.arange(kv_all.shape[1], dtype=jnp.int32)
    visible = (at >= first[..., None]) & (at <= positions[:, None])
    return jnp.where(visible, sigmoid_of(raw, scale, shift), 0.0)


def per_device(
    inputs,
    cotangent,
    doc_ids,
    gain_attn,
    w_query,
    w_key,
    w_value,
    w_out,
    gain_ffn,
    w_gate,
    w_up,
    w_down,
):
    dp_size = lax.axis_size("dp")
    mp_size = lax.axis_size("mp")
    micro_count, row_count, seq_count, width = inputs.shape
    slice_len = row_count * mp_size
    total_len = slice_len * dp_size
    rows_here = row_count * seq_count
    shift = math.log(total_len)
    scale = HEAD ** (-0.5)
    dp_at = lax.axis_index("dp")
    first_row = dp_at * slice_len
    positions = first_row + jnp.arange(slice_len, dtype=jnp.int32)
    head_width = w_query.shape[1]
    heads = head_width // HEAD
    hidden = w_gate.shape[1]
    pairs = seq_count * heads
    whole_pairs = pairs == dp_size
    cos_slice, sin_slice = full_tables(positions)
    cos_all, sin_all = full_tables(jnp.arange(total_len, dtype=jnp.int32))
    first_all = first_visible(doc_ids)

    def by_row(table):
        shaped = table.reshape(mp_size, 1, row_count, 1, HEAD)
        return jnp.broadcast_to(shaped, (mp_size, seq_count, row_count, 1, HEAD))

    def rotate(values, back=False):
        sine = -by_row(sin_slice) if back else by_row(sin_slice)
        return values * by_row(cos_slice) + swap_halves(values) * sine

    def to_pairs(values):
        shaped = values.reshape(mp_size, seq_count, row_count, heads, -1)
        return shaped.transpose(1, 3, 0, 2, 4).reshape(pairs, slice_len, -1)

    def from_pairs(values):
        shaped = values.reshape(seq_count, heads, mp_size, row_count, -1)
        return shaped.transpose(2, 0, 3, 1, 4).reshape(mp_size * rows_here, heads, -1)

    def to_rows(values):
        return jnp.swapaxes(values, 0, 1).reshape(rows_here, width)

    def from_rows(values):
        return jnp.swapaxes(values.reshape(seq_count, row_count, width), 0, 1)

    def gather_mp(values):
        return lax.all_gather(values, "mp", axis=0, tiled=True)

    def scatter_mp(values):
        return lax.psum_scatter(values, "mp", scatter_dimension=0, tiled=True).astype(F32)

    qkv_full = lax.all_gather(
        jnp.concatenate([w_query, w_key, w_value], axis=1), "dp", axis=0, tiled=True
    )
    out_full = lax.all_gather(w_out, "dp", axis=1, tiled=True)
    gate_full = lax.all_gather(w_gate, "dp", axis=0, tiled=True)
    up_full = lax.all_gather(w_up, "dp", axis=0, tiled=True)
    down_full = lax.all_gather(w_down, "dp", axis=1, tiled=True)

    grad_qkv = jnp.zeros((width, 3 * head_width), F32)
    grad_out_w = jnp.zeros((head_width, width), F32)
    grad_gate_w = jnp.zeros((width, hidden), F32)
    grad_up_w = jnp.zeros((width, hidden), F32)
    grad_down_w = jnp.zeros((hidden, width), F32)
    gain_attn_grad = jnp.zeros((width,), F32)
    gain_ffn_grad = jnp.zeros((width,), F32)
    results = []
    input_grads = []
    for micro in range(micro_count):
        local_rows = to_rows(inputs[micro]).astype(F32)
        local_cot = to_rows(cotangent[micro])
        factor_one = norm_factor(local_rows)
        rows_one = gather_mp((local_rows * factor_one * gain_attn).astype(BF16))
        projected = dot(rows_one, qkv_full).reshape(
            mp_size, seq_count, row_count, 3, heads, HEAD
        )
        packed = jnp.concatenate(
            [
                rotate(projected[:, :, :, 0]).astype(BF16),
                rotate(projected[:, :, :, 1]).astype(BF16),
                projected[:, :, :, 2].astype(BF16),
            ],
            axis=-1,
        )
        packed = to_pairs(packed)
        if whole_pairs:
            qkv = exchange(packed).reshape(total_len, 3 * HEAD)
            first = lax.dynamic_index_in_dim(first_all[micro], dp_at // heads, 0, keepdims=False)
            attended = attend(qkv, first[:, None], scale, shift)
            attended = exchange(attended.reshape(dp_size, slice_len, HEAD))
        else:
            kv_all = lax.all_gather(packed[..., HEAD:], "dp", axis=1, tiled=True)
            first = lax.dynamic_slice_in_dim(first_all[micro], first_row, slice_len, 1)
            first = jnp.repeat(first, heads, axis=0)
            weights = sliced_scores(packed, kv_all, first, positions, scale, shift)
            attended = jnp.einsum(
                "pqk,pkd->pqd", weights.astype(BF16), kv_all[..., HEAD:], preferred_element_type=F32
            ).astype(BF16)
        mixture = from_pairs(attended).reshape(mp_size * rows_here, head_width)
        middle = local_rows + scatter_mp(dot(mixture, out_full).astype(BF16))
        factor_two = norm_factor(middle)
        rows_two = gather_mp((middle * factor_two * gain_ffn).astype(BF16))
        gate_value = dot(rows_two, gate_full)
        up_value = dot(rows_two, up_full)
        sig_gate = jax.nn.sigmoid(gate_value)
        silu_gate = gate_value * sig_gate
        activated = (silu_gate * up_value).astype(BF16)
        block_output = middle + scatter_mp(dot(activated, down_full).astype(BF16))
        results.append(from_rows(block_output.astype(BF16)))

        portion = gather_mp(local_cot)
        act_grad = dot_nt(portion, down_full)
        grad_down_w = grad_down_w + dot_tn(activated, portion)
        gate_grad = (act_grad * up_value * sig_gate * (1.0 + gate_value * (1.0 - sig_gate))).astype(BF16)
        up_grad = (act_grad * silu_gate).astype(BF16)
        grad_gate_w = grad_gate_w + dot_tn(rows_two, gate_grad)
        grad_up_w = grad_up_w + dot_tn(rows_two, up_grad)
        normed_grad_two = scatter_mp(
            (dot_nt(gate_grad, gate_full) + dot_nt(up_grad, up_full)).astype(BF16)
        )
        middle_term, gain_part = norm_back(middle, factor_two, gain_ffn, normed_grad_two)
        gain_ffn_grad = gain_ffn_grad + gain_part
        middle_grad = local_cot.astype(F32) + middle_term
        attn_portion = gather_mp(middle_grad.astype(BF16))
        grad_out_w = grad_out_w + dot_tn(mixture, attn_portion)
        mix_grad = to_pairs(dot_nt(attn_portion, out_full).astype(BF16))
        if whole_pairs:
            mix_grad = exchange(mix_grad).reshape(total_len, HEAD)
            proj_grad = attend_back(qkv, mix_grad, first[None, :], cos_all, sin_all, scale, shift)
            proj_grad = exchange(proj_grad.reshape(dp_size, slice_len, 3 * HEAD))
            proj_grad = from_pairs(proj_grad)
        else:
            sig = sliced_scores(packed, kv_all, first, positions, scale, shift)
            prob_grad = jnp.einsum(
                "pqd,pkd->pqk", mix_grad, kv_all[..., HEAD:], preferred_element_type=F32
            )
            score_grad = (prob_grad * sig * (1.0 - sig)).astype(BF16)
            dq = jnp.einsum("pqk,pkd->pqd", score_grad, kv_all[..., :HEAD], preferred_element_type=F32)
            dk = jnp.einsum("pqk,pqd->pkd", score_grad, packed[..., :HEAD], preferred_element_type=F32)
            dv = jnp.einsum("pqk,pqd->pkd", sig.astype(BF16), mix_grad, preferred_element_type=F32)
            dkv = lax.psum_scatter(
                jnp.concatenate([dk * scale, dv], axis=-1).astype(BF16), "dp", scatter_dimension=1, tiled=True
            ).astype(F32)
            back = from_pairs(jnp.concatenate([dq * scale, dkv], axis=-1))
            back = back.reshape(mp_size, seq_count, row_count, heads, 3 * HEAD)
            proj_grad = jnp.concatenate(
                [
                    rotate(back[..., :HEAD], True),
                    rotate(back[..., HEAD : 2 * HEAD], True),
                    back[..., 2 * HEAD :],
                ],
                axis=-1,
            ).astype(BF16).reshape(mp_size * rows_here, heads, 3 * HEAD)
        proj_grad = jnp.swapaxes(
            proj_grad.reshape(mp_size * rows_here, heads, 3, HEAD), 1, 2
        ).reshape(mp_size * rows_here, 3 * head_width)
        grad_qkv = grad_qkv + dot_tn(rows_one, proj_grad)
        normed_grad_one = scatter_mp(dot_nt(proj_grad, qkv_full).astype(BF16))
        input_term, gain_part = norm_back(local_rows, factor_one, gain_attn, normed_grad_one)
        gain_attn_grad = gain_attn_grad + gain_part
        input_grads.append(from_rows(middle_grad + input_term))

    def scatter_dp(values, dimension):
        return lax.psum_scatter(
            values.astype(BF16), "dp", scatter_dimension=dimension, tiled=True
        ).astype(F32)

    sum_gate = scatter_dp(grad_gate_w, 0)
    sum_up = scatter_dp(grad_up_w, 0)
    sum_down = scatter_dp(grad_down_w, 1)
    sum_out = scatter_dp(grad_out_w, 1)
    sum_qkv = scatter_dp(grad_qkv, 0)
    gain_sums = lax.psum(jnp.stack([gain_attn_grad, gain_ffn_grad]), ("dp", "mp"))
    return (
        jnp.stack(results),
        jnp.stack(input_grads),
        gain_sums[0],
        sum_qkv[:, :head_width],
        sum_qkv[:, head_width : 2 * head_width],
        sum_qkv[:, 2 * head_width :],
        sum_out,
        gain_sums[1],
        sum_gate,
        sum_up,
        sum_down,
    )


def solution(mesh):
    tokens = P(None, ("dp", "mp"), None, None)
    column = P("dp", "mp")
    row = P("mp", "dp")
    return jax.shard_map(
        per_device,
        mesh=mesh,
        in_specs=(
            tokens, tokens, P(), P(), column, column, column, row, P(), column, column, row,
        ),
        out_specs=(
            tokens, tokens, P(), column, column, column, row, P(), column, column, row,
        ),
        check_vma=False,
    )
```

```python
import functools
import math

import jax
import jax.numpy as jnp
from jax import lax
from jax.experimental import pallas as pl
from jax.experimental.pallas import tpu as pltpu
from jax.sharding import PartitionSpec as P

HEAD = 128
epsilon = 1e-05
rope_base = 10000.0
F32 = jnp.float32
BF16 = jnp.bfloat16


def rope_tables(positions):
    half_size = HEAD // 2
    inverse = jnp.power(rope_base, -(jnp.arange(half_size, dtype=F32) * 2.0 / HEAD))
    angles = positions.astype(F32)[:, None] * inverse[None, :]
    return (jnp.cos(angles), jnp.sin(angles))


def full_tables(positions):
    cosine, sine = rope_tables(positions)
    return (
        jnp.concatenate([cosine, cosine], axis=-1),
        jnp.concatenate([-sine, sine], axis=-1),
    )


def swap_halves(values):
    half_size = HEAD // 2
    return jnp.concatenate([values[..., half_size:], values[..., :half_size]], axis=-1)


def dot(left, right):
    return jnp.dot(left, right, preferred_element_type=F32)


def dot_tn(left, right):
    return lax.dot_general(left, right, (((0,), (0,)), ((), ())), preferred_element_type=F32)


def dot_nt(left, right):
    return lax.dot_general(left, right, (((1,), (1,)), ((), ())), preferred_element_type=F32)


def norm_factor(values):
    return lax.rsqrt(jnp.mean(values * values, axis=-1, keepdims=True) + epsilon)


def norm_back(values, factor, gain, incoming):
    scaled = incoming * gain
    gain_term = jnp.sum(incoming * values * factor, axis=0)
    input_term = factor * scaled - values * factor**3 * jnp.mean(
        scaled * values, axis=-1, keepdims=True
    )
    return (input_term, gain_term)


def sigmoid_of(raw, scale, shift):
    return 1.0 / (1.0 + jnp.exp(shift - raw * scale))


def join_blocks(at_ref, refs, joined):
    rows = refs[0].shape[0]
    for k, ref in enumerate(refs):
        start = pl.multiple_of((at_ref[0] ^ k) * rows, rows)
        joined[pl.ds(start, rows), :] = ref[...]


def split_blocks(at_ref, joined, refs):
    rows = refs[0].shape[0]
    for k, ref in enumerate(refs):
        start = pl.multiple_of((at_ref[0] ^ k) * rows, rows)
        ref[...] = joined[pl.ds(start, rows), :]


def attend_kernel(count, block, scale, shift, at_ref, *refs):
    qkv_refs, (first_ref,) = refs[:count], refs[count : count + 1]
    out_refs, (qkv_ref, out_ref) = refs[count + 1 : 2 * count + 1], refs[2 * count + 1 :]
    join_blocks(at_ref, qkv_refs, qkv_ref)
    total = qkv_ref.shape[0]
    row_at = lax.broadcasted_iota(jnp.int32, (block, block), 0)
    col_at = lax.broadcasted_iota(jnp.int32, (block, block), 1)

    def at_block(index):
        return pl.ds(pl.multiple_of(index * block, block), block)

    @pl.loop(0, total // block)
    def _(i):
        rows = at_block(i)
        queries = qkv_ref[rows, 0:HEAD]
        first = first_ref[rows, :]

        def add_block(j, acc, diagonal=False):
            cols = at_block(j)
            sig = sigmoid_of(dot_nt(queries, qkv_ref[cols, HEAD : 2 * HEAD]), scale, shift)
            visible = col_at >= first - j * block
            if diagonal:
                visible = visible & (col_at <= row_at)
            weights = jnp.where(visible, sig, 0.0).astype(BF16)
            return acc + dot(weights, qkv_ref[cols, 2 * HEAD :])

        acc = add_block(i, jnp.zeros((block, HEAD), F32), True)
        out_ref[rows, :] = lax.fori_loop(0, i, add_block, acc).astype(BF16)

    split_blocks(at_ref, out_ref, out_refs)


def attend_back_kernel(parts, block, scale, shift, at_ref, *refs):
    qkv_refs, grad_refs, refs = refs[:parts], refs[parts : 2 * parts], refs[2 * parts :]
    (first_ref, cos_ref, sin_ref), refs = refs[:3], refs[3:]
    out_refs, (qkv_ref, grad_ref, out_ref, dq_ref) = refs[:parts], refs[parts:]
    join_blocks(at_ref, qkv_refs, qkv_ref)
    join_blocks(at_ref, grad_refs, grad_ref)
    total = qkv_ref.shape[0]
    count = total // block

    def unrotate(values, rows):
        swapped = pltpu.roll(values, HEAD // 2, 1)
        return (values * cos_ref[rows, :] - swapped * sin_ref[rows, :]).astype(BF16)

    def at_block(index):
        return pl.ds(pl.multiple_of(index * block, block), block)

    col_at = lax.broadcasted_iota(jnp.int32, (block, block), 0)
    row_at = lax.broadcasted_iota(jnp.int32, (block, block), 1)
    dq_ref[...] = jnp.zeros_like(dq_ref)

    @pl.loop(0, count)
    def _(j):
        cols = at_block(j)
        keys = qkv_ref[cols, HEAD : 2 * HEAD]
        values = qkv_ref[cols, 2 * HEAD :]
        keys_t = keys.T

        def add_block(i, sums, diagonal=False):
            dk, dv = sums
            rows = at_block(i)
            queries = qkv_ref[rows, 0:HEAD]
            grads = grad_ref[rows, :]
            sig = sigmoid_of(dot_nt(keys, queries), scale, shift)
            visible = col_at >= first_ref[:, rows] - j * block
            if diagonal:
                visible = visible & (col_at <= row_at)
            sig = jnp.where(visible, sig, 0.0)
            prob_grad = dot_nt(values, grads)
            score_grad = (prob_grad * sig * (1.0 - sig)).astype(BF16)
            dq_ref[:, rows] += dot(keys_t, score_grad)
            return dk + dot(score_grad, queries), dv + dot(sig.astype(BF16), grads)

        zero = jnp.zeros((block, HEAD), F32)
        dk, dv = lax.fori_loop(j + 1, count, add_block, add_block(j, (zero, zero), True))
        out_ref[cols, HEAD : 2 * HEAD] = unrotate(dk * scale, cols)
        out_ref[cols, 2 * HEAD :] = dv.astype(BF16)

    @pl.loop(0, count)
    def _(i):
        rows = at_block(i)
        out_ref[rows, 0:HEAD] = unrotate(dq_ref[:, rows].T * scale, rows)

    split_blocks(at_ref, out_ref, out_refs)


def split_cores(core, values, rows_here):
    shaped = values.reshape(-1, 2, rows_here, values.shape[-1])
    first, second = shaped[:, 0], shaped[:, 1]
    is_first = core == 0
    return jnp.where(is_first, first, second), jnp.where(is_first, second, first)


def project_kernel(heads, toks, at_ref, rows_ref, weight_ref, cos_ref, sin_ref, *refs):
    out_refs, (made, paired) = refs[:-2], refs[-2:]
    pairs, slice_len = paired.shape[:2]
    seqs = pairs // heads
    owner_rows = toks * seqs
    step = min(512, rows_ref.shape[0])

    @pl.loop(0, rows_ref.shape[0] // step)
    def _(i):
        rows = pl.ds(pl.multiple_of(i * step, step), step)
        made[...] = dot(rows_ref[rows, :], weight_ref[...])
        for j in range(step // owner_rows):
            to = pl.ds(pl.multiple_of((i * (step // owner_rows) + j) * toks, toks), toks)
            cosine, sine = cos_ref[to, :], sin_ref[to, :]
            for p in range(pairs):
                s, h = p // heads, p % heads
                here = pl.ds(j * owner_rows + s * toks, toks)
                for part in range(3):
                    piece = made[here, pl.ds((part * heads + h) * HEAD, HEAD)]
                    if part < 2:
                        piece = piece * cosine + pltpu.roll(piece, HEAD // 2, 1) * sine
                    paired[p, to, part * HEAD : (part + 1) * HEAD] = piece.astype(BF16)

    for k, ref in enumerate(out_refs):
        ref[...] = paired[at_ref[0] ^ k]


def out_kernel(heads, toks, rows_here, at_ref, *refs):
    pairs = len(refs) - 6
    blocks, (weight_ref, keep_ref, send_ref, mix_ref, paired, _) = refs[:pairs], refs[pairs:]
    for k, ref in enumerate(blocks):
        paired[at_ref[0] ^ k] = ref[...]
    total = mix_ref.shape[0]
    owner_rows = toks * (pairs // heads)
    for o in range(total // owner_rows):
        for p in range(pairs):
            s, h = p // heads, p % heads
            mix_ref[pl.ds(o * owner_rows + s * toks, toks), h * HEAD : (h + 1) * HEAD] = paired[
                p, pl.ds(o * toks, toks), :
            ]
    step = 2 * rows_here

    @pl.loop(0, total // step)
    def _(i):
        rows = pl.ds(pl.multiple_of(i * step, step), step)
        made = dot(mix_ref[rows, :], weight_ref[...]).astype(BF16)
        keep, send = split_cores(at_ref[1], made, rows_here)
        keep_ref[pl.ds(i, 1)] = keep
        send_ref[pl.ds(i, 1)] = send


def out_back_kernel(heads, toks, at_ref, rows_ref, weight_ref, *refs):
    out_refs, (paired,) = refs[:-1], refs[-1:]
    pairs = len(out_refs)
    seqs = pairs // heads
    owner_rows = toks * seqs
    step = min(512, rows_ref.shape[0])

    @pl.loop(0, rows_ref.shape[0] // step)
    def _(i):
        rows = pl.ds(pl.multiple_of(i * step, step), step)
        made = dot_nt(rows_ref[rows, :], weight_ref[...]).astype(BF16)
        for j in range(step // owner_rows):
            to = pl.ds(pl.multiple_of((i * (step // owner_rows) + j) * toks, toks), toks)
            for p in range(pairs):
                s, h = p // heads, p % heads
                start = j * owner_rows + s * toks
                paired[p, to, :] = made[start : start + toks, h * HEAD : (h + 1) * HEAD]

    for k, ref in enumerate(out_refs):
        ref[...] = paired[at_ref[0] ^ k]


def project_back_kernel(heads, toks, rows_here, at_ref, *refs):
    pairs = len(refs) - 7
    blocks, refs = refs[:pairs], refs[pairs:]
    rows_ref, weight_ref, keep_ref, send_ref, proj_ref, gain_ref, paired = refs
    for k, ref in enumerate(blocks):
        paired[at_ref[0] ^ k] = ref[...]
    total = proj_ref.shape[0]
    owner_rows = toks * (pairs // heads)
    for o in range(total // owner_rows):
        for p in range(pairs):
            s, h = p // heads, p % heads
            for part in range(3):
                proj_ref[
                    pl.ds(o * owner_rows + s * toks, toks),
                    (part * heads + h) * HEAD : (part * heads + h + 1) * HEAD,
                ] = paired[p, pl.ds(o * toks, toks), part * HEAD : (part + 1) * HEAD]
    step = 2 * rows_here
    gain_ref[...] = jnp.zeros_like(gain_ref)

    @pl.loop(0, total // step)
    def _(i):
        rows = pl.ds(pl.multiple_of(i * step, step), step)
        made = dot_nt(proj_ref[rows, :], weight_ref[...])
        gain_ref[...] += jnp.sum(made * rows_ref[rows, :].astype(F32), axis=0, keepdims=True)
        keep, send = split_cores(at_ref[1], made.astype(BF16), rows_here)
        keep_ref[pl.ds(i, 1)] = keep
        send_ref[pl.ds(i, 1)] = send


def ffn_kernel(
    rows_here, at_ref, rows_ref, cot_ref, gate_ref, up_ref, down_ref,
    y_keep, y_send, dh_keep, dh_send, act_ref, dgate_ref, dup_ref,
):
    hidden = gate_ref.shape[1]
    width = rows_ref.shape[1]
    tile = min(256, hidden)

    @pl.loop(0, hidden // tile)
    def _(t):
        cols = pl.ds(pl.multiple_of(t * tile, tile), tile)
        gate = dot(rows_ref[...], gate_ref[:, cols])
        up = dot(rows_ref[...], up_ref[:, cols])
        sig = jax.nn.sigmoid(gate)
        silu = gate * sig
        act_ref[:, cols] = (silu * up).astype(BF16)
        grad = dot_nt(cot_ref[...], down_ref[cols, :])
        dgate_ref[:, cols] = (grad * up * sig * (1.0 + gate * (1.0 - sig))).astype(BF16)
        dup_ref[:, cols] = (grad * silu).astype(BF16)

    @pl.loop(0, width // 256)
    def _(t):
        cols = pl.ds(pl.multiple_of(t * 256, 256), 256)
        core = at_ref[1]
        y = dot(act_ref[...], down_ref[:, cols]).astype(BF16)
        y_keep[:, :, cols], y_send[:, :, cols] = split_cores(core, y, rows_here)
        dh = dot_nt(dgate_ref[...], gate_ref[cols, :]) + dot_nt(dup_ref[...], up_ref[cols, :])
        dh_keep[:, :, cols], dh_send[:, :, cols] = split_cores(core, dh.astype(BF16), rows_here)


def grad_kernel(count, _, *refs):
    lefts, rights, (out_ref, turned) = refs[:count], refs[count : 2 * count], refs[2 * count :]
    rows = lefts[0].shape[0]
    for m, left in enumerate(lefts):
        turned[:, m * rows : (m + 1) * rows] = left[...].T

    @pl.loop(0, out_ref.shape[1] // 256)
    def _(t):
        cols = pl.ds(pl.multiple_of(t * 256, 256), 256)
        total = dot(turned[:, :rows], rights[0][:, cols])
        for m in range(1, count):
            total += dot(turned[:, m * rows : (m + 1) * rows], rights[m][:, cols])
        out_ref[:, cols] = total.astype(BF16)


VMEM = pl.BlockSpec(memory_space=pltpu.VMEM)
SMEM = pl.BlockSpec(memory_space=pltpu.SMEM)


def cost(flops, nbytes):
    return pl.CostEstimate(flops=flops, bytes_accessed=nbytes, transcendentals=0)


def limits(mebibytes):
    return pltpu.CompilerParams(vmem_limit_bytes=mebibytes * 2**20)


def shape(*dims, dtype=BF16):
    return jax.ShapeDtypeStruct(dims, dtype)


def project(at, rows, weight, cosine, sine, heads, pairs, toks):
    slice_len = cosine.shape[0]
    total, width = rows.shape
    return pl.pallas_call(
        functools.partial(project_kernel, heads, toks),
        out_shape=[shape(slice_len, 3 * HEAD)] * pairs,
        in_specs=[SMEM] + [VMEM] * 4,
        out_specs=[VMEM] * pairs,
        scratch_shapes=[
            pltpu.VMEM((min(512, total), 3 * heads * HEAD), F32),
            pltpu.VMEM((pairs, slice_len, 3 * HEAD), BF16),
        ],
        compiler_params=limits(40),
        cost_estimate=cost(2 * total * width * 3 * heads * HEAD, 12 * 2**20),
        name="project",
    )(at, rows, weight, cosine, sine)


def project_out(at, blocks, weight, heads, toks, rows_here):
    pairs = len(blocks)
    slice_len = blocks[0].shape[0]
    total = slice_len * (pairs // heads)
    width = weight.shape[1]
    half = shape(total // (2 * rows_here), rows_here, width)
    return pl.pallas_call(
        functools.partial(out_kernel, heads, toks, rows_here),
        out_shape=[half, half, shape(total, heads * HEAD)],
        in_specs=[SMEM] + [VMEM] * (pairs + 1),
        out_specs=[VMEM] * 3,
        scratch_shapes=[pltpu.VMEM((pairs, slice_len, HEAD), BF16), pltpu.VMEM((8, HEAD), F32)],
        compiler_params=limits(40),
        cost_estimate=cost(2 * total * width * heads * HEAD, 7 * 2**20),
        name="project_out",
    )(at, *blocks, weight)


def project_out_back(at, rows, weight, heads, pairs, toks):
    total, width = rows.shape
    slice_len = total // (pairs // heads)
    return pl.pallas_call(
        functools.partial(out_back_kernel, heads, toks),
        out_shape=[shape(slice_len, HEAD)] * pairs,
        in_specs=[SMEM] + [VMEM] * 2,
        out_specs=[VMEM] * pairs,
        scratch_shapes=[pltpu.VMEM((pairs, slice_len, HEAD), BF16)],
        compiler_params=limits(40),
        cost_estimate=cost(2 * total * width * heads * HEAD, 7 * 2**20),
        name="project_out_back",
    )(at, rows, weight)


def project_back(at, blocks, rows, weight, heads, toks, rows_here):
    pairs = len(blocks)
    slice_len = blocks[0].shape[0]
    total, width = rows.shape
    half = shape(total // (2 * rows_here), rows_here, width)
    return pl.pallas_call(
        functools.partial(project_back_kernel, heads, toks, rows_here),
        out_shape=[half, half, shape(total, 3 * heads * HEAD), shape(1, width, dtype=F32)],
        in_specs=[SMEM] + [VMEM] * (pairs + 2),
        out_specs=[VMEM] * 4,
        scratch_shapes=[pltpu.VMEM((pairs, slice_len, 3 * HEAD), BF16)],
        compiler_params=limits(48),
        cost_estimate=cost(2 * total * width * 3 * heads * HEAD, 16 * 2**20),
        name="project_back",
    )(at, *blocks, rows, weight)


def ffn(at, rows, cot, gate, up, down, rows_here):
    total, width = rows.shape
    hidden = gate.shape[1]
    step = min(512, total)
    half = shape(total // (2 * rows_here), rows_here, width)
    by_rows = pl.BlockSpec((step, width), lambda i: (i, 0))
    by_hidden = pl.BlockSpec((step, hidden), lambda i: (i, 0))
    by_half = pl.BlockSpec((step // (2 * rows_here), rows_here, width), lambda i: (i, 0, 0))
    held = lambda array: pl.BlockSpec(array.shape, lambda i: (0, 0), pipeline_mode=pl.Buffered(1))
    return pl.pallas_call(
        functools.partial(ffn_kernel, rows_here),
        grid=(total // step,),
        out_shape=[half] * 4 + [shape(total, hidden)] * 3,
        in_specs=[SMEM, by_rows, by_rows, held(gate), held(up), held(down)],
        out_specs=[by_half] * 4 + [by_hidden] * 3,
        compiler_params=limits(56),
        cost_estimate=cost(12 * total * width * hidden, 34 * 2**20),
        name="ffn",
    )(at, rows, cot, gate, up, down)


def weight_grad(at, lefts, rights, step, left_blocked):
    count = len(lefts)
    size = lax.axis_size("dp")
    rows = lefts[0].shape[0]
    m, n = lefts[0].shape[1], rights[0].shape[1]
    moving = lambda width: pl.BlockSpec((rows, width // size), lambda i, at: (0, at[0] ^ step))
    fixed = lambda width: pl.BlockSpec((rows, width), lambda i, at: (0, 0))
    left_spec = moving(m) if left_blocked else fixed(m)
    right_spec = fixed(n) if left_blocked else moving(n)
    out = (m // size, n) if left_blocked else (m, n // size)
    return pl.pallas_call(
        functools.partial(grad_kernel, count),
        grid_spec=pltpu.PrefetchScalarGridSpec(
            num_scalar_prefetch=1,
            grid=(1,),
            in_specs=[left_spec] * count + [right_spec] * count,
            out_specs=pl.BlockSpec(out, lambda i, at: (0, 0)),
            scratch_shapes=[pltpu.VMEM((out[0], count * rows), BF16)],
        ),
        out_shape=shape(*out),
        compiler_params=limits(48),
        cost_estimate=cost(2 * count * rows * out[0] * out[1], 12 * 2**20),
        name="weight_grad",
    )(at, *lefts, *rights)


def summed_grad(at, lefts, rights, left_blocked):
    size = lax.axis_size("dp")
    received = []
    for step in range(size - 1, 0, -1):
        received.append(send_dp(weight_grad(at, lefts, rights, step, left_blocked), step))
    total = weight_grad(at, lefts, rights, 0, left_blocked).astype(F32)
    for block in received:
        total = total + block.astype(F32)
    return total


def attend(at, qkv, first_col, scale, shift):
    count = len(qkv)
    rows = qkv[0].shape[0]
    total = rows * count
    pairs = total * total // 2
    vmem = pl.BlockSpec(memory_space=pltpu.VMEM)
    return pl.pallas_call(
        functools.partial(attend_kernel, count, min(512, total), scale, shift),
        out_shape=[jax.ShapeDtypeStruct((rows, HEAD), BF16)] * count,
        in_specs=[pl.BlockSpec(memory_space=pltpu.SMEM)] + [vmem] * (count + 1),
        out_specs=[vmem] * count,
        scratch_shapes=[pltpu.VMEM((total, 3 * HEAD), BF16), pltpu.VMEM((total, HEAD), BF16)],
        compiler_params=pltpu.CompilerParams(vmem_limit_bytes=40 * 2**20),
        cost_estimate=pl.CostEstimate(
            flops=4 * pairs * HEAD, bytes_accessed=total * HEAD * 8, transcendentals=2 * pairs
        ),
        name="attend",
    )(at, *qkv, first_col)


def attend_back(at, qkv, grads, first_row, cos_full, sin_full, scale, shift):
    count = len(qkv)
    rows = qkv[0].shape[0]
    total = rows * count
    pairs = total * total // 2
    vmem = pl.BlockSpec(memory_space=pltpu.VMEM)
    return pl.pallas_call(
        functools.partial(attend_back_kernel, count, min(512, total), scale, shift),
        out_shape=[jax.ShapeDtypeStruct((rows, 3 * HEAD), BF16)] * count,
        in_specs=[pl.BlockSpec(memory_space=pltpu.SMEM)] + [vmem] * (2 * count + 3),
        out_specs=[vmem] * count,
        scratch_shapes=[
            pltpu.VMEM((total, 3 * HEAD), BF16),
            pltpu.VMEM((total, HEAD), BF16),
            pltpu.VMEM((total, 3 * HEAD), BF16),
            pltpu.VMEM((HEAD, total), F32),
        ],
        compiler_params=pltpu.CompilerParams(vmem_limit_bytes=40 * 2**20),
        cost_estimate=pl.CostEstimate(
            flops=10 * pairs * HEAD, bytes_accessed=total * HEAD * 20, transcendentals=2 * pairs
        ),
        name="attend_back",
    )(at, *qkv, *grads, first_row, cos_full, sin_full)


def first_visible(ids):
    at = jnp.arange(ids.shape[-1], dtype=jnp.int32)
    starts = jnp.concatenate([jnp.ones_like(ids[..., :1], jnp.bool_), ids[..., 1:] != ids[..., :-1]], axis=-1)
    return lax.cummax(jnp.where(starts, at, 0), axis=ids.ndim - 1)


def send_dp(values, step):
    size = lax.axis_size("dp")
    return lax.ppermute(values, "dp", [(i, i ^ step) for i in range(size)])


def exchange(own_first):
    return [own_first[0]] + [send_dp(block, k) for k, block in enumerate(own_first) if k]


def block_at(values, index):
    return lax.dynamic_index_in_dim(values, index, 0, keepdims=False)


def gather_dp(values, axis=0):
    at = lax.axis_index("dp")
    size = lax.axis_size("dp")
    shape = list(values.shape)
    step = shape[axis]
    shape[axis] = step * size
    full = jnp.zeros(shape, values.dtype)
    for k in range(size):
        block = send_dp(values, k) if k else values
        full = lax.dynamic_update_slice_in_dim(full, block, (at ^ k) * step, axis)
    return full


def scatter_mp(keep, send):
    size = lax.axis_size("mp")
    places = size // 2
    place = lax.axis_index("mp") // 2
    other = lax.ppermute(send, "mp", [(i, i ^ 1) for i in range(size)])
    mine = (keep.astype(F32) + other.astype(F32)).astype(BF16)
    right, left = None, None
    for step in range(1, places):
        to_right = block_at(mine, jnp.minimum(place + places - step, places - 1))
        to_left = block_at(mine, jnp.maximum(place - places + step, 0))
        if right is not None:
            to_right = (to_right.astype(F32) + right.astype(F32)).astype(BF16)
            to_left = (to_left.astype(F32) + left.astype(F32)).astype(BF16)
        hops = [(p, p + 1) for p in range(step)]
        right = lax.ppermute(
            to_right, "mp", [(2 * p + c, 2 * q + c) for p, q in hops for c in range(2)]
        )
        hops = [(places - 1 - p, places - 1 - q) for p, q in hops]
        left = lax.ppermute(
            to_left, "mp", [(2 * p + c, 2 * q + c) for p, q in hops for c in range(2)]
        )
    total = block_at(mine, place).astype(F32)
    return total + right.astype(F32) + left.astype(F32)


def sum_all(values):
    for name in ("dp", "mp"):
        size = lax.axis_size(name)
        step = 1
        while step < size:
            values = values + lax.ppermute(values, name, [(i, i ^ step) for i in range(size)])
            step *= 2
    return values


def sliced_scores(qkv, kv_all, first, positions, scale, shift):
    raw = jnp.einsum("pqd,pkd->pqk", qkv[..., :HEAD], kv_all[..., :HEAD], preferred_element_type=F32)
    at = jnp.arange(kv_all.shape[1], dtype=jnp.int32)
    visible = (at >= first[..., None]) & (at <= positions[:, None])
    return jnp.where(visible, sigmoid_of(raw, scale, shift), 0.0)


def per_device(
    inputs,
    cotangent,
    doc_ids,
    gain_attn,
    w_query,
    w_key,
    w_value,
    w_out,
    gain_ffn,
    w_gate,
    w_up,
    w_down,
):
    dp_size = lax.axis_size("dp")
    mp_size = lax.axis_size("mp")
    micro_count, row_count, seq_count, width = inputs.shape
    slice_len = row_count * mp_size
    total_len = slice_len * dp_size
    rows_here = row_count * seq_count
    shift = math.log(total_len)
    scale = HEAD ** (-0.5)
    dp_at = lax.axis_index("dp")
    mp_at = lax.axis_index("mp")
    first_row = dp_at * slice_len
    positions = first_row + jnp.arange(slice_len, dtype=jnp.int32)
    head_width = w_query.shape[1]
    heads = head_width // HEAD
    hidden = w_gate.shape[1]
    pairs = seq_count * heads
    whole_pairs = pairs == dp_size
    cos_slice, sin_slice = full_tables(positions)
    cos_all, sin_all = full_tables(jnp.arange(total_len, dtype=jnp.int32))
    first_all = first_visible(doc_ids)

    def by_row(table):
        shaped = table.reshape(mp_size, 1, row_count, 1, HEAD)
        return jnp.broadcast_to(shaped, (mp_size, seq_count, row_count, 1, HEAD))

    def rotate(values, back=False):
        sine = -by_row(sin_slice) if back else by_row(sin_slice)
        return values * by_row(cos_slice) + swap_halves(values) * sine

    def halves(values):
        return split_cores(mp_at % 2, values.astype(BF16), rows_here)

    def to_pairs(values):
        shaped = values.reshape(mp_size, seq_count, row_count, heads, -1)
        return shaped.transpose(1, 3, 0, 2, 4).reshape(pairs, slice_len, -1)

    def from_pairs(values):
        shaped = values.reshape(seq_count, heads, mp_size, row_count, -1)
        return shaped.transpose(2, 0, 3, 1, 4).reshape(mp_size * rows_here, heads, -1)

    def to_rows(values):
        return jnp.swapaxes(values, 0, 1).reshape(rows_here, width)

    def from_rows(values):
        return jnp.swapaxes(values.reshape(seq_count, row_count, width), 0, 1)

    def gather_mp(values):
        return lax.all_gather(values, "mp", axis=0, tiled=True)

    qkv_full = gather_dp(jnp.concatenate([w_query, w_key, w_value], axis=1))
    out_full = gather_dp(w_out, 1)
    gate_full = gather_dp(w_gate)
    up_full = gather_dp(w_up)
    down_full = gather_dp(w_down, 1)
    at_array = jnp.stack([dp_at, mp_at % 2]).astype(jnp.int32)
    gain_attn_grad = jnp.zeros((width,), F32)
    gain_ffn_grad = jnp.zeros((width,), F32)
    results = []
    input_grads = []
    kept = [[] for _ in range(9)]
    for micro in range(micro_count):
        local_rows = to_rows(inputs[micro]).astype(F32)
        local_cot = to_rows(cotangent[micro])
        factor_one = norm_factor(local_rows)
        rows_one = gather_mp((local_rows * factor_one * gain_attn).astype(BF16))
        if whole_pairs:
            packed = project(
                at_array, rows_one, qkv_full, cos_slice, sin_slice, heads, pairs, row_count
            )
            qkv = exchange(packed)
            first = block_at(first_all[micro], dp_at // heads)
            attended = exchange(attend(at_array, qkv, first[:, None], scale, shift))
            keep, send, mixture = project_out(
                at_array, attended, out_full, heads, row_count, rows_here
            )
        else:
            projected = dot(rows_one, qkv_full).reshape(
                mp_size, seq_count, row_count, 3, heads, HEAD
            )
            packed = to_pairs(
                jnp.concatenate(
                    [
                        rotate(projected[:, :, :, 0]).astype(BF16),
                        rotate(projected[:, :, :, 1]).astype(BF16),
                        projected[:, :, :, 2].astype(BF16),
                    ],
                    axis=-1,
                )
            )
            kv_all = lax.all_gather(packed[..., HEAD:], "dp", axis=1, tiled=True)
            first = lax.dynamic_slice_in_dim(first_all[micro], first_row, slice_len, 1)
            first = jnp.repeat(first, heads, axis=0)
            weights = sliced_scores(packed, kv_all, first, positions, scale, shift)
            attended = jnp.einsum(
                "pqk,pkd->pqd", weights.astype(BF16), kv_all[..., HEAD:], preferred_element_type=F32
            ).astype(BF16)
            mixture = from_pairs(attended).reshape(mp_size * rows_here, head_width)
            keep, send = halves(dot(mixture, out_full))
        middle = local_rows + scatter_mp(keep, send)
        factor_two = norm_factor(middle)
        rows_two = gather_mp((middle * factor_two * gain_ffn).astype(BF16))
        portion = gather_mp(local_cot)
        y_keep, y_send, dh_keep, dh_send, activated, gate_grad, up_grad = ffn(
            at_array, rows_two, portion, gate_full, up_full, down_full, rows_here
        )
        normed_grad_two = scatter_mp(dh_keep, dh_send)
        block_output = middle + scatter_mp(y_keep, y_send)
        results.append(from_rows(block_output.astype(BF16)))
        middle_term, gain_part = norm_back(middle, factor_two, gain_ffn, normed_grad_two)
        gain_ffn_grad = gain_ffn_grad + gain_part
        middle_grad = local_cot.astype(F32) + middle_term
        attn_portion = gather_mp(middle_grad.astype(BF16))
        if whole_pairs:
            mix_grad = exchange(
                project_out_back(at_array, attn_portion, out_full, heads, pairs, row_count)
            )
            proj_grad = exchange(
                attend_back(
                    at_array, qkv, mix_grad, first[None, :], cos_all, sin_all, scale, shift
                )
            )
            keep, send, proj_grad, gain_part = project_back(
                at_array, proj_grad, rows_one, qkv_full, heads, row_count, rows_here
            )
            gain_attn_grad = gain_attn_grad + gain_part[0]
        else:
            mix_grad = to_pairs(dot_nt(attn_portion, out_full).astype(BF16))
            sig = sliced_scores(packed, kv_all, first, positions, scale, shift)
            prob_grad = jnp.einsum(
                "pqd,pkd->pqk", mix_grad, kv_all[..., HEAD:], preferred_element_type=F32
            )
            score_grad = (prob_grad * sig * (1.0 - sig)).astype(BF16)
            dq = jnp.einsum("pqk,pkd->pqd", score_grad, kv_all[..., :HEAD], preferred_element_type=F32)
            dk = jnp.einsum("pqk,pqd->pkd", score_grad, packed[..., :HEAD], preferred_element_type=F32)
            dv = jnp.einsum("pqk,pqd->pkd", sig.astype(BF16), mix_grad, preferred_element_type=F32)
            dkv = lax.psum_scatter(
                jnp.concatenate([dk * scale, dv], axis=-1).astype(BF16), "dp", scatter_dimension=1, tiled=True
            ).astype(F32)
            back = from_pairs(jnp.concatenate([dq * scale, dkv], axis=-1))
            back = back.reshape(mp_size, seq_count, row_count, heads, 3 * HEAD)
            proj_grad = jnp.stack(
                [
                    rotate(back[..., :HEAD], True),
                    rotate(back[..., HEAD : 2 * HEAD], True),
                    back[..., 2 * HEAD :],
                ],
                axis=3,
            ).astype(BF16).reshape(mp_size * rows_here, 3 * head_width)
            partial_grad = dot_nt(proj_grad, qkv_full)
            gain_attn_grad = gain_attn_grad + jnp.sum(partial_grad * rows_one.astype(F32), axis=0)
            keep, send = halves(partial_grad)
        normed_grad_one = scatter_mp(keep, send)
        input_term, _ = norm_back(local_rows, factor_one, gain_attn, normed_grad_one)
        input_grads.append(from_rows(middle_grad + input_term))
        for held, array in zip(
            kept,
            (rows_one, proj_grad, mixture, attn_portion, rows_two, gate_grad, up_grad, activated, portion),
        ):
            held.append(array)

    ones, projs, mixtures, attns, twos, gates, ups, acts, portions = kept
    sum_gate = summed_grad(at_array, twos, gates, True)
    sum_up = summed_grad(at_array, twos, ups, True)
    sum_down = summed_grad(at_array, acts, portions, False)
    sum_out = summed_grad(at_array, mixtures, attns, False)
    sum_qkv = summed_grad(at_array, ones, projs, True)
    gain_sums = (sum_all(gain_attn_grad / gain_attn), sum_all(gain_ffn_grad))
    return (
        jnp.stack(results),
        jnp.stack(input_grads),
        gain_sums[0],
        sum_qkv[:, :head_width],
        sum_qkv[:, head_width : 2 * head_width],
        sum_qkv[:, 2 * head_width :],
        sum_out,
        gain_sums[1],
        sum_gate,
        sum_up,
        sum_down,
    )


def solution(mesh):
    tokens = P(None, ("dp", "mp"), None, None)
    column = P("dp", "mp")
    row = P("mp", "dp")
    return jax.shard_map(
        per_device,
        mesh=mesh,
        in_specs=(
            tokens, tokens, P(), P(), column, column, column, row, P(), column, column, row,
        ),
        out_specs=(
            tokens, tokens, P(), column, column, column, row, P(), column, column, row,
        ),
        check_vma=False,
    )
```

```python
import functools
import math

import jax
import jax.numpy as jnp
from jax import lax
from jax.experimental import pallas as pl
from jax.experimental.pallas import tpu as pltpu
from jax.sharding import PartitionSpec as P

HEAD = 128
epsilon = 1e-05
rope_base = 10000.0
F32 = jnp.float32
BF16 = jnp.bfloat16


def rope_tables(positions):
    half_size = HEAD // 2
    inverse = jnp.power(rope_base, -(jnp.arange(half_size, dtype=F32) * 2.0 / HEAD))
    angles = positions.astype(F32)[:, None] * inverse[None, :]
    return (jnp.cos(angles), jnp.sin(angles))


def full_tables(positions):
    cosine, sine = rope_tables(positions)
    return (
        jnp.concatenate([cosine, cosine], axis=-1),
        jnp.concatenate([-sine, sine], axis=-1),
    )


def swap_halves(values):
    half_size = HEAD // 2
    return jnp.concatenate([values[..., half_size:], values[..., :half_size]], axis=-1)


def dot(left, right):
    return jnp.dot(left, right, preferred_element_type=F32)


def dot_tn(left, right):
    return lax.dot_general(left, right, (((0,), (0,)), ((), ())), preferred_element_type=F32)


def dot_nt(left, right):
    return lax.dot_general(left, right, (((1,), (1,)), ((), ())), preferred_element_type=F32)


def norm_factor(values):
    return lax.rsqrt(jnp.mean(values * values, axis=-1, keepdims=True) + epsilon)


def norm_back(values, factor, gain, incoming):
    scaled = incoming * gain
    gain_term = jnp.sum(incoming * values * factor, axis=0)
    input_term = factor * scaled - values * factor**3 * jnp.mean(
        scaled * values, axis=-1, keepdims=True
    )
    return (input_term, gain_term)


def sigmoid_of(raw, scale, shift):
    return 1.0 / (1.0 + jnp.exp(shift - raw * scale))


def split_cores(core, values, rows_here):
    shaped = values.reshape(-1, 2, rows_here, values.shape[-1])
    first, second = shaped[:, 0], shaped[:, 1]
    is_first = core == 0
    return jnp.where(is_first, first, second), jnp.where(is_first, second, first)

MESH = pl.DeviceIdType.MESH


class Spot:
    def __init__(self):
        self.dp, self.mp = lax.axis_index("dp"), lax.axis_index("mp")
        self.dp_size, self.mp_size = lax.axis_size("dp"), lax.axis_size("mp")
        self.places = self.mp_size // 2
        self.place, self.core = lax.div(self.mp, 2), lax.rem(self.mp, 2)
        self.sibling = (self.dp, self.mp + 1 - 2 * self.core)
        self.right = (self.dp, self.mp + 2)
        self.left = (self.dp, self.mp - 2)
        self.has_right = self.place < self.places - 1
        self.has_left = self.place > 0

    def peer(self, step):
        return lax.rem(self.dp + step, self.dp_size)

    def enter(self, with_dp):
        barrier = pltpu.get_barrier_semaphore()

        def greet(device):
            pl.semaphore_signal(barrier, inc=1, device_id=device, device_id_type=MESH)

        greet(self.sibling)
        pl.when(self.has_right)(lambda: greet(self.right))
        pl.when(self.has_left)(lambda: greet(self.left))
        if with_dp:
            for step in range(1, self.dp_size):
                greet((self.peer(step), self.mp))
        neighbours = self.has_right.astype(jnp.int32) + self.has_left.astype(jnp.int32)
        pl.semaphore_wait(barrier, neighbours + (self.dp_size if with_dp else 1))


class Swap:
    def __init__(self, spot, source, target, send, receive):
        self.spot, self.source, self.target = spot, source, target
        self.copies = [
            pltpu.make_async_remote_copy(
                src_ref=source.at[spot.peer(step)],
                dst_ref=target.at[spot.dp],
                send_sem=send.at[step],
                recv_sem=receive.at[step],
                device_id=(spot.peer(step), spot.mp),
                device_id_type=MESH,
            )
            for step in range(1, spot.dp_size)
        ]

    def start(self):
        for copy in self.copies:
            copy.start()
        self.target[self.spot.dp] = self.source[self.spot.dp]

    def wait(self):
        for copy in self.copies:
            copy.wait()


def swap_scratch(size, *block):
    return [
        pltpu.VMEM((size, *block), BF16),
        pltpu.VMEM((size, *block), BF16),
        pltpu.SemaphoreType.DMA((size,)),
        pltpu.SemaphoreType.DMA((size,)),
    ]


def far_first(places):
    orders = []
    for place in range(places):
        right, left, order = list(range(places - 1, place, -1)), list(range(place)), []
        while right or left:
            order += right[:1] + left[:1]
            right, left = right[1:], left[1:]
        orders.append(order + [place])
    rounds = []
    for q in range(places - 1):
        at = [order.index(places - 1 - q) for p, order in enumerate(orders) if p < places - 1 - q]
        at += [order.index(q) for p, order in enumerate(orders) if p > q]
        rounds.append(max(at))
    return orders, rounds


class Sum:
    def __init__(self, spot, mine, out, from_sibling, from_left, from_right, sems):
        self.spot = spot
        self.mine, self.out = mine, out
        self.from_sibling, self.from_left, self.from_right = from_sibling, from_left, from_right
        self.sems = sems
        self.orders, self.rounds = far_first(spot.places)

    def copy(self, source, target, kind, t, device):
        return pltpu.make_async_remote_copy(
            src_ref=source.at[t],
            dst_ref=target.at[t],
            send_sem=self.sems.at[kind, t],
            recv_sem=self.sems.at[kind + 1, t],
            device_id=device,
            device_id_type=MESH,
        )

    def sibling(self, t):
        return self.copy(self.out, self.from_sibling, 0, t, self.spot.sibling)

    def rightward(self, t):
        return self.copy(self.mine, self.from_left, 2, t, self.spot.right)

    def leftward(self, t):
        return self.copy(self.mine, self.from_right, 4, t, self.spot.left)

    def term(self, s):
        chosen = 0
        for place, order in enumerate(self.orders):
            for at, t in enumerate(order):
                if t:
                    chosen = chosen + jnp.where((self.spot.place == place) & (s == at), t, 0)
        return chosen

    def add(self, t, arrived):
        self.mine[t] = (self.mine[t].astype(F32) + arrived[t].astype(F32)).astype(BF16)

    def absorb(self, t):
        self.sibling(t).wait_recv()
        self.add(t, self.from_sibling)

    def go_on(self, q):
        spot = self.spot
        to_right, to_left = spot.places - 1 - q, q

        @pl.when(spot.place < to_right)
        def _():
            self.absorb(to_right)

            @pl.when(spot.has_left)
            def _():
                self.rightward(to_right).wait_recv()
                self.add(to_right, self.from_left)

            self.rightward(to_right).start()

        @pl.when(spot.place > to_left)
        def _():
            self.absorb(to_left)

            @pl.when(spot.has_right)
            def _():
                self.leftward(to_left).wait_recv()
                self.add(to_left, self.from_right)

            self.leftward(to_left).start()

    def finish(self):
        spot = self.spot
        t = spot.place
        self.absorb(t)

        @pl.when(spot.has_left)
        def _():
            self.rightward(t).wait_recv()
            self.add(t, self.from_left)

        @pl.when(spot.has_right)
        def _():
            self.leftward(t).wait_recv()
            self.add(t, self.from_right)

        for t in range(spot.places):
            self.sibling(t).wait_send()
            pl.when(spot.place < t)(lambda: self.rightward(t).wait_send())
            pl.when(spot.place > t)(lambda: self.leftward(t).wait_send())
        return self.mine[spot.place].astype(F32)


def sum_scratch(places, rows_here, width):
    return [pltpu.VMEM((places, rows_here, width), BF16)] * 5 + [
        pltpu.SemaphoreType.DMA((6, places))
    ]


def attend_blocks(qkv, first_ref, out, scale, shift):
    count, block = out.shape[:2]
    row_at = lax.broadcasted_iota(jnp.int32, (block, block), 0)
    col_at = lax.broadcasted_iota(jnp.int32, (block, block), 1)

    @pl.loop(0, count)
    def _(i):
        queries = qkv[i, :, 0:HEAD]
        first = first_ref[pl.ds(pl.multiple_of(i * block, block), block), :]

        def add_block(j, acc, diagonal=False):
            sig = sigmoid_of(dot_nt(queries, qkv[j, :, HEAD : 2 * HEAD]), scale, shift)
            visible = col_at >= first - j * block
            if diagonal:
                visible = visible & (col_at <= row_at)
            weights = jnp.where(visible, sig, 0.0).astype(BF16)
            return acc + dot(weights, qkv[j, :, 2 * HEAD :])

        acc = add_block(i, jnp.zeros((block, HEAD), F32), True)
        out[i] = lax.fori_loop(0, i, add_block, acc).astype(BF16)


def attend_back_blocks(qkv, grad, first_ref, cos_ref, sin_ref, out, dq, scale, shift):
    count, block = grad.shape[:2]
    col_at = lax.broadcasted_iota(jnp.int32, (block, block), 0)
    row_at = lax.broadcasted_iota(jnp.int32, (block, block), 1)
    dq[...] = jnp.zeros_like(dq)

    def unrotate(values, i):
        rows = pl.ds(pl.multiple_of(i * block, block), block)
        swapped = pltpu.roll(values, HEAD // 2, 1)
        return (values * cos_ref[rows, :] - swapped * sin_ref[rows, :]).astype(BF16)

    @pl.loop(0, count)
    def _(j):
        keys = qkv[j, :, HEAD : 2 * HEAD]
        values = qkv[j, :, 2 * HEAD :]
        keys_t = keys.T

        def add_block(i, sums, diagonal=False):
            dk, dv = sums
            queries, grads = qkv[i, :, 0:HEAD], grad[i]
            sig = sigmoid_of(dot_nt(keys, queries), scale, shift)
            visible = col_at >= first_ref[i] - j * block
            if diagonal:
                visible = visible & (col_at <= row_at)
            sig = jnp.where(visible, sig, 0.0)
            prob_grad = dot_nt(values, grads)
            score_grad = (prob_grad * sig * (1.0 - sig)).astype(BF16)
            dq[i] += dot(keys_t, score_grad)
            return dk + dot(score_grad, queries), dv + dot(sig.astype(BF16), grads)

        zero = jnp.zeros((block, HEAD), F32)
        dk, dv = lax.fori_loop(j + 1, count, add_block, add_block(j, (zero, zero), True))
        out[j, :, HEAD : 2 * HEAD] = unrotate(dk * scale, j)
        out[j, :, 2 * HEAD :] = dv.astype(BF16)

    @pl.loop(0, count)
    def _(i):
        out[i, :, 0:HEAD] = unrotate(dq[i].T * scale, i)


def forward_kernel(
    heads, toks, scale, shift,
    rows_ref, weight_ref, out_weight_ref, cos_ref, sin_ref, first_ref, x_ref, gain_ref,
    middle_ref, normed_ref, qkv_ref, mix_ref,
    made, paired, qkv, qkv_send, qkv_recv, part, got, part_send, part_recv, *sum_refs,
):
    spot = Spot()
    spot.enter(True)
    pairs, slice_len = paired.shape[:2]
    seqs = pairs // heads
    owner_rows = toks * seqs
    total = rows_ref.shape[0]
    step = made.shape[0]

    @pl.loop(0, total // step)
    def _(i):
        rows = pl.ds(pl.multiple_of(i * step, step), step)
        made[...] = dot(rows_ref[rows, :], weight_ref[...])
        for j in range(step // owner_rows):
            to = pl.ds(pl.multiple_of((i * (step // owner_rows) + j) * toks, toks), toks)
            cosine, sine = cos_ref[to, :], sin_ref[to, :]
            for p in range(pairs):
                s, h = p // heads, p % heads
                here = pl.ds(j * owner_rows + s * toks, toks)
                for kind in range(3):
                    piece = made[here, pl.ds((kind * heads + h) * HEAD, HEAD)]
                    if kind < 2:
                        piece = piece * cosine + pltpu.roll(piece, HEAD // 2, 1) * sine
                    paired[p, to, kind * HEAD : (kind + 1) * HEAD] = piece.astype(BF16)

    swap = Swap(spot, paired, qkv, qkv_send, qkv_recv)
    swap.start()
    swap.wait()
    attend_blocks(qkv, first_ref, part, scale, shift)
    swap = Swap(spot, part, got, part_send, part_recv)
    swap.start()
    qkv_ref[...] = qkv[...]
    swap.wait()
    for o in range(total // owner_rows):
        for p in range(pairs):
            s, h = p // heads, p % heads
            mix_ref[pl.ds(o * owner_rows + s * toks, toks), h * HEAD : (h + 1) * HEAD] = got[
                p, pl.ds(o * toks, toks), :
            ]
    summed = Sum(spot, *sum_refs)
    chip_rows = 2 * owner_rows

    @pl.loop(0, spot.places)
    def _(s):
        t = summed.term(s)
        rows = pl.ds(pl.multiple_of(t * chip_rows, chip_rows), chip_rows)
        value = dot(mix_ref[rows, :], out_weight_ref[...]).astype(BF16)
        keep, send = split_cores(spot.core, value, owner_rows)
        summed.mine[t] = keep[0]
        summed.out[t] = send[0]
        summed.sibling(t).start()

    for q in range(spot.places - 1):
        summed.go_on(q)
    middle = x_ref[...].astype(F32) + summed.finish()
    middle_ref[...] = middle
    normed_ref[...] = (middle * norm_factor(middle) * gain_ref[...]).astype(BF16)


def middle_kernel(
    owner_rows,
    rows_ref, cot_ref, gate_ref, up_ref, down_ref, middle_ref, local_cot_ref, gain_ref,
    y_ref, act_ref, dgate_ref, dup_ref, grad_ref, low_ref, gain_grad_ref,
    *sum_refs,
):
    spot = Spot()
    spot.enter(False)
    summed = Sum(spot, *sum_refs)
    hidden, width = gate_ref.shape[1], rows_ref.shape[1]
    chip_rows = 2 * owner_rows
    tile = min(256, hidden)

    @pl.loop(0, spot.places)
    def _(s):
        place = summed.term(s)
        rows = pl.ds(pl.multiple_of(place * chip_rows, chip_rows), chip_rows)

        @pl.loop(0, hidden // tile)
        def _(t):
            cols = pl.ds(pl.multiple_of(t * tile, tile), tile)
            gate = dot(rows_ref[rows, :], gate_ref[:, cols])
            up = dot(rows_ref[rows, :], up_ref[:, cols])
            sig = jax.nn.sigmoid(gate)
            silu = gate * sig
            act_ref[rows, cols] = (silu * up).astype(BF16)
            grad = dot_nt(cot_ref[rows, :], down_ref[cols, :])
            dgate_ref[rows, cols] = (grad * up * sig * (1.0 + gate * (1.0 - sig))).astype(BF16)
            dup_ref[rows, cols] = (grad * silu).astype(BF16)

        @pl.loop(0, width // 256)
        def _(t):
            cols = pl.ds(pl.multiple_of(t * 256, 256), 256)
            y_ref[rows, cols] = dot(act_ref[rows, :], down_ref[:, cols]).astype(BF16)
            value = dot_nt(dgate_ref[rows, :], gate_ref[cols, :])
            value += dot_nt(dup_ref[rows, :], up_ref[cols, :])
            keep, send = split_cores(spot.core, value.astype(BF16), owner_rows)
            summed.mine[place, :, cols] = keep[0]
            summed.out[place, :, cols] = send[0]

        summed.sibling(place).start()
        for q, after in enumerate(summed.rounds):
            pl.when(s == after)(lambda: summed.go_on(q))

    incoming = summed.finish()
    middle = middle_ref[...]
    term, gain_grad = norm_back(middle, norm_factor(middle), gain_ref[...], incoming)
    gain_grad_ref[...] = gain_grad[None]
    grad = local_cot_ref[...].astype(F32) + term
    grad_ref[...] = grad
    low_ref[...] = grad.astype(BF16)


def backward_kernel(
    heads, toks, scale, shift,
    rows_ref, out_weight_ref, qkv, first_ref, cos_ref, sin_ref, weight_ref, rows_one_ref,
    x_ref, grad_ref, gain_ref,
    result_ref, proj_ref, gain_grad_ref,
    part, got, part_send, part_recv, blocks, paired, blocks_send, blocks_recv, dq, *sum_refs,
):
    spot = Spot()
    spot.enter(True)
    pairs = part.shape[0]
    owner_rows = toks * (pairs // heads)
    total = rows_ref.shape[0]
    step = min(512, total)

    @pl.loop(0, total // step)
    def _(i):
        rows = pl.ds(pl.multiple_of(i * step, step), step)
        made = dot_nt(rows_ref[rows, :], out_weight_ref[...]).astype(BF16)
        for j in range(step // owner_rows):
            to = pl.ds(pl.multiple_of((i * (step // owner_rows) + j) * toks, toks), toks)
            for p in range(pairs):
                s, h = p // heads, p % heads
                start = j * owner_rows + s * toks
                part[p, to, :] = made[start : start + toks, h * HEAD : (h + 1) * HEAD]

    swap = Swap(spot, part, got, part_send, part_recv)
    swap.start()
    swap.wait()
    attend_back_blocks(qkv, got, first_ref, cos_ref, sin_ref, blocks, dq, scale, shift)
    swap = Swap(spot, blocks, paired, blocks_send, blocks_recv)
    swap.start()
    swap.wait()
    for o in range(total // owner_rows):
        for p in range(pairs):
            s, h = p // heads, p % heads
            for kind in range(3):
                proj_ref[
                    pl.ds(o * owner_rows + s * toks, toks),
                    (kind * heads + h) * HEAD : (kind * heads + h + 1) * HEAD,
                ] = paired[p, pl.ds(o * toks, toks), kind * HEAD : (kind + 1) * HEAD]
    summed = Sum(spot, *sum_refs)
    chip_rows = 2 * owner_rows
    gain_grad_ref[...] = jnp.zeros_like(gain_grad_ref)

    @pl.loop(0, spot.places)
    def _(s):
        t = summed.term(s)
        rows = pl.ds(pl.multiple_of(t * chip_rows, chip_rows), chip_rows)
        value = dot_nt(proj_ref[rows, :], weight_ref[...])
        gain_grad_ref[...] += jnp.sum(
            value * rows_one_ref[rows, :].astype(F32), axis=0, keepdims=True
        )
        keep, send = split_cores(spot.core, value.astype(BF16), owner_rows)
        summed.mine[t] = keep[0]
        summed.out[t] = send[0]
        summed.sibling(t).start()

    for q in range(spot.places - 1):
        summed.go_on(q)
    incoming = summed.finish()
    x = x_ref[...].astype(F32)
    term, _ = norm_back(x, norm_factor(x), gain_ref[...], incoming)
    result_ref[...] = grad_ref[...] + term


def ffn_kernel(
    rows_ref, cot_ref, gate_ref, up_ref, down_ref, y_ref, dh_ref, act_ref, dgate_ref, dup_ref
):
    hidden = gate_ref.shape[1]
    width = rows_ref.shape[1]
    tile = min(256, hidden)

    @pl.loop(0, hidden // tile)
    def _(t):
        cols = pl.ds(pl.multiple_of(t * tile, tile), tile)
        gate = dot(rows_ref[...], gate_ref[:, cols])
        up = dot(rows_ref[...], up_ref[:, cols])
        sig = jax.nn.sigmoid(gate)
        silu = gate * sig
        act_ref[:, cols] = (silu * up).astype(BF16)
        grad = dot_nt(cot_ref[...], down_ref[cols, :])
        dgate_ref[:, cols] = (grad * up * sig * (1.0 + gate * (1.0 - sig))).astype(BF16)
        dup_ref[:, cols] = (grad * silu).astype(BF16)

    @pl.loop(0, width // 256)
    def _(t):
        cols = pl.ds(pl.multiple_of(t * 256, 256), 256)
        y_ref[:, cols] = dot(act_ref[...], down_ref[:, cols]).astype(BF16)
        dh = dot_nt(dgate_ref[...], gate_ref[cols, :]) + dot_nt(dup_ref[...], up_ref[cols, :])
        dh_ref[:, cols] = dh.astype(BF16)


def grad_kernel(count, _, *refs):
    lefts, rights, (out_ref, turned) = refs[:count], refs[count : 2 * count], refs[2 * count :]
    rows = lefts[0].shape[0]
    for m, left in enumerate(lefts):
        turned[:, m * rows : (m + 1) * rows] = left[...].T

    tile = math.gcd(out_ref.shape[1], 256)

    @pl.loop(0, out_ref.shape[1] // tile)
    def _(t):
        cols = pl.ds(pl.multiple_of(t * tile, tile), tile)
        total = dot(turned[:, :rows], rights[0][:, cols])
        for m in range(1, count):
            total += dot(turned[:, m * rows : (m + 1) * rows], rights[m][:, cols])
        out_ref[:, cols] = total.astype(BF16)


VMEM = pl.BlockSpec(memory_space=pltpu.VMEM)
SMEM = pl.BlockSpec(memory_space=pltpu.SMEM)


def cost(flops, nbytes):
    return pl.CostEstimate(flops=flops, bytes_accessed=nbytes, transcendentals=0)


def limits(mebibytes):
    return pltpu.CompilerParams(vmem_limit_bytes=mebibytes * 2**20)


def shape(*dims, dtype=BF16):
    return jax.ShapeDtypeStruct(dims, dtype)


def comm_params(collective_id, mebibytes):
    return pltpu.CompilerParams(
        collective_id=collective_id, has_side_effects=True, vmem_limit_bytes=mebibytes * 2**20
    )


def forward_attention(rows, weight, out_weight, tables, first, x, gain, heads, toks, scale, shift):
    total, width = rows.shape
    size, places = lax.axis_size("dp"), lax.axis_size("mp") // 2
    slice_len = tables[0].shape[0]
    owner_rows = x.shape[0]
    return pl.pallas_call(
        functools.partial(forward_kernel, heads, toks, scale, shift),
        out_shape=[
            shape(owner_rows, width, dtype=F32),
            shape(owner_rows, width),
            shape(size, slice_len, 3 * HEAD),
            shape(total, heads * HEAD),
        ],
        in_specs=[VMEM] * 8,
        out_specs=[VMEM] * 4,
        scratch_shapes=[
            pltpu.VMEM((min(512, total), 3 * heads * HEAD), F32),
            *swap_scratch(size, slice_len, 3 * HEAD),
            *swap_scratch(size, slice_len, HEAD),
            *sum_scratch(places, owner_rows, width),
        ],
        compiler_params=comm_params(0, 52),
        cost_estimate=cost(8 * total * width * heads * HEAD, 100 * 2**20),
        name="forward_attention",
    )(rows, weight, out_weight, *tables, first, x, gain)


def middle_part(rows, cot, gate, up, down, middle, local_cot, gain):
    total, width = rows.shape
    hidden = gate.shape[1]
    places = lax.axis_size("mp") // 2
    owner_rows = middle.shape[0]
    return pl.pallas_call(
        functools.partial(middle_kernel, owner_rows),
        out_shape=[
            shape(total, width),
            shape(total, hidden),
            shape(total, hidden),
            shape(total, hidden),
            shape(owner_rows, width, dtype=F32),
            shape(owner_rows, width),
            shape(1, width, dtype=F32),
        ],
        in_specs=[VMEM] * 8,
        out_specs=[VMEM] * 7,
        scratch_shapes=sum_scratch(places, owner_rows, width),
        compiler_params=comm_params(1, 60),
        cost_estimate=cost(12 * total * width * hidden, 34 * 2**20),
        name="middle_part",
    )(rows, cot, gate, up, down, middle, local_cot, gain)


def backward_attention(
    rows, out_weight, qkv, first, tables, weight, rows_one, x, grad, gain, heads, toks, scale, shift
):
    total, width = rows.shape
    size, places = lax.axis_size("dp"), lax.axis_size("mp") // 2
    slice_len = qkv.shape[1]
    owner_rows = x.shape[0]
    return pl.pallas_call(
        functools.partial(backward_kernel, heads, toks, scale, shift),
        out_shape=[
            shape(owner_rows, width, dtype=F32),
            shape(total, 3 * heads * HEAD),
            shape(1, width, dtype=F32),
        ],
        in_specs=[VMEM] * 11,
        out_specs=[VMEM] * 3,
        scratch_shapes=[
            *swap_scratch(size, slice_len, HEAD),
            *swap_scratch(size, slice_len, 3 * HEAD),
            pltpu.VMEM((size, HEAD, slice_len), F32),
            *sum_scratch(places, owner_rows, width),
        ],
        compiler_params=comm_params(2, 56),
        cost_estimate=cost(8 * total * width * heads * HEAD, 100 * 2**20),
        name="backward_attention",
    )(rows, out_weight, qkv, first, *tables, weight, rows_one, x, grad, gain)


def ffn(rows, cot, gate, up, down):
    total, width = rows.shape
    hidden = gate.shape[1]
    step = min(512, total)
    by_rows = pl.BlockSpec((step, width), lambda i: (i, 0))
    by_hidden = pl.BlockSpec((step, hidden), lambda i: (i, 0))
    held = lambda array: pl.BlockSpec(array.shape, lambda i: (0, 0), pipeline_mode=pl.Buffered(1))
    return pl.pallas_call(
        ffn_kernel,
        grid=(total // step,),
        out_shape=[shape(total, width)] * 2 + [shape(total, hidden)] * 3,
        in_specs=[by_rows, by_rows, held(gate), held(up), held(down)],
        out_specs=[by_rows] * 2 + [by_hidden] * 3,
        compiler_params=limits(56),
        cost_estimate=cost(12 * total * width * hidden, 34 * 2**20),
        name="ffn",
    )(rows, cot, gate, up, down)


def weight_grad(at, lefts, rights, step, left_blocked):
    count = len(lefts)
    size = lax.axis_size("dp")
    rows = lefts[0].shape[0]
    m, n = lefts[0].shape[1], rights[0].shape[1]
    moving = lambda width: pl.BlockSpec((rows, width // size), lambda i, at: (0, at[0] ^ step))
    fixed = lambda width: pl.BlockSpec((rows, width), lambda i, at: (0, 0))
    left_spec = moving(m) if left_blocked else fixed(m)
    right_spec = fixed(n) if left_blocked else moving(n)
    out = (m // size, n) if left_blocked else (m, n // size)
    return pl.pallas_call(
        functools.partial(grad_kernel, count),
        grid_spec=pltpu.PrefetchScalarGridSpec(
            num_scalar_prefetch=1,
            grid=(1,),
            in_specs=[left_spec] * count + [right_spec] * count,
            out_specs=pl.BlockSpec(out, lambda i, at: (0, 0)),
            scratch_shapes=[pltpu.VMEM((out[0], count * rows), BF16)],
        ),
        out_shape=shape(*out),
        compiler_params=limits(48),
        cost_estimate=cost(2 * count * rows * out[0] * out[1], 12 * 2**20),
        name="weight_grad",
    )(at, *lefts, *rights)


def summed_grad(at, lefts, rights, left_blocked):
    size = lax.axis_size("dp")
    received = []
    for step in range(size - 1, 0, -1):
        received.append(send_dp(weight_grad(at, lefts, rights, step, left_blocked), step))
    total = weight_grad(at, lefts, rights, 0, left_blocked).astype(F32)
    for block in received:
        total = total + block.astype(F32)
    return total


def first_visible(ids):
    at = jnp.arange(ids.shape[-1], dtype=jnp.int32)
    starts = jnp.concatenate([jnp.ones_like(ids[..., :1], jnp.bool_), ids[..., 1:] != ids[..., :-1]], axis=-1)
    return lax.cummax(jnp.where(starts, at, 0), axis=ids.ndim - 1)


def send_dp(values, step):
    size = lax.axis_size("dp")
    return lax.ppermute(values, "dp", [(i, i ^ step) for i in range(size)])


def block_at(values, index):
    return lax.dynamic_index_in_dim(values, index, 0, keepdims=False)


def gather_dp(values, axis=0):
    at = lax.axis_index("dp")
    size = lax.axis_size("dp")
    shape = list(values.shape)
    step = shape[axis]
    shape[axis] = step * size
    full = jnp.zeros(shape, values.dtype)
    for k in range(size):
        block = send_dp(values, k) if k else values
        full = lax.dynamic_update_slice_in_dim(full, block, (at ^ k) * step, axis)
    return full


def scatter_mp(values):
    return lax.psum_scatter(values, "mp", scatter_dimension=0, tiled=True).astype(F32)


def sum_all(values):
    for name in ("dp", "mp"):
        size = lax.axis_size(name)
        step = 1
        while step < size:
            values = values + lax.ppermute(values, name, [(i, i ^ step) for i in range(size)])
            step *= 2
    return values


def sliced_scores(qkv, kv_all, first, positions, scale, shift):
    raw = jnp.einsum("pqd,pkd->pqk", qkv[..., :HEAD], kv_all[..., :HEAD], preferred_element_type=F32)
    at = jnp.arange(kv_all.shape[1], dtype=jnp.int32)
    visible = (at >= first[..., None]) & (at <= positions[:, None])
    return jnp.where(visible, sigmoid_of(raw, scale, shift), 0.0)


def per_device(
    inputs,
    cotangent,
    doc_ids,
    gain_attn,
    w_query,
    w_key,
    w_value,
    w_out,
    gain_ffn,
    w_gate,
    w_up,
    w_down,
):
    dp_size = lax.axis_size("dp")
    mp_size = lax.axis_size("mp")
    micro_count, row_count, seq_count, width = inputs.shape
    slice_len = row_count * mp_size
    total_len = slice_len * dp_size
    rows_here = row_count * seq_count
    shift = math.log(total_len)
    scale = HEAD ** (-0.5)
    dp_at = lax.axis_index("dp")
    mp_at = lax.axis_index("mp")
    first_row = dp_at * slice_len
    positions = first_row + jnp.arange(slice_len, dtype=jnp.int32)
    head_width = w_query.shape[1]
    heads = head_width // HEAD
    hidden = w_gate.shape[1]
    pairs = seq_count * heads
    whole_pairs = pairs == dp_size
    cos_slice, sin_slice = full_tables(positions)
    cos_all, sin_all = full_tables(jnp.arange(total_len, dtype=jnp.int32))
    first_all = first_visible(doc_ids)

    def by_row(table):
        shaped = table.reshape(mp_size, 1, row_count, 1, HEAD)
        return jnp.broadcast_to(shaped, (mp_size, seq_count, row_count, 1, HEAD))

    def rotate(values, back=False):
        sine = -by_row(sin_slice) if back else by_row(sin_slice)
        return values * by_row(cos_slice) + swap_halves(values) * sine

    def to_pairs(values):
        shaped = values.reshape(mp_size, seq_count, row_count, heads, -1)
        return shaped.transpose(1, 3, 0, 2, 4).reshape(pairs, slice_len, -1)

    def from_pairs(values):
        shaped = values.reshape(seq_count, heads, mp_size, row_count, -1)
        return shaped.transpose(2, 0, 3, 1, 4).reshape(mp_size * rows_here, heads, -1)

    def to_rows(values):
        return jnp.swapaxes(values, 0, 1).reshape(rows_here, width)

    def from_rows(values):
        return jnp.swapaxes(values.reshape(seq_count, row_count, width), 0, 1)

    def gather_mp(values):
        return lax.all_gather(values, "mp", axis=0, tiled=True)

    qkv_full = gather_dp(jnp.concatenate([w_query, w_key, w_value], axis=1))
    out_full = gather_dp(w_out, 1)
    gate_full = gather_dp(w_gate)
    up_full = gather_dp(w_up)
    down_full = gather_dp(w_down, 1)
    at_array = jnp.stack([dp_at, mp_at % 2]).astype(jnp.int32)
    gain_attn_grad = jnp.zeros((width,), F32)
    gain_ffn_grad = jnp.zeros((width,), F32)
    results = []
    input_grads = []
    kept = [[] for _ in range(9)]
    for micro in range(micro_count):
        x = to_rows(inputs[micro])
        local_rows = x.astype(F32)
        local_cot = to_rows(cotangent[micro])
        factor_one = norm_factor(local_rows)
        rows_one = gather_mp((local_rows * factor_one * gain_attn).astype(BF16))
        portion = gather_mp(local_cot)
        if whole_pairs:
            first = block_at(first_all[micro], dp_at // heads)
            middle, normed_two, qkv, mixture = forward_attention(
                rows_one, qkv_full, out_full, (cos_slice, sin_slice), first[:, None], x,
                gain_ffn[None], heads, row_count, scale, shift,
            )
            rows_two = gather_mp(normed_two)
            y, activated, gate_grad, up_grad, middle_grad, branch_grad, gain_part = middle_part(
                rows_two, portion, gate_full, up_full, down_full, middle, local_cot, gain_ffn[None]
            )
            gain_ffn_grad = gain_ffn_grad + gain_part[0]
            attn_portion = gather_mp(branch_grad)
            results.append(from_rows((middle + scatter_mp(y)).astype(BF16)))
            input_grad, proj_grad, gain_part = backward_attention(
                attn_portion, out_full, qkv, first.reshape(dp_size, 1, slice_len),
                (cos_all, sin_all), qkv_full, rows_one, x, middle_grad, gain_attn[None],
                heads, row_count, scale, shift,
            )
            gain_attn_grad = gain_attn_grad + gain_part[0]
            input_grads.append(from_rows(input_grad))
        else:
            projected = dot(rows_one, qkv_full).reshape(
                mp_size, seq_count, row_count, 3, heads, HEAD
            )
            packed = to_pairs(
                jnp.concatenate(
                    [
                        rotate(projected[:, :, :, 0]).astype(BF16),
                        rotate(projected[:, :, :, 1]).astype(BF16),
                        projected[:, :, :, 2].astype(BF16),
                    ],
                    axis=-1,
                )
            )
            kv_all = lax.all_gather(packed[..., HEAD:], "dp", axis=1, tiled=True)
            first = lax.dynamic_slice_in_dim(first_all[micro], first_row, slice_len, 1)
            first = jnp.repeat(first, heads, axis=0)
            weights = sliced_scores(packed, kv_all, first, positions, scale, shift)
            attended = jnp.einsum(
                "pqk,pkd->pqd", weights.astype(BF16), kv_all[..., HEAD:], preferred_element_type=F32
            ).astype(BF16)
            mixture = from_pairs(attended).reshape(mp_size * rows_here, head_width)
            middle = local_rows + scatter_mp(dot(mixture, out_full).astype(BF16))
            factor_two = norm_factor(middle)
            rows_two = gather_mp((middle * factor_two * gain_ffn).astype(BF16))
            y, dh, activated, gate_grad, up_grad = ffn(
                rows_two, portion, gate_full, up_full, down_full
            )
            results.append(from_rows((middle + scatter_mp(y)).astype(BF16)))
            middle_term, gain_part = norm_back(middle, factor_two, gain_ffn, scatter_mp(dh))
            gain_ffn_grad = gain_ffn_grad + gain_part
            middle_grad = local_cot.astype(F32) + middle_term
            attn_portion = gather_mp(middle_grad.astype(BF16))
            mix_grad = to_pairs(dot_nt(attn_portion, out_full).astype(BF16))
            sig = sliced_scores(packed, kv_all, first, positions, scale, shift)
            prob_grad = jnp.einsum(
                "pqd,pkd->pqk", mix_grad, kv_all[..., HEAD:], preferred_element_type=F32
            )
            score_grad = (prob_grad * sig * (1.0 - sig)).astype(BF16)
            dq = jnp.einsum("pqk,pkd->pqd", score_grad, kv_all[..., :HEAD], preferred_element_type=F32)
            dk = jnp.einsum("pqk,pqd->pkd", score_grad, packed[..., :HEAD], preferred_element_type=F32)
            dv = jnp.einsum("pqk,pqd->pkd", sig.astype(BF16), mix_grad, preferred_element_type=F32)
            dkv = lax.psum_scatter(
                jnp.concatenate([dk * scale, dv], axis=-1).astype(BF16), "dp", scatter_dimension=1, tiled=True
            ).astype(F32)
            back = from_pairs(jnp.concatenate([dq * scale, dkv], axis=-1))
            back = back.reshape(mp_size, seq_count, row_count, heads, 3 * HEAD)
            proj_grad = jnp.stack(
                [
                    rotate(back[..., :HEAD], True),
                    rotate(back[..., HEAD : 2 * HEAD], True),
                    back[..., 2 * HEAD :],
                ],
                axis=3,
            ).astype(BF16).reshape(mp_size * rows_here, 3 * head_width)
            partial_grad = dot_nt(proj_grad, qkv_full)
            gain_attn_grad = gain_attn_grad + jnp.sum(partial_grad * rows_one.astype(F32), axis=0)
            input_term, _ = norm_back(
                local_rows, factor_one, gain_attn, scatter_mp(partial_grad.astype(BF16))
            )
            input_grads.append(from_rows(middle_grad + input_term))
        for held, array in zip(
            kept,
            (rows_one, proj_grad, mixture, attn_portion, rows_two, gate_grad, up_grad, activated, portion),
        ):
            held.append(array)

    ones, projs, mixtures, attns, twos, gates, ups, acts, portions = kept
    sum_gate = summed_grad(at_array, twos, gates, True)
    sum_up = summed_grad(at_array, twos, ups, True)
    sum_down = summed_grad(at_array, acts, portions, False)
    sum_out = summed_grad(at_array, mixtures, attns, False)
    sum_qkv = summed_grad(at_array, ones, projs, True)
    gain_sums = (sum_all(gain_attn_grad / gain_attn), sum_all(gain_ffn_grad))
    return (
        jnp.stack(results),
        jnp.stack(input_grads),
        gain_sums[0],
        sum_qkv[:, :head_width],
        sum_qkv[:, head_width : 2 * head_width],
        sum_qkv[:, 2 * head_width :],
        sum_out,
        gain_sums[1],
        sum_gate,
        sum_up,
        sum_down,
    )


def solution(mesh):
    tokens = P(None, ("dp", "mp"), None, None)
    column = P("dp", "mp")
    row = P("mp", "dp")
    return jax.shard_map(
        per_device,
        mesh=mesh,
        in_specs=(
            tokens, tokens, P(), P(), column, column, column, row, P(), column, column, row,
        ),
        out_specs=(
            tokens, tokens, P(), column, column, column, row, P(), column, column, row,
        ),
        check_vma=False,
    )
```

```python
import functools
import math

import jax
import jax.numpy as jnp
from jax import lax
from jax.experimental import pallas as pl
from jax.experimental.pallas import tpu as pltpu
from jax.sharding import PartitionSpec as P

HEAD = 128
epsilon = 1e-05
rope_base = 10000.0
F32 = jnp.float32
BF16 = jnp.bfloat16


def rope_tables(positions):
    half_size = HEAD // 2
    inverse = jnp.power(rope_base, -(jnp.arange(half_size, dtype=F32) * 2.0 / HEAD))
    angles = positions.astype(F32)[:, None] * inverse[None, :]
    return (jnp.cos(angles), jnp.sin(angles))


def full_tables(positions):
    cosine, sine = rope_tables(positions)
    return (
        jnp.concatenate([cosine, cosine], axis=-1),
        jnp.concatenate([-sine, sine], axis=-1),
    )


def swap_halves(values):
    half_size = HEAD // 2
    return jnp.concatenate([values[..., half_size:], values[..., :half_size]], axis=-1)


def dot(left, right):
    return jnp.dot(left, right, preferred_element_type=F32)


def dot_tn(left, right):
    return lax.dot_general(left, right, (((0,), (0,)), ((), ())), preferred_element_type=F32)


def dot_nt(left, right):
    return lax.dot_general(left, right, (((1,), (1,)), ((), ())), preferred_element_type=F32)


def norm_factor(values):
    return lax.rsqrt(jnp.mean(values * values, axis=-1, keepdims=True) + epsilon)


def norm_back(values, factor, gain, incoming):
    scaled = incoming * gain
    gain_term = jnp.sum(incoming * values * factor, axis=0)
    input_term = factor * scaled - values * factor**3 * jnp.mean(
        scaled * values, axis=-1, keepdims=True
    )
    return (input_term, gain_term)


def sigmoid_of(raw, scale, shift):
    return 1.0 / (1.0 + jnp.exp(shift - raw * scale))


def split_cores(core, values, rows_here):
    shaped = values.reshape(-1, 2, rows_here, values.shape[-1])
    first, second = shaped[:, 0], shaped[:, 1]
    is_first = core == 0
    return jnp.where(is_first, first, second), jnp.where(is_first, second, first)

MESH = pl.DeviceIdType.MESH


class Spot:
    def __init__(self):
        self.dp, self.mp = lax.axis_index("dp"), lax.axis_index("mp")
        self.dp_size, self.mp_size = lax.axis_size("dp"), lax.axis_size("mp")
        self.places = self.mp_size // 2
        self.place, self.core = lax.div(self.mp, 2), lax.rem(self.mp, 2)
        self.sibling = (self.dp, self.mp + 1 - 2 * self.core)
        self.right = (self.dp, self.mp + 2)
        self.left = (self.dp, self.mp - 2)
        self.has_right = self.place < self.places - 1
        self.has_left = self.place > 0

    def peer(self, step):
        return lax.rem(self.dp + step, self.dp_size)

    def enter(self, with_dp, with_mp):
        barrier = pltpu.get_barrier_semaphore()
        count = 0

        def greet(device):
            pl.semaphore_signal(barrier, inc=1, device_id=device, device_id_type=MESH)

        if with_mp:
            greet(self.sibling)
            pl.when(self.has_right)(lambda: greet(self.right))
            pl.when(self.has_left)(lambda: greet(self.left))
            count += 1 + self.has_right.astype(jnp.int32) + self.has_left.astype(jnp.int32)
        if with_dp:
            for step in range(1, self.dp_size):
                greet((self.peer(step), self.mp))
            count += self.dp_size - 1
        pl.semaphore_wait(barrier, count)


class Swap:
    def __init__(self, spot, source, target, send, receive):
        self.spot, self.source, self.target = spot, source, target
        self.copies = [
            pltpu.make_async_remote_copy(
                src_ref=source.at[spot.peer(step)],
                dst_ref=target.at[spot.dp],
                send_sem=send.at[step],
                recv_sem=receive.at[step],
                device_id=(spot.peer(step), spot.mp),
                device_id_type=MESH,
            )
            for step in range(1, spot.dp_size)
        ]

    def start(self):
        for copy in self.copies:
            copy.start()
        self.target[self.spot.dp] = self.source[self.spot.dp]

    def wait(self):
        for copy in self.copies:
            copy.wait()


class Gather:
    def __init__(self, spot, shard, window, sems):
        self.local = pltpu.make_async_copy(shard, window(spot.dp), sems.at[0, 0])
        self.copies = [
            pltpu.make_async_remote_copy(
                src_ref=shard,
                dst_ref=window(spot.dp),
                send_sem=sems.at[0, step],
                recv_sem=sems.at[1, step],
                device_id=(spot.peer(step), spot.mp),
                device_id_type=MESH,
            )
            for step in range(1, spot.dp_size)
        ]

    def start(self):
        for copy in self.copies:
            copy.start()
        self.local.start()

    def wait(self):
        for copy in self.copies:
            copy.wait()
        self.local.wait()


class Ship(Swap):
    def __init__(self, spot, source, target, sems):
        super().__init__(spot, source, target, sems.at[0], sems.at[1])
        self.local = pltpu.make_async_copy(source.at[spot.dp], target.at[spot.dp], sems.at[0, 0])

    def start(self):
        for copy in self.copies:
            copy.start()
        self.local.start()

    def wait(self):
        super().wait()
        self.local.wait()


def window_of(full, axis, step, column=0, columns=None):
    def window(index):
        along = pl.ds(pl.multiple_of(index * step, step), step)
        if axis == 1:
            return full.at[:, along]
        if columns is None:
            return full.at[along, :]
        return full.at[along, pl.ds(column, columns)]

    return window


def swap_scratch(size, *block):
    return [
        pltpu.VMEM((size, *block), BF16),
        pltpu.VMEM((size, *block), BF16),
        pltpu.SemaphoreType.DMA((size,)),
        pltpu.SemaphoreType.DMA((size,)),
    ]


def far_first(places):
    orders = []
    for place in range(places):
        right, left, order = list(range(places - 1, place, -1)), list(range(place)), []
        while right or left:
            order += right[:1] + left[:1]
            right, left = right[1:], left[1:]
        orders.append(order + [place])
    return orders


class Sum:
    def __init__(self, spot, mine, out, from_sibling, from_left, from_right, sems):
        self.spot = spot
        self.mine, self.out = mine, out
        self.from_sibling, self.from_left, self.from_right = from_sibling, from_left, from_right
        self.sems = sems
        self.orders = far_first(spot.places)

    def copy(self, source, target, kind, t, device):
        return pltpu.make_async_remote_copy(
            src_ref=source.at[t],
            dst_ref=target.at[t],
            send_sem=self.sems.at[kind, t],
            recv_sem=self.sems.at[kind + 1, t],
            device_id=device,
            device_id_type=MESH,
        )

    def sibling(self, t):
        return self.copy(self.out, self.from_sibling, 0, t, self.spot.sibling)

    def rightward(self, t):
        return self.copy(self.mine, self.from_left, 2, t, self.spot.right)

    def leftward(self, t):
        return self.copy(self.mine, self.from_right, 4, t, self.spot.left)

    def term(self, s):
        chosen = 0
        for place, order in enumerate(self.orders):
            for at, t in enumerate(order):
                if t:
                    chosen = chosen + jnp.where((self.spot.place == place) & (s == at), t, 0)
        return chosen

    def add(self, t, arrived):
        self.mine[t] = (self.mine[t].astype(F32) + arrived[t].astype(F32)).astype(BF16)

    def absorb(self, t):
        self.sibling(t).wait_recv()
        self.add(t, self.from_sibling)

    def send(self, t, arrives, arrived, hop):
        self.absorb(t)
        if arrives:
            hop(t).wait_recv()
            self.add(t, arrived)
        hop(t).start()

    def begin(self, s):
        spot = self.spot

        @pl.when((spot.place == 0) & (s < spot.places - 1))
        def _():
            self.send(spot.places - 1 - s, False, None, self.rightward)

        @pl.when((spot.place == spot.places - 1) & (s < spot.places - 1))
        def _():
            self.send(s, False, None, self.leftward)

    def go_on(self, hop):
        spot = self.spot
        last = spot.places - 1

        @pl.when((spot.place > 0) & (spot.place <= hop))
        def _():
            self.send(last + spot.place - hop, True, self.from_left, self.rightward)

        @pl.when((spot.place < last) & (last - spot.place <= hop))
        def _():
            self.send(hop - last + spot.place, True, self.from_right, self.leftward)

    def finish(self):
        spot = self.spot
        t = spot.place
        self.absorb(t)

        @pl.when(spot.has_left)
        def _():
            self.rightward(t).wait_recv()
            self.add(t, self.from_left)

        @pl.when(spot.has_right)
        def _():
            self.leftward(t).wait_recv()
            self.add(t, self.from_right)

        for t in range(spot.places):
            self.sibling(t).wait_send()
            pl.when(spot.place < t)(lambda: self.rightward(t).wait_send())
            pl.when(spot.place > t)(lambda: self.leftward(t).wait_send())
        return self.mine[spot.place].astype(F32)


def sum_scratch(places, rows_here, width):
    return [pltpu.VMEM((places, rows_here, width), BF16)] * 5 + [
        pltpu.SemaphoreType.DMA((6, places))
    ]


def attend_blocks(qkv, first_ref, out, scale, shift):
    count, block = out.shape[:2]
    row_at = lax.broadcasted_iota(jnp.int32, (block, block), 0)
    col_at = lax.broadcasted_iota(jnp.int32, (block, block), 1)

    @pl.loop(0, count)
    def _(i):
        queries = qkv[i, :, 0:HEAD]
        first = first_ref[pl.ds(pl.multiple_of(i * block, block), block), :]

        def add_block(j, acc, diagonal=False):
            sig = sigmoid_of(dot_nt(queries, qkv[j, :, HEAD : 2 * HEAD]), scale, shift)
            visible = col_at >= first - j * block
            if diagonal:
                visible = visible & (col_at <= row_at)
            weights = jnp.where(visible, sig, 0.0).astype(BF16)
            return acc + dot(weights, qkv[j, :, 2 * HEAD :])

        acc = add_block(i, jnp.zeros((block, HEAD), F32), True)
        out[i] = lax.fori_loop(0, i, add_block, acc).astype(BF16)


def attend_back_blocks(qkv, grad, first_ref, cos_ref, sin_ref, out, dq, scale, shift):
    count, block = grad.shape[:2]
    col_at = lax.broadcasted_iota(jnp.int32, (block, block), 0)
    row_at = lax.broadcasted_iota(jnp.int32, (block, block), 1)
    dq[...] = jnp.zeros_like(dq)

    def unrotate(values, i):
        rows = pl.ds(pl.multiple_of(i * block, block), block)
        swapped = pltpu.roll(values, HEAD // 2, 1)
        return (values * cos_ref[rows, :] - swapped * sin_ref[rows, :]).astype(BF16)

    @pl.loop(0, count)
    def _(j):
        keys = qkv[j, :, HEAD : 2 * HEAD]
        values = qkv[j, :, 2 * HEAD :]
        keys_t = keys.T

        def add_block(i, sums, diagonal=False):
            dk, dv = sums
            queries, grads = qkv[i, :, 0:HEAD], grad[i]
            sig = sigmoid_of(dot_nt(keys, queries), scale, shift)
            visible = col_at >= first_ref[i] - j * block
            if diagonal:
                visible = visible & (col_at <= row_at)
            sig = jnp.where(visible, sig, 0.0)
            prob_grad = dot_nt(values, grads)
            score_grad = (prob_grad * sig * (1.0 - sig)).astype(BF16)
            dq[i] += dot(keys_t, score_grad)
            return dk + dot(score_grad, queries), dv + dot(sig.astype(BF16), grads)

        zero = jnp.zeros((block, HEAD), F32)
        dk, dv = lax.fori_loop(j + 1, count, add_block, add_block(j, (zero, zero), True))
        out[j, :, HEAD : 2 * HEAD] = unrotate(dk * scale, j)
        out[j, :, 2 * HEAD :] = dv.astype(BF16)

    @pl.loop(0, count)
    def _(i):
        out[i, :, 0:HEAD] = unrotate(dq[i].T * scale, i)


def take(refs, count):
    return refs[:count], refs[count:]


def gather_weights_kernel(query, key, value, out, gate, qkv_full, out_full, gate_full, sems):
    spot = Spot()
    spot.enter(True, False)
    rows, columns = query.shape
    jobs = [
        (shard, window_of(qkv_full, 0, rows, i * columns, columns))
        for i, shard in enumerate((query, key, value))
    ]
    jobs.append((out, window_of(out_full, 1, out.shape[1])))
    jobs.append((gate, window_of(gate_full, 0, gate.shape[0])))
    gathers = [Gather(spot, shard, window, sems.at[i]) for i, (shard, window) in enumerate(jobs)]
    for gather in gathers:
        gather.start()
    for gather in gathers:
        gather.wait()


def forward_kernel(tail, head, gather_axis, heads, toks, scale, shift, *refs):
    gathers = gather_axis is not None
    tail_in, refs = take(refs, 4 * tail)
    head_in, refs = take(refs, 5 * head)
    gather_in, refs = take(refs, gathers)
    tail_out, refs = take(refs, 3 * tail)
    head_out, refs = take(refs, 2 * head)
    gather_out, refs = take(refs, gathers)
    sum_refs, refs = take(refs, 6 * tail)
    head_refs, refs = take(refs, 9 * head)
    spot = Spot()
    spot.enter(head or gathers, tail)
    gather = None
    if gathers:
        window = window_of(gather_out[0], gather_axis, gather_in[0].shape[gather_axis])
        gather = Gather(spot, gather_in[0], window, refs[0])

    if tail:
        got, out_weight, x_ref, gain_ref = tail_in
        middle_ref, normed_ref, mix_ref = tail_out
        pairs = got.shape[0]
        owner_rows = toks * (pairs // heads)
        for o in range(mix_ref.shape[0] // owner_rows):
            for p in range(pairs):
                s, h = p // heads, p % heads
                mix_ref[pl.ds(o * owner_rows + s * toks, toks), h * HEAD : (h + 1) * HEAD] = got[
                    p, pl.ds(o * toks, toks), :
                ]
        summed = Sum(spot, *sum_refs)
        chip_rows = 2 * owner_rows

        @pl.loop(0, spot.places)
        def _(s):
            t = summed.term(s)
            rows = pl.ds(pl.multiple_of(t * chip_rows, chip_rows), chip_rows)
            value = dot(mix_ref[rows, :], out_weight[...]).astype(BF16)
            keep, send = split_cores(spot.core, value, owner_rows)
            summed.mine[t] = keep[0]
            summed.out[t] = send[0]
            summed.sibling(t).start()

        @pl.loop(0, spot.places - 1)
        def _(s):
            summed.begin(s)

    if head:
        rows_ref, weight_ref, cos_ref, sin_ref, first_ref = head_in
        qkv_ref, got_ref = head_out
        made, paired, qkv, qkv_send, qkv_recv, part, got, part_send, part_recv = head_refs
        pairs = paired.shape[0]
        owner_rows = toks * (pairs // heads)
        step = made.shape[0]

        @pl.loop(0, rows_ref.shape[0] // step)
        def _(i):
            rows = pl.ds(pl.multiple_of(i * step, step), step)
            made[...] = dot(rows_ref[rows, :], weight_ref[...])
            for j in range(step // owner_rows):
                to = pl.ds(pl.multiple_of((i * (step // owner_rows) + j) * toks, toks), toks)
                cosine, sine = cos_ref[to, :], sin_ref[to, :]
                for p in range(pairs):
                    s, h = p // heads, p % heads
                    here = pl.ds(j * owner_rows + s * toks, toks)
                    for kind in range(3):
                        piece = made[here, pl.ds((kind * heads + h) * HEAD, HEAD)]
                        if kind < 2:
                            piece = piece * cosine + pltpu.roll(piece, HEAD // 2, 1) * sine
                        paired[p, to, kind * HEAD : (kind + 1) * HEAD] = piece.astype(BF16)

        swap = Swap(spot, paired, qkv, qkv_send, qkv_recv)
        swap.start()
    if tail and spot.places > 2:
        summed.go_on(1)
    if head:
        swap.wait()
    if gathers:
        gather.start()
    if tail:
        for hop in range(2, spot.places - 1):
            summed.go_on(hop)
    if head:
        attend_blocks(qkv, first_ref, part, scale, shift)
        swap = Swap(spot, part, got, part_send, part_recv)
        swap.start()
        qkv_ref[...] = qkv[...]
        swap.wait()
        got_ref[...] = got[...]
    if tail:
        middle = x_ref[...].astype(F32) + summed.finish()
        middle_ref[...] = middle
        normed_ref[...] = (middle * norm_factor(middle) * gain_ref[...]).astype(BF16)
    if gathers:
        gather.wait()


def middle_kernel(
    owner_rows,
    rows_ref, cot_ref, gate_ref, up_ref, down_ref, middle_ref, local_cot_ref, gain_ref,
    y_ref, act_ref, dgate_ref, dup_ref, grad_ref, low_ref, gain_grad_ref,
    *sum_refs,
):
    spot = Spot()
    spot.enter(False, True)
    summed = Sum(spot, *sum_refs)
    hidden, width = gate_ref.shape[1], rows_ref.shape[1]
    chip_rows = 2 * owner_rows
    tile = min(256, hidden)

    @pl.loop(0, spot.places)
    def _(s):
        place = summed.term(s)
        rows = pl.ds(pl.multiple_of(place * chip_rows, chip_rows), chip_rows)

        @pl.loop(0, hidden // tile)
        def _(t):
            cols = pl.ds(pl.multiple_of(t * tile, tile), tile)
            gate = dot(rows_ref[rows, :], gate_ref[:, cols])
            up = dot(rows_ref[rows, :], up_ref[:, cols])
            sig = jax.nn.sigmoid(gate)
            silu = gate * sig
            act_ref[rows, cols] = (silu * up).astype(BF16)
            grad = dot_nt(cot_ref[rows, :], down_ref[cols, :])
            dgate_ref[rows, cols] = (grad * up * sig * (1.0 + gate * (1.0 - sig))).astype(BF16)
            dup_ref[rows, cols] = (grad * silu).astype(BF16)

        pl.when(s > 0)(lambda: summed.begin(s - 1))
        for hop in range(1, spot.places - 1):
            pl.when(s == hop + 1)(lambda: summed.go_on(hop))

        @pl.loop(0, width // 256)
        def _(t):
            cols = pl.ds(pl.multiple_of(t * 256, 256), 256)
            y_ref[rows, cols] = dot(act_ref[rows, :], down_ref[:, cols]).astype(BF16)
            value = dot_nt(dgate_ref[rows, :], gate_ref[cols, :])
            value += dot_nt(dup_ref[rows, :], up_ref[cols, :])
            keep, send = split_cores(spot.core, value.astype(BF16), owner_rows)
            summed.mine[place, :, cols] = keep[0]
            summed.out[place, :, cols] = send[0]

        summed.sibling(place).start()

    incoming = summed.finish()
    middle = middle_ref[...]
    term, gain_grad = norm_back(middle, norm_factor(middle), gain_ref[...], incoming)
    gain_grad_ref[...] = gain_grad[None]
    grad = local_cot_ref[...].astype(F32) + term
    grad_ref[...] = grad
    low_ref[...] = grad.astype(BF16)


def backward_kernel(tail, head, ships, heads, toks, scale, shift, *refs):
    tail_in, refs = take(refs, 6 * tail)
    head_in, refs = take(refs, 6 * head)
    ship_in, refs = take(refs, ships)
    tail_out, refs = take(refs, 2 * tail)
    head_out, refs = take(refs, head)
    ship_out, refs = take(refs, ships)
    sum_refs, refs = take(refs, 6 * tail)
    head_refs, refs = take(refs, 9 * head)
    spot = Spot()
    spot.enter(head or ships > 0, tail)
    shipped = [
        Ship(spot, source, target, refs[0].at[i])
        for i, (source, target) in enumerate(zip(ship_in, ship_out))
    ]

    if tail:
        proj_ref, weight_ref, rows_one_ref, x_ref, grad_ref, gain_ref = tail_in
        result_ref, gain_grad_ref = tail_out
        owner_rows = x_ref.shape[0]
        summed = Sum(spot, *sum_refs)
        chip_rows = 2 * owner_rows
        gain_grad_ref[...] = jnp.zeros_like(gain_grad_ref)

        @pl.loop(0, spot.places)
        def _(s):
            t = summed.term(s)
            rows = pl.ds(pl.multiple_of(t * chip_rows, chip_rows), chip_rows)
            value = dot_nt(proj_ref[rows, :], weight_ref[...])
            gain_grad_ref[...] += jnp.sum(
                value * rows_one_ref[rows, :].astype(F32), axis=0, keepdims=True
            )
            keep, send = split_cores(spot.core, value.astype(BF16), owner_rows)
            summed.mine[t] = keep[0]
            summed.out[t] = send[0]
            summed.sibling(t).start()
            pl.when(s > 0)(lambda: summed.begin(s - 1))

    if head:
        rows_ref, out_weight_ref, qkv, first_ref, cos_ref, sin_ref = head_in
        (head_proj_ref,) = head_out
        part, got, part_send, part_recv, blocks, paired, blocks_send, blocks_recv, dq = head_refs
        pairs = part.shape[0]
        owner_rows = toks * (pairs // heads)
        total = rows_ref.shape[0]
        step = min(512, total)

        @pl.loop(0, total // step)
        def _(i):
            rows = pl.ds(pl.multiple_of(i * step, step), step)
            made = dot_nt(rows_ref[rows, :], out_weight_ref[...]).astype(BF16)
            for j in range(step // owner_rows):
                to = pl.ds(pl.multiple_of((i * (step // owner_rows) + j) * toks, toks), toks)
                for p in range(pairs):
                    s, h = p // heads, p % heads
                    start = j * owner_rows + s * toks
                    part[p, to, :] = made[start : start + toks, h * HEAD : (h + 1) * HEAD]

        swap = Swap(spot, part, got, part_send, part_recv)
        swap.start()
        swap.wait()
    for ship in shipped:
        ship.start()
    if tail and spot.places > 2:
        summed.go_on(1)
    if head:
        attend_back_blocks(qkv, got, first_ref, cos_ref, sin_ref, blocks, dq, scale, shift)
        swap = Swap(spot, blocks, paired, blocks_send, blocks_recv)
        swap.start()
    if tail:
        for hop in range(2, spot.places - 1):
            summed.go_on(hop)
    if head:
        swap.wait()
        for o in range(total // owner_rows):
            for p in range(pairs):
                s, h = p // heads, p % heads
                for kind in range(3):
                    head_proj_ref[
                        pl.ds(o * owner_rows + s * toks, toks),
                        (kind * heads + h) * HEAD : (kind * heads + h + 1) * HEAD,
                    ] = paired[p, pl.ds(o * toks, toks), kind * HEAD : (kind + 1) * HEAD]
    if tail:
        incoming = summed.finish()
        x = x_ref[...].astype(F32)
        term, _ = norm_back(x, norm_factor(x), gain_ref[...], incoming)
        result_ref[...] = grad_ref[...] + term
    for ship in shipped:
        ship.wait()


def ffn_kernel(
    rows_ref, cot_ref, gate_ref, up_ref, down_ref, y_ref, dh_ref, act_ref, dgate_ref, dup_ref
):
    hidden = gate_ref.shape[1]
    width = rows_ref.shape[1]
    tile = min(256, hidden)

    @pl.loop(0, hidden // tile)
    def _(t):
        cols = pl.ds(pl.multiple_of(t * tile, tile), tile)
        gate = dot(rows_ref[...], gate_ref[:, cols])
        up = dot(rows_ref[...], up_ref[:, cols])
        sig = jax.nn.sigmoid(gate)
        silu = gate * sig
        act_ref[:, cols] = (silu * up).astype(BF16)
        grad = dot_nt(cot_ref[...], down_ref[cols, :])
        dgate_ref[:, cols] = (grad * up * sig * (1.0 + gate * (1.0 - sig))).astype(BF16)
        dup_ref[:, cols] = (grad * silu).astype(BF16)

    @pl.loop(0, width // 256)
    def _(t):
        cols = pl.ds(pl.multiple_of(t * 256, 256), 256)
        y_ref[:, cols] = dot(act_ref[...], down_ref[:, cols]).astype(BF16)
        dh = dot_nt(dgate_ref[...], gate_ref[cols, :]) + dot_nt(dup_ref[...], up_ref[cols, :])
        dh_ref[:, cols] = dh.astype(BF16)


def grad_kernel(count, left_blocked, *refs):
    lefts, rights, (out_ref, turned) = refs[:count], refs[count : 2 * count], refs[2 * count :]
    rows = lefts[0].shape[0]

    def turn():
        for m, left in enumerate(lefts):
            turned[:, m * rows : (m + 1) * rows] = left[...].T

    if left_blocked:
        turn()
    else:
        pl.when(pl.program_id(0) == 0)(turn)
    tile = math.gcd(out_ref.shape[2], 256)

    @pl.loop(0, out_ref.shape[2] // tile)
    def _(t):
        cols = pl.ds(pl.multiple_of(t * tile, tile), tile)
        total = dot(turned[:, :rows], rights[0][:, cols])
        for m in range(1, count):
            total += dot(turned[:, m * rows : (m + 1) * rows], rights[m][:, cols])
        out_ref[0, :, cols] = total.astype(BF16)


VMEM = pl.BlockSpec(memory_space=pltpu.VMEM)
ANY = pl.BlockSpec(memory_space=pl.ANY)


def cost(flops, nbytes):
    return pl.CostEstimate(flops=flops, bytes_accessed=nbytes, transcendentals=0)


def limits(mebibytes):
    return pltpu.CompilerParams(vmem_limit_bytes=mebibytes * 2**20)


def shape(*dims, dtype=BF16):
    return jax.ShapeDtypeStruct(dims, dtype)


def comm_params(collective_id, mebibytes):
    return pltpu.CompilerParams(
        collective_id=collective_id, has_side_effects=True, vmem_limit_bytes=mebibytes * 2**20
    )


def gather_weights(query, key, value, out, gate):
    size = lax.axis_size("dp")
    rows, columns = query.shape
    return pl.pallas_call(
        gather_weights_kernel,
        out_shape=[
            shape(rows * size, 3 * columns),
            shape(out.shape[0], out.shape[1] * size),
            shape(gate.shape[0] * size, gate.shape[1]),
        ],
        in_specs=[ANY] * 5,
        out_specs=[ANY] * 3,
        scratch_shapes=[pltpu.SemaphoreType.DMA((5, 2, size))],
        compiler_params=comm_params(0, 8),
        cost_estimate=cost(0, 60 * 2**20),
        name="gather_weights",
    )(query, key, value, out, gate)


def forward_stage(collective_id, tail, head, gather, heads, toks, scale, shift):
    size, places = lax.axis_size("dp"), lax.axis_size("mp") // 2
    out_shape, scratch = [], []
    if tail:
        blocks, _, x, _ = tail
        owner_rows, width = x.shape
        total = blocks.shape[1] * blocks.shape[0] // heads
        out_shape += [
            shape(owner_rows, width, dtype=F32),
            shape(owner_rows, width),
            shape(total, heads * HEAD),
        ]
        scratch += sum_scratch(places, owner_rows, width)
    if head:
        total, slice_len = head[0].shape[0], head[2].shape[0]
        out_shape += [shape(size, slice_len, 3 * HEAD), shape(size, slice_len, HEAD)]
        scratch += [
            pltpu.VMEM((min(512, total), 3 * heads * HEAD), F32),
            *swap_scratch(size, slice_len, 3 * HEAD),
            *swap_scratch(size, slice_len, HEAD),
        ]
    here = len(out_shape)
    axis = None
    if gather:
        shard, axis = gather
        dims = list(shard.shape)
        dims[axis] *= size
        out_shape.append(shape(*dims))
        scratch.append(pltpu.SemaphoreType.DMA((2, size)))
    arrays = [*tail, *head]
    return pl.pallas_call(
        functools.partial(
            forward_kernel, bool(tail), bool(head), axis, heads, toks, scale, shift
        ),
        out_shape=out_shape,
        in_specs=[VMEM] * len(arrays) + [ANY] * bool(gather),
        out_specs=[VMEM] * here + [ANY] * bool(gather),
        scratch_shapes=scratch,
        compiler_params=comm_params(collective_id, 52),
        cost_estimate=cost(10**10, 100 * 2**20),
        name="forward_stage",
    )(*arrays, *([gather[0]] if gather else []))


def middle_part(rows, cot, gate, up, down, middle, local_cot, gain):
    total, width = rows.shape
    hidden = gate.shape[1]
    places = lax.axis_size("mp") // 2
    owner_rows = middle.shape[0]
    return pl.pallas_call(
        functools.partial(middle_kernel, owner_rows),
        out_shape=[
            shape(total, width),
            shape(total, hidden),
            shape(total, hidden),
            shape(total, hidden),
            shape(owner_rows, width, dtype=F32),
            shape(owner_rows, width),
            shape(1, width, dtype=F32),
        ],
        in_specs=[VMEM] * 8,
        out_specs=[VMEM] * 7,
        scratch_shapes=sum_scratch(places, owner_rows, width),
        compiler_params=comm_params(1, 60),
        cost_estimate=cost(12 * total * width * hidden, 34 * 2**20),
        name="middle_part",
    )(rows, cot, gate, up, down, middle, local_cot, gain)


def backward_stage(collective_id, tail, head, ships, heads, toks, scale, shift):
    size, places = lax.axis_size("dp"), lax.axis_size("mp") // 2
    out_shape, scratch = [], []
    if tail:
        owner_rows, width = tail[3].shape
        out_shape += [shape(owner_rows, width, dtype=F32), shape(1, width, dtype=F32)]
        scratch += sum_scratch(places, owner_rows, width)
    if head:
        total, slice_len = head[0].shape[0], head[2].shape[1]
        out_shape.append(shape(total, 3 * heads * HEAD))
        scratch += [
            *swap_scratch(size, slice_len, HEAD),
            *swap_scratch(size, slice_len, 3 * HEAD),
            pltpu.VMEM((size, HEAD, slice_len), F32),
        ]
    here = len(out_shape)
    if ships:
        out_shape += [shape(*array.shape) for array in ships]
        scratch.append(pltpu.SemaphoreType.DMA((len(ships), 2, size)))
    arrays = [*tail, *head]
    return pl.pallas_call(
        functools.partial(
            backward_kernel, bool(tail), bool(head), len(ships), heads, toks, scale, shift
        ),
        out_shape=out_shape,
        in_specs=[VMEM] * len(arrays) + [ANY] * len(ships),
        out_specs=[VMEM] * here + [ANY] * len(ships),
        scratch_shapes=scratch,
        compiler_params=comm_params(collective_id, 56),
        cost_estimate=cost(10**10, 100 * 2**20),
        name="backward_stage",
    )(*arrays, *ships)


def ffn(rows, cot, gate, up, down):
    total, width = rows.shape
    hidden = gate.shape[1]
    step = min(512, total)
    by_rows = pl.BlockSpec((step, width), lambda i: (i, 0))
    by_hidden = pl.BlockSpec((step, hidden), lambda i: (i, 0))
    held = lambda array: pl.BlockSpec(array.shape, lambda i: (0, 0), pipeline_mode=pl.Buffered(1))
    return pl.pallas_call(
        ffn_kernel,
        grid=(total // step,),
        out_shape=[shape(total, width)] * 2 + [shape(total, hidden)] * 3,
        in_specs=[by_rows, by_rows, held(gate), held(up), held(down)],
        out_specs=[by_rows] * 2 + [by_hidden] * 3,
        compiler_params=limits(56),
        cost_estimate=cost(12 * total * width * hidden, 34 * 2**20),
        name="ffn",
    )(rows, cot, gate, up, down)


def weight_grad(lefts, rights, left_blocked):
    count = len(lefts)
    size = lax.axis_size("dp")
    rows = lefts[0].shape[0]
    m, n = lefts[0].shape[1], rights[0].shape[1]
    moving = lambda width: pl.BlockSpec((rows, width // size), lambda e: (0, e))
    fixed = lambda width: pl.BlockSpec(
        (rows, width), lambda e: (0, 0), pipeline_mode=pl.Buffered(1)
    )
    left_spec = moving(m) if left_blocked else fixed(m)
    right_spec = fixed(n) if left_blocked else moving(n)
    out = (m // size, n) if left_blocked else (m, n // size)
    return pl.pallas_call(
        functools.partial(grad_kernel, count, left_blocked),
        grid=(size,),
        in_specs=[left_spec] * count + [right_spec] * count,
        out_specs=pl.BlockSpec((1, *out), lambda e: (e, 0, 0)),
        out_shape=shape(size, *out),
        scratch_shapes=[pltpu.VMEM((out[0], count * rows), BF16)],
        compiler_params=limits(48),
        cost_estimate=cost(2 * count * rows * m * n, 24 * 2**20),
        name="weight_grad",
    )(*lefts, *rights)


def first_visible(ids):
    at = jnp.arange(ids.shape[-1], dtype=jnp.int32)
    starts = jnp.concatenate([jnp.ones_like(ids[..., :1], jnp.bool_), ids[..., 1:] != ids[..., :-1]], axis=-1)
    return lax.cummax(jnp.where(starts, at, 0), axis=ids.ndim - 1)


def block_at(values, index):
    return lax.dynamic_index_in_dim(values, index, 0, keepdims=False)


def scatter_mp(values):
    return lax.psum_scatter(values, "mp", scatter_dimension=0, tiled=True).astype(F32)


def sum_all(values):
    for name in ("dp", "mp"):
        size = lax.axis_size(name)
        step = 1
        while step < size:
            values = values + lax.ppermute(values, name, [(i, i ^ step) for i in range(size)])
            step *= 2
    return values


def sliced_scores(qkv, kv_all, first, positions, scale, shift):
    raw = jnp.einsum("pqd,pkd->pqk", qkv[..., :HEAD], kv_all[..., :HEAD], preferred_element_type=F32)
    at = jnp.arange(kv_all.shape[1], dtype=jnp.int32)
    visible = (at >= first[..., None]) & (at <= positions[:, None])
    return jnp.where(visible, sigmoid_of(raw, scale, shift), 0.0)


def per_device(
    inputs,
    cotangent,
    doc_ids,
    gain_attn,
    w_query,
    w_key,
    w_value,
    w_out,
    gain_ffn,
    w_gate,
    w_up,
    w_down,
):
    dp_size = lax.axis_size("dp")
    mp_size = lax.axis_size("mp")
    micro_count, row_count, seq_count, width = inputs.shape
    slice_len = row_count * mp_size
    total_len = slice_len * dp_size
    rows_here = row_count * seq_count
    shift = math.log(total_len)
    scale = HEAD ** (-0.5)
    dp_at = lax.axis_index("dp")
    mp_at = lax.axis_index("mp")
    first_row = dp_at * slice_len
    positions = first_row + jnp.arange(slice_len, dtype=jnp.int32)
    head_width = w_query.shape[1]
    heads = head_width // HEAD
    hidden = w_gate.shape[1]
    pairs = seq_count * heads
    whole_pairs = pairs == dp_size
    cos_slice, sin_slice = full_tables(positions)
    cos_all, sin_all = full_tables(jnp.arange(total_len, dtype=jnp.int32))
    first_all = first_visible(doc_ids)

    def by_row(table):
        shaped = table.reshape(mp_size, 1, row_count, 1, HEAD)
        return jnp.broadcast_to(shaped, (mp_size, seq_count, row_count, 1, HEAD))

    def rotate(values, back=False):
        sine = -by_row(sin_slice) if back else by_row(sin_slice)
        return values * by_row(cos_slice) + swap_halves(values) * sine

    def to_pairs(values):
        shaped = values.reshape(mp_size, seq_count, row_count, heads, -1)
        return shaped.transpose(1, 3, 0, 2, 4).reshape(pairs, slice_len, -1)

    def from_pairs(values):
        shaped = values.reshape(seq_count, heads, mp_size, row_count, -1)
        return shaped.transpose(2, 0, 3, 1, 4).reshape(mp_size * rows_here, heads, -1)

    def to_rows(values):
        return jnp.swapaxes(values, 0, 1).reshape(rows_here, width)

    def from_rows(values):
        return jnp.swapaxes(values.reshape(seq_count, row_count, width), 0, 1)

    def gather_mp(values):
        return lax.all_gather(values, "mp", axis=0, tiled=True)

    gain_attn_grad = jnp.zeros((width,), F32)
    gain_ffn_grad = jnp.zeros((width,), F32)
    results = []
    input_grads = []
    kept = [[] for _ in range(9)]
    xs = [to_rows(inputs[m]) for m in range(micro_count)]
    cots = [to_rows(cotangent[m]) for m in range(micro_count)]
    normed = [
        (x.astype(F32) * norm_factor(x.astype(F32)) * gain_attn).astype(BF16) for x in xs
    ]
    micros = range(micro_count)
    if whole_pairs:
        stage = (heads, row_count, scale, shift)
        qkv_full, out_full, gate_full = gather_weights(w_query, w_key, w_value, w_out, w_gate)
        firsts = [block_at(first_all[m], dp_at // heads) for m in micros]
        ones = [gather_mp(rows) for rows in normed]
        portions = [gather_mp(cot) for cot in cots]

        def forward_head(m):
            return (ones[m], qkv_full, cos_slice, sin_slice, firsts[m][:, None])

        def forward_tail(m):
            return (got[m], out_full, xs[m], gain_ffn[None])

        def backward_head(m):
            first = firsts[m].reshape(dp_size, 1, slice_len)
            return (attns[m], out_full, qkvs[m], first, cos_all, sin_all)

        def backward_tail(m):
            return (projs[m], qkv_full, ones[m], xs[m], grads[m], gain_attn[None])

        qkvs, got, middles, twos, mixtures = [], [], [], [], []
        gathers = {0: (w_up, 0), 1: (w_down, 1)}
        gathered = []
        for m in range(micro_count + 1):
            tail = forward_tail(m - 1) if m else ()
            head = forward_head(m) if m < micro_count else ()
            gather = gathers.get(m, ())
            outs = forward_stage(10 + m, tail, head, gather, *stage)
            if tail:
                (middle, rows, mixture), outs = take(outs, 3)
                middles.append(middle)
                twos.append(gather_mp(rows))
                mixtures.append(mixture)
            if head:
                (qkv, block), outs = take(outs, 2)
                qkvs.append(qkv)
                got.append(block)
            gathered += outs
        up_full, down_full = gathered
        acts, gates, ups, grads, attns, projs = [], [], [], [], [], []
        for m in micros:
            y, act, gate_grad, up_grad, grad, low, gain_part = middle_part(
                twos[m], portions[m], gate_full, up_full, down_full, middles[m], cots[m],
                gain_ffn[None],
            )
            for held, array in zip((acts, gates, ups, grads), (act, gate_grad, up_grad, grad)):
                held.append(array)
            gain_ffn_grad = gain_ffn_grad + gain_part[0]
            attns.append(gather_mp(low))
            results.append(from_rows((middles[m] + scatter_mp(y)).astype(BF16)))
        shipped = []
        for m in range(micro_count + 1):
            tail = backward_tail(m - 1) if m else ()
            head = backward_head(m) if m < micro_count else ()
            ships = []
            if m == 0:
                ships = [weight_grad(twos, gates, True)]
            if m == 1:
                ships = [weight_grad(twos, ups, True)]
            if m == 2:
                ships = [weight_grad(acts, portions, False)]
            if m == micro_count:
                ships += [weight_grad(mixtures, attns, False), weight_grad(ones, projs, True)]
            outs = backward_stage(20 + m, tail, head, ships, *stage)
            if tail:
                (input_grad, gain_part), outs = take(outs, 2)
                input_grads.append(from_rows(input_grad))
                gain_attn_grad = gain_attn_grad + gain_part[0]
            if head:
                (proj,), outs = take(outs, 1)
                projs.append(proj)
            shipped += outs
        sum_gate, sum_up, sum_down, sum_out, sum_qkv = (
            jnp.sum(blocks.astype(F32), axis=0) for blocks in shipped
        )
    else:
        qkv_full = lax.all_gather(
            jnp.concatenate([w_query, w_key, w_value], axis=1), "dp", axis=0, tiled=True
        )
        out_full = lax.all_gather(w_out, "dp", axis=1, tiled=True)
        gate_full = lax.all_gather(w_gate, "dp", axis=0, tiled=True)
        up_full = lax.all_gather(w_up, "dp", axis=0, tiled=True)
        down_full = lax.all_gather(w_down, "dp", axis=1, tiled=True)
        for micro in micros:
            local_rows = xs[micro].astype(F32)
            local_cot = cots[micro]
            factor_one = norm_factor(local_rows)
            rows_one = gather_mp(normed[micro])
            portion = gather_mp(local_cot)
            projected = dot(rows_one, qkv_full).reshape(
                mp_size, seq_count, row_count, 3, heads, HEAD
            )
            packed = to_pairs(
                jnp.concatenate(
                    [
                        rotate(projected[:, :, :, 0]).astype(BF16),
                        rotate(projected[:, :, :, 1]).astype(BF16),
                        projected[:, :, :, 2].astype(BF16),
                    ],
                    axis=-1,
                )
            )
            kv_all = lax.all_gather(packed[..., HEAD:], "dp", axis=1, tiled=True)
            first = lax.dynamic_slice_in_dim(first_all[micro], first_row, slice_len, 1)
            first = jnp.repeat(first, heads, axis=0)
            weights = sliced_scores(packed, kv_all, first, positions, scale, shift)
            attended = jnp.einsum(
                "pqk,pkd->pqd", weights.astype(BF16), kv_all[..., HEAD:], preferred_element_type=F32
            ).astype(BF16)
            mixture = from_pairs(attended).reshape(mp_size * rows_here, head_width)
            middle = local_rows + scatter_mp(dot(mixture, out_full).astype(BF16))
            factor_two = norm_factor(middle)
            rows_two = gather_mp((middle * factor_two * gain_ffn).astype(BF16))
            y, dh, activated, gate_grad, up_grad = ffn(
                rows_two, portion, gate_full, up_full, down_full
            )
            results.append(from_rows((middle + scatter_mp(y)).astype(BF16)))
            middle_term, gain_part = norm_back(middle, factor_two, gain_ffn, scatter_mp(dh))
            gain_ffn_grad = gain_ffn_grad + gain_part
            middle_grad = local_cot.astype(F32) + middle_term
            attn_portion = gather_mp(middle_grad.astype(BF16))
            mix_grad = to_pairs(dot_nt(attn_portion, out_full).astype(BF16))
            sig = sliced_scores(packed, kv_all, first, positions, scale, shift)
            prob_grad = jnp.einsum(
                "pqd,pkd->pqk", mix_grad, kv_all[..., HEAD:], preferred_element_type=F32
            )
            score_grad = (prob_grad * sig * (1.0 - sig)).astype(BF16)
            dq = jnp.einsum("pqk,pkd->pqd", score_grad, kv_all[..., :HEAD], preferred_element_type=F32)
            dk = jnp.einsum("pqk,pqd->pkd", score_grad, packed[..., :HEAD], preferred_element_type=F32)
            dv = jnp.einsum("pqk,pqd->pkd", sig.astype(BF16), mix_grad, preferred_element_type=F32)
            dkv = lax.psum_scatter(
                jnp.concatenate([dk * scale, dv], axis=-1).astype(BF16), "dp", scatter_dimension=1, tiled=True
            ).astype(F32)
            back = from_pairs(jnp.concatenate([dq * scale, dkv], axis=-1))
            back = back.reshape(mp_size, seq_count, row_count, heads, 3 * HEAD)
            proj_grad = jnp.stack(
                [
                    rotate(back[..., :HEAD], True),
                    rotate(back[..., HEAD : 2 * HEAD], True),
                    back[..., 2 * HEAD :],
                ],
                axis=3,
            ).astype(BF16).reshape(mp_size * rows_here, 3 * head_width)
            partial_grad = dot_nt(proj_grad, qkv_full)
            gain_attn_grad = gain_attn_grad + jnp.sum(partial_grad * rows_one.astype(F32), axis=0)
            input_term, _ = norm_back(
                local_rows, factor_one, gain_attn, scatter_mp(partial_grad.astype(BF16))
            )
            input_grads.append(from_rows(middle_grad + input_term))
            for held, array in zip(
                kept,
                (rows_one, proj_grad, mixture, attn_portion, rows_two, gate_grad, up_grad, activated, portion),
            ):
                held.append(array)

        def scatter_dp(lefts, rights, left_blocked):
            blocks = weight_grad(lefts, rights, left_blocked)
            return lax.psum_scatter(blocks, "dp", scatter_dimension=0, tiled=True)[0].astype(F32)

        ones, projs, mixtures, attns, twos, gates, ups, acts, portions = kept
        sum_gate = scatter_dp(twos, gates, True)
        sum_up = scatter_dp(twos, ups, True)
        sum_down = scatter_dp(acts, portions, False)
        sum_out = scatter_dp(mixtures, attns, False)
        sum_qkv = scatter_dp(ones, projs, True)
    gain_sums = (sum_all(gain_attn_grad / gain_attn), sum_all(gain_ffn_grad))
    return (
        jnp.stack(results),
        jnp.stack(input_grads),
        gain_sums[0],
        sum_qkv[:, :head_width],
        sum_qkv[:, head_width : 2 * head_width],
        sum_qkv[:, 2 * head_width :],
        sum_out,
        gain_sums[1],
        sum_gate,
        sum_up,
        sum_down,
    )


def solution(mesh):
    tokens = P(None, ("dp", "mp"), None, None)
    column = P("dp", "mp")
    row = P("mp", "dp")
    return jax.shard_map(
        per_device,
        mesh=mesh,
        in_specs=(
            tokens, tokens, P(), P(), column, column, column, row, P(), column, column, row,
        ),
        out_specs=(
            tokens, tokens, P(), column, column, column, row, P(), column, column, row,
        ),
        check_vma=False,
    )
```

```python
import functools
import math

import jax
import jax.numpy as jnp
from jax import lax
from jax.experimental import pallas as pl
from jax.experimental.pallas import tpu as pltpu
from jax.sharding import PartitionSpec as P

HEAD = 128
epsilon = 1e-05
rope_base = 10000.0
F32 = jnp.float32
BF16 = jnp.bfloat16


def rope_tables(positions):
    half_size = HEAD // 2
    inverse = jnp.power(rope_base, -(jnp.arange(half_size, dtype=F32) * 2.0 / HEAD))
    angles = positions.astype(F32)[:, None] * inverse[None, :]
    return (jnp.cos(angles), jnp.sin(angles))


def full_tables(positions):
    cosine, sine = rope_tables(positions)
    return (
        jnp.concatenate([cosine, cosine], axis=-1),
        jnp.concatenate([-sine, sine], axis=-1),
    )


def swap_halves(values):
    half_size = HEAD // 2
    return jnp.concatenate([values[..., half_size:], values[..., :half_size]], axis=-1)


def dot(left, right):
    return jnp.dot(left, right, preferred_element_type=F32)


def dot_tn(left, right):
    return lax.dot_general(left, right, (((0,), (0,)), ((), ())), preferred_element_type=F32)


def dot_nt(left, right):
    return lax.dot_general(left, right, (((1,), (1,)), ((), ())), preferred_element_type=F32)


def norm_factor(values):
    return lax.rsqrt(jnp.mean(values * values, axis=-1, keepdims=True) + epsilon)


def norm_back(values, factor, gain, incoming):
    scaled = incoming * gain
    gain_term = jnp.sum(incoming * values * factor, axis=0)
    input_term = factor * scaled - values * factor**3 * jnp.mean(
        scaled * values, axis=-1, keepdims=True
    )
    return (input_term, gain_term)


def sigmoid_of(raw, scale, shift):
    return 1.0 / (1.0 + jnp.exp(shift - raw * scale))


def split_cores(core, values, rows_here):
    shaped = values.reshape(-1, 2, rows_here, values.shape[-1])
    first, second = shaped[:, 0], shaped[:, 1]
    is_first = core == 0
    return jnp.where(is_first, first, second), jnp.where(is_first, second, first)

MESH = pl.DeviceIdType.MESH


class Spot:
    def __init__(self):
        self.dp, self.mp = lax.axis_index("dp"), lax.axis_index("mp")
        self.dp_size, self.mp_size = lax.axis_size("dp"), lax.axis_size("mp")
        self.places = self.mp_size // 2
        self.place, self.core = lax.div(self.mp, 2), lax.rem(self.mp, 2)
        self.sibling = (self.dp, self.mp + 1 - 2 * self.core)
        self.right = (self.dp, self.mp + 2)
        self.left = (self.dp, self.mp - 2)
        self.has_right = self.place < self.places - 1
        self.has_left = self.place > 0

    def peer(self, step):
        return lax.rem(self.dp + step, self.dp_size)

    def enter(self, with_dp, with_mp):
        barrier = pltpu.get_barrier_semaphore()
        count = 0

        def greet(device):
            pl.semaphore_signal(barrier, inc=1, device_id=device, device_id_type=MESH)

        if with_mp:
            greet(self.sibling)
            pl.when(self.has_right)(lambda: greet(self.right))
            pl.when(self.has_left)(lambda: greet(self.left))
            count += 1 + self.has_right.astype(jnp.int32) + self.has_left.astype(jnp.int32)
        if with_dp:
            for step in range(1, self.dp_size):
                greet((self.peer(step), self.mp))
            count += self.dp_size - 1
        pl.semaphore_wait(barrier, count)


class Swap:
    def __init__(self, spot, source, target, send, receive):
        self.spot, self.source, self.target = spot, source, target
        self.copies = [
            pltpu.make_async_remote_copy(
                src_ref=source.at[spot.peer(step)],
                dst_ref=target.at[spot.dp],
                send_sem=send.at[step],
                recv_sem=receive.at[step],
                device_id=(spot.peer(step), spot.mp),
                device_id_type=MESH,
            )
            for step in range(1, spot.dp_size)
        ]

    def start(self):
        for copy in self.copies:
            copy.start()
        self.target[self.spot.dp] = self.source[self.spot.dp]

    def wait(self):
        for copy in self.copies:
            copy.wait()


class Gather:
    def __init__(self, spot, shard, window, sems):
        self.local = pltpu.make_async_copy(shard, window(spot.dp), sems.at[0, 0])
        self.copies = [
            pltpu.make_async_remote_copy(
                src_ref=shard,
                dst_ref=window(spot.dp),
                send_sem=sems.at[0, step],
                recv_sem=sems.at[1, step],
                device_id=(spot.peer(step), spot.mp),
                device_id_type=MESH,
            )
            for step in range(1, spot.dp_size)
        ]

    def start(self):
        for copy in self.copies:
            copy.start()
        self.local.start()

    def wait(self):
        for copy in self.copies:
            copy.wait()
        self.local.wait()


class Spread:
    def __init__(self, spot, shard, full, sems):
        self.spot, self.shard, self.full, self.sems = spot, shard, full, sems
        self.local = pltpu.make_async_copy(shard, full.at[spot.mp], sems.at[6, 0])

    def copy(self, kind, device, p, source=None, core=None):
        at = 2 * p + (self.spot.core if core is None else core)
        return pltpu.make_async_remote_copy(
            src_ref=self.full.at[at] if source is None else source,
            dst_ref=self.full.at[at],
            send_sem=self.sems.at[kind, p],
            recv_sem=self.sems.at[kind + 1, p],
            device_id=device,
            device_id_type=MESH,
        )

    def rightward(self, p, source=None):
        return self.copy(0, self.spot.right, p, source)

    def leftward(self, p, source=None):
        return self.copy(2, self.spot.left, p, source)

    def across(self, p, source=None):
        return self.copy(4, self.spot.sibling, p, source)

    def begin(self):
        spot = self.spot
        pl.when(spot.has_right)(lambda: self.rightward(spot.place, self.shard).start())
        pl.when(spot.has_left)(lambda: self.leftward(spot.place, self.shard).start())
        self.across(spot.place, self.shard).start()
        self.local.start()

    def go_on(self, hop):
        spot = self.spot

        @pl.when(spot.place >= hop)
        def _():
            p = spot.place - hop
            self.rightward(p).wait_recv()
            pl.when(spot.has_right)(lambda: self.rightward(p).start())
            self.across(p).start()

        @pl.when(spot.place + hop < spot.places)
        def _():
            p = spot.place + hop
            self.leftward(p).wait_recv()
            pl.when(spot.has_left)(lambda: self.leftward(p).start())
            self.across(p).start()

    def finish(self):
        spot = self.spot
        for p in range(spot.places):
            self.copy(4, spot.sibling, p, core=1 - spot.core).wait_recv()
            self.across(p).wait_send()
            pl.when(spot.has_right & (spot.place >= p))(lambda: self.rightward(p).wait_send())
            pl.when(spot.has_left & (spot.place <= p))(lambda: self.leftward(p).wait_send())
        self.local.wait()


def spread_scratch(places):
    return [pltpu.SemaphoreType.DMA((7, places))]


class Ship(Swap):
    def __init__(self, spot, source, target, sems):
        super().__init__(spot, source, target, sems.at[0], sems.at[1])
        self.local = pltpu.make_async_copy(source.at[spot.dp], target.at[spot.dp], sems.at[0, 0])

    def start(self):
        for copy in self.copies:
            copy.start()
        self.local.start()

    def wait(self):
        super().wait()
        self.local.wait()


def window_of(full, axis, step, column=0, columns=None):
    def window(index):
        along = pl.ds(pl.multiple_of(index * step, step), step)
        if axis == 1:
            return full.at[:, along]
        if columns is None:
            return full.at[along, :]
        return full.at[along, pl.ds(column, columns)]

    return window


def swap_scratch(size, *block):
    return [
        pltpu.VMEM((size, *block), BF16),
        pltpu.VMEM((size, *block), BF16),
        pltpu.SemaphoreType.DMA((size,)),
        pltpu.SemaphoreType.DMA((size,)),
    ]


def far_first(places):
    orders = []
    for place in range(places):
        right, left, order = list(range(places - 1, place, -1)), list(range(place)), []
        while right or left:
            order += right[:1] + left[:1]
            right, left = right[1:], left[1:]
        orders.append(order + [place])
    return orders


class Sum:
    def __init__(self, spot, mine, out, from_sibling, from_left, from_right, sems):
        self.spot = spot
        self.mine, self.out = mine, out
        self.from_sibling, self.from_left, self.from_right = from_sibling, from_left, from_right
        self.sems = sems
        self.orders = far_first(spot.places)

    def copy(self, source, target, kind, t, device):
        return pltpu.make_async_remote_copy(
            src_ref=source.at[t],
            dst_ref=target.at[t],
            send_sem=self.sems.at[kind, t],
            recv_sem=self.sems.at[kind + 1, t],
            device_id=device,
            device_id_type=MESH,
        )

    def sibling(self, t):
        return self.copy(self.out, self.from_sibling, 0, t, self.spot.sibling)

    def rightward(self, t):
        return self.copy(self.mine, self.from_left, 2, t, self.spot.right)

    def leftward(self, t):
        return self.copy(self.mine, self.from_right, 4, t, self.spot.left)

    def term(self, s):
        chosen = 0
        for place, order in enumerate(self.orders):
            for at, t in enumerate(order):
                if t:
                    chosen = chosen + jnp.where((self.spot.place == place) & (s == at), t, 0)
        return chosen

    def add(self, t, arrived):
        self.mine[t] = (self.mine[t].astype(F32) + arrived[t].astype(F32)).astype(BF16)

    def absorb(self, t):
        self.sibling(t).wait_recv()
        self.add(t, self.from_sibling)

    def send(self, t, arrives, arrived, hop):
        self.absorb(t)
        if arrives:
            hop(t).wait_recv()
            self.add(t, arrived)
        hop(t).start()

    def begin(self, s):
        spot = self.spot

        @pl.when((spot.place == 0) & (s < spot.places - 1))
        def _():
            self.send(spot.places - 1 - s, False, None, self.rightward)

        @pl.when((spot.place == spot.places - 1) & (s < spot.places - 1))
        def _():
            self.send(s, False, None, self.leftward)

    def go_on(self, hop):
        spot = self.spot
        last = spot.places - 1

        @pl.when((spot.place > 0) & (spot.place <= hop))
        def _():
            self.send(last + spot.place - hop, True, self.from_left, self.rightward)

        @pl.when((spot.place < last) & (last - spot.place <= hop))
        def _():
            self.send(hop - last + spot.place, True, self.from_right, self.leftward)

    def finish(self):
        spot = self.spot
        t = spot.place
        self.absorb(t)

        @pl.when(spot.has_left)
        def _():
            self.rightward(t).wait_recv()
            self.add(t, self.from_left)

        @pl.when(spot.has_right)
        def _():
            self.leftward(t).wait_recv()
            self.add(t, self.from_right)

        for t in range(spot.places):
            self.sibling(t).wait_send()
            pl.when(spot.place < t)(lambda: self.rightward(t).wait_send())
            pl.when(spot.place > t)(lambda: self.leftward(t).wait_send())
        return self.mine[spot.place].astype(F32)


def sum_scratch(places, rows_here, width):
    return [pltpu.VMEM((places, rows_here, width), BF16)] * 5 + [
        pltpu.SemaphoreType.DMA((6, places))
    ]


def attend_blocks(qkv, first_ref, out, scale, shift):
    count, block = out.shape[:2]
    row_at = lax.broadcasted_iota(jnp.int32, (block, block), 0)
    col_at = lax.broadcasted_iota(jnp.int32, (block, block), 1)

    @pl.loop(0, count)
    def _(i):
        queries = qkv[i, :, 0:HEAD]
        first = first_ref[pl.ds(pl.multiple_of(i * block, block), block), :]

        def add_block(j, acc, diagonal=False):
            sig = sigmoid_of(dot_nt(queries, qkv[j, :, HEAD : 2 * HEAD]), scale, shift)
            visible = col_at >= first - j * block
            if diagonal:
                visible = visible & (col_at <= row_at)
            weights = jnp.where(visible, sig, 0.0).astype(BF16)
            return acc + dot(weights, qkv[j, :, 2 * HEAD :])

        acc = add_block(i, jnp.zeros((block, HEAD), F32), True)
        out[i] = lax.fori_loop(0, i, add_block, acc).astype(BF16)


def attend_back_blocks(qkv, grad, first_ref, cos_ref, sin_ref, out, dq, scale, shift):
    count, block = grad.shape[:2]
    col_at = lax.broadcasted_iota(jnp.int32, (block, block), 0)
    row_at = lax.broadcasted_iota(jnp.int32, (block, block), 1)
    dq[...] = jnp.zeros_like(dq)

    def unrotate(values, i):
        rows = pl.ds(pl.multiple_of(i * block, block), block)
        swapped = pltpu.roll(values, HEAD // 2, 1)
        return (values * cos_ref[rows, :] - swapped * sin_ref[rows, :]).astype(BF16)

    @pl.loop(0, count)
    def _(j):
        keys = qkv[j, :, HEAD : 2 * HEAD]
        values = qkv[j, :, 2 * HEAD :]
        keys_t = keys.T

        def add_block(i, sums, diagonal=False):
            dk, dv = sums
            queries, grads = qkv[i, :, 0:HEAD], grad[i]
            sig = sigmoid_of(dot_nt(keys, queries), scale, shift)
            visible = col_at >= first_ref[i] - j * block
            if diagonal:
                visible = visible & (col_at <= row_at)
            sig = jnp.where(visible, sig, 0.0)
            prob_grad = dot_nt(values, grads)
            score_grad = (prob_grad * sig * (1.0 - sig)).astype(BF16)
            dq[i] += dot(keys_t, score_grad)
            return dk + dot(score_grad, queries), dv + dot(sig.astype(BF16), grads)

        zero = jnp.zeros((block, HEAD), F32)
        dk, dv = lax.fori_loop(j + 1, count, add_block, add_block(j, (zero, zero), True))
        out[j, :, HEAD : 2 * HEAD] = unrotate(dk * scale, j)
        out[j, :, 2 * HEAD :] = dv.astype(BF16)

    @pl.loop(0, count)
    def _(i):
        out[i, :, 0:HEAD] = unrotate(dq[i].T * scale, i)


def take(refs, count):
    return refs[:count], refs[count:]


def begin_kernel(query, key, value, out, first, qkv_full, out_full, first_full, sems, spread_sems):
    spot = Spot()
    spot.enter(True, True)
    rows, columns = query.shape
    jobs = [
        (shard, window_of(qkv_full, 0, rows, i * columns, columns))
        for i, shard in enumerate((query, key, value))
    ]
    jobs.append((out, window_of(out_full, 1, out.shape[1])))
    gathers = [Gather(spot, shard, window, sems.at[i]) for i, (shard, window) in enumerate(jobs)]
    spread = Spread(spot, first, first_full, spread_sems)
    spread.begin()
    for gather in gathers:
        gather.start()
    for hop in range(1, spot.places):
        spread.go_on(hop)
    for gather in gathers:
        gather.wait()
    spread.finish()


def forward_kernel(tail, head, spreads, heads, toks, scale, shift, *refs):
    tail_in, refs = take(refs, 4 * tail)
    head_in, refs = take(refs, 5 * head)
    spread_in, refs = take(refs, spreads)
    tail_out, refs = take(refs, 3 * tail)
    head_out, refs = take(refs, 2 * head)
    spread_out, refs = take(refs, spreads)
    sum_refs, refs = take(refs, 6 * tail)
    head_refs, refs = take(refs, 9 * head)
    spot = Spot()
    spot.enter(head, tail or spreads)
    if spreads:
        spread = Spread(spot, *spread_in, *spread_out, *refs)
        spread.begin()

    if tail:
        got, out_weight, x_ref, gain_ref = tail_in
        middle_ref, normed_ref, mix_ref = tail_out
        pairs = got.shape[0]
        owner_rows = toks * (pairs // heads)
        for o in range(mix_ref.shape[0] // owner_rows):
            for p in range(pairs):
                s, h = p // heads, p % heads
                mix_ref[pl.ds(o * owner_rows + s * toks, toks), h * HEAD : (h + 1) * HEAD] = got[
                    p, pl.ds(o * toks, toks), :
                ]
        summed = Sum(spot, *sum_refs)
        chip_rows = 2 * owner_rows

        @pl.loop(0, spot.places)
        def _(s):
            t = summed.term(s)
            rows = pl.ds(pl.multiple_of(t * chip_rows, chip_rows), chip_rows)
            value = dot(mix_ref[rows, :], out_weight[...]).astype(BF16)
            keep, send = split_cores(spot.core, value, owner_rows)
            summed.mine[t] = keep[0]
            summed.out[t] = send[0]
            summed.sibling(t).start()

        @pl.loop(0, spot.places - 1)
        def _(s):
            summed.begin(s)

    if head:
        rows_ref, weight_ref, cos_ref, sin_ref, first_ref = head_in
        qkv_ref, got_ref = head_out
        made, paired, qkv, qkv_send, qkv_recv, part, got, part_send, part_recv = head_refs
        pairs = paired.shape[0]
        owner_rows = toks * (pairs // heads)
        step = made.shape[0]

        @pl.loop(0, rows_ref.shape[0] // step)
        def _(i):
            rows = pl.ds(pl.multiple_of(i * step, step), step)
            made[...] = dot(rows_ref[rows, :], weight_ref[...])
            for j in range(step // owner_rows):
                to = pl.ds(pl.multiple_of((i * (step // owner_rows) + j) * toks, toks), toks)
                cosine, sine = cos_ref[to, :], sin_ref[to, :]
                for p in range(pairs):
                    s, h = p // heads, p % heads
                    here = pl.ds(j * owner_rows + s * toks, toks)
                    for kind in range(3):
                        piece = made[here, pl.ds((kind * heads + h) * HEAD, HEAD)]
                        if kind < 2:
                            piece = piece * cosine + pltpu.roll(piece, HEAD // 2, 1) * sine
                        paired[p, to, kind * HEAD : (kind + 1) * HEAD] = piece.astype(BF16)

        swap = Swap(spot, paired, qkv, qkv_send, qkv_recv)
        swap.start()
    if spreads:
        spread.go_on(1)
    if tail and spot.places > 2:
        summed.go_on(1)
    if head:
        swap.wait()
    for hop in range(2, spot.places - 1):
        if spreads:
            spread.go_on(hop)
        if tail:
            summed.go_on(hop)
    if head:
        attend_blocks(qkv, first_ref, part, scale, shift)
        swap = Swap(spot, part, got, part_send, part_recv)
        swap.start()
        qkv_ref[...] = qkv[...]
        swap.wait()
        got_ref[...] = got[...]
    if spreads:
        if spot.places > 2:
            spread.go_on(spot.places - 1)
    if tail:
        middle = x_ref[...].astype(F32) + summed.finish()
        middle_ref[...] = middle
        normed_ref[...] = (middle * norm_factor(middle) * gain_ref[...]).astype(BF16)
    if spreads:
        spread.finish()


def middle_kernel(
    owner_rows,
    rows_ref, cot_ref, gate_ref, up_ref, down_ref, middle_ref, local_cot_ref, gain_ref, shard,
    y_ref, act_ref, dgate_ref, dup_ref, grad_ref, low_ref, gain_grad_ref, full,
    spread_sems, *sum_refs,
):
    spot = Spot()
    spot.enter(False, True)
    summed = Sum(spot, *sum_refs)
    spread = Spread(spot, shard, full, spread_sems)
    spread.begin()
    hidden, width = gate_ref.shape[1], rows_ref.shape[1]
    chip_rows = 2 * owner_rows
    tile = min(256, hidden)

    @pl.loop(0, spot.places)
    def _(s):
        place = summed.term(s)
        rows = pl.ds(pl.multiple_of(place * chip_rows, chip_rows), chip_rows)

        @pl.loop(0, hidden // tile)
        def _(t):
            cols = pl.ds(pl.multiple_of(t * tile, tile), tile)
            gate = dot(rows_ref[rows, :], gate_ref[:, cols])
            up = dot(rows_ref[rows, :], up_ref[:, cols])
            sig = jax.nn.sigmoid(gate)
            silu = gate * sig
            act_ref[rows, cols] = (silu * up).astype(BF16)
            grad = dot_nt(cot_ref[rows, :], down_ref[cols, :])
            dgate_ref[rows, cols] = (grad * up * sig * (1.0 + gate * (1.0 - sig))).astype(BF16)
            dup_ref[rows, cols] = (grad * silu).astype(BF16)

        pl.when(s > 0)(lambda: summed.begin(s - 1))
        for hop in range(1, spot.places - 1):
            @pl.when(s == hop + 1)
            def _():
                spread.go_on(hop)
                summed.go_on(hop)

        @pl.loop(0, width // 256)
        def _(t):
            cols = pl.ds(pl.multiple_of(t * 256, 256), 256)
            y_ref[rows, cols] = dot(act_ref[rows, :], down_ref[:, cols]).astype(BF16)
            value = dot_nt(dgate_ref[rows, :], gate_ref[cols, :])
            value += dot_nt(dup_ref[rows, :], up_ref[cols, :])
            keep, send = split_cores(spot.core, value.astype(BF16), owner_rows)
            summed.mine[place, :, cols] = keep[0]
            summed.out[place, :, cols] = send[0]

        summed.sibling(place).start()

    spread.go_on(spot.places - 1)
    incoming = summed.finish()
    middle = middle_ref[...]
    term, gain_grad = norm_back(middle, norm_factor(middle), gain_ref[...], incoming)
    gain_grad_ref[...] = gain_grad[None]
    grad = local_cot_ref[...].astype(F32) + term
    grad_ref[...] = grad
    low_ref[...] = grad.astype(BF16)
    spread.finish()


def backward_kernel(tail, head, ships, spreads, heads, toks, scale, shift, *refs):
    tail_in, refs = take(refs, 6 * tail)
    head_in, refs = take(refs, 6 * head)
    ship_in, refs = take(refs, ships)
    spread_in, refs = take(refs, spreads)
    tail_out, refs = take(refs, 2 * tail)
    head_out, refs = take(refs, head)
    ship_out, refs = take(refs, ships)
    spread_out, refs = take(refs, spreads)
    sum_refs, refs = take(refs, 6 * tail)
    head_refs, refs = take(refs, 9 * head)
    spot = Spot()
    spot.enter(head or ships > 0, tail or spreads)
    shipped = [
        Ship(spot, source, target, refs[-1].at[i])
        for i, (source, target) in enumerate(zip(ship_in, ship_out))
    ]
    if spreads:
        spread = Spread(spot, *spread_in, *spread_out, refs[0])
        spread.begin()

    if tail:
        proj_ref, weight_ref, rows_one_ref, x_ref, grad_ref, gain_ref = tail_in
        result_ref, gain_grad_ref = tail_out
        owner_rows = x_ref.shape[0]
        summed = Sum(spot, *sum_refs)
        chip_rows = 2 * owner_rows
        gain_grad_ref[...] = jnp.zeros_like(gain_grad_ref)

        @pl.loop(0, spot.places)
        def _(s):
            t = summed.term(s)
            rows = pl.ds(pl.multiple_of(t * chip_rows, chip_rows), chip_rows)
            value = dot_nt(proj_ref[rows, :], weight_ref[...])
            gain_grad_ref[...] += jnp.sum(
                value * rows_one_ref[rows, :].astype(F32), axis=0, keepdims=True
            )
            keep, send = split_cores(spot.core, value.astype(BF16), owner_rows)
            summed.mine[t] = keep[0]
            summed.out[t] = send[0]
            summed.sibling(t).start()
            pl.when(s > 0)(lambda: summed.begin(s - 1))

    if head:
        rows_ref, out_weight_ref, qkv, first_ref, cos_ref, sin_ref = head_in
        (head_proj_ref,) = head_out
        part, got, part_send, part_recv, blocks, paired, blocks_send, blocks_recv, dq = head_refs
        pairs = part.shape[0]
        owner_rows = toks * (pairs // heads)
        total = rows_ref.shape[0]
        step = min(512, total)

        @pl.loop(0, total // step)
        def _(i):
            rows = pl.ds(pl.multiple_of(i * step, step), step)
            made = dot_nt(rows_ref[rows, :], out_weight_ref[...]).astype(BF16)
            for j in range(step // owner_rows):
                to = pl.ds(pl.multiple_of((i * (step // owner_rows) + j) * toks, toks), toks)
                for p in range(pairs):
                    s, h = p // heads, p % heads
                    start = j * owner_rows + s * toks
                    part[p, to, :] = made[start : start + toks, h * HEAD : (h + 1) * HEAD]

        swap = Swap(spot, part, got, part_send, part_recv)
        swap.start()
        swap.wait()
    for ship in shipped:
        ship.start()
    if spreads:
        spread.go_on(1)
    if tail and spot.places > 2:
        summed.go_on(1)
    if head:
        attend_back_blocks(qkv, got, first_ref, cos_ref, sin_ref, blocks, dq, scale, shift)
        swap = Swap(spot, blocks, paired, blocks_send, blocks_recv)
        swap.start()
    for hop in range(2, spot.places - 1):
        if spreads:
            spread.go_on(hop)
        if tail:
            summed.go_on(hop)
    if head:
        swap.wait()
        for o in range(total // owner_rows):
            for p in range(pairs):
                s, h = p // heads, p % heads
                for kind in range(3):
                    head_proj_ref[
                        pl.ds(o * owner_rows + s * toks, toks),
                        (kind * heads + h) * HEAD : (kind * heads + h + 1) * HEAD,
                    ] = paired[p, pl.ds(o * toks, toks), kind * HEAD : (kind + 1) * HEAD]
    if spreads and spot.places > 2:
        spread.go_on(spot.places - 1)
    if tail:
        incoming = summed.finish()
        x = x_ref[...].astype(F32)
        term, _ = norm_back(x, norm_factor(x), gain_ref[...], incoming)
        result_ref[...] = grad_ref[...] + term
    for ship in shipped:
        ship.wait()
    if spreads:
        spread.finish()


def ffn_kernel(
    rows_ref, cot_ref, gate_ref, up_ref, down_ref, y_ref, dh_ref, act_ref, dgate_ref, dup_ref
):
    hidden = gate_ref.shape[1]
    width = rows_ref.shape[1]
    tile = min(256, hidden)

    @pl.loop(0, hidden // tile)
    def _(t):
        cols = pl.ds(pl.multiple_of(t * tile, tile), tile)
        gate = dot(rows_ref[...], gate_ref[:, cols])
        up = dot(rows_ref[...], up_ref[:, cols])
        sig = jax.nn.sigmoid(gate)
        silu = gate * sig
        act_ref[:, cols] = (silu * up).astype(BF16)
        grad = dot_nt(cot_ref[...], down_ref[cols, :])
        dgate_ref[:, cols] = (grad * up * sig * (1.0 + gate * (1.0 - sig))).astype(BF16)
        dup_ref[:, cols] = (grad * silu).astype(BF16)

    @pl.loop(0, width // 256)
    def _(t):
        cols = pl.ds(pl.multiple_of(t * 256, 256), 256)
        y_ref[:, cols] = dot(act_ref[...], down_ref[:, cols]).astype(BF16)
        dh = dot_nt(dgate_ref[...], gate_ref[cols, :]) + dot_nt(dup_ref[...], up_ref[cols, :])
        dh_ref[:, cols] = dh.astype(BF16)


def grad_kernel(count, groups, left_blocked, *refs):
    lefts, refs = take(refs, count)
    rights, refs = take(refs, count * groups)
    out_refs, (turned,) = take(refs, groups)
    rows = lefts[0].shape[0]

    def turn():
        for m, left in enumerate(lefts):
            turned[:, m * rows : (m + 1) * rows] = left[...].T

    if left_blocked:
        turn()
    else:
        pl.when(pl.program_id(0) == 0)(turn)
    tile = math.gcd(out_refs[0].shape[2], 256)
    for g, out_ref in enumerate(out_refs):
        own = rights[g * count : (g + 1) * count]

        @pl.loop(0, out_ref.shape[2] // tile)
        def _(t):
            cols = pl.ds(pl.multiple_of(t * tile, tile), tile)
            total = dot(turned[:, :rows], own[0][:, cols])
            for m in range(1, count):
                total += dot(turned[:, m * rows : (m + 1) * rows], own[m][:, cols])
            out_ref[0, :, cols] = total.astype(BF16)


VMEM = pl.BlockSpec(memory_space=pltpu.VMEM)
ANY = pl.BlockSpec(memory_space=pl.ANY)


def cost(flops, nbytes):
    return pl.CostEstimate(flops=flops, bytes_accessed=nbytes, transcendentals=0)


def limits(mebibytes):
    return pltpu.CompilerParams(vmem_limit_bytes=mebibytes * 2**20)


def shape(*dims, dtype=BF16):
    return jax.ShapeDtypeStruct(dims, dtype)


def comm_params(collective_id, mebibytes):
    return pltpu.CompilerParams(
        collective_id=collective_id, has_side_effects=True, vmem_limit_bytes=mebibytes * 2**20
    )


def begin(query, key, value, out, first):
    size, mp_size = lax.axis_size("dp"), lax.axis_size("mp")
    rows, columns = query.shape
    return pl.pallas_call(
        begin_kernel,
        out_shape=[
            shape(rows * size, 3 * columns),
            shape(out.shape[0], out.shape[1] * size),
            shape(mp_size, *first.shape),
        ],
        in_specs=[ANY] * 5,
        out_specs=[ANY] * 3,
        scratch_shapes=[
            pltpu.SemaphoreType.DMA((4, 2, size)),
            *spread_scratch(mp_size // 2),
        ],
        compiler_params=comm_params(0, 8),
        cost_estimate=cost(0, 60 * 2**20),
        name="begin",
    )(query, key, value, out, first)


def forward_stage(collective_id, tail, head, shard, heads, toks, scale, shift):
    size, mp_size = lax.axis_size("dp"), lax.axis_size("mp")
    out_shape, scratch = [], []
    if tail:
        blocks, _, x, _ = tail
        owner_rows, width = x.shape
        total = blocks.shape[1] * blocks.shape[0] // heads
        out_shape += [
            shape(owner_rows, width, dtype=F32),
            shape(owner_rows, width),
            shape(total, heads * HEAD),
        ]
        scratch += sum_scratch(mp_size // 2, owner_rows, width)
    if head:
        total, slice_len = head[0].shape[0], head[2].shape[0]
        out_shape += [shape(size, slice_len, 3 * HEAD), shape(size, slice_len, HEAD)]
        scratch += [
            pltpu.VMEM((min(512, total), 3 * heads * HEAD), F32),
            *swap_scratch(size, slice_len, 3 * HEAD),
            *swap_scratch(size, slice_len, HEAD),
        ]
    here, spreads = len(out_shape), len(shard)
    if spreads:
        out_shape.append(shape(mp_size, *shard[0].shape))
        scratch += spread_scratch(mp_size // 2)
    arrays = [*tail, *head]
    return pl.pallas_call(
        functools.partial(
            forward_kernel, bool(tail), bool(head), spreads, heads, toks, scale, shift
        ),
        out_shape=out_shape,
        in_specs=[VMEM] * len(arrays) + [ANY] * spreads,
        out_specs=[VMEM] * here + [ANY] * spreads,
        scratch_shapes=scratch,
        compiler_params=comm_params(collective_id, 52),
        cost_estimate=cost(10**10, 100 * 2**20),
        name="forward_stage",
    )(*arrays, *shard)


def middle_part(rows, cot, gate, up, down, middle, local_cot, gain, shard):
    total, width = rows.shape
    hidden = gate.shape[1]
    mp_size = lax.axis_size("mp")
    owner_rows = middle.shape[0]
    return pl.pallas_call(
        functools.partial(middle_kernel, owner_rows),
        out_shape=[
            shape(total, width),
            shape(total, hidden),
            shape(total, hidden),
            shape(total, hidden),
            shape(owner_rows, width, dtype=F32),
            shape(owner_rows, width),
            shape(1, width, dtype=F32),
            shape(mp_size, *shard.shape),
        ],
        in_specs=[VMEM] * 8 + [ANY],
        out_specs=[VMEM] * 7 + [ANY],
        scratch_shapes=spread_scratch(mp_size // 2)
        + sum_scratch(mp_size // 2, owner_rows, width),
        compiler_params=comm_params(1, 60),
        cost_estimate=cost(12 * total * width * hidden, 34 * 2**20),
        name="middle_part",
    )(rows, cot, gate, up, down, middle, local_cot, gain, shard)


def backward_stage(collective_id, tail, head, ships, shard, heads, toks, scale, shift):
    size, mp_size = lax.axis_size("dp"), lax.axis_size("mp")
    places = mp_size // 2
    out_shape, scratch = [], []
    if tail:
        owner_rows, width = tail[3].shape
        out_shape += [shape(owner_rows, width, dtype=F32), shape(1, width, dtype=F32)]
        scratch += sum_scratch(places, owner_rows, width)
    if head:
        total, slice_len = head[0].shape[0], head[2].shape[1]
        out_shape.append(shape(total, 3 * heads * HEAD))
        scratch += [
            *swap_scratch(size, slice_len, HEAD),
            *swap_scratch(size, slice_len, 3 * HEAD),
            pltpu.VMEM((size, HEAD, slice_len), F32),
        ]
    here, spreads = len(out_shape), len(shard)
    if spreads:
        scratch += spread_scratch(places)
    if ships:
        scratch.append(pltpu.SemaphoreType.DMA((len(ships), 2, size)))
    out_shape += [shape(*array.shape) for array in ships]
    out_shape += [shape(mp_size, *array.shape) for array in shard]
    arrays = [*tail, *head]
    passing = len(ships) + spreads
    return pl.pallas_call(
        functools.partial(
            backward_kernel,
            bool(tail), bool(head), len(ships), spreads, heads, toks, scale, shift,
        ),
        out_shape=out_shape,
        in_specs=[VMEM] * len(arrays) + [ANY] * passing,
        out_specs=[VMEM] * here + [ANY] * passing,
        scratch_shapes=scratch,
        compiler_params=comm_params(collective_id, 56),
        cost_estimate=cost(10**10, 100 * 2**20),
        name="backward_stage",
    )(*arrays, *ships, *shard)


def ffn(rows, cot, gate, up, down):
    total, width = rows.shape
    hidden = gate.shape[1]
    step = min(512, total)
    by_rows = pl.BlockSpec((step, width), lambda i: (i, 0))
    by_hidden = pl.BlockSpec((step, hidden), lambda i: (i, 0))
    held = lambda array: pl.BlockSpec(array.shape, lambda i: (0, 0), pipeline_mode=pl.Buffered(1))
    return pl.pallas_call(
        ffn_kernel,
        grid=(total // step,),
        out_shape=[shape(total, width)] * 2 + [shape(total, hidden)] * 3,
        in_specs=[by_rows, by_rows, held(gate), held(up), held(down)],
        out_specs=[by_rows] * 2 + [by_hidden] * 3,
        compiler_params=limits(56),
        cost_estimate=cost(12 * total * width * hidden, 34 * 2**20),
        name="ffn",
    )(rows, cot, gate, up, down)


def weight_grad(lefts, groups, left_blocked):
    count = len(lefts)
    size = lax.axis_size("dp")
    rows = lefts[0].shape[0]
    m, n = lefts[0].shape[1], groups[0][0].shape[1]
    moving = lambda width: pl.BlockSpec((rows, width // size), lambda e: (0, e))
    fixed = lambda width: pl.BlockSpec(
        (rows, width), lambda e: (0, 0), pipeline_mode=pl.Buffered(1)
    )
    left_spec = moving(m) if left_blocked else fixed(m)
    right_spec = fixed(n) if left_blocked else moving(n)
    out = (m // size, n) if left_blocked else (m, n // size)
    return pl.pallas_call(
        functools.partial(grad_kernel, count, len(groups), left_blocked),
        grid=(size,),
        in_specs=[left_spec] * count + [right_spec] * (count * len(groups)),
        out_specs=[pl.BlockSpec((1, *out), lambda e: (e, 0, 0))] * len(groups),
        out_shape=[shape(size, *out)] * len(groups),
        scratch_shapes=[pltpu.VMEM((out[0], count * rows), BF16)],
        compiler_params=limits(52),
        cost_estimate=cost(2 * count * rows * m * n * len(groups), 24 * 2**20),
        name="weight_grad",
    )(*lefts, *(right for group in groups for right in group))


def first_visible(ids):
    at = jnp.arange(ids.shape[-1], dtype=jnp.int32)
    starts = jnp.concatenate([jnp.ones_like(ids[..., :1], jnp.bool_), ids[..., 1:] != ids[..., :-1]], axis=-1)
    return lax.cummax(jnp.where(starts, at, 0), axis=ids.ndim - 1)


def block_at(values, index):
    return lax.dynamic_index_in_dim(values, index, 0, keepdims=False)


def scatter_mp(values):
    return lax.psum_scatter(values, "mp", scatter_dimension=0, tiled=True).astype(F32)


def sum_all(values):
    for name in ("dp", "mp"):
        size = lax.axis_size(name)
        step = 1
        while step < size:
            values = values + lax.ppermute(values, name, [(i, i ^ step) for i in range(size)])
            step *= 2
    return values


def sliced_scores(qkv, kv_all, first, positions, scale, shift):
    raw = jnp.einsum("pqd,pkd->pqk", qkv[..., :HEAD], kv_all[..., :HEAD], preferred_element_type=F32)
    at = jnp.arange(kv_all.shape[1], dtype=jnp.int32)
    visible = (at >= first[..., None]) & (at <= positions[:, None])
    return jnp.where(visible, sigmoid_of(raw, scale, shift), 0.0)


def per_device(
    inputs,
    cotangent,
    doc_ids,
    gain_attn,
    w_query,
    w_key,
    w_value,
    w_out,
    gain_ffn,
    w_gate,
    w_up,
    w_down,
):
    dp_size = lax.axis_size("dp")
    mp_size = lax.axis_size("mp")
    micro_count, row_count, seq_count, width = inputs.shape
    slice_len = row_count * mp_size
    total_len = slice_len * dp_size
    rows_here = row_count * seq_count
    shift = math.log(total_len)
    scale = HEAD ** (-0.5)
    dp_at = lax.axis_index("dp")
    mp_at = lax.axis_index("mp")
    first_row = dp_at * slice_len
    positions = first_row + jnp.arange(slice_len, dtype=jnp.int32)
    head_width = w_query.shape[1]
    heads = head_width // HEAD
    hidden = w_gate.shape[1]
    pairs = seq_count * heads
    whole_pairs = pairs == dp_size
    cos_slice, sin_slice = full_tables(positions)
    cos_all, sin_all = full_tables(jnp.arange(total_len, dtype=jnp.int32))
    first_all = first_visible(doc_ids)

    def by_row(table):
        shaped = table.reshape(mp_size, 1, row_count, 1, HEAD)
        return jnp.broadcast_to(shaped, (mp_size, seq_count, row_count, 1, HEAD))

    def rotate(values, back=False):
        sine = -by_row(sin_slice) if back else by_row(sin_slice)
        return values * by_row(cos_slice) + swap_halves(values) * sine

    def to_pairs(values):
        shaped = values.reshape(mp_size, seq_count, row_count, heads, -1)
        return shaped.transpose(1, 3, 0, 2, 4).reshape(pairs, slice_len, -1)

    def from_pairs(values):
        shaped = values.reshape(seq_count, heads, mp_size, row_count, -1)
        return shaped.transpose(2, 0, 3, 1, 4).reshape(mp_size * rows_here, heads, -1)

    def to_rows(values):
        return jnp.swapaxes(values, 0, 1).reshape(rows_here, width)

    def from_rows(values):
        return jnp.swapaxes(values.reshape(seq_count, row_count, width), 0, 1)

    def gather_mp(values):
        return lax.all_gather(values, "mp", axis=0, tiled=True)

    gain_attn_grad = jnp.zeros((width,), F32)
    gain_ffn_grad = jnp.zeros((width,), F32)
    results = []
    input_grads = []
    kept = [[] for _ in range(9)]
    xs = [to_rows(inputs[m]) for m in range(micro_count)]
    cots = [to_rows(cotangent[m]) for m in range(micro_count)]
    normed = [
        (x.astype(F32) * norm_factor(x.astype(F32)) * gain_attn).astype(BF16) for x in xs
    ]
    micros = range(micro_count)
    if whole_pairs:
        stage = (heads, row_count, scale, shift)
        firsts = [block_at(first_all[m], dp_at // heads) for m in micros]
        last = micro_count - 1

        def whole(blocks):
            return blocks.reshape(mp_size * rows_here, width)

        def gather_dp(values, axis):
            return lax.all_gather(values, "dp", axis=axis, tiled=True)

        def scatter_dp(blocks):
            return lax.psum_scatter(blocks, "dp", scatter_dimension=0, tiled=True)[0].astype(F32)

        qkv_full, out_full, rows_one = begin(w_query, w_key, w_value, w_out, normed[0])
        gate_shard, up_shard, down_shard, cots, _ = lax.optimization_barrier(
            (w_gate, w_up, w_down, cots, rows_one)
        )
        gate_full = gather_dp(gate_shard, 0)
        up_full = gather_dp(up_shard, 0)
        portions = [gather_mp(cots[0])]
        down_full = gather_dp(down_shard, 1)
        portions += [gather_mp(cot) for cot in cots[1:]]
        ones, qkvs, got, middles, lows, twos, mixtures = [whole(rows_one)], [], [], [], [], [], []
        for m in range(micro_count + 1):
            tail, head, shard = (), (), ()
            if m:
                tail = (got[m - 1], out_full, xs[m - 1], gain_ffn[None])
            if m < micro_count:
                head = (ones[m], qkv_full, cos_slice, sin_slice, firsts[m][:, None])
            if m < last:
                shard = (normed[m + 1],)
            elif lows:
                shard = (lows[m - last],)
            outs = forward_stage(10 + m, tail, head, shard, *stage)
            if tail:
                (middle, low, mixture), outs = take(outs, 3)
                middles.append(middle)
                lows.append(low)
                mixtures.append(mixture)
            if head:
                (qkv, block), outs = take(outs, 2)
                qkvs.append(qkv)
                got.append(block)
            if shard:
                (ones if m < last else twos).append(whole(outs[0]))
        acts, gates, ups, grads, low_grads, attns, projs = [], [], [], [], [], [], []
        for m in micros:
            shard = lows[len(twos)] if len(twos) < micro_count else low_grads[len(attns)]
            y, act, gate_grad, up_grad, grad, low, gain_part, full = middle_part(
                twos[m], portions[m], gate_full, up_full, down_full, middles[m], cots[m],
                gain_ffn[None], shard,
            )
            (twos if len(twos) < micro_count else attns).append(whole(full))
            for held, array in zip(
                (acts, gates, ups, grads, low_grads), (act, gate_grad, up_grad, grad, low)
            ):
                held.append(array)
            gain_ffn_grad = gain_ffn_grad + gain_part[0]
            results.append(from_rows((middles[m] + scatter_mp(y)).astype(BF16)))
        sum_gate, sum_up = [scatter_dp(grad) for grad in weight_grad(twos, (gates, ups), True)]
        sum_down = scatter_dp(weight_grad(acts, (portions,), False)[0])
        for m in range(micro_count + 1):
            tail, head, ships, shard = (), (), (), ()
            if m:
                tail = (projs[m - 1], qkv_full, ones[m - 1], xs[m - 1], grads[m - 1], gain_attn[None])
            if m < micro_count:
                first = firsts[m].reshape(dp_size, 1, slice_len)
                head = (attns[m], out_full, qkvs[m], first, cos_all, sin_all)
            if len(attns) < micro_count:
                shard = (low_grads[len(attns)],)
            if m == micro_count:
                ships = (
                    *weight_grad(mixtures, (attns,), False),
                    *weight_grad(ones, (projs,), True),
                )
            outs = backward_stage(20 + m, tail, head, ships, shard, *stage)
            if tail:
                (input_grad, gain_part), outs = take(outs, 2)
                input_grads.append(from_rows(input_grad))
                gain_attn_grad = gain_attn_grad + gain_part[0]
            if head:
                (proj,), outs = take(outs, 1)
                projs.append(proj)
            if shard:
                attns.append(whole(outs[-1]))
        sum_out, sum_qkv = (jnp.sum(blocks.astype(F32), axis=0) for blocks in outs)
    else:
        qkv_full = lax.all_gather(
            jnp.concatenate([w_query, w_key, w_value], axis=1), "dp", axis=0, tiled=True
        )
        out_full = lax.all_gather(w_out, "dp", axis=1, tiled=True)
        gate_full = lax.all_gather(w_gate, "dp", axis=0, tiled=True)
        up_full = lax.all_gather(w_up, "dp", axis=0, tiled=True)
        down_full = lax.all_gather(w_down, "dp", axis=1, tiled=True)
        for micro in micros:
            local_rows = xs[micro].astype(F32)
            local_cot = cots[micro]
            factor_one = norm_factor(local_rows)
            rows_one = gather_mp(normed[micro])
            portion = gather_mp(local_cot)
            projected = dot(rows_one, qkv_full).reshape(
                mp_size, seq_count, row_count, 3, heads, HEAD
            )
            packed = to_pairs(
                jnp.concatenate(
                    [
                        rotate(projected[:, :, :, 0]).astype(BF16),
                        rotate(projected[:, :, :, 1]).astype(BF16),
                        projected[:, :, :, 2].astype(BF16),
                    ],
                    axis=-1,
                )
            )
            kv_all = lax.all_gather(packed[..., HEAD:], "dp", axis=1, tiled=True)
            first = lax.dynamic_slice_in_dim(first_all[micro], first_row, slice_len, 1)
            first = jnp.repeat(first, heads, axis=0)
            weights = sliced_scores(packed, kv_all, first, positions, scale, shift)
            attended = jnp.einsum(
                "pqk,pkd->pqd", weights.astype(BF16), kv_all[..., HEAD:], preferred_element_type=F32
            ).astype(BF16)
            mixture = from_pairs(attended).reshape(mp_size * rows_here, head_width)
            middle = local_rows + scatter_mp(dot(mixture, out_full).astype(BF16))
            factor_two = norm_factor(middle)
            rows_two = gather_mp((middle * factor_two * gain_ffn).astype(BF16))
            y, dh, activated, gate_grad, up_grad = ffn(
                rows_two, portion, gate_full, up_full, down_full
            )
            results.append(from_rows((middle + scatter_mp(y)).astype(BF16)))
            middle_term, gain_part = norm_back(middle, factor_two, gain_ffn, scatter_mp(dh))
            gain_ffn_grad = gain_ffn_grad + gain_part
            middle_grad = local_cot.astype(F32) + middle_term
            attn_portion = gather_mp(middle_grad.astype(BF16))
            mix_grad = to_pairs(dot_nt(attn_portion, out_full).astype(BF16))
            sig = sliced_scores(packed, kv_all, first, positions, scale, shift)
            prob_grad = jnp.einsum(
                "pqd,pkd->pqk", mix_grad, kv_all[..., HEAD:], preferred_element_type=F32
            )
            score_grad = (prob_grad * sig * (1.0 - sig)).astype(BF16)
            dq = jnp.einsum("pqk,pkd->pqd", score_grad, kv_all[..., :HEAD], preferred_element_type=F32)
            dk = jnp.einsum("pqk,pqd->pkd", score_grad, packed[..., :HEAD], preferred_element_type=F32)
            dv = jnp.einsum("pqk,pqd->pkd", sig.astype(BF16), mix_grad, preferred_element_type=F32)
            dkv = lax.psum_scatter(
                jnp.concatenate([dk * scale, dv], axis=-1).astype(BF16), "dp", scatter_dimension=1, tiled=True
            ).astype(F32)
            back = from_pairs(jnp.concatenate([dq * scale, dkv], axis=-1))
            back = back.reshape(mp_size, seq_count, row_count, heads, 3 * HEAD)
            proj_grad = jnp.stack(
                [
                    rotate(back[..., :HEAD], True),
                    rotate(back[..., HEAD : 2 * HEAD], True),
                    back[..., 2 * HEAD :],
                ],
                axis=3,
            ).astype(BF16).reshape(mp_size * rows_here, 3 * head_width)
            partial_grad = dot_nt(proj_grad, qkv_full)
            gain_attn_grad = gain_attn_grad + jnp.sum(partial_grad * rows_one.astype(F32), axis=0)
            input_term, _ = norm_back(
                local_rows, factor_one, gain_attn, scatter_mp(partial_grad.astype(BF16))
            )
            input_grads.append(from_rows(middle_grad + input_term))
            for held, array in zip(
                kept,
                (rows_one, proj_grad, mixture, attn_portion, rows_two, gate_grad, up_grad, activated, portion),
            ):
                held.append(array)

        def scatter_dp(lefts, rights, left_blocked):
            (blocks,) = weight_grad(lefts, (rights,), left_blocked)
            return lax.psum_scatter(blocks, "dp", scatter_dimension=0, tiled=True)[0].astype(F32)

        ones, projs, mixtures, attns, twos, gates, ups, acts, portions = kept
        sum_gate = scatter_dp(twos, gates, True)
        sum_up = scatter_dp(twos, ups, True)
        sum_down = scatter_dp(acts, portions, False)
        sum_out = scatter_dp(mixtures, attns, False)
        sum_qkv = scatter_dp(ones, projs, True)
    gain_sums = (sum_all(gain_attn_grad / gain_attn), sum_all(gain_ffn_grad))
    return (
        jnp.stack(results),
        jnp.stack(input_grads),
        gain_sums[0],
        sum_qkv[:, :head_width],
        sum_qkv[:, head_width : 2 * head_width],
        sum_qkv[:, 2 * head_width :],
        sum_out,
        gain_sums[1],
        sum_gate,
        sum_up,
        sum_down,
    )


def solution(mesh):
    tokens = P(None, ("dp", "mp"), None, None)
    column = P("dp", "mp")
    row = P("mp", "dp")
    return jax.shard_map(
        per_device,
        mesh=mesh,
        in_specs=(
            tokens, tokens, P(), P(), column, column, column, row, P(), column, column, row,
        ),
        out_specs=(
            tokens, tokens, P(), column, column, column, row, P(), column, column, row,
        ),
        check_vma=False,
    )
```

```python
import functools
import math

import jax
import jax.numpy as jnp
from jax import lax
from jax.experimental import pallas as pl
from jax.experimental.pallas import tpu as pltpu
from jax.sharding import PartitionSpec as P

HEAD = 128
epsilon = 1e-05
rope_base = 10000.0
F32 = jnp.float32
BF16 = jnp.bfloat16


def rope_tables(positions):
    half_size = HEAD // 2
    inverse = jnp.power(rope_base, -(jnp.arange(half_size, dtype=F32) * 2.0 / HEAD))
    angles = positions.astype(F32)[:, None] * inverse[None, :]
    return (jnp.cos(angles), jnp.sin(angles))


def full_tables(positions):
    cosine, sine = rope_tables(positions)
    return (
        jnp.concatenate([cosine, cosine], axis=-1),
        jnp.concatenate([-sine, sine], axis=-1),
    )


def swap_halves(values):
    half_size = HEAD // 2
    return jnp.concatenate([values[..., half_size:], values[..., :half_size]], axis=-1)


def dot(left, right):
    return jnp.dot(left, right, preferred_element_type=F32)


def dot_tn(left, right):
    return lax.dot_general(left, right, (((0,), (0,)), ((), ())), preferred_element_type=F32)


def dot_nt(left, right):
    return lax.dot_general(left, right, (((1,), (1,)), ((), ())), preferred_element_type=F32)


def norm_factor(values):
    return lax.rsqrt(jnp.mean(values * values, axis=-1, keepdims=True) + epsilon)


def norm_back(values, factor, gain, incoming):
    scaled = incoming * gain
    gain_term = jnp.sum(incoming * values * factor, axis=0)
    input_term = factor * scaled - values * factor**3 * jnp.mean(
        scaled * values, axis=-1, keepdims=True
    )
    return (input_term, gain_term)


def sigmoid_of(raw, scale, shift):
    return 1.0 / (1.0 + jnp.exp(shift - raw * scale))


def split_cores(core, values, rows_here):
    shaped = values.reshape(-1, 2, rows_here, values.shape[-1])
    first, second = shaped[:, 0], shaped[:, 1]
    is_first = core == 0
    return jnp.where(is_first, first, second), jnp.where(is_first, second, first)

MESH = pl.DeviceIdType.MESH


class Spot:
    def __init__(self):
        self.dp, self.mp = lax.axis_index("dp"), lax.axis_index("mp")
        self.dp_size, self.mp_size = lax.axis_size("dp"), lax.axis_size("mp")
        self.places = self.mp_size // 2
        self.place, self.core = lax.div(self.mp, 2), lax.rem(self.mp, 2)
        self.sibling = (self.dp, self.mp + 1 - 2 * self.core)
        self.right = (self.dp, self.mp + 2)
        self.left = (self.dp, self.mp - 2)
        self.has_right = self.place < self.places - 1
        self.has_left = self.place > 0

    def peer(self, step):
        return lax.rem(self.dp + step, self.dp_size)

    def enter(self, with_dp, with_mp):
        barrier = pltpu.get_barrier_semaphore()
        count = 0

        def greet(device):
            pl.semaphore_signal(barrier, inc=1, device_id=device, device_id_type=MESH)

        if with_mp:
            greet(self.sibling)
            pl.when(self.has_right)(lambda: greet(self.right))
            pl.when(self.has_left)(lambda: greet(self.left))
            count += 1 + self.has_right.astype(jnp.int32) + self.has_left.astype(jnp.int32)
        if with_dp:
            for step in range(1, self.dp_size):
                greet((self.peer(step), self.mp))
            count += self.dp_size - 1
        pl.semaphore_wait(barrier, count)


class Swap:
    def __init__(self, spot, source, target, send, receive):
        self.spot, self.source, self.target = spot, source, target
        self.send, self.receive = send, receive
        self.copies = [self.copy(step) for step in range(1, spot.dp_size)]

    def copy(self, step):
        spot = self.spot
        return pltpu.make_async_remote_copy(
            src_ref=self.source.at[spot.peer(step)],
            dst_ref=self.target.at[spot.dp],
            send_sem=self.send.at[step],
            recv_sem=self.receive.at[step],
            device_id=(spot.peer(step), spot.mp),
            device_id_type=MESH,
        )

    def start(self):
        for copy in self.copies:
            copy.start()
        self.keep()

    def keep(self):
        self.target[self.spot.dp] = self.source[self.spot.dp]

    def wait(self):
        for copy in self.copies:
            copy.wait()


class Gather:
    def __init__(self, spot, shard, window, sems):
        self.local = pltpu.make_async_copy(shard, window(spot.dp), sems.at[0, 0])
        self.copies = [
            pltpu.make_async_remote_copy(
                src_ref=shard,
                dst_ref=window(spot.dp),
                send_sem=sems.at[0, step],
                recv_sem=sems.at[1, step],
                device_id=(spot.peer(step), spot.mp),
                device_id_type=MESH,
            )
            for step in range(1, spot.dp_size)
        ]

    def start(self):
        for copy in self.copies:
            copy.start()
        self.local.start()

    def wait(self):
        for copy in self.copies:
            copy.wait()
        self.local.wait()


class Spread:
    def __init__(self, spot, shard, full, sems):
        self.spot, self.shard, self.full, self.sems = spot, shard, full, sems
        self.local = pltpu.make_async_copy(shard, full.at[spot.mp], sems.at[6, 0])

    def copy(self, kind, device, p, source=None, core=None):
        at = 2 * p + (self.spot.core if core is None else core)
        return pltpu.make_async_remote_copy(
            src_ref=self.full.at[at] if source is None else source,
            dst_ref=self.full.at[at],
            send_sem=self.sems.at[kind, p],
            recv_sem=self.sems.at[kind + 1, p],
            device_id=device,
            device_id_type=MESH,
        )

    def rightward(self, p, source=None):
        return self.copy(0, self.spot.right, p, source)

    def leftward(self, p, source=None):
        return self.copy(2, self.spot.left, p, source)

    def across(self, p, source=None):
        return self.copy(4, self.spot.sibling, p, source)

    def begin(self):
        spot = self.spot
        pl.when(spot.has_right)(lambda: self.rightward(spot.place, self.shard).start())
        pl.when(spot.has_left)(lambda: self.leftward(spot.place, self.shard).start())
        self.across(spot.place, self.shard).start()
        self.local.start()

    def go_on(self, hop):
        spot = self.spot

        @pl.when(spot.place >= hop)
        def _():
            p = spot.place - hop
            self.rightward(p).wait_recv()
            pl.when(spot.has_right)(lambda: self.rightward(p).start())
            self.across(p).start()

        @pl.when(spot.place + hop < spot.places)
        def _():
            p = spot.place + hop
            self.leftward(p).wait_recv()
            pl.when(spot.has_left)(lambda: self.leftward(p).start())
            self.across(p).start()

    def finish(self):
        spot = self.spot
        for p in range(spot.places):
            self.copy(4, spot.sibling, p, core=1 - spot.core).wait_recv()
            self.across(p).wait_send()
            pl.when(spot.has_right & (spot.place >= p))(lambda: self.rightward(p).wait_send())
            pl.when(spot.has_left & (spot.place <= p))(lambda: self.leftward(p).wait_send())
        self.local.wait()


def spread_scratch(places):
    return [pltpu.SemaphoreType.DMA((7, places))]


class Ship(Swap):
    def __init__(self, spot, source, target, sems):
        super().__init__(spot, source, target, sems.at[0], sems.at[1])
        self.local = pltpu.make_async_copy(source.at[spot.dp], target.at[spot.dp], sems.at[0, 0])

    def start(self):
        for copy in self.copies:
            copy.start()
        self.local.start()

    def wait(self):
        super().wait()
        self.local.wait()


def window_of(full, axis, step, column=0, columns=None):
    def window(index):
        along = pl.ds(pl.multiple_of(index * step, step), step)
        if axis == 1:
            return full.at[:, along]
        if columns is None:
            return full.at[along, :]
        return full.at[along, pl.ds(column, columns)]

    return window


def swap_scratch(size, *block):
    return [
        pltpu.VMEM((size, *block), BF16),
        pltpu.VMEM((size, *block), BF16),
        pltpu.SemaphoreType.DMA((size,)),
        pltpu.SemaphoreType.DMA((size,)),
    ]


def far_first(places):
    orders = []
    for place in range(places):
        right, left, order = list(range(places - 1, place, -1)), list(range(place)), []
        while right or left:
            order += right[:1] + left[:1]
            right, left = right[1:], left[1:]
        orders.append(order + [place])
    return orders


class Sum:
    def __init__(self, spot, mine, out, from_sibling, from_left, from_right, sems):
        self.spot = spot
        self.mine, self.out = mine, out
        self.from_sibling, self.from_left, self.from_right = from_sibling, from_left, from_right
        self.sems = sems
        self.orders = far_first(spot.places)

    def copy(self, source, target, kind, t, device):
        return pltpu.make_async_remote_copy(
            src_ref=source.at[t],
            dst_ref=target.at[t],
            send_sem=self.sems.at[kind, t],
            recv_sem=self.sems.at[kind + 1, t],
            device_id=device,
            device_id_type=MESH,
        )

    def sibling(self, t):
        return self.copy(self.out, self.from_sibling, 0, t, self.spot.sibling)

    def rightward(self, t):
        return self.copy(self.mine, self.from_left, 2, t, self.spot.right)

    def leftward(self, t):
        return self.copy(self.mine, self.from_right, 4, t, self.spot.left)

    def term(self, s):
        chosen = 0
        for place, order in enumerate(self.orders):
            for at, t in enumerate(order):
                if t:
                    chosen = chosen + jnp.where((self.spot.place == place) & (s == at), t, 0)
        return chosen

    def add(self, t, arrived):
        self.mine[t] = (self.mine[t].astype(F32) + arrived[t].astype(F32)).astype(BF16)

    def absorb(self, t):
        self.sibling(t).wait_recv()
        self.add(t, self.from_sibling)

    def send(self, t, arrives, arrived, hop):
        self.absorb(t)
        if arrives:
            hop(t).wait_recv()
            self.add(t, arrived)
        hop(t).start()

    def begin(self, s):
        spot = self.spot

        @pl.when((spot.place == 0) & (s < spot.places - 1))
        def _():
            self.send(spot.places - 1 - s, False, None, self.rightward)

        @pl.when((spot.place == spot.places - 1) & (s < spot.places - 1))
        def _():
            self.send(s, False, None, self.leftward)

    def go_on(self, hop):
        spot = self.spot
        last = spot.places - 1

        @pl.when((spot.place > 0) & (spot.place <= hop))
        def _():
            self.send(last + spot.place - hop, True, self.from_left, self.rightward)

        @pl.when((spot.place < last) & (last - spot.place <= hop))
        def _():
            self.send(hop - last + spot.place, True, self.from_right, self.leftward)

    def finish(self):
        spot = self.spot
        t = spot.place
        self.absorb(t)

        @pl.when(spot.has_left)
        def _():
            self.rightward(t).wait_recv()
            self.add(t, self.from_left)

        @pl.when(spot.has_right)
        def _():
            self.leftward(t).wait_recv()
            self.add(t, self.from_right)

        for t in range(spot.places):
            self.sibling(t).wait_send()
            pl.when(spot.place < t)(lambda: self.rightward(t).wait_send())
            pl.when(spot.place > t)(lambda: self.leftward(t).wait_send())
        return self.mine[spot.place].astype(F32)


def sum_scratch(places, rows_here, width):
    return [pltpu.VMEM((places, rows_here, width), BF16)] * 5 + [
        pltpu.SemaphoreType.DMA((6, places))
    ]


def attend_blocks(qkv, first_ref, out, scale, shift):
    count, block = out.shape[:2]
    row_at = lax.broadcasted_iota(jnp.int32, (block, block), 0)
    col_at = lax.broadcasted_iota(jnp.int32, (block, block), 1)

    @pl.loop(0, count)
    def _(i):
        queries = qkv[i, :, 0:HEAD]
        first = first_ref[pl.ds(pl.multiple_of(i * block, block), block), :]

        def add_block(j, acc, diagonal=False):
            sig = sigmoid_of(dot_nt(queries, qkv[j, :, HEAD : 2 * HEAD]), scale, shift)
            visible = col_at >= first - j * block
            if diagonal:
                visible = visible & (col_at <= row_at)
            weights = jnp.where(visible, sig, 0.0).astype(BF16)
            return acc + dot(weights, qkv[j, :, 2 * HEAD :])

        acc = add_block(i, jnp.zeros((block, HEAD), F32), True)
        out[i] = lax.fori_loop(0, i, add_block, acc).astype(BF16)


def attend_back_blocks(
    spot, qkv, grad, first_ref, cos_ref, sin_ref, out_q, out_kv, dq, made, scale, shift
):
    count, block = grad.shape[:2]
    col_at = lax.broadcasted_iota(jnp.int32, (block, block), 0)
    row_at = lax.broadcasted_iota(jnp.int32, (block, block), 1)
    dq[...] = jnp.zeros_like(dq)

    def unrotate(values, i):
        rows = pl.ds(pl.multiple_of(i * block, block), block)
        swapped = pltpu.roll(values, HEAD // 2, 1)
        return (values * cos_ref[rows, :] - swapped * sin_ref[rows, :]).astype(BF16)

    @pl.loop(0, count)
    def _(at):
        j = spot.peer(at + 1)
        keys = qkv[j, :, HEAD : 2 * HEAD]
        values = qkv[j, :, 2 * HEAD :]
        keys_t = keys.T

        def add_block(i, sums, diagonal=False):
            dk, dv = sums
            queries, grads = qkv[i, :, 0:HEAD], grad[i]
            sig = sigmoid_of(dot_nt(keys, queries), scale, shift)
            visible = col_at >= first_ref[i] - j * block
            if diagonal:
                visible = visible & (col_at <= row_at)
            sig = jnp.where(visible, sig, 0.0)
            prob_grad = dot_nt(values, grads)
            score_grad = (prob_grad * sig * (1.0 - sig)).astype(BF16)
            dq[i] += dot(keys_t, score_grad)
            return dk + dot(score_grad, queries), dv + dot(sig.astype(BF16), grads)

        zero = jnp.zeros((block, HEAD), F32)
        dk, dv = lax.fori_loop(j + 1, count, add_block, add_block(j, (zero, zero), True))
        out_kv[j, :, 0:HEAD] = unrotate(dk * scale, j)
        out_kv[j, :, HEAD:] = dv.astype(BF16)
        pl.when(at < count - 1)(lambda: made(at + 1))

    @pl.loop(0, count)
    def _(i):
        out_q[i] = unrotate(dq[i].T * scale, i)


def take(refs, count):
    return refs[:count], refs[count:]


def begin_kernel(query, key, value, out, first, qkv_full, out_full, first_full, sems, spread_sems):
    spot = Spot()
    spot.enter(True, True)
    rows, columns = query.shape
    jobs = [
        (shard, window_of(qkv_full, 0, rows, i * columns, columns))
        for i, shard in enumerate((query, key, value))
    ]
    jobs.append((out, window_of(out_full, 1, out.shape[1])))
    gathers = [Gather(spot, shard, window, sems.at[i]) for i, (shard, window) in enumerate(jobs)]
    spread = Spread(spot, first, first_full, spread_sems)
    spread.begin()
    for gather in gathers:
        gather.start()
    for hop in range(1, spot.places):
        spread.go_on(hop)
    for gather in gathers:
        gather.wait()
    spread.finish()


def forward_kernel(tail, head, spreads, gather_axis, heads, toks, scale, shift, *refs):
    gathers = gather_axis is not None
    tail_in, refs = take(refs, 4 * tail)
    head_in, refs = take(refs, 5 * head)
    spread_in, refs = take(refs, spreads)
    gather_in, refs = take(refs, gathers)
    tail_out, refs = take(refs, 3 * tail)
    head_out, refs = take(refs, 2 * head)
    spread_out, refs = take(refs, spreads)
    gather_out, refs = take(refs, gathers)
    sum_refs, refs = take(refs, 6 * tail)
    head_refs, refs = take(refs, 9 * head)
    spot = Spot()
    spot.enter(head or gathers, tail or spreads)
    if spreads:
        spread = Spread(spot, *spread_in, *spread_out, refs[0])
        spread.begin()
    if gathers:
        window = window_of(gather_out[0], gather_axis, gather_in[0].shape[gather_axis])
        gather = Gather(spot, gather_in[0], window, refs[-1])

    if tail:
        got, out_weight, x_ref, gain_ref = tail_in
        middle_ref, normed_ref, mix_ref = tail_out
        pairs = got.shape[0]
        owner_rows = toks * (pairs // heads)
        for o in range(mix_ref.shape[0] // owner_rows):
            for p in range(pairs):
                s, h = p // heads, p % heads
                mix_ref[pl.ds(o * owner_rows + s * toks, toks), h * HEAD : (h + 1) * HEAD] = got[
                    p, pl.ds(o * toks, toks), :
                ]
        summed = Sum(spot, *sum_refs)
        chip_rows = 2 * owner_rows

        @pl.loop(0, spot.places)
        def _(s):
            t = summed.term(s)
            rows = pl.ds(pl.multiple_of(t * chip_rows, chip_rows), chip_rows)
            value = dot(mix_ref[rows, :], out_weight[...]).astype(BF16)
            keep, send = split_cores(spot.core, value, owner_rows)
            summed.mine[t] = keep[0]
            summed.out[t] = send[0]
            summed.sibling(t).start()

        @pl.loop(0, spot.places - 1)
        def _(s):
            summed.begin(s)

    if head:
        rows_ref, weight_ref, cos_ref, sin_ref, first_ref = head_in
        qkv_ref, got_ref = head_out
        made, paired, qkv, qkv_send, qkv_recv, part, got, part_send, part_recv = head_refs
        pairs = paired.shape[0]
        owner_rows = toks * (pairs // heads)
        step = made.shape[0]

        @pl.loop(0, rows_ref.shape[0] // step)
        def _(i):
            rows = pl.ds(pl.multiple_of(i * step, step), step)
            made[...] = dot(rows_ref[rows, :], weight_ref[...])
            for j in range(step // owner_rows):
                to = pl.ds(pl.multiple_of((i * (step // owner_rows) + j) * toks, toks), toks)
                cosine, sine = cos_ref[to, :], sin_ref[to, :]
                for p in range(pairs):
                    s, h = p // heads, p % heads
                    here = pl.ds(j * owner_rows + s * toks, toks)
                    for kind in range(3):
                        piece = made[here, pl.ds((kind * heads + h) * HEAD, HEAD)]
                        if kind < 2:
                            piece = piece * cosine + pltpu.roll(piece, HEAD // 2, 1) * sine
                        paired[p, to, kind * HEAD : (kind + 1) * HEAD] = piece.astype(BF16)

        swap = Swap(spot, paired, qkv, qkv_send, qkv_recv)
        swap.start()
    if gathers:
        gather.start()
    if spreads:
        spread.go_on(1)
    if tail and spot.places > 2:
        summed.go_on(1)
    if head:
        swap.wait()
    for hop in range(2, spot.places - 1):
        if spreads:
            spread.go_on(hop)
        if tail:
            summed.go_on(hop)
    if head:
        attend_blocks(qkv, first_ref, part, scale, shift)
        swap = Swap(spot, part, got, part_send, part_recv)
        swap.start()
        qkv_ref[...] = qkv[...]
        swap.wait()
        got_ref[...] = got[...]
    if spreads:
        if spot.places > 2:
            spread.go_on(spot.places - 1)
    if tail:
        middle = x_ref[...].astype(F32) + summed.finish()
        middle_ref[...] = middle
        normed_ref[...] = (middle * norm_factor(middle) * gain_ref[...]).astype(BF16)
    if spreads:
        spread.finish()
    if gathers:
        gather.wait()


def middle_kernel(
    first, owner_rows,
    rows_ref, cot_ref, gate_ref, up_ref, down_ref, middle_ref, local_cot_ref, gain_ref, shard,
    *refs,
):
    before, refs = take(refs, 0 if first else 3)
    (y_ref, grad_ref, low_ref, gain_grad_ref, full), refs = take(refs, 5)
    after, refs = take(refs, 3)
    (act_ref, dgate_ref, dup_ref, turned, new_rows, new_cols, old_rows, old_cols), refs = take(refs, 8)
    wide_sems, spread_sems, *sum_refs = refs
    spot = Spot()
    spot.enter(False, True)
    summed = Sum(spot, *sum_refs)
    spread = Spread(spot, shard, full, spread_sems)
    spread.begin()
    hidden, width = gate_ref.shape[1], rows_ref.shape[1]
    chip_rows = 2 * owner_rows
    tile = min(256, hidden)
    blocks = after[0].shape[0]
    block = width // blocks
    new = (new_rows.at[0], new_rows.at[1], new_cols)
    old = (old_rows.at[0], old_rows.at[1], old_cols)

    def load(g, e):
        return pltpu.make_async_copy(before[g].at[e], old[g], wide_sems.at[0, g])

    def store(g, e):
        return pltpu.make_async_copy(new[g], after[g].at[e], wide_sems.at[1, g])

    if not first:
        for g in range(3):
            load(g, 0).start()

    @pl.loop(0, spot.places)
    def _(s):
        place = summed.term(s)
        rows = pl.ds(pl.multiple_of(place * chip_rows, chip_rows), chip_rows)

        @pl.loop(0, hidden // tile)
        def _(t):
            cols = pl.ds(pl.multiple_of(t * tile, tile), tile)
            gate = dot(rows_ref[rows, :], gate_ref[:, cols])
            up = dot(rows_ref[rows, :], up_ref[:, cols])
            sig = jax.nn.sigmoid(gate)
            silu = gate * sig
            act_ref[rows, cols] = (silu * up).astype(BF16)
            grad = dot_nt(cot_ref[rows, :], down_ref[cols, :])
            dgate_ref[rows, cols] = (grad * up * sig * (1.0 + gate * (1.0 - sig))).astype(BF16)
            dup_ref[rows, cols] = (grad * silu).astype(BF16)

        pl.when(s > 0)(lambda: summed.begin(s - 1))
        for hop in range(1, spot.places - 1):

            @pl.when(s == hop + 1)
            def _():
                spread.go_on(hop)
                summed.go_on(hop)

        @pl.loop(0, width // 256)
        def _(t):
            cols = pl.ds(pl.multiple_of(t * 256, 256), 256)
            y_ref[rows, cols] = dot(act_ref[rows, :], down_ref[:, cols]).astype(BF16)
            value = dot_nt(dgate_ref[rows, :], gate_ref[cols, :])
            value += dot_nt(dup_ref[rows, :], up_ref[cols, :])
            keep, send = split_cores(spot.core, value.astype(BF16), owner_rows)
            summed.mine[place, :, cols] = keep[0]
            summed.out[place, :, cols] = send[0]

        summed.sibling(place).start()

    def make(g, e, left, right, right_at, columns):
        pl.when(e > 0)(lambda: store(g, e - 1).wait())
        if not first:
            load(g, e).wait()
        step = math.gcd(columns, 256)

        @pl.loop(0, columns // step)
        def _(t):
            cols = pl.ds(pl.multiple_of(t * step, step), step)
            total = dot(left[...], right[:, pl.ds(pl.multiple_of(right_at + t * step, step), step)])
            if not first:
                total += old[g][:, cols].astype(F32)
            new[g][:, cols] = total.astype(BF16)

        if not first:
            pl.when(e < blocks - 1)(lambda: load(g, e + 1).start())
        store(g, e).start()

    @pl.loop(0, blocks)
    def _(e):
        left = turned.at[pl.ds(0, block), :]
        left[...] = rows_ref[:, pl.ds(pl.multiple_of(e * block, block), block)].T
        make(0, e, left, dgate_ref, 0, hidden)
        make(1, e, left, dup_ref, 0, hidden)

    spread.go_on(spot.places - 1)
    left = turned.at[pl.ds(0, hidden), :]
    left[...] = act_ref[...].T

    @pl.loop(0, blocks)
    def _(e):
        make(2, e, left, cot_ref, e * block, block)

    incoming = summed.finish()
    middle = middle_ref[...]
    term, gain_grad = norm_back(middle, norm_factor(middle), gain_ref[...], incoming)
    gain_grad_ref[...] = gain_grad[None]
    grad = local_cot_ref[...].astype(F32) + term
    grad_ref[...] = grad
    low_ref[...] = grad.astype(BF16)
    spread.finish()
    for g in range(3):
        store(g, blocks - 1).wait()


def backward_kernel(tail, head, ships, spreads, heads, toks, scale, shift, *refs):
    tail_in, refs = take(refs, 6 * tail)
    head_in, refs = take(refs, 6 * head)
    ship_in, refs = take(refs, ships)
    spread_in, refs = take(refs, spreads)
    tail_out, refs = take(refs, 2 * tail)
    head_out, refs = take(refs, head)
    ship_out, refs = take(refs, ships)
    spread_out, refs = take(refs, spreads)
    sum_refs, refs = take(refs, 6 * tail)
    head_refs, refs = take(refs, 13 * head)
    spot = Spot()
    spot.enter(head or ships > 0, tail or spreads)
    shipped = [
        Ship(spot, source, target, refs[-1].at[i])
        for i, (source, target) in enumerate(zip(ship_in, ship_out))
    ]
    if spreads:
        spread = Spread(spot, *spread_in, *spread_out, refs[0])
        spread.begin()

    if tail:
        proj_ref, weight_ref, rows_one_ref, x_ref, grad_ref, gain_ref = tail_in
        result_ref, gain_grad_ref = tail_out
        owner_rows = x_ref.shape[0]
        summed = Sum(spot, *sum_refs)
        chip_rows = 2 * owner_rows
        gain_grad_ref[...] = jnp.zeros_like(gain_grad_ref)

        @pl.loop(0, spot.places)
        def _(s):
            t = summed.term(s)
            rows = pl.ds(pl.multiple_of(t * chip_rows, chip_rows), chip_rows)
            value = dot_nt(proj_ref[rows, :], weight_ref[...])
            gain_grad_ref[...] += jnp.sum(
                value * rows_one_ref[rows, :].astype(F32), axis=0, keepdims=True
            )
            keep, send = split_cores(spot.core, value.astype(BF16), owner_rows)
            summed.mine[t] = keep[0]
            summed.out[t] = send[0]
            summed.sibling(t).start()
            pl.when(s > 0)(lambda: summed.begin(s - 1))

    if head:
        rows_ref, out_weight_ref, qkv, first_ref, cos_ref, sin_ref = head_in
        (head_proj_ref,) = head_out
        part, got, part_send, part_recv = head_refs[:4]
        made_q, got_q, q_send, q_recv, made_kv, got_kv, kv_send, kv_recv, dq = head_refs[4:]
        pairs = part.shape[0]
        owner_rows = toks * (pairs // heads)
        total = rows_ref.shape[0]
        step = min(512, total)

        @pl.loop(0, total // step)
        def _(i):
            rows = pl.ds(pl.multiple_of(i * step, step), step)
            made = dot_nt(rows_ref[rows, :], out_weight_ref[...]).astype(BF16)
            for j in range(step // owner_rows):
                to = pl.ds(pl.multiple_of((i * (step // owner_rows) + j) * toks, toks), toks)
                for p in range(pairs):
                    s, h = p // heads, p % heads
                    start = j * owner_rows + s * toks
                    part[p, to, :] = made[start : start + toks, h * HEAD : (h + 1) * HEAD]

        swap = Swap(spot, part, got, part_send, part_recv)
        swap.start()
        swap.wait()
    for ship in shipped:
        ship.start()
    if spreads:
        spread.go_on(1)
    if tail and spot.places > 2:
        summed.go_on(1)
    if head:
        swap_kv = Swap(spot, made_kv, got_kv, kv_send, kv_recv)
        attend_back_blocks(
            spot, qkv, got, first_ref, cos_ref, sin_ref, made_q, made_kv, dq,
            lambda step: swap_kv.copy(step).start(), scale, shift,
        )
        swap_kv.keep()
        swap = Swap(spot, made_q, got_q, q_send, q_recv)
        swap.start()
    for hop in range(2, spot.places - 1):
        if spreads:
            spread.go_on(hop)
        if tail:
            summed.go_on(hop)
    if head:
        swap_kv.wait()
        swap.wait()
        for o in range(total // owner_rows):
            for p in range(pairs):
                s, h = p // heads, p % heads
                here, there = pl.ds(o * owner_rows + s * toks, toks), pl.ds(o * toks, toks)
                for kind in range(3):
                    piece = (
                        got_kv[p, there, (kind - 1) * HEAD : kind * HEAD] if kind else got_q[p, there, :]
                    )
                    head_proj_ref[
                        here, (kind * heads + h) * HEAD : (kind * heads + h + 1) * HEAD
                    ] = piece
    if spreads and spot.places > 2:
        spread.go_on(spot.places - 1)
    if tail:
        incoming = summed.finish()
        x = x_ref[...].astype(F32)
        term, _ = norm_back(x, norm_factor(x), gain_ref[...], incoming)
        result_ref[...] = grad_ref[...] + term
    for ship in shipped:
        ship.wait()
    if spreads:
        spread.finish()


def ffn_kernel(
    rows_ref, cot_ref, gate_ref, up_ref, down_ref, y_ref, dh_ref, act_ref, dgate_ref, dup_ref
):
    hidden = gate_ref.shape[1]
    width = rows_ref.shape[1]
    tile = min(256, hidden)

    @pl.loop(0, hidden // tile)
    def _(t):
        cols = pl.ds(pl.multiple_of(t * tile, tile), tile)
        gate = dot(rows_ref[...], gate_ref[:, cols])
        up = dot(rows_ref[...], up_ref[:, cols])
        sig = jax.nn.sigmoid(gate)
        silu = gate * sig
        act_ref[:, cols] = (silu * up).astype(BF16)
        grad = dot_nt(cot_ref[...], down_ref[cols, :])
        dgate_ref[:, cols] = (grad * up * sig * (1.0 + gate * (1.0 - sig))).astype(BF16)
        dup_ref[:, cols] = (grad * silu).astype(BF16)

    @pl.loop(0, width // 256)
    def _(t):
        cols = pl.ds(pl.multiple_of(t * 256, 256), 256)
        y_ref[:, cols] = dot(act_ref[...], down_ref[:, cols]).astype(BF16)
        dh = dot_nt(dgate_ref[...], gate_ref[cols, :]) + dot_nt(dup_ref[...], up_ref[cols, :])
        dh_ref[:, cols] = dh.astype(BF16)


def grad_kernel(count, groups, left_blocked, *refs):
    lefts, refs = take(refs, count)
    rights, refs = take(refs, count * groups)
    out_refs, (turned,) = take(refs, groups)
    rows = lefts[0].shape[0]

    def turn():
        for m, left in enumerate(lefts):
            turned[:, m * rows : (m + 1) * rows] = left[...].T

    if left_blocked:
        turn()
    else:
        pl.when(pl.program_id(0) == 0)(turn)
    tile = math.gcd(out_refs[0].shape[2], 256)
    for g, out_ref in enumerate(out_refs):
        own = rights[g * count : (g + 1) * count]

        @pl.loop(0, out_ref.shape[2] // tile)
        def _(t):
            cols = pl.ds(pl.multiple_of(t * tile, tile), tile)
            total = dot(turned[:, :rows], own[0][:, cols])
            for m in range(1, count):
                total += dot(turned[:, m * rows : (m + 1) * rows], own[m][:, cols])
            out_ref[0, :, cols] = total.astype(BF16)


VMEM = pl.BlockSpec(memory_space=pltpu.VMEM)
ANY = pl.BlockSpec(memory_space=pl.ANY)


def cost(flops, nbytes):
    return pl.CostEstimate(flops=flops, bytes_accessed=nbytes, transcendentals=0)


def limits(mebibytes):
    return pltpu.CompilerParams(vmem_limit_bytes=mebibytes * 2**20)


def shape(*dims, dtype=BF16):
    return jax.ShapeDtypeStruct(dims, dtype)


def comm_params(collective_id, mebibytes):
    return pltpu.CompilerParams(
        collective_id=collective_id, has_side_effects=True, vmem_limit_bytes=mebibytes * 2**20
    )


def begin(query, key, value, out, first):
    size, mp_size = lax.axis_size("dp"), lax.axis_size("mp")
    rows, columns = query.shape
    return pl.pallas_call(
        begin_kernel,
        out_shape=[
            shape(rows * size, 3 * columns),
            shape(out.shape[0], out.shape[1] * size),
            shape(mp_size, *first.shape),
        ],
        in_specs=[ANY] * 5,
        out_specs=[ANY] * 3,
        scratch_shapes=[
            pltpu.SemaphoreType.DMA((4, 2, size)),
            *spread_scratch(mp_size // 2),
        ],
        compiler_params=comm_params(0, 8),
        cost_estimate=cost(0, 60 * 2**20),
        name="begin",
    )(query, key, value, out, first)


def forward_stage(collective_id, tail, head, shard, gather, heads, toks, scale, shift):
    size, mp_size = lax.axis_size("dp"), lax.axis_size("mp")
    out_shape, scratch = [], []
    if tail:
        blocks, _, x, _ = tail
        owner_rows, width = x.shape
        total = blocks.shape[1] * blocks.shape[0] // heads
        out_shape += [
            shape(owner_rows, width, dtype=F32),
            shape(owner_rows, width),
            shape(total, heads * HEAD),
        ]
        scratch += sum_scratch(mp_size // 2, owner_rows, width)
    if head:
        total, slice_len = head[0].shape[0], head[2].shape[0]
        out_shape += [shape(size, slice_len, 3 * HEAD), shape(size, slice_len, HEAD)]
        scratch += [
            pltpu.VMEM((min(512, total), 3 * heads * HEAD), F32),
            *swap_scratch(size, slice_len, 3 * HEAD),
            *swap_scratch(size, slice_len, HEAD),
        ]
    here, spreads = len(out_shape), len(shard)
    if spreads:
        out_shape.append(shape(mp_size, *shard[0].shape))
        scratch += spread_scratch(mp_size // 2)
    axis = None
    if gather:
        weight, axis = gather
        dims = list(weight.shape)
        dims[axis] *= size
        out_shape.append(shape(*dims))
        scratch.append(pltpu.SemaphoreType.DMA((2, size)))
    arrays = [*tail, *head]
    passing = spreads + bool(gather)
    return pl.pallas_call(
        functools.partial(
            forward_kernel, bool(tail), bool(head), spreads, axis, heads, toks, scale, shift
        ),
        out_shape=out_shape,
        in_specs=[VMEM] * len(arrays) + [ANY] * passing,
        out_specs=[VMEM] * here + [ANY] * passing,
        scratch_shapes=scratch,
        compiler_params=comm_params(collective_id, 52),
        cost_estimate=cost(10**10, 100 * 2**20),
        name="forward_stage",
    )(*arrays, *shard, *gather[:1])


def middle_part(
    collective_id, rows, cot, gate, up, down, middle, local_cot, gain, shard, before
):
    total, width = rows.shape
    hidden = gate.shape[1]
    size, mp_size = lax.axis_size("dp"), lax.axis_size("mp")
    owner_rows = middle.shape[0]
    block = width // size
    wide = [shape(size, block, hidden)] * 2 + [shape(size, hidden, block)]
    return pl.pallas_call(
        functools.partial(middle_kernel, not before, owner_rows),
        out_shape=[
            shape(total, width),
            shape(owner_rows, width, dtype=F32),
            shape(owner_rows, width),
            shape(1, width, dtype=F32),
            shape(mp_size, *shard.shape),
            *wide,
        ],
        in_specs=[VMEM] * 8 + [ANY] * (1 + len(before)),
        out_specs=[VMEM] * 4 + [ANY] * 4,
        scratch_shapes=[
            *[pltpu.VMEM((total, hidden), BF16)] * 3,
            pltpu.VMEM((max(block, hidden), total), BF16),
            pltpu.VMEM((2, block, hidden), BF16),
            pltpu.VMEM((hidden, block), BF16),
            pltpu.VMEM((2, block, hidden), BF16),
            pltpu.VMEM((hidden, block), BF16),
            pltpu.SemaphoreType.DMA((2, 3)),
            *spread_scratch(mp_size // 2),
            *sum_scratch(mp_size // 2, owner_rows, width),
        ],
        compiler_params=comm_params(collective_id, 60),
        cost_estimate=cost(18 * total * width * hidden, 60 * 2**20),
        name="middle_part",
    )(rows, cot, gate, up, down, middle, local_cot, gain, shard, *before)


def backward_stage(collective_id, tail, head, ships, shard, heads, toks, scale, shift):
    size, mp_size = lax.axis_size("dp"), lax.axis_size("mp")
    places = mp_size // 2
    out_shape, scratch = [], []
    if tail:
        owner_rows, width = tail[3].shape
        out_shape += [shape(owner_rows, width, dtype=F32), shape(1, width, dtype=F32)]
        scratch += sum_scratch(places, owner_rows, width)
    if head:
        total, slice_len = head[0].shape[0], head[2].shape[1]
        out_shape.append(shape(total, 3 * heads * HEAD))
        scratch += [
            *swap_scratch(size, slice_len, HEAD),
            *swap_scratch(size, slice_len, HEAD),
            *swap_scratch(size, slice_len, 2 * HEAD),
            pltpu.VMEM((size, HEAD, slice_len), F32),
        ]
    here, spreads = len(out_shape), len(shard)
    if spreads:
        scratch += spread_scratch(places)
    if ships:
        scratch.append(pltpu.SemaphoreType.DMA((len(ships), 2, size)))
    out_shape += [shape(*array.shape) for array in ships]
    out_shape += [shape(mp_size, *array.shape) for array in shard]
    arrays = [*tail, *head]
    passing = len(ships) + spreads
    return pl.pallas_call(
        functools.partial(
            backward_kernel,
            bool(tail), bool(head), len(ships), spreads, heads, toks, scale, shift,
        ),
        out_shape=out_shape,
        in_specs=[VMEM] * len(arrays) + [ANY] * passing,
        out_specs=[VMEM] * here + [ANY] * passing,
        scratch_shapes=scratch,
        compiler_params=comm_params(collective_id, 56),
        cost_estimate=cost(10**10, 100 * 2**20),
        name="backward_stage",
    )(*arrays, *ships, *shard)


def ffn(rows, cot, gate, up, down):
    total, width = rows.shape
    hidden = gate.shape[1]
    step = min(512, total)
    by_rows = pl.BlockSpec((step, width), lambda i: (i, 0))
    by_hidden = pl.BlockSpec((step, hidden), lambda i: (i, 0))
    held = lambda array: pl.BlockSpec(array.shape, lambda i: (0, 0), pipeline_mode=pl.Buffered(1))
    return pl.pallas_call(
        ffn_kernel,
        grid=(total // step,),
        out_shape=[shape(total, width)] * 2 + [shape(total, hidden)] * 3,
        in_specs=[by_rows, by_rows, held(gate), held(up), held(down)],
        out_specs=[by_rows] * 2 + [by_hidden] * 3,
        compiler_params=limits(56),
        cost_estimate=cost(12 * total * width * hidden, 34 * 2**20),
        name="ffn",
    )(rows, cot, gate, up, down)


def weight_grad(lefts, groups, left_blocked):
    count = len(lefts)
    size = lax.axis_size("dp")
    rows = lefts[0].shape[0]
    m, n = lefts[0].shape[1], groups[0][0].shape[1]
    moving = lambda width: pl.BlockSpec((rows, width // size), lambda e: (0, e))
    fixed = lambda width: pl.BlockSpec(
        (rows, width), lambda e: (0, 0), pipeline_mode=pl.Buffered(1)
    )
    left_spec = moving(m) if left_blocked else fixed(m)
    right_spec = fixed(n) if left_blocked else moving(n)
    out = (m // size, n) if left_blocked else (m, n // size)
    return pl.pallas_call(
        functools.partial(grad_kernel, count, len(groups), left_blocked),
        grid=(size,),
        in_specs=[left_spec] * count + [right_spec] * (count * len(groups)),
        out_specs=[pl.BlockSpec((1, *out), lambda e: (e, 0, 0))] * len(groups),
        out_shape=[shape(size, *out)] * len(groups),
        scratch_shapes=[pltpu.VMEM((out[0], count * rows), BF16)],
        compiler_params=limits(52),
        cost_estimate=cost(2 * count * rows * m * n * len(groups), 24 * 2**20),
        name="weight_grad",
    )(*lefts, *(right for group in groups for right in group))


def first_visible(ids):
    at = jnp.arange(ids.shape[-1], dtype=jnp.int32)
    starts = jnp.concatenate([jnp.ones_like(ids[..., :1], jnp.bool_), ids[..., 1:] != ids[..., :-1]], axis=-1)
    return lax.cummax(jnp.where(starts, at, 0), axis=ids.ndim - 1)


def block_at(values, index):
    return lax.dynamic_index_in_dim(values, index, 0, keepdims=False)


def scatter_mp(values):
    return lax.psum_scatter(values, "mp", scatter_dimension=0, tiled=True).astype(F32)


def sum_all(values):
    for name in ("dp", "mp"):
        size = lax.axis_size(name)
        step = 1
        while step < size:
            values = values + lax.ppermute(values, name, [(i, i ^ step) for i in range(size)])
            step *= 2
    return values


def sliced_scores(qkv, kv_all, first, positions, scale, shift):
    raw = jnp.einsum("pqd,pkd->pqk", qkv[..., :HEAD], kv_all[..., :HEAD], preferred_element_type=F32)
    at = jnp.arange(kv_all.shape[1], dtype=jnp.int32)
    visible = (at >= first[..., None]) & (at <= positions[:, None])
    return jnp.where(visible, sigmoid_of(raw, scale, shift), 0.0)


def per_device(
    inputs,
    cotangent,
    doc_ids,
    gain_attn,
    w_query,
    w_key,
    w_value,
    w_out,
    gain_ffn,
    w_gate,
    w_up,
    w_down,
):
    dp_size = lax.axis_size("dp")
    mp_size = lax.axis_size("mp")
    micro_count, row_count, seq_count, width = inputs.shape
    slice_len = row_count * mp_size
    total_len = slice_len * dp_size
    rows_here = row_count * seq_count
    shift = math.log(total_len)
    scale = HEAD ** (-0.5)
    dp_at = lax.axis_index("dp")
    mp_at = lax.axis_index("mp")
    first_row = dp_at * slice_len
    positions = first_row + jnp.arange(slice_len, dtype=jnp.int32)
    head_width = w_query.shape[1]
    heads = head_width // HEAD
    hidden = w_gate.shape[1]
    pairs = seq_count * heads
    whole_pairs = pairs == dp_size
    cos_slice, sin_slice = full_tables(positions)
    cos_all, sin_all = full_tables(jnp.arange(total_len, dtype=jnp.int32))
    first_all = first_visible(doc_ids)

    def by_row(table):
        shaped = table.reshape(mp_size, 1, row_count, 1, HEAD)
        return jnp.broadcast_to(shaped, (mp_size, seq_count, row_count, 1, HEAD))

    def rotate(values, back=False):
        sine = -by_row(sin_slice) if back else by_row(sin_slice)
        return values * by_row(cos_slice) + swap_halves(values) * sine

    def to_pairs(values):
        shaped = values.reshape(mp_size, seq_count, row_count, heads, -1)
        return shaped.transpose(1, 3, 0, 2, 4).reshape(pairs, slice_len, -1)

    def from_pairs(values):
        shaped = values.reshape(seq_count, heads, mp_size, row_count, -1)
        return shaped.transpose(2, 0, 3, 1, 4).reshape(mp_size * rows_here, heads, -1)

    def to_rows(values):
        return jnp.swapaxes(values, 0, 1).reshape(rows_here, width)

    def from_rows(values):
        return jnp.swapaxes(values.reshape(seq_count, row_count, width), 0, 1)

    def gather_mp(values):
        return lax.all_gather(values, "mp", axis=0, tiled=True)

    gain_attn_grad = jnp.zeros((width,), F32)
    gain_ffn_grad = jnp.zeros((width,), F32)
    results = []
    input_grads = []
    kept = [[] for _ in range(9)]
    xs = [to_rows(inputs[m]) for m in range(micro_count)]
    cots = [to_rows(cotangent[m]) for m in range(micro_count)]
    normed = [
        (x.astype(F32) * norm_factor(x.astype(F32)) * gain_attn).astype(BF16) for x in xs
    ]
    micros = range(micro_count)
    if whole_pairs:
        stage = (heads, row_count, scale, shift)
        firsts = [block_at(first_all[m], dp_at // heads) for m in micros]
        last = micro_count - 1

        def whole(blocks):
            return blocks.reshape(mp_size * rows_here, width)

        def scatter_dp(blocks):
            return lax.psum_scatter(blocks, "dp", scatter_dimension=0, tiled=True)[0].astype(F32)

        qkv_full, out_full, rows_one = begin(w_query, w_key, w_value, w_out, normed[0])
        cots, rows_one = lax.optimization_barrier((cots, rows_one))
        portions = [gather_mp(cot) for cot in cots]
        gathers = {0: (w_gate, 0), 1: (w_up, 0), micro_count: (w_down, 1)}
        wide = []
        ones, qkvs, got, middles, lows, twos, mixtures = [whole(rows_one)], [], [], [], [], [], []
        for m in range(micro_count + 1):
            tail, head, shard = (), (), ()
            if m:
                tail = (got[m - 1], out_full, xs[m - 1], gain_ffn[None])
            if m < micro_count:
                head = (ones[m], qkv_full, cos_slice, sin_slice, firsts[m][:, None])
            if m < last:
                shard = (normed[m + 1],)
            elif lows:
                shard = (lows[m - last],)
            outs = forward_stage(10 + m, tail, head, shard, gathers.get(m, ()), *stage)
            if tail:
                (middle, low, mixture), outs = take(outs, 3)
                middles.append(middle)
                lows.append(low)
                mixtures.append(mixture)
            if head:
                (qkv, block), outs = take(outs, 2)
                qkvs.append(qkv)
                got.append(block)
            if shard:
                (ones if m < last else twos).append(whole(outs[0]))
            if m in gathers:
                wide.append(outs[-1])
        grads, low_grads, attns, projs, sums = [], [], [], [], []
        for m in micros:
            shard = lows[len(twos)] if len(twos) < micro_count else low_grads[len(attns)]
            y, grad, low, gain_part, full, *sums = middle_part(
                30 + m, twos[m], portions[m], *wide, middles[m], cots[m], gain_ffn[None], shard, sums
            )
            (twos if len(twos) < micro_count else attns).append(whole(full))
            grads.append(grad)
            low_grads.append(low)
            gain_ffn_grad = gain_ffn_grad + gain_part[0]
            results.append(from_rows((middles[m] + scatter_mp(y)).astype(BF16)))
        sum_gate, sum_up, sum_down = [scatter_dp(blocks) for blocks in sums]
        for m in range(micro_count + 1):
            tail, head, ships, shard = (), (), (), ()
            if m:
                tail = (projs[m - 1], qkv_full, ones[m - 1], xs[m - 1], grads[m - 1], gain_attn[None])
            if m < micro_count:
                first = firsts[m].reshape(dp_size, 1, slice_len)
                head = (attns[m], out_full, qkvs[m], first, cos_all, sin_all)
            if len(attns) < micro_count:
                shard = (low_grads[len(attns)],)
            if m == micro_count:
                ships = (
                    *weight_grad(mixtures, (attns,), False),
                    *weight_grad(ones, (projs,), True),
                )
            outs = backward_stage(20 + m, tail, head, ships, shard, *stage)
            if tail:
                (input_grad, gain_part), outs = take(outs, 2)
                input_grads.append(from_rows(input_grad))
                gain_attn_grad = gain_attn_grad + gain_part[0]
            if head:
                (proj,), outs = take(outs, 1)
                projs.append(proj)
            if shard:
                attns.append(whole(outs[-1]))
        sum_out, sum_qkv = (jnp.sum(blocks.astype(F32), axis=0) for blocks in outs)
    else:
        qkv_full = lax.all_gather(
            jnp.concatenate([w_query, w_key, w_value], axis=1), "dp", axis=0, tiled=True
        )
        out_full = lax.all_gather(w_out, "dp", axis=1, tiled=True)
        gate_full = lax.all_gather(w_gate, "dp", axis=0, tiled=True)
        up_full = lax.all_gather(w_up, "dp", axis=0, tiled=True)
        down_full = lax.all_gather(w_down, "dp", axis=1, tiled=True)
        for micro in micros:
            local_rows = xs[micro].astype(F32)
            local_cot = cots[micro]
            factor_one = norm_factor(local_rows)
            rows_one = gather_mp(normed[micro])
            portion = gather_mp(local_cot)
            projected = dot(rows_one, qkv_full).reshape(
                mp_size, seq_count, row_count, 3, heads, HEAD
            )
            packed = to_pairs(
                jnp.concatenate(
                    [
                        rotate(projected[:, :, :, 0]).astype(BF16),
                        rotate(projected[:, :, :, 1]).astype(BF16),
                        projected[:, :, :, 2].astype(BF16),
                    ],
                    axis=-1,
                )
            )
            kv_all = lax.all_gather(packed[..., HEAD:], "dp", axis=1, tiled=True)
            first = lax.dynamic_slice_in_dim(first_all[micro], first_row, slice_len, 1)
            first = jnp.repeat(first, heads, axis=0)
            weights = sliced_scores(packed, kv_all, first, positions, scale, shift)
            attended = jnp.einsum(
                "pqk,pkd->pqd", weights.astype(BF16), kv_all[..., HEAD:], preferred_element_type=F32
            ).astype(BF16)
            mixture = from_pairs(attended).reshape(mp_size * rows_here, head_width)
            middle = local_rows + scatter_mp(dot(mixture, out_full).astype(BF16))
            factor_two = norm_factor(middle)
            rows_two = gather_mp((middle * factor_two * gain_ffn).astype(BF16))
            y, dh, activated, gate_grad, up_grad = ffn(
                rows_two, portion, gate_full, up_full, down_full
            )
            results.append(from_rows((middle + scatter_mp(y)).astype(BF16)))
            middle_term, gain_part = norm_back(middle, factor_two, gain_ffn, scatter_mp(dh))
            gain_ffn_grad = gain_ffn_grad + gain_part
            middle_grad = local_cot.astype(F32) + middle_term
            attn_portion = gather_mp(middle_grad.astype(BF16))
            mix_grad = to_pairs(dot_nt(attn_portion, out_full).astype(BF16))
            sig = sliced_scores(packed, kv_all, first, positions, scale, shift)
            prob_grad = jnp.einsum(
                "pqd,pkd->pqk", mix_grad, kv_all[..., HEAD:], preferred_element_type=F32
            )
            score_grad = (prob_grad * sig * (1.0 - sig)).astype(BF16)
            dq = jnp.einsum("pqk,pkd->pqd", score_grad, kv_all[..., :HEAD], preferred_element_type=F32)
            dk = jnp.einsum("pqk,pqd->pkd", score_grad, packed[..., :HEAD], preferred_element_type=F32)
            dv = jnp.einsum("pqk,pqd->pkd", sig.astype(BF16), mix_grad, preferred_element_type=F32)
            dkv = lax.psum_scatter(
                jnp.concatenate([dk * scale, dv], axis=-1).astype(BF16), "dp", scatter_dimension=1, tiled=True
            ).astype(F32)
            back = from_pairs(jnp.concatenate([dq * scale, dkv], axis=-1))
            back = back.reshape(mp_size, seq_count, row_count, heads, 3 * HEAD)
            proj_grad = jnp.stack(
                [
                    rotate(back[..., :HEAD], True),
                    rotate(back[..., HEAD : 2 * HEAD], True),
                    back[..., 2 * HEAD :],
                ],
                axis=3,
            ).astype(BF16).reshape(mp_size * rows_here, 3 * head_width)
            partial_grad = dot_nt(proj_grad, qkv_full)
            gain_attn_grad = gain_attn_grad + jnp.sum(partial_grad * rows_one.astype(F32), axis=0)
            input_term, _ = norm_back(
                local_rows, factor_one, gain_attn, scatter_mp(partial_grad.astype(BF16))
            )
            input_grads.append(from_rows(middle_grad + input_term))
            for held, array in zip(
                kept,
                (rows_one, proj_grad, mixture, attn_portion, rows_two, gate_grad, up_grad, activated, portion),
            ):
                held.append(array)

        def scatter_dp(lefts, rights, left_blocked):
            (blocks,) = weight_grad(lefts, (rights,), left_blocked)
            return lax.psum_scatter(blocks, "dp", scatter_dimension=0, tiled=True)[0].astype(F32)

        ones, projs, mixtures, attns, twos, gates, ups, acts, portions = kept
        sum_gate = scatter_dp(twos, gates, True)
        sum_up = scatter_dp(twos, ups, True)
        sum_down = scatter_dp(acts, portions, False)
        sum_out = scatter_dp(mixtures, attns, False)
        sum_qkv = scatter_dp(ones, projs, True)
    gain_sums = (sum_all(gain_attn_grad / gain_attn), sum_all(gain_ffn_grad))
    return (
        jnp.stack(results),
        jnp.stack(input_grads),
        gain_sums[0],
        sum_qkv[:, :head_width],
        sum_qkv[:, head_width : 2 * head_width],
        sum_qkv[:, 2 * head_width :],
        sum_out,
        gain_sums[1],
        sum_gate,
        sum_up,
        sum_down,
    )


def solution(mesh):
    tokens = P(None, ("dp", "mp"), None, None)
    column = P("dp", "mp")
    row = P("mp", "dp")
    return jax.shard_map(
        per_device,
        mesh=mesh,
        in_specs=(
            tokens, tokens, P(), P(), column, column, column, row, P(), column, column, row,
        ),
        out_specs=(
            tokens, tokens, P(), column, column, column, row, P(), column, column, row,
        ),
        check_vma=False,
    )
```

```python
import functools
import math

import jax
import jax.numpy as jnp
from jax import lax
from jax.experimental import pallas as pl
from jax.experimental.pallas import tpu as pltpu
from jax.sharding import PartitionSpec as P

HEAD = 128
epsilon = 1e-05
rope_base = 10000.0
F32 = jnp.float32
BF16 = jnp.bfloat16


def rope_tables(positions):
    half_size = HEAD // 2
    inverse = jnp.power(rope_base, -(jnp.arange(half_size, dtype=F32) * 2.0 / HEAD))
    angles = positions.astype(F32)[:, None] * inverse[None, :]
    return (jnp.cos(angles), jnp.sin(angles))


def full_tables(positions):
    cosine, sine = rope_tables(positions)
    return (
        jnp.concatenate([cosine, cosine], axis=-1),
        jnp.concatenate([-sine, sine], axis=-1),
    )


def swap_halves(values):
    half_size = HEAD // 2
    return jnp.concatenate([values[..., half_size:], values[..., :half_size]], axis=-1)


def dot(left, right):
    return jnp.dot(left, right, preferred_element_type=F32)


def dot_tn(left, right):
    return lax.dot_general(left, right, (((0,), (0,)), ((), ())), preferred_element_type=F32)


def dot_nt(left, right):
    return lax.dot_general(left, right, (((1,), (1,)), ((), ())), preferred_element_type=F32)


def norm_factor(values):
    return lax.rsqrt(jnp.mean(values * values, axis=-1, keepdims=True) + epsilon)


def norm_back(values, factor, gain, incoming):
    scaled = incoming * gain
    gain_term = jnp.sum(incoming * values * factor, axis=0)
    input_term = factor * scaled - values * factor**3 * jnp.mean(
        scaled * values, axis=-1, keepdims=True
    )
    return (input_term, gain_term)


def sigmoid_of(raw, scale, shift):
    return 1.0 / (1.0 + jnp.exp(shift - raw * scale))


def split_cores(core, values, rows_here):
    shaped = values.reshape(-1, 2, rows_here, values.shape[-1])
    first, second = shaped[:, 0], shaped[:, 1]
    is_first = core == 0
    return jnp.where(is_first, first, second), jnp.where(is_first, second, first)

MESH = pl.DeviceIdType.MESH


class Spot:
    def __init__(self):
        self.dp, self.mp = lax.axis_index("dp"), lax.axis_index("mp")
        self.dp_size, self.mp_size = lax.axis_size("dp"), lax.axis_size("mp")
        self.places = self.mp_size // 2
        self.place, self.core = lax.div(self.mp, 2), lax.rem(self.mp, 2)
        self.sibling = (self.dp, self.mp + 1 - 2 * self.core)
        self.right = (self.dp, self.mp + 2)
        self.left = (self.dp, self.mp - 2)
        self.has_right = self.place < self.places - 1
        self.has_left = self.place > 0

    def peer(self, step):
        return lax.rem(self.dp + step, self.dp_size)

    def enter(self, with_dp, with_mp):
        barrier = pltpu.get_barrier_semaphore()
        count = 0

        def greet(device):
            pl.semaphore_signal(barrier, inc=1, device_id=device, device_id_type=MESH)

        if with_mp:
            greet(self.sibling)
            pl.when(self.has_right)(lambda: greet(self.right))
            pl.when(self.has_left)(lambda: greet(self.left))
            count += 1 + self.has_right.astype(jnp.int32) + self.has_left.astype(jnp.int32)
        if with_dp:
            for step in range(1, self.dp_size):
                greet((self.peer(step), self.mp))
            count += self.dp_size - 1
        pl.semaphore_wait(barrier, count)


class Swap:
    def __init__(self, spot, source, target, send, receive):
        self.spot, self.source, self.target = spot, source, target
        self.send, self.receive = send, receive
        self.copies = [self.copy(step) for step in range(1, spot.dp_size)]

    def copy(self, step):
        spot = self.spot
        return pltpu.make_async_remote_copy(
            src_ref=self.source.at[spot.peer(step)],
            dst_ref=self.target.at[spot.dp],
            send_sem=self.send.at[step],
            recv_sem=self.receive.at[step],
            device_id=(spot.peer(step), spot.mp),
            device_id_type=MESH,
        )

    def start(self):
        for copy in self.copies:
            copy.start()
        self.keep()

    def keep(self):
        self.target[self.spot.dp] = self.source[self.spot.dp]

    def wait(self):
        for copy in self.copies:
            copy.wait()


class Gather:
    def __init__(self, spot, shard, window, sems):
        self.local = pltpu.make_async_copy(shard, window(spot.dp), sems.at[0, 0])
        self.copies = [
            pltpu.make_async_remote_copy(
                src_ref=shard,
                dst_ref=window(spot.dp),
                send_sem=sems.at[0, step],
                recv_sem=sems.at[1, step],
                device_id=(spot.peer(step), spot.mp),
                device_id_type=MESH,
            )
            for step in range(1, spot.dp_size)
        ]

    def start(self):
        for copy in self.copies:
            copy.start()
        self.local.start()

    def wait(self):
        for copy in self.copies:
            copy.wait()
        self.local.wait()


class Spread:
    def __init__(self, spot, shard, full, sems):
        self.spot, self.shard, self.full, self.sems = spot, shard, full, sems
        self.local = pltpu.make_async_copy(shard, full.at[spot.mp], sems.at[6, 0])

    def copy(self, kind, device, p, source=None, core=None):
        at = 2 * p + (self.spot.core if core is None else core)
        return pltpu.make_async_remote_copy(
            src_ref=self.full.at[at] if source is None else source,
            dst_ref=self.full.at[at],
            send_sem=self.sems.at[kind, p],
            recv_sem=self.sems.at[kind + 1, p],
            device_id=device,
            device_id_type=MESH,
        )

    def rightward(self, p, source=None):
        return self.copy(0, self.spot.right, p, source)

    def leftward(self, p, source=None):
        return self.copy(2, self.spot.left, p, source)

    def across(self, p, source=None):
        return self.copy(4, self.spot.sibling, p, source)

    def begin(self):
        spot = self.spot
        pl.when(spot.has_right)(lambda: self.rightward(spot.place, self.shard).start())
        pl.when(spot.has_left)(lambda: self.leftward(spot.place, self.shard).start())
        self.across(spot.place, self.shard).start()
        self.local.start()

    def go_on(self, hop):
        spot = self.spot

        @pl.when(spot.place >= hop)
        def _():
            p = spot.place - hop
            self.rightward(p).wait_recv()
            pl.when(spot.has_right)(lambda: self.rightward(p).start())
            self.across(p).start()

        @pl.when(spot.place + hop < spot.places)
        def _():
            p = spot.place + hop
            self.leftward(p).wait_recv()
            pl.when(spot.has_left)(lambda: self.leftward(p).start())
            self.across(p).start()

    def finish(self):
        spot = self.spot
        for p in range(spot.places):
            self.copy(4, spot.sibling, p, core=1 - spot.core).wait_recv()
            self.across(p).wait_send()
            pl.when(spot.has_right & (spot.place >= p))(lambda: self.rightward(p).wait_send())
            pl.when(spot.has_left & (spot.place <= p))(lambda: self.leftward(p).wait_send())
        self.local.wait()


def spread_scratch(places):
    return [pltpu.SemaphoreType.DMA((7, places))]


class Ship(Swap):
    def __init__(self, spot, source, target, sems):
        super().__init__(spot, source, target, sems.at[0], sems.at[1])
        self.local = pltpu.make_async_copy(source.at[spot.dp], target.at[spot.dp], sems.at[0, 0])

    def start(self):
        for copy in self.copies:
            copy.start()
        self.local.start()

    def wait(self):
        super().wait()
        self.local.wait()


def window_of(full, axis, step, column=0, columns=None):
    def window(index):
        along = pl.ds(pl.multiple_of(index * step, step), step)
        if axis == 1:
            return full.at[:, along]
        if columns is None:
            return full.at[along, :]
        return full.at[along, pl.ds(column, columns)]

    return window


def swap_scratch(size, *block):
    return [
        pltpu.VMEM((size, *block), BF16),
        pltpu.VMEM((size, *block), BF16),
        pltpu.SemaphoreType.DMA((size,)),
        pltpu.SemaphoreType.DMA((size,)),
    ]


def far_first(places):
    orders = []
    for place in range(places):
        right, left, order = list(range(places - 1, place, -1)), list(range(place)), []
        while right or left:
            order += right[:1] + left[:1]
            right, left = right[1:], left[1:]
        orders.append(order + [place])
    return orders


class Sum:
    def __init__(self, spot, mine, out, from_sibling, passed, sems):
        self.spot = spot
        self.mine, self.out = mine, out
        self.from_sibling, self.passed = from_sibling, passed
        self.sems = sems
        self.orders = far_first(spot.places)

    def copy(self, source, target, kind, t, device, to=None):
        return pltpu.make_async_remote_copy(
            src_ref=source.at[t],
            dst_ref=target.at[t if to is None else to],
            send_sem=self.sems.at[kind, t],
            recv_sem=self.sems.at[kind + 1, t],
            device_id=device,
            device_id_type=MESH,
        )

    def sibling(self, t):
        return self.copy(self.out, self.from_sibling, 0, t, self.spot.sibling)

    def rightward(self, t):
        return self.copy(self.mine, self.passed, 2, t, self.spot.right)

    def leftward(self, t, place):
        to = jnp.where(t == place, self.spot.places, t)
        return self.copy(self.mine, self.passed, 4, t, self.spot.left, to)

    def leftward_out(self, t):
        return self.leftward(t, self.spot.place - 1)

    def leftward_in(self, t):
        return self.leftward(t, self.spot.place)

    def term(self, s):
        chosen = 0
        for place, order in enumerate(self.orders):
            for at, t in enumerate(order):
                if t:
                    chosen = chosen + jnp.where((self.spot.place == place) & (s == at), t, 0)
        return chosen

    def add(self, t, arrived):
        self.mine[t] = (self.mine[t].astype(F32) + arrived.astype(F32)).astype(BF16)

    def absorb(self, t):
        self.sibling(t).wait_recv()
        self.add(t, self.from_sibling[t])

    def begin(self, s):
        spot = self.spot

        @pl.when((spot.place == 0) & (s < spot.places - 1))
        def _():
            t = spot.places - 1 - s
            self.absorb(t)
            self.rightward(t).start()

        @pl.when((spot.place == spot.places - 1) & (s < spot.places - 1))
        def _():
            self.absorb(s)
            self.leftward_out(s).start()

    def go_on(self, hop):
        spot = self.spot
        last = spot.places - 1

        @pl.when((spot.place > 0) & (spot.place <= hop))
        def _():
            t = last + spot.place - hop
            self.absorb(t)
            self.rightward(t).wait_recv()
            self.add(t, self.passed[t])
            self.rightward(t).start()

        @pl.when((spot.place < last) & (last - spot.place <= hop))
        def _():
            t = hop - last + spot.place
            self.absorb(t)
            self.leftward_in(t).wait_recv()
            self.add(t, self.passed[t])
            self.leftward_out(t).start()

    def finish(self):
        spot = self.spot
        t = spot.place
        self.absorb(t)

        @pl.when(spot.has_left)
        def _():
            self.rightward(t).wait_recv()
            self.add(t, self.passed[t])

        @pl.when(spot.has_right)
        def _():
            self.leftward_in(t).wait_recv()
            self.add(t, self.passed[spot.places])

        for t in range(spot.places):
            self.sibling(t).wait_send()
            pl.when(spot.place < t)(lambda: self.rightward(t).wait_send())
            pl.when(spot.place > t)(lambda: self.leftward_out(t).wait_send())
        return self.mine[spot.place].astype(F32)


def sum_scratch(places, rows_here, width):
    return [
        *[pltpu.VMEM((places, rows_here, width), BF16)] * 3,
        pltpu.VMEM((places + 1, rows_here, width), BF16),
        pltpu.SemaphoreType.DMA((6, places)),
    ]


def attend_blocks(qkv, first_ref, out, scale, shift):
    count, block = out.shape[:2]
    row_at = lax.broadcasted_iota(jnp.int32, (block, block), 0)
    col_at = lax.broadcasted_iota(jnp.int32, (block, block), 1)

    @pl.loop(0, count)
    def _(i):
        queries = qkv[i, :, 0:HEAD]
        first = first_ref[pl.ds(pl.multiple_of(i * block, block), block), :]

        def add_block(j, acc, diagonal=False):
            sig = sigmoid_of(dot_nt(queries, qkv[j, :, HEAD : 2 * HEAD]), scale, shift)
            visible = col_at >= first - j * block
            if diagonal:
                visible = visible & (col_at <= row_at)
            weights = jnp.where(visible, sig, 0.0).astype(BF16)
            return acc + dot(weights, qkv[j, :, 2 * HEAD :])

        acc = add_block(i, jnp.zeros((block, HEAD), F32), True)
        out[i] = lax.fori_loop(0, i, add_block, acc).astype(BF16)


def attend_back_blocks(
    spot, qkv, grad, first_ref, cos_ref, sin_ref, out_q, out_kv, dq, made, scale, shift
):
    count, block = grad.shape[:2]
    col_at = lax.broadcasted_iota(jnp.int32, (block, block), 0)
    row_at = lax.broadcasted_iota(jnp.int32, (block, block), 1)
    dq[...] = jnp.zeros_like(dq)

    def unrotate(values, i):
        rows = pl.ds(pl.multiple_of(i * block, block), block)
        swapped = pltpu.roll(values, HEAD // 2, 1)
        return (values * cos_ref[rows, :] - swapped * sin_ref[rows, :]).astype(BF16)

    @pl.loop(0, count)
    def _(at):
        j = spot.peer(at + 1)
        keys = qkv[j, :, HEAD : 2 * HEAD]
        values = qkv[j, :, 2 * HEAD :]
        keys_t = keys.T

        def add_block(i, sums, diagonal=False):
            dk, dv = sums
            queries, grads = qkv[i, :, 0:HEAD], grad[i]
            sig = sigmoid_of(dot_nt(keys, queries), scale, shift)
            visible = col_at >= first_ref[i] - j * block
            if diagonal:
                visible = visible & (col_at <= row_at)
            sig = jnp.where(visible, sig, 0.0)
            prob_grad = dot_nt(values, grads)
            score_grad = (prob_grad * sig * (1.0 - sig)).astype(BF16)
            dq[i] += dot(keys_t, score_grad)
            return dk + dot(score_grad, queries), dv + dot(sig.astype(BF16), grads)

        zero = jnp.zeros((block, HEAD), F32)
        dk, dv = lax.fori_loop(j + 1, count, add_block, add_block(j, (zero, zero), True))
        out_kv[j, :, 0:HEAD] = unrotate(dk * scale, j)
        out_kv[j, :, HEAD:] = dv.astype(BF16)
        pl.when(at < count - 1)(lambda: made(at + 1))

    @pl.loop(0, count)
    def _(i):
        out_q[i] = unrotate(dq[i].T * scale, i)


def take(refs, count):
    return refs[:count], refs[count:]


def begin_kernel(query, key, value, out, first, qkv_full, out_full, first_full, sems, spread_sems):
    spot = Spot()
    spot.enter(True, True)
    rows, columns = query.shape
    jobs = [
        (shard, window_of(qkv_full, 0, rows, i * columns, columns))
        for i, shard in enumerate((query, key, value))
    ]
    jobs.append((out, window_of(out_full, 1, out.shape[1])))
    gathers = [Gather(spot, shard, window, sems.at[i]) for i, (shard, window) in enumerate(jobs)]
    spread = Spread(spot, first, first_full, spread_sems)
    spread.begin()
    for gather in gathers:
        gather.start()
    for hop in range(1, spot.places):
        spread.go_on(hop)
    for gather in gathers:
        gather.wait()
    spread.finish()


def forward_kernel(tail, head, spreads, gather_axis, heads, toks, scale, shift, *refs):
    gathers = gather_axis is not None
    tail_in, refs = take(refs, 4 * tail)
    head_in, refs = take(refs, 5 * head)
    spread_in, refs = take(refs, spreads)
    gather_in, refs = take(refs, gathers)
    tail_out, refs = take(refs, 3 * tail)
    head_out, refs = take(refs, 2 * head)
    spread_out, refs = take(refs, spreads)
    gather_out, refs = take(refs, gathers)
    sum_refs, refs = take(refs, 5 * tail)
    head_refs, refs = take(refs, 9 * head)
    spot = Spot()
    spot.enter(head or gathers, tail or spreads)
    moving = [Spread(spot, *refs) for refs in zip(spread_in, spread_out, refs)]
    for spread in moving:
        spread.begin()
    if gathers:
        window = window_of(gather_out[0], gather_axis, gather_in[0].shape[gather_axis])
        gather = Gather(spot, gather_in[0], window, refs[-1])

    if tail:
        got, out_weight, x_ref, gain_ref = tail_in
        middle_ref, normed_ref, mix_ref = tail_out
        pairs = got.shape[0]
        owner_rows = toks * (pairs // heads)
        for o in range(mix_ref.shape[0] // owner_rows):
            for p in range(pairs):
                s, h = p // heads, p % heads
                mix_ref[pl.ds(o * owner_rows + s * toks, toks), h * HEAD : (h + 1) * HEAD] = got[
                    p, pl.ds(o * toks, toks), :
                ]
        summed = Sum(spot, *sum_refs)
        chip_rows = 2 * owner_rows

        @pl.loop(0, spot.places)
        def _(s):
            t = summed.term(s)
            rows = pl.ds(pl.multiple_of(t * chip_rows, chip_rows), chip_rows)
            value = dot(mix_ref[rows, :], out_weight[...]).astype(BF16)
            keep, send = split_cores(spot.core, value, owner_rows)
            summed.mine[t] = keep[0]
            summed.out[t] = send[0]
            summed.sibling(t).start()

        @pl.loop(0, spot.places - 1)
        def _(s):
            summed.begin(s)

    if head:
        rows_ref, weight_ref, cos_ref, sin_ref, first_ref = head_in
        qkv_ref, got_ref = head_out
        made, paired, qkv, qkv_send, qkv_recv, part, got, part_send, part_recv = head_refs
        pairs = paired.shape[0]
        owner_rows = toks * (pairs // heads)
        step = made.shape[0]

        @pl.loop(0, rows_ref.shape[0] // step)
        def _(i):
            rows = pl.ds(pl.multiple_of(i * step, step), step)
            made[...] = dot(rows_ref[rows, :], weight_ref[...])
            for j in range(step // owner_rows):
                to = pl.ds(pl.multiple_of((i * (step // owner_rows) + j) * toks, toks), toks)
                cosine, sine = cos_ref[to, :], sin_ref[to, :]
                for p in range(pairs):
                    s, h = p // heads, p % heads
                    here = pl.ds(j * owner_rows + s * toks, toks)
                    for kind in range(3):
                        piece = made[here, pl.ds((kind * heads + h) * HEAD, HEAD)]
                        if kind < 2:
                            piece = piece * cosine + pltpu.roll(piece, HEAD // 2, 1) * sine
                        paired[p, to, kind * HEAD : (kind + 1) * HEAD] = piece.astype(BF16)

        swap = Swap(spot, paired, qkv, qkv_send, qkv_recv)
        swap.start()
    if gathers:
        gather.start()
    for spread in moving:
        spread.go_on(1)
    if tail and spot.places > 2:
        summed.go_on(1)
    if head:
        swap.wait()
    for hop in range(2, spot.places - 1):
        for spread in moving:
            spread.go_on(hop)
        if tail:
            summed.go_on(hop)
    if head:
        attend_blocks(qkv, first_ref, part, scale, shift)
        swap = Swap(spot, part, got, part_send, part_recv)
        swap.start()
        qkv_ref[...] = qkv[...]
        swap.wait()
        got_ref[...] = got[...]
    for spread in moving:
        if spot.places > 2:
            spread.go_on(spot.places - 1)
    if tail:
        middle = x_ref[...].astype(F32) + summed.finish()
        middle_ref[...] = middle
        normed_ref[...] = (middle * norm_factor(middle) * gain_ref[...]).astype(BF16)
    for spread in moving:
        spread.finish()
    if gathers:
        gather.wait()


def middle_kernel(
    first, spreads, owner_rows,
    rows_ref, cot_ref, gate_ref, up_ref, down_ref, middle_ref, local_cot_ref, gain_ref,
    *refs,
):
    shards, refs = take(refs, spreads)
    before, refs = take(refs, 0 if first else 3)
    (result_ref, grad_ref, low_ref, gain_grad_ref), refs = take(refs, 4)
    fulls, refs = take(refs, spreads)
    after, refs = take(refs, 3)
    (act_ref, dgate_ref, dup_ref, turned, new_rows, new_cols, old_rows, old_cols), refs = take(refs, 8)
    (wide_sems,), refs = take(refs, 1)
    sum_refs, refs = take(refs, 10)
    spot = Spot()
    spot.enter(False, True)
    summed, summed_y = Sum(spot, *sum_refs[:5]), Sum(spot, *sum_refs[5:])
    moving = [Spread(spot, *refs) for refs in zip(shards, fulls, refs)]
    for spread in moving:
        spread.begin()
    hidden, width = gate_ref.shape[1], rows_ref.shape[1]
    chip_rows = 2 * owner_rows
    tile = min(256, hidden)
    blocks = after[0].shape[0]
    block = width // blocks
    new = (new_rows.at[0], new_rows.at[1], new_cols)
    old = (old_rows.at[0], old_rows.at[1], old_cols)

    def load(g, e):
        return pltpu.make_async_copy(before[g].at[e], old[g], wide_sems.at[0, g])

    def store(g, e):
        return pltpu.make_async_copy(new[g], after[g].at[e], wide_sems.at[1, g])

    if not first:
        for g in range(3):
            load(g, 0).start()

    @pl.loop(0, spot.places)
    def _(s):
        place = summed.term(s)
        rows = pl.ds(pl.multiple_of(place * chip_rows, chip_rows), chip_rows)

        @pl.loop(0, hidden // tile)
        def _(t):
            cols = pl.ds(pl.multiple_of(t * tile, tile), tile)
            gate = dot(rows_ref[rows, :], gate_ref[:, cols])
            up = dot(rows_ref[rows, :], up_ref[:, cols])
            sig = jax.nn.sigmoid(gate)
            silu = gate * sig
            act_ref[rows, cols] = (silu * up).astype(BF16)
            grad = dot_nt(cot_ref[rows, :], down_ref[cols, :])
            dgate_ref[rows, cols] = (grad * up * sig * (1.0 + gate * (1.0 - sig))).astype(BF16)
            dup_ref[rows, cols] = (grad * silu).astype(BF16)

        @pl.when(s > 0)
        def _():
            summed.begin(s - 1)
            summed_y.begin(s - 1)

        for hop in range(1, spot.places - 1):

            @pl.when(s == hop + 1)
            def _():
                for spread in moving:
                    spread.go_on(hop)
                summed.go_on(hop)
                summed_y.go_on(hop)

        @pl.loop(0, width // 256)
        def _(t):
            cols = pl.ds(pl.multiple_of(t * 256, 256), 256)
            value = dot(act_ref[rows, :], down_ref[:, cols])
            keep, send = split_cores(spot.core, value.astype(BF16), owner_rows)
            summed_y.mine[place, :, cols] = keep[0]
            summed_y.out[place, :, cols] = send[0]
            value = dot_nt(dgate_ref[rows, :], gate_ref[cols, :])
            value += dot_nt(dup_ref[rows, :], up_ref[cols, :])
            keep, send = split_cores(spot.core, value.astype(BF16), owner_rows)
            summed.mine[place, :, cols] = keep[0]
            summed.out[place, :, cols] = send[0]

        summed.sibling(place).start()
        summed_y.sibling(place).start()

    def make(g, e, left, right, right_at, columns):
        pl.when(e > 0)(lambda: store(g, e - 1).wait())
        if not first:
            load(g, e).wait()
        step = math.gcd(columns, 256)

        @pl.loop(0, columns // step)
        def _(t):
            cols = pl.ds(pl.multiple_of(t * step, step), step)
            total = dot(left[...], right[:, pl.ds(pl.multiple_of(right_at + t * step, step), step)])
            if not first:
                total += old[g][:, cols].astype(F32)
            new[g][:, cols] = total.astype(BF16)

        if not first:
            pl.when(e < blocks - 1)(lambda: load(g, e + 1).start())
        store(g, e).start()

    @pl.loop(0, blocks)
    def _(e):
        left = turned.at[pl.ds(0, block), :]
        left[...] = rows_ref[:, pl.ds(pl.multiple_of(e * block, block), block)].T
        make(0, e, left, dgate_ref, 0, hidden)
        make(1, e, left, dup_ref, 0, hidden)

    for spread in moving:
        spread.go_on(spot.places - 1)
    left = turned.at[pl.ds(0, hidden), :]
    left[...] = act_ref[...].T

    @pl.loop(0, blocks)
    def _(e):
        make(2, e, left, cot_ref, e * block, block)

    incoming = summed.finish()
    middle = middle_ref[...]
    term, gain_grad = norm_back(middle, norm_factor(middle), gain_ref[...], incoming)
    gain_grad_ref[...] = gain_grad[None]
    grad = local_cot_ref[...].astype(F32) + term
    grad_ref[...] = grad
    low_ref[...] = grad.astype(BF16)
    result_ref[...] = (middle + summed_y.finish()).astype(BF16)
    for spread in moving:
        spread.finish()
    for g in range(3):
        store(g, blocks - 1).wait()


def backward_kernel(tail, head, ships, spreads, heads, toks, scale, shift, *refs):
    tail_in, refs = take(refs, 6 * tail)
    head_in, refs = take(refs, 6 * head)
    ship_in, refs = take(refs, ships)
    spread_in, refs = take(refs, spreads)
    tail_out, refs = take(refs, 2 * tail)
    head_out, refs = take(refs, head)
    ship_out, refs = take(refs, ships)
    spread_out, refs = take(refs, spreads)
    sum_refs, refs = take(refs, 5 * tail)
    head_refs, refs = take(refs, 13 * head)
    spot = Spot()
    spot.enter(head or ships > 0, tail or spreads)
    shipped = [
        Ship(spot, source, target, refs[-1].at[i])
        for i, (source, target) in enumerate(zip(ship_in, ship_out))
    ]
    if spreads:
        spread = Spread(spot, *spread_in, *spread_out, refs[0])
        spread.begin()

    if tail:
        proj_ref, weight_ref, rows_one_ref, x_ref, grad_ref, gain_ref = tail_in
        result_ref, gain_grad_ref = tail_out
        owner_rows = x_ref.shape[0]
        summed = Sum(spot, *sum_refs)
        chip_rows = 2 * owner_rows
        gain_grad_ref[...] = jnp.zeros_like(gain_grad_ref)

        @pl.loop(0, spot.places)
        def _(s):
            t = summed.term(s)
            rows = pl.ds(pl.multiple_of(t * chip_rows, chip_rows), chip_rows)
            value = dot_nt(proj_ref[rows, :], weight_ref[...])
            gain_grad_ref[...] += jnp.sum(
                value * rows_one_ref[rows, :].astype(F32), axis=0, keepdims=True
            )
            keep, send = split_cores(spot.core, value.astype(BF16), owner_rows)
            summed.mine[t] = keep[0]
            summed.out[t] = send[0]
            summed.sibling(t).start()
            pl.when(s > 0)(lambda: summed.begin(s - 1))

    if head:
        rows_ref, out_weight_ref, qkv, first_ref, cos_ref, sin_ref = head_in
        (head_proj_ref,) = head_out
        part, got, part_send, part_recv = head_refs[:4]
        made_q, got_q, q_send, q_recv, made_kv, got_kv, kv_send, kv_recv, dq = head_refs[4:]
        pairs = part.shape[0]
        owner_rows = toks * (pairs // heads)
        total = rows_ref.shape[0]
        step = min(512, total)

        @pl.loop(0, total // step)
        def _(i):
            rows = pl.ds(pl.multiple_of(i * step, step), step)
            made = dot_nt(rows_ref[rows, :], out_weight_ref[...]).astype(BF16)
            for j in range(step // owner_rows):
                to = pl.ds(pl.multiple_of((i * (step // owner_rows) + j) * toks, toks), toks)
                for p in range(pairs):
                    s, h = p // heads, p % heads
                    start = j * owner_rows + s * toks
                    part[p, to, :] = made[start : start + toks, h * HEAD : (h + 1) * HEAD]

        swap = Swap(spot, part, got, part_send, part_recv)
        swap.start()
        swap.wait()
    for ship in shipped:
        ship.start()
    if spreads:
        spread.go_on(1)
    if tail and spot.places > 2:
        summed.go_on(1)
    if head:
        swap_kv = Swap(spot, made_kv, got_kv, kv_send, kv_recv)
        attend_back_blocks(
            spot, qkv, got, first_ref, cos_ref, sin_ref, made_q, made_kv, dq,
            lambda step: swap_kv.copy(step).start(), scale, shift,
        )
        swap_kv.keep()
        swap = Swap(spot, made_q, got_q, q_send, q_recv)
        swap.start()
    for hop in range(2, spot.places - 1):
        if spreads:
            spread.go_on(hop)
        if tail:
            summed.go_on(hop)
    if head:
        swap_kv.wait()
        swap.wait()
        for o in range(total // owner_rows):
            for p in range(pairs):
                s, h = p // heads, p % heads
                here, there = pl.ds(o * owner_rows + s * toks, toks), pl.ds(o * toks, toks)
                for kind in range(3):
                    piece = (
                        got_kv[p, there, (kind - 1) * HEAD : kind * HEAD] if kind else got_q[p, there, :]
                    )
                    head_proj_ref[
                        here, (kind * heads + h) * HEAD : (kind * heads + h + 1) * HEAD
                    ] = piece
    if spreads and spot.places > 2:
        spread.go_on(spot.places - 1)
    if tail:
        incoming = summed.finish()
        x = x_ref[...].astype(F32)
        term, _ = norm_back(x, norm_factor(x), gain_ref[...], incoming)
        result_ref[...] = grad_ref[...] + term
    for ship in shipped:
        ship.wait()
    if spreads:
        spread.finish()


def ffn_kernel(
    rows_ref, cot_ref, gate_ref, up_ref, down_ref, y_ref, dh_ref, act_ref, dgate_ref, dup_ref
):
    hidden = gate_ref.shape[1]
    width = rows_ref.shape[1]
    tile = min(256, hidden)

    @pl.loop(0, hidden // tile)
    def _(t):
        cols = pl.ds(pl.multiple_of(t * tile, tile), tile)
        gate = dot(rows_ref[...], gate_ref[:, cols])
        up = dot(rows_ref[...], up_ref[:, cols])
        sig = jax.nn.sigmoid(gate)
        silu = gate * sig
        act_ref[:, cols] = (silu * up).astype(BF16)
        grad = dot_nt(cot_ref[...], down_ref[cols, :])
        dgate_ref[:, cols] = (grad * up * sig * (1.0 + gate * (1.0 - sig))).astype(BF16)
        dup_ref[:, cols] = (grad * silu).astype(BF16)

    @pl.loop(0, width // 256)
    def _(t):
        cols = pl.ds(pl.multiple_of(t * 256, 256), 256)
        y_ref[:, cols] = dot(act_ref[...], down_ref[:, cols]).astype(BF16)
        dh = dot_nt(dgate_ref[...], gate_ref[cols, :]) + dot_nt(dup_ref[...], up_ref[cols, :])
        dh_ref[:, cols] = dh.astype(BF16)


def grad_kernel(count, groups, left_blocked, *refs):
    lefts, refs = take(refs, count)
    rights, refs = take(refs, count * groups)
    out_refs, (turned,) = take(refs, groups)
    rows = lefts[0].shape[0]

    def turn():
        for m, left in enumerate(lefts):
            turned[:, m * rows : (m + 1) * rows] = left[...].T

    if left_blocked:
        turn()
    else:
        pl.when(pl.program_id(0) == 0)(turn)
    tile = math.gcd(out_refs[0].shape[2], 256)
    for g, out_ref in enumerate(out_refs):
        own = rights[g * count : (g + 1) * count]

        @pl.loop(0, out_ref.shape[2] // tile)
        def _(t):
            cols = pl.ds(pl.multiple_of(t * tile, tile), tile)
            total = dot(turned[:, :rows], own[0][:, cols])
            for m in range(1, count):
                total += dot(turned[:, m * rows : (m + 1) * rows], own[m][:, cols])
            out_ref[0, :, cols] = total.astype(BF16)


VMEM = pl.BlockSpec(memory_space=pltpu.VMEM)
ANY = pl.BlockSpec(memory_space=pl.ANY)


def cost(flops, nbytes):
    return pl.CostEstimate(flops=flops, bytes_accessed=nbytes, transcendentals=0)


def limits(mebibytes):
    return pltpu.CompilerParams(vmem_limit_bytes=mebibytes * 2**20)


def shape(*dims, dtype=BF16):
    return jax.ShapeDtypeStruct(dims, dtype)


def comm_params(collective_id, mebibytes):
    return pltpu.CompilerParams(
        collective_id=collective_id, has_side_effects=True, vmem_limit_bytes=mebibytes * 2**20
    )


def begin(query, key, value, out, first):
    size, mp_size = lax.axis_size("dp"), lax.axis_size("mp")
    rows, columns = query.shape
    return pl.pallas_call(
        begin_kernel,
        out_shape=[
            shape(rows * size, 3 * columns),
            shape(out.shape[0], out.shape[1] * size),
            shape(mp_size, *first.shape),
        ],
        in_specs=[ANY] * 5,
        out_specs=[ANY] * 3,
        scratch_shapes=[
            pltpu.SemaphoreType.DMA((4, 2, size)),
            *spread_scratch(mp_size // 2),
        ],
        compiler_params=comm_params(0, 8),
        cost_estimate=cost(0, 60 * 2**20),
        name="begin",
    )(query, key, value, out, first)


def forward_stage(collective_id, tail, head, shard, gather, heads, toks, scale, shift):
    size, mp_size = lax.axis_size("dp"), lax.axis_size("mp")
    out_shape, scratch = [], []
    if tail:
        blocks, _, x, _ = tail
        owner_rows, width = x.shape
        total = blocks.shape[1] * blocks.shape[0] // heads
        out_shape += [
            shape(owner_rows, width, dtype=F32),
            shape(owner_rows, width),
            shape(total, heads * HEAD),
        ]
        scratch += sum_scratch(mp_size // 2, owner_rows, width)
    if head:
        total, slice_len = head[0].shape[0], head[2].shape[0]
        out_shape += [shape(size, slice_len, 3 * HEAD), shape(size, slice_len, HEAD)]
        scratch += [
            pltpu.VMEM((min(512, total), 3 * heads * HEAD), F32),
            *swap_scratch(size, slice_len, 3 * HEAD),
            *swap_scratch(size, slice_len, HEAD),
        ]
    here, spreads = len(out_shape), len(shard)
    out_shape += [shape(mp_size, *array.shape) for array in shard]
    scratch += spread_scratch(mp_size // 2) * spreads
    axis = None
    if gather:
        weight, axis = gather
        dims = list(weight.shape)
        dims[axis] *= size
        out_shape.append(shape(*dims))
        scratch.append(pltpu.SemaphoreType.DMA((2, size)))
    arrays = [*tail, *head]
    passing = spreads + bool(gather)
    return pl.pallas_call(
        functools.partial(
            forward_kernel, bool(tail), bool(head), spreads, axis, heads, toks, scale, shift
        ),
        out_shape=out_shape,
        in_specs=[VMEM] * len(arrays) + [ANY] * passing,
        out_specs=[VMEM] * here + [ANY] * passing,
        scratch_shapes=scratch,
        compiler_params=comm_params(collective_id, 52),
        cost_estimate=cost(10**10, 100 * 2**20),
        name="forward_stage",
    )(*arrays, *shard, *gather[:1])


def middle_part(
    collective_id, rows, cot, gate, up, down, middle, local_cot, gain, shards, before
):
    total, width = rows.shape
    hidden = gate.shape[1]
    size, mp_size = lax.axis_size("dp"), lax.axis_size("mp")
    owner_rows = middle.shape[0]
    block = width // size
    wide = [shape(size, block, hidden)] * 2 + [shape(size, hidden, block)]
    return pl.pallas_call(
        functools.partial(middle_kernel, not before, len(shards), owner_rows),
        out_shape=[
            shape(owner_rows, width),
            shape(owner_rows, width, dtype=F32),
            shape(owner_rows, width),
            shape(1, width, dtype=F32),
            *[shape(mp_size, *array.shape) for array in shards],
            *wide,
        ],
        in_specs=[VMEM] * 8 + [ANY] * (len(shards) + len(before)),
        out_specs=[VMEM] * 4 + [ANY] * (len(shards) + 3),
        scratch_shapes=[
            *[pltpu.VMEM((total, hidden), BF16)] * 3,
            pltpu.VMEM((max(block, hidden), total), BF16),
            pltpu.VMEM((2, block, hidden), BF16),
            pltpu.VMEM((hidden, block), BF16),
            pltpu.VMEM((2, block, hidden), BF16),
            pltpu.VMEM((hidden, block), BF16),
            pltpu.SemaphoreType.DMA((2, 3)),
            *sum_scratch(mp_size // 2, owner_rows, width) * 2,
            *spread_scratch(mp_size // 2) * len(shards),
        ],
        compiler_params=comm_params(collective_id, 61),
        cost_estimate=cost(18 * total * width * hidden, 60 * 2**20),
        name="middle_part",
    )(rows, cot, gate, up, down, middle, local_cot, gain, *shards, *before)


def backward_stage(collective_id, tail, head, ships, shard, heads, toks, scale, shift):
    size, mp_size = lax.axis_size("dp"), lax.axis_size("mp")
    places = mp_size // 2
    out_shape, scratch = [], []
    if tail:
        owner_rows, width = tail[3].shape
        out_shape += [shape(owner_rows, width, dtype=F32), shape(1, width, dtype=F32)]
        scratch += sum_scratch(places, owner_rows, width)
    if head:
        total, slice_len = head[0].shape[0], head[2].shape[1]
        out_shape.append(shape(total, 3 * heads * HEAD))
        scratch += [
            *swap_scratch(size, slice_len, HEAD),
            *swap_scratch(size, slice_len, HEAD),
            *swap_scratch(size, slice_len, 2 * HEAD),
            pltpu.VMEM((size, HEAD, slice_len), F32),
        ]
    here, spreads = len(out_shape), len(shard)
    if spreads:
        scratch += spread_scratch(places)
    if ships:
        scratch.append(pltpu.SemaphoreType.DMA((len(ships), 2, size)))
    out_shape += [shape(*array.shape) for array in ships]
    out_shape += [shape(mp_size, *array.shape) for array in shard]
    arrays = [*tail, *head]
    passing = len(ships) + spreads
    return pl.pallas_call(
        functools.partial(
            backward_kernel,
            bool(tail), bool(head), len(ships), spreads, heads, toks, scale, shift,
        ),
        out_shape=out_shape,
        in_specs=[VMEM] * len(arrays) + [ANY] * passing,
        out_specs=[VMEM] * here + [ANY] * passing,
        scratch_shapes=scratch,
        compiler_params=comm_params(collective_id, 56),
        cost_estimate=cost(10**10, 100 * 2**20),
        name="backward_stage",
    )(*arrays, *ships, *shard)


def ffn(rows, cot, gate, up, down):
    total, width = rows.shape
    hidden = gate.shape[1]
    step = min(512, total)
    by_rows = pl.BlockSpec((step, width), lambda i: (i, 0))
    by_hidden = pl.BlockSpec((step, hidden), lambda i: (i, 0))
    held = lambda array: pl.BlockSpec(array.shape, lambda i: (0, 0), pipeline_mode=pl.Buffered(1))
    return pl.pallas_call(
        ffn_kernel,
        grid=(total // step,),
        out_shape=[shape(total, width)] * 2 + [shape(total, hidden)] * 3,
        in_specs=[by_rows, by_rows, held(gate), held(up), held(down)],
        out_specs=[by_rows] * 2 + [by_hidden] * 3,
        compiler_params=limits(56),
        cost_estimate=cost(12 * total * width * hidden, 34 * 2**20),
        name="ffn",
    )(rows, cot, gate, up, down)


def weight_grad(lefts, groups, left_blocked):
    count = len(lefts)
    size = lax.axis_size("dp")
    rows = lefts[0].shape[0]
    m, n = lefts[0].shape[1], groups[0][0].shape[1]
    moving = lambda width: pl.BlockSpec((rows, width // size), lambda e: (0, e))
    fixed = lambda width: pl.BlockSpec(
        (rows, width), lambda e: (0, 0), pipeline_mode=pl.Buffered(1)
    )
    left_spec = moving(m) if left_blocked else fixed(m)
    right_spec = fixed(n) if left_blocked else moving(n)
    out = (m // size, n) if left_blocked else (m, n // size)
    return pl.pallas_call(
        functools.partial(grad_kernel, count, len(groups), left_blocked),
        grid=(size,),
        in_specs=[left_spec] * count + [right_spec] * (count * len(groups)),
        out_specs=[pl.BlockSpec((1, *out), lambda e: (e, 0, 0))] * len(groups),
        out_shape=[shape(size, *out)] * len(groups),
        scratch_shapes=[pltpu.VMEM((out[0], count * rows), BF16)],
        compiler_params=limits(52),
        cost_estimate=cost(2 * count * rows * m * n * len(groups), 24 * 2**20),
        name="weight_grad",
    )(*lefts, *(right for group in groups for right in group))


def first_visible(ids):
    at = jnp.arange(ids.shape[-1], dtype=jnp.int32)
    starts = jnp.concatenate([jnp.ones_like(ids[..., :1], jnp.bool_), ids[..., 1:] != ids[..., :-1]], axis=-1)
    return lax.cummax(jnp.where(starts, at, 0), axis=ids.ndim - 1)


def block_at(values, index):
    return lax.dynamic_index_in_dim(values, index, 0, keepdims=False)


def scatter_mp(values):
    return lax.psum_scatter(values, "mp", scatter_dimension=0, tiled=True).astype(F32)


def sum_all(values):
    for name in ("dp", "mp"):
        size = lax.axis_size(name)
        step = 1
        while step < size:
            values = values + lax.ppermute(values, name, [(i, i ^ step) for i in range(size)])
            step *= 2
    return values


def sliced_scores(qkv, kv_all, first, positions, scale, shift):
    raw = jnp.einsum("pqd,pkd->pqk", qkv[..., :HEAD], kv_all[..., :HEAD], preferred_element_type=F32)
    at = jnp.arange(kv_all.shape[1], dtype=jnp.int32)
    visible = (at >= first[..., None]) & (at <= positions[:, None])
    return jnp.where(visible, sigmoid_of(raw, scale, shift), 0.0)


def per_device(
    inputs,
    cotangent,
    doc_ids,
    gain_attn,
    w_query,
    w_key,
    w_value,
    w_out,
    gain_ffn,
    w_gate,
    w_up,
    w_down,
):
    dp_size = lax.axis_size("dp")
    mp_size = lax.axis_size("mp")
    micro_count, row_count, seq_count, width = inputs.shape
    slice_len = row_count * mp_size
    total_len = slice_len * dp_size
    rows_here = row_count * seq_count
    shift = math.log(total_len)
    scale = HEAD ** (-0.5)
    dp_at = lax.axis_index("dp")
    mp_at = lax.axis_index("mp")
    first_row = dp_at * slice_len
    positions = first_row + jnp.arange(slice_len, dtype=jnp.int32)
    head_width = w_query.shape[1]
    heads = head_width // HEAD
    hidden = w_gate.shape[1]
    pairs = seq_count * heads
    whole_pairs = pairs == dp_size
    cos_slice, sin_slice = full_tables(positions)
    cos_all, sin_all = full_tables(jnp.arange(total_len, dtype=jnp.int32))
    first_all = first_visible(doc_ids)

    def by_row(table):
        shaped = table.reshape(mp_size, 1, row_count, 1, HEAD)
        return jnp.broadcast_to(shaped, (mp_size, seq_count, row_count, 1, HEAD))

    def rotate(values, back=False):
        sine = -by_row(sin_slice) if back else by_row(sin_slice)
        return values * by_row(cos_slice) + swap_halves(values) * sine

    def to_pairs(values):
        shaped = values.reshape(mp_size, seq_count, row_count, heads, -1)
        return shaped.transpose(1, 3, 0, 2, 4).reshape(pairs, slice_len, -1)

    def from_pairs(values):
        shaped = values.reshape(seq_count, heads, mp_size, row_count, -1)
        return shaped.transpose(2, 0, 3, 1, 4).reshape(mp_size * rows_here, heads, -1)

    def to_rows(values):
        return jnp.swapaxes(values, 0, 1).reshape(rows_here, width)

    def from_rows(values):
        return jnp.swapaxes(values.reshape(seq_count, row_count, width), 0, 1)

    def gather_mp(values):
        return lax.all_gather(values, "mp", axis=0, tiled=True)

    gain_attn_grad = jnp.zeros((width,), F32)
    gain_ffn_grad = jnp.zeros((width,), F32)
    results = []
    input_grads = []
    kept = [[] for _ in range(9)]
    xs = [to_rows(inputs[m]) for m in range(micro_count)]
    cots = [to_rows(cotangent[m]) for m in range(micro_count)]
    normed = [
        (x.astype(F32) * norm_factor(x.astype(F32)) * gain_attn).astype(BF16) for x in xs
    ]
    micros = range(micro_count)
    if whole_pairs:
        stage = (heads, row_count, scale, shift)
        firsts = [block_at(first_all[m], dp_at // heads) for m in micros]
        last = micro_count - 1

        def whole(blocks):
            return blocks.reshape(mp_size * rows_here, width)

        def scatter_dp(blocks):
            return lax.psum_scatter(blocks, "dp", scatter_dimension=0, tiled=True)[0].astype(F32)

        qkv_full, out_full, rows_one = begin(w_query, w_key, w_value, w_out, normed[0])
        gathers = {0: (w_gate, 0), last: (w_up, 0), micro_count: (w_down, 1)}
        wide = []
        ones, qkvs, got, middles, lows, twos, mixtures = [whole(rows_one)], [], [], [], [], [], []
        for m in range(micro_count + 1):
            tail, head, shard = (), (), ()
            if m:
                tail = (got[m - 1], out_full, xs[m - 1], gain_ffn[None])
            if m < micro_count:
                head = (ones[m], qkv_full, cos_slice, sin_slice, firsts[m][:, None])
            if m < last:
                shard = (normed[m + 1],)
            elif lows:
                shard = (lows[m - last],)
            if m == 0:
                shard += (cots[0],)
            outs = forward_stage(10 + m, tail, head, shard, gathers.get(m, ()), *stage)
            if tail:
                (middle, low, mixture), outs = take(outs, 3)
                middles.append(middle)
                lows.append(low)
                mixtures.append(mixture)
            if head:
                (qkv, block), outs = take(outs, 2)
                qkvs.append(qkv)
                got.append(block)
            if shard:
                (ones if m < last else twos).append(whole(outs[0]))
            if m == 0:
                portions = [whole(outs[1])]
            if m in gathers:
                wide.append(outs[-1])
        grads, low_grads, attns, projs, sums = [], [], [], [], []
        for m in micros:
            shard = (lows[len(twos)] if len(twos) < micro_count else low_grads[len(attns)],)
            if m < last:
                shard += (cots[m + 1],)
            result, grad, low, gain_part, full, *others = middle_part(
                30 + m, twos[m], portions[m], *wide, middles[m], cots[m], gain_ffn[None], shard, sums
            )
            (twos if len(twos) < micro_count else attns).append(whole(full))
            if m < last:
                portions.append(whole(others[0]))
            sums = others[-3:]
            grads.append(grad)
            low_grads.append(low)
            gain_ffn_grad = gain_ffn_grad + gain_part[0]
            results.append(from_rows(result))
        sum_gate, sum_up, sum_down = [scatter_dp(blocks) for blocks in sums]
        for m in range(micro_count + 1):
            tail, head, ships, shard = (), (), (), ()
            if m:
                tail = (projs[m - 1], qkv_full, ones[m - 1], xs[m - 1], grads[m - 1], gain_attn[None])
            if m < micro_count:
                first = firsts[m].reshape(dp_size, 1, slice_len)
                head = (attns[m], out_full, qkvs[m], first, cos_all, sin_all)
            if len(attns) < micro_count:
                shard = (low_grads[len(attns)],)
            if m == micro_count:
                ships = (
                    *weight_grad(mixtures, (attns,), False),
                    *weight_grad(ones, (projs,), True),
                )
            outs = backward_stage(20 + m, tail, head, ships, shard, *stage)
            if tail:
                (input_grad, gain_part), outs = take(outs, 2)
                input_grads.append(from_rows(input_grad))
                gain_attn_grad = gain_attn_grad + gain_part[0]
            if head:
                (proj,), outs = take(outs, 1)
                projs.append(proj)
            if shard:
                attns.append(whole(outs[-1]))
        sum_out, sum_qkv = (jnp.sum(blocks.astype(F32), axis=0) for blocks in outs)
    else:
        qkv_full = lax.all_gather(
            jnp.concatenate([w_query, w_key, w_value], axis=1), "dp", axis=0, tiled=True
        )
        out_full = lax.all_gather(w_out, "dp", axis=1, tiled=True)
        gate_full = lax.all_gather(w_gate, "dp", axis=0, tiled=True)
        up_full = lax.all_gather(w_up, "dp", axis=0, tiled=True)
        down_full = lax.all_gather(w_down, "dp", axis=1, tiled=True)
        for micro in micros:
            local_rows = xs[micro].astype(F32)
            local_cot = cots[micro]
            factor_one = norm_factor(local_rows)
            rows_one = gather_mp(normed[micro])
            portion = gather_mp(local_cot)
            projected = dot(rows_one, qkv_full).reshape(
                mp_size, seq_count, row_count, 3, heads, HEAD
            )
            packed = to_pairs(
                jnp.concatenate(
                    [
                        rotate(projected[:, :, :, 0]).astype(BF16),
                        rotate(projected[:, :, :, 1]).astype(BF16),
                        projected[:, :, :, 2].astype(BF16),
                    ],
                    axis=-1,
                )
            )
            kv_all = lax.all_gather(packed[..., HEAD:], "dp", axis=1, tiled=True)
            first = lax.dynamic_slice_in_dim(first_all[micro], first_row, slice_len, 1)
            first = jnp.repeat(first, heads, axis=0)
            weights = sliced_scores(packed, kv_all, first, positions, scale, shift)
            attended = jnp.einsum(
                "pqk,pkd->pqd", weights.astype(BF16), kv_all[..., HEAD:], preferred_element_type=F32
            ).astype(BF16)
            mixture = from_pairs(attended).reshape(mp_size * rows_here, head_width)
            middle = local_rows + scatter_mp(dot(mixture, out_full).astype(BF16))
            factor_two = norm_factor(middle)
            rows_two = gather_mp((middle * factor_two * gain_ffn).astype(BF16))
            y, dh, activated, gate_grad, up_grad = ffn(
                rows_two, portion, gate_full, up_full, down_full
            )
            results.append(from_rows((middle + scatter_mp(y)).astype(BF16)))
            middle_term, gain_part = norm_back(middle, factor_two, gain_ffn, scatter_mp(dh))
            gain_ffn_grad = gain_ffn_grad + gain_part
            middle_grad = local_cot.astype(F32) + middle_term
            attn_portion = gather_mp(middle_grad.astype(BF16))
            mix_grad = to_pairs(dot_nt(attn_portion, out_full).astype(BF16))
            sig = sliced_scores(packed, kv_all, first, positions, scale, shift)
            prob_grad = jnp.einsum(
                "pqd,pkd->pqk", mix_grad, kv_all[..., HEAD:], preferred_element_type=F32
            )
            score_grad = (prob_grad * sig * (1.0 - sig)).astype(BF16)
            dq = jnp.einsum("pqk,pkd->pqd", score_grad, kv_all[..., :HEAD], preferred_element_type=F32)
            dk = jnp.einsum("pqk,pqd->pkd", score_grad, packed[..., :HEAD], preferred_element_type=F32)
            dv = jnp.einsum("pqk,pqd->pkd", sig.astype(BF16), mix_grad, preferred_element_type=F32)
            dkv = lax.psum_scatter(
                jnp.concatenate([dk * scale, dv], axis=-1).astype(BF16), "dp", scatter_dimension=1, tiled=True
            ).astype(F32)
            back = from_pairs(jnp.concatenate([dq * scale, dkv], axis=-1))
            back = back.reshape(mp_size, seq_count, row_count, heads, 3 * HEAD)
            proj_grad = jnp.stack(
                [
                    rotate(back[..., :HEAD], True),
                    rotate(back[..., HEAD : 2 * HEAD], True),
                    back[..., 2 * HEAD :],
                ],
                axis=3,
            ).astype(BF16).reshape(mp_size * rows_here, 3 * head_width)
            partial_grad = dot_nt(proj_grad, qkv_full)
            gain_attn_grad = gain_attn_grad + jnp.sum(partial_grad * rows_one.astype(F32), axis=0)
            input_term, _ = norm_back(
                local_rows, factor_one, gain_attn, scatter_mp(partial_grad.astype(BF16))
            )
            input_grads.append(from_rows(middle_grad + input_term))
            for held, array in zip(
                kept,
                (rows_one, proj_grad, mixture, attn_portion, rows_two, gate_grad, up_grad, activated, portion),
            ):
                held.append(array)

        def scatter_dp(lefts, rights, left_blocked):
            (blocks,) = weight_grad(lefts, (rights,), left_blocked)
            return lax.psum_scatter(blocks, "dp", scatter_dimension=0, tiled=True)[0].astype(F32)

        ones, projs, mixtures, attns, twos, gates, ups, acts, portions = kept
        sum_gate = scatter_dp(twos, gates, True)
        sum_up = scatter_dp(twos, ups, True)
        sum_down = scatter_dp(acts, portions, False)
        sum_out = scatter_dp(mixtures, attns, False)
        sum_qkv = scatter_dp(ones, projs, True)
    gain_sums = (sum_all(gain_attn_grad / gain_attn), sum_all(gain_ffn_grad))
    return (
        jnp.stack(results),
        jnp.stack(input_grads),
        gain_sums[0],
        sum_qkv[:, :head_width],
        sum_qkv[:, head_width : 2 * head_width],
        sum_qkv[:, 2 * head_width :],
        sum_out,
        gain_sums[1],
        sum_gate,
        sum_up,
        sum_down,
    )


def solution(mesh):
    tokens = P(None, ("dp", "mp"), None, None)
    column = P("dp", "mp")
    row = P("mp", "dp")
    return jax.shard_map(
        per_device,
        mesh=mesh,
        in_specs=(
            tokens, tokens, P(), P(), column, column, column, row, P(), column, column, row,
        ),
        out_specs=(
            tokens, tokens, P(), column, column, column, row, P(), column, column, row,
        ),
        check_vma=False,
    )
```

```python
import functools
import math

import jax
import jax.numpy as jnp
import numpy as np
from jax import lax
from jax.experimental import pallas as pl
from jax.experimental.pallas import tpu as pltpu
from jax.sharding import PartitionSpec as P

HEAD = 128
epsilon = 1e-05
rope_base = 10000.0
F32 = jnp.float32
BF16 = jnp.bfloat16


def full_tables(total):
    half_size = HEAD // 2
    exponents = -(np.arange(half_size, dtype=np.float32) * np.float32(2.0 / HEAD))
    inverse = np.power(np.float32(rope_base), exponents)
    angles = np.arange(total, dtype=np.float32)[:, None] * inverse[None, :]
    cosine, sine = np.cos(angles), np.sin(angles)
    return (
        jnp.asarray(np.concatenate([cosine, cosine], axis=-1)),
        jnp.asarray(np.concatenate([-sine, sine], axis=-1)),
    )


def swap_halves(values):
    half_size = HEAD // 2
    return jnp.concatenate([values[..., half_size:], values[..., :half_size]], axis=-1)


def dot(left, right):
    return jnp.dot(left, right, preferred_element_type=F32)


def dot_tn(left, right):
    return lax.dot_general(left, right, (((0,), (0,)), ((), ())), preferred_element_type=F32)


def dot_nt(left, right):
    return lax.dot_general(left, right, (((1,), (1,)), ((), ())), preferred_element_type=F32)


def norm_factor(values):
    return lax.rsqrt(jnp.mean(values * values, axis=-1, keepdims=True) + epsilon)


def norm_back(values, factor, gain, incoming):
    scaled = incoming * gain
    gain_term = jnp.sum(incoming * values * factor, axis=0)
    input_term = factor * scaled - values * factor**3 * jnp.mean(
        scaled * values, axis=-1, keepdims=True
    )
    return (input_term, gain_term)


def sigmoid_of(raw, scale, shift):
    return 1.0 / (1.0 + jnp.exp(shift - raw * scale))


def split_cores(core, values, rows_here):
    shaped = values.reshape(-1, 2, rows_here, values.shape[-1])
    first, second = shaped[:, 0], shaped[:, 1]
    is_first = core == 0
    return jnp.where(is_first, first, second), jnp.where(is_first, second, first)

MESH = pl.DeviceIdType.MESH


class Spot:
    def __init__(self):
        self.dp, self.mp = lax.axis_index("dp"), lax.axis_index("mp")
        self.dp_size, self.mp_size = lax.axis_size("dp"), lax.axis_size("mp")
        self.places = self.mp_size // 2
        self.place, self.core = lax.div(self.mp, 2), lax.rem(self.mp, 2)
        self.sibling = (self.dp, self.mp + 1 - 2 * self.core)
        self.right = (self.dp, self.mp + 2)
        self.left = (self.dp, self.mp - 2)
        self.has_right = self.place < self.places - 1
        self.has_left = self.place > 0

    def peer(self, step):
        return lax.rem(self.dp + step, self.dp_size)

    def enter(self, with_dp, with_mp):
        barrier = pltpu.get_barrier_semaphore()
        count = 0

        def greet(device):
            pl.semaphore_signal(barrier, inc=1, device_id=device, device_id_type=MESH)

        if with_mp:
            greet(self.sibling)
            pl.when(self.has_right)(lambda: greet(self.right))
            pl.when(self.has_left)(lambda: greet(self.left))
            count += 1 + self.has_right.astype(jnp.int32) + self.has_left.astype(jnp.int32)
        if with_dp:
            for step in range(1, self.dp_size):
                greet((self.peer(step), self.mp))
            count += self.dp_size - 1
        pl.semaphore_wait(barrier, count)


class Swap:
    def __init__(self, spot, source, target, send, receive):
        self.spot, self.source, self.target = spot, source, target
        self.send, self.receive = send, receive
        self.copies = [self.copy(step) for step in range(1, spot.dp_size)]

    def copy(self, step):
        spot = self.spot
        return pltpu.make_async_remote_copy(
            src_ref=self.source.at[spot.peer(step)],
            dst_ref=self.target.at[spot.dp],
            send_sem=self.send.at[step],
            recv_sem=self.receive.at[step],
            device_id=(spot.peer(step), spot.mp),
            device_id_type=MESH,
        )

    def start(self):
        for copy in self.copies:
            copy.start()
        self.keep()

    def keep(self):
        self.target[self.spot.dp] = self.source[self.spot.dp]

    def wait(self):
        for copy in self.copies:
            copy.wait()


class Gather:
    def __init__(self, spot, shard, window, sems):
        self.local = pltpu.make_async_copy(shard, window(spot.dp), sems.at[0, 0])
        self.copies = [
            pltpu.make_async_remote_copy(
                src_ref=shard,
                dst_ref=window(spot.dp),
                send_sem=sems.at[0, step],
                recv_sem=sems.at[1, step],
                device_id=(spot.peer(step), spot.mp),
                device_id_type=MESH,
            )
            for step in range(1, spot.dp_size)
        ]

    def start(self):
        for copy in self.copies:
            copy.start()
        self.local.start()

    def go_on(self):
        pass

    def wait(self):
        for copy in self.copies:
            copy.wait()
        self.local.wait()


def gather_of(spot, *arguments):
    return (RingGather if spot.dp_size == 4 else Gather)(spot, *arguments)


class RingGather:
    def __init__(self, spot, shard, window, sems):
        side = spot.dp + 1 - 2 * lax.rem(spot.dp, 2)
        across = spot.dp + 2 - 4 * lax.div(spot.dp, 2)

        def copy(source, index, kind, to, half=None):
            return pltpu.make_async_remote_copy(
                src_ref=source,
                dst_ref=window(index, half),
                send_sem=sems.at[0, kind],
                recv_sem=sems.at[1, kind],
                device_id=(to, spot.mp),
                device_id_type=MESH,
            )

        self.local = pltpu.make_async_copy(shard, window(spot.dp), sems.at[0, 4])
        self.to_side = copy(shard, spot.dp, 0, side)
        self.to_across = copy(shard, spot.dp, 1, across)
        self.on_across = copy(window(side, 0), side, 2, across, 0)
        self.on_side = copy(window(across, 1), across, 3, side, 1)

    def start(self):
        self.to_side.start()
        self.to_across.start()
        self.local.start()

    def go_on(self):
        self.to_side.wait_recv()
        self.on_across.start()
        self.to_across.wait_recv()
        self.on_side.start()

    def wait(self):
        self.to_side.wait_send()
        self.to_across.wait_send()
        self.on_across.wait()
        self.on_side.wait()
        self.local.wait()


class Spread:
    def __init__(self, spot, shard, full, sems):
        self.spot, self.shard, self.full, self.sems = spot, shard, full, sems
        self.local = pltpu.make_async_copy(shard, full.at[spot.mp], sems.at[6, 0])

    def copy(self, kind, device, p, source=None, core=None):
        at = 2 * p + (self.spot.core if core is None else core)
        return pltpu.make_async_remote_copy(
            src_ref=self.full.at[at] if source is None else source,
            dst_ref=self.full.at[at],
            send_sem=self.sems.at[kind, p],
            recv_sem=self.sems.at[kind + 1, p],
            device_id=device,
            device_id_type=MESH,
        )

    def rightward(self, p, source=None):
        return self.copy(0, self.spot.right, p, source)

    def leftward(self, p, source=None):
        return self.copy(2, self.spot.left, p, source)

    def across(self, p, source=None):
        return self.copy(4, self.spot.sibling, p, source)

    def begin(self):
        spot = self.spot
        pl.when(spot.has_right)(lambda: self.rightward(spot.place, self.shard).start())
        pl.when(spot.has_left)(lambda: self.leftward(spot.place, self.shard).start())
        self.across(spot.place, self.shard).start()
        self.local.start()

    def go_on(self, hop):
        spot = self.spot

        @pl.when(spot.place >= hop)
        def _():
            p = spot.place - hop
            self.rightward(p).wait_recv()
            pl.when(spot.has_right)(lambda: self.rightward(p).start())
            self.across(p).start()

        @pl.when(spot.place + hop < spot.places)
        def _():
            p = spot.place + hop
            self.leftward(p).wait_recv()
            pl.when(spot.has_left)(lambda: self.leftward(p).start())
            self.across(p).start()

    def finish(self):
        spot = self.spot
        for p in range(spot.places):
            self.copy(4, spot.sibling, p, core=1 - spot.core).wait_recv()
            self.across(p).wait_send()
            pl.when(spot.has_right & (spot.place >= p))(lambda: self.rightward(p).wait_send())
            pl.when(spot.has_left & (spot.place <= p))(lambda: self.leftward(p).wait_send())
        self.local.wait()


def spread_scratch(places):
    return [pltpu.SemaphoreType.DMA((7, places))]


class Ship(Swap):
    def __init__(self, spot, source, target, sems):
        super().__init__(spot, source, target, sems.at[0], sems.at[1])
        self.local = pltpu.make_async_copy(source.at[spot.dp], target.at[spot.dp], sems.at[0, 0])

    def start(self):
        for copy in self.copies:
            copy.start()
        self.local.start()

    def wait(self):
        super().wait()
        self.local.wait()


def window_of(full, axis, step, column=0, columns=None):
    def window(index, half=None):
        rows = step if axis == 0 else full.shape[0]
        first, count = (0, rows) if half is None else (half * (rows // 2), rows // 2)
        if axis == 1:
            return full.at[
                pl.ds(first, count), pl.ds(pl.multiple_of(index * step, step), step)
            ]
        along = pl.ds(pl.multiple_of(index * step + first, count), count)
        return full.at[along, pl.ds(column, full.shape[1] if columns is None else columns)]

    return window


def swap_scratch(size, *block):
    return [
        pltpu.VMEM((size, *block), BF16),
        pltpu.VMEM((size, *block), BF16),
        pltpu.SemaphoreType.DMA((size,)),
        pltpu.SemaphoreType.DMA((size,)),
    ]


def far_first(places):
    orders = []
    for place in range(places):
        right, left, order = list(range(places - 1, place, -1)), list(range(place)), []
        while right or left:
            order += right[:1] + left[:1]
            right, left = right[1:], left[1:]
        orders.append(order + [place])
    return orders


class Sum:
    def __init__(self, spot, mine, out, from_sibling, passed, sems):
        self.spot = spot
        self.mine, self.out = mine, out
        self.from_sibling, self.passed = from_sibling, passed
        self.sems = sems
        self.orders = far_first(spot.places)

    def copy(self, source, target, kind, t, device, to=None):
        return pltpu.make_async_remote_copy(
            src_ref=source.at[t],
            dst_ref=target.at[t if to is None else to],
            send_sem=self.sems.at[kind, t],
            recv_sem=self.sems.at[kind + 1, t],
            device_id=device,
            device_id_type=MESH,
        )

    def sibling(self, t):
        return self.copy(self.out, self.from_sibling, 0, t, self.spot.sibling)

    def rightward(self, t):
        return self.copy(self.mine, self.passed, 2, t, self.spot.right)

    def leftward(self, t, place):
        to = jnp.where(t == place, self.spot.places, t)
        return self.copy(self.mine, self.passed, 4, t, self.spot.left, to)

    def leftward_out(self, t):
        return self.leftward(t, self.spot.place - 1)

    def leftward_in(self, t):
        return self.leftward(t, self.spot.place)

    def term(self, s):
        chosen = 0
        for place, order in enumerate(self.orders):
            for at, t in enumerate(order):
                if t:
                    chosen = chosen + jnp.where((self.spot.place == place) & (s == at), t, 0)
        return chosen

    def add(self, t, arrived):
        self.mine[t] = (self.mine[t].astype(F32) + arrived.astype(F32)).astype(BF16)

    def absorb(self, t):
        self.sibling(t).wait_recv()
        self.add(t, self.from_sibling[t])

    def begin(self, s):
        spot = self.spot

        @pl.when((spot.place == 0) & (s < spot.places - 1))
        def _():
            t = spot.places - 1 - s
            self.absorb(t)
            self.rightward(t).start()

        @pl.when((spot.place == spot.places - 1) & (s < spot.places - 1))
        def _():
            self.absorb(s)
            self.leftward_out(s).start()

    def go_on(self, hop):
        spot = self.spot
        last = spot.places - 1

        @pl.when((spot.place > 0) & (spot.place <= hop))
        def _():
            t = last + spot.place - hop
            self.absorb(t)
            self.rightward(t).wait_recv()
            self.add(t, self.passed[t])
            self.rightward(t).start()

        @pl.when((spot.place < last) & (last - spot.place <= hop))
        def _():
            t = hop - last + spot.place
            self.absorb(t)
            self.leftward_in(t).wait_recv()
            self.add(t, self.passed[t])
            self.leftward_out(t).start()

    def finish(self):
        spot = self.spot
        t = spot.place
        self.absorb(t)

        @pl.when(spot.has_left)
        def _():
            self.rightward(t).wait_recv()
            self.add(t, self.passed[t])

        @pl.when(spot.has_right)
        def _():
            self.leftward_in(t).wait_recv()
            self.add(t, self.passed[spot.places])

        for t in range(spot.places):
            self.sibling(t).wait_send()
            pl.when(spot.place < t)(lambda: self.rightward(t).wait_send())
            pl.when(spot.place > t)(lambda: self.leftward_out(t).wait_send())
        return self.mine[spot.place].astype(F32)


def sum_scratch(places, rows_here, width):
    return [
        *[pltpu.VMEM((places, rows_here, width), BF16)] * 3,
        pltpu.VMEM((places + 1, rows_here, width), BF16),
        pltpu.SemaphoreType.DMA((6, places)),
    ]


def as_column(row):
    return jnp.broadcast_to(row, (HEAD, row.shape[1])).T[:, 0:1]


def attend_blocks(qkv, ids_ref, out, scale, shift):
    count, block = out.shape[:2]
    row_at = lax.broadcasted_iota(jnp.int32, (block, block), 0)
    col_at = lax.broadcasted_iota(jnp.int32, (block, block), 1)

    @pl.loop(0, count)
    def _(i):
        queries = qkv[i, :, 0:HEAD]
        ids = as_column(ids_ref[i])

        def add_block(j, acc, diagonal=False):
            sig = sigmoid_of(dot_nt(queries, qkv[j, :, HEAD : 2 * HEAD]), scale, shift)
            visible = ids == ids_ref[j]
            if diagonal:
                visible = visible & (col_at <= row_at)
            weights = jnp.where(visible, sig, 0.0).astype(BF16)
            return acc + dot(weights, qkv[j, :, 2 * HEAD :])

        acc = add_block(i, jnp.zeros((block, HEAD), F32), True)
        out[i] = lax.fori_loop(0, i, add_block, acc).astype(BF16)


def attend_back_blocks(
    spot, qkv, grad, ids_ref, cos_ref, sin_ref, out_q, out_kv, dq, made, scale, shift
):
    count, block = grad.shape[:2]
    col_at = lax.broadcasted_iota(jnp.int32, (block, block), 0)
    row_at = lax.broadcasted_iota(jnp.int32, (block, block), 1)
    dq[...] = jnp.zeros_like(dq)

    def unrotate(values, i):
        rows = pl.ds(pl.multiple_of(i * block, block), block)
        swapped = pltpu.roll(values, HEAD // 2, 1)
        return (values * cos_ref[rows, :] - swapped * sin_ref[rows, :]).astype(BF16)

    @pl.loop(0, count)
    def _(at):
        j = spot.peer(at + 1)
        keys = qkv[j, :, HEAD : 2 * HEAD]
        values = qkv[j, :, 2 * HEAD :]
        keys_t = keys.T
        ids = as_column(ids_ref[j])

        def add_block(i, sums, diagonal=False):
            dk, dv = sums
            queries, grads = qkv[i, :, 0:HEAD], grad[i]
            sig = sigmoid_of(dot_nt(keys, queries), scale, shift)
            visible = ids == ids_ref[i]
            if diagonal:
                visible = visible & (col_at <= row_at)
            sig = jnp.where(visible, sig, 0.0)
            prob_grad = dot_nt(values, grads)
            score_grad = (prob_grad * sig * (1.0 - sig)).astype(BF16)
            dq[i] += dot(keys_t, score_grad)
            return dk + dot(score_grad, queries), dv + dot(sig.astype(BF16), grads)

        zero = jnp.zeros((block, HEAD), F32)
        dk, dv = lax.fori_loop(j + 1, count, add_block, add_block(j, (zero, zero), True))
        out_kv[j, :, 0:HEAD] = unrotate(dk * scale, j)
        out_kv[j, :, HEAD:] = dv.astype(BF16)
        pl.when(at < count - 1)(lambda: made(at + 1))

    @pl.loop(0, count)
    def _(i):
        out_q[i] = unrotate(dq[i].T * scale, i)


def take(refs, count):
    return refs[:count], refs[count:]


def put_norm(x_ref, gain_ref, out_ref):
    x = x_ref[...].astype(F32)
    out_ref[...] = (x * norm_factor(x) * gain_ref[...]).astype(BF16)


def begin_kernel(
    x_ref, gain_ref, query, key, value, out, qkv_full, out_full, first_full,
    normed, sems, spread_sems,
):
    spot = Spot()
    spot.enter(True, True)
    rows, columns = query.shape
    jobs = [
        (shard, window_of(qkv_full, 0, rows, i * columns, columns))
        for i, shard in enumerate((query, key, value))
    ]
    jobs.append((out, window_of(out_full, 1, out.shape[1])))
    gathers = [
        gather_of(spot, shard, window, sems.at[i]) for i, (shard, window) in enumerate(jobs)
    ]
    for gather in gathers:
        gather.start()
    put_norm(x_ref, gain_ref, normed)
    spread = Spread(spot, normed, first_full, spread_sems)
    spread.begin()
    spread.go_on(1)
    for gather in gathers:
        gather.go_on()
    for hop in range(2, spot.places):
        spread.go_on(hop)
    for gather in gathers:
        gather.wait()
    spread.finish()


def forward_kernel(tail, head, norms, spreads, gather_axis, heads, toks, scale, shift, *refs):
    gathers = gather_axis is not None
    tail_in, refs = take(refs, 4 * tail)
    head_in, refs = take(refs, 5 * head)
    norm_in, refs = take(refs, 2 * norms)
    spread_in, refs = take(refs, spreads - norms)
    gather_in, refs = take(refs, gathers)
    tail_out, refs = take(refs, 3 * tail)
    head_out, refs = take(refs, 2 * head)
    spread_out, refs = take(refs, spreads)
    gather_out, refs = take(refs, gathers)
    sum_refs, refs = take(refs, 5 * tail)
    head_refs, refs = take(refs, 9 * head)
    normed, refs = take(refs, norms)
    spot = Spot()
    spot.enter(head or gathers, tail or spreads)
    if norms:
        put_norm(*norm_in, *normed)
        spread_in = (*normed, *spread_in)
    moving = [Spread(spot, *refs) for refs in zip(spread_in, spread_out, refs)]
    for spread in moving:
        spread.begin()
    if gathers:
        window = window_of(gather_out[0], gather_axis, gather_in[0].shape[gather_axis])
        gather = gather_of(spot, gather_in[0], window, refs[-1])

    if tail:
        got, out_weight, x_ref, gain_ref = tail_in
        middle_ref, normed_ref, mix_ref = tail_out
        pairs = got.shape[0]
        owner_rows = toks * (pairs // heads)
        for o in range(mix_ref.shape[0] // owner_rows):
            for p in range(pairs):
                s, h = p // heads, p % heads
                mix_ref[pl.ds(o * owner_rows + s * toks, toks), h * HEAD : (h + 1) * HEAD] = got[
                    p, pl.ds(o * toks, toks), :
                ]
        summed = Sum(spot, *sum_refs)
        chip_rows = 2 * owner_rows

        @pl.loop(0, spot.places)
        def _(s):
            t = summed.term(s)
            rows = pl.ds(pl.multiple_of(t * chip_rows, chip_rows), chip_rows)
            value = dot(mix_ref[rows, :], out_weight[...]).astype(BF16)
            keep, send = split_cores(spot.core, value, owner_rows)
            summed.mine[t] = keep[0]
            summed.out[t] = send[0]
            summed.sibling(t).start()

        @pl.loop(0, spot.places - 1)
        def _(s):
            summed.begin(s)

    if head:
        rows_ref, weight_ref, cos_ref, sin_ref, ids_ref = head_in
        qkv_ref, got_ref = head_out
        made, paired, qkv, qkv_send, qkv_recv, part, got, part_send, part_recv = head_refs
        pairs = paired.shape[0]
        owner_rows = toks * (pairs // heads)
        step = made.shape[0]

        @pl.loop(0, rows_ref.shape[0] // step)
        def _(i):
            rows = pl.ds(pl.multiple_of(i * step, step), step)
            made[...] = dot(rows_ref[rows, :], weight_ref[...])
            for j in range(step // owner_rows):
                to = pl.ds(pl.multiple_of((i * (step // owner_rows) + j) * toks, toks), toks)
                cosine, sine = cos_ref[to, :], sin_ref[to, :]
                for p in range(pairs):
                    s, h = p // heads, p % heads
                    here = pl.ds(j * owner_rows + s * toks, toks)
                    for kind in range(3):
                        piece = made[here, pl.ds((kind * heads + h) * HEAD, HEAD)]
                        if kind < 2:
                            piece = piece * cosine + pltpu.roll(piece, HEAD // 2, 1) * sine
                        paired[p, to, kind * HEAD : (kind + 1) * HEAD] = piece.astype(BF16)

        swap = Swap(spot, paired, qkv, qkv_send, qkv_recv)
        swap.start()
    if gathers:
        gather.start()
    for spread in moving:
        spread.go_on(1)
    if tail and spot.places > 2:
        summed.go_on(1)
    if head:
        swap.wait()
    for hop in range(2, spot.places - 1):
        for spread in moving:
            spread.go_on(hop)
        if tail:
            summed.go_on(hop)
    if gathers:
        gather.go_on()
    if head:
        attend_blocks(qkv, ids_ref, part, scale, shift)
        swap = Swap(spot, part, got, part_send, part_recv)
        swap.start()
        qkv_ref[...] = qkv[...]
        swap.wait()
        got_ref[...] = got[...]
    for spread in moving:
        if spot.places > 2:
            spread.go_on(spot.places - 1)
    if tail:
        middle = x_ref[...].astype(F32) + summed.finish()
        middle_ref[...] = middle
        normed_ref[...] = (middle * norm_factor(middle) * gain_ref[...]).astype(BF16)
    for spread in moving:
        spread.finish()
    if gathers:
        gather.wait()


def middle_kernel(
    first, spreads, owner_rows,
    rows_ref, cot_ref, gate_ref, up_ref, down_ref, middle_ref, local_cot_ref, gain_ref,
    *refs,
):
    shards, refs = take(refs, spreads)
    before, refs = take(refs, 0 if first else 3)
    (result_ref, grad_ref, low_ref, gain_grad_ref), refs = take(refs, 4)
    fulls, refs = take(refs, spreads)
    after, refs = take(refs, 3)
    (act_ref, dgate_ref, dup_ref, turned, new_rows, new_cols, old_rows, old_cols), refs = take(refs, 8)
    (wide_sems,), refs = take(refs, 1)
    sum_refs, refs = take(refs, 10)
    spot = Spot()
    spot.enter(False, True)
    summed, summed_y = Sum(spot, *sum_refs[:5]), Sum(spot, *sum_refs[5:])
    moving = [Spread(spot, *refs) for refs in zip(shards, fulls, refs)]
    for spread in moving:
        spread.begin()
    hidden, width = gate_ref.shape[1], rows_ref.shape[1]
    chip_rows = 2 * owner_rows
    tile = min(256, hidden)
    blocks = after[0].shape[0]
    block = width // blocks
    new = (new_rows.at[0], new_rows.at[1], new_cols)
    old = (old_rows.at[0], old_rows.at[1], old_cols)

    def load(g, e):
        return pltpu.make_async_copy(before[g].at[e], old[g], wide_sems.at[0, g])

    def store(g, e):
        return pltpu.make_async_copy(new[g], after[g].at[e], wide_sems.at[1, g])

    if not first:
        for g in range(3):
            load(g, 0).start()

    @pl.loop(0, spot.places)
    def _(s):
        place = summed.term(s)
        rows = pl.ds(pl.multiple_of(place * chip_rows, chip_rows), chip_rows)

        @pl.loop(0, hidden // tile)
        def _(t):
            cols = pl.ds(pl.multiple_of(t * tile, tile), tile)
            gate = dot(rows_ref[rows, :], gate_ref[:, cols])
            up = dot(rows_ref[rows, :], up_ref[:, cols])
            sig = jax.nn.sigmoid(gate)
            silu = gate * sig
            act_ref[rows, cols] = (silu * up).astype(BF16)
            grad = dot_nt(cot_ref[rows, :], down_ref[cols, :])
            dgate_ref[rows, cols] = (grad * up * sig * (1.0 + gate * (1.0 - sig))).astype(BF16)
            dup_ref[rows, cols] = (grad * silu).astype(BF16)

        @pl.when(s > 0)
        def _():
            summed.begin(s - 1)
            summed_y.begin(s - 1)

        for hop in range(1, spot.places - 1):

            @pl.when(s == hop + 1)
            def _():
                for spread in moving:
                    spread.go_on(hop)
                summed.go_on(hop)
                summed_y.go_on(hop)

        @pl.loop(0, width // 256)
        def _(t):
            cols = pl.ds(pl.multiple_of(t * 256, 256), 256)
            value = dot(act_ref[rows, :], down_ref[:, cols])
            keep, send = split_cores(spot.core, value.astype(BF16), owner_rows)
            summed_y.mine[place, :, cols] = keep[0]
            summed_y.out[place, :, cols] = send[0]
            value = dot_nt(dgate_ref[rows, :], gate_ref[cols, :])
            value += dot_nt(dup_ref[rows, :], up_ref[cols, :])
            keep, send = split_cores(spot.core, value.astype(BF16), owner_rows)
            summed.mine[place, :, cols] = keep[0]
            summed.out[place, :, cols] = send[0]

        summed.sibling(place).start()
        summed_y.sibling(place).start()

    def make(g, e, left, right, right_at, columns):
        pl.when(e > 0)(lambda: store(g, e - 1).wait())
        if not first:
            load(g, e).wait()
        step = math.gcd(columns, 256)

        @pl.loop(0, columns // step)
        def _(t):
            cols = pl.ds(pl.multiple_of(t * step, step), step)
            total = dot(left[...], right[:, pl.ds(pl.multiple_of(right_at + t * step, step), step)])
            if not first:
                total += old[g][:, cols].astype(F32)
            new[g][:, cols] = total.astype(BF16)

        if not first:
            pl.when(e < blocks - 1)(lambda: load(g, e + 1).start())
        store(g, e).start()

    @pl.loop(0, blocks)
    def _(e):
        left = turned.at[pl.ds(0, block), :]
        left[...] = rows_ref[:, pl.ds(pl.multiple_of(e * block, block), block)].T
        make(0, e, left, dgate_ref, 0, hidden)
        make(1, e, left, dup_ref, 0, hidden)

    for spread in moving:
        spread.go_on(spot.places - 1)
    left = turned.at[pl.ds(0, hidden), :]
    left[...] = act_ref[...].T

    @pl.loop(0, blocks)
    def _(e):
        make(2, e, left, cot_ref, e * block, block)

    incoming = summed.finish()
    middle = middle_ref[...]
    term, gain_grad = norm_back(middle, norm_factor(middle), gain_ref[...], incoming)
    gain_grad_ref[...] = gain_grad[None]
    grad = local_cot_ref[...].astype(F32) + term
    grad_ref[...] = grad
    low_ref[...] = grad.astype(BF16)
    result_ref[...] = (middle + summed_y.finish()).astype(BF16)
    for spread in moving:
        spread.finish()
    for g in range(3):
        store(g, blocks - 1).wait()


def add_grads(blocks, left, right, turned, before, after):
    size, rows, columns = after.shape

    @pl.loop(0, size)
    def _(e):
        if rows < left.shape[1]:
            turned[...] = left[:, pl.ds(pl.multiple_of(e * rows, rows), rows)].T
            total = dot(turned[...], right[...])
        else:

            @pl.when(e == 0)
            def _():
                turned[...] = left[...].T

            cut = pl.ds(pl.multiple_of(e * columns, columns), columns)
            total = dot(turned[...], right[:, cut])
        if before is not None:
            total += before[e].astype(F32)
        after[e] = total.astype(BF16)


def backward_kernel(
    tail, head, last, old_tail, old_head, spreads, heads, toks, scale, shift, *refs
):
    tail_in, refs = take(refs, 6 * tail)
    old_qkv, refs = take(refs, old_tail)
    head_in, refs = take(refs, 7 * head)
    old_out, refs = take(refs, old_head)
    last_in, refs = take(refs, 2 * last)
    spread_in, refs = take(refs, spreads)
    tail_out, refs = take(refs, (1 if last else 3) * tail)
    head_out, refs = take(refs, 2 * head)
    last_out, refs = take(refs, 3 * last)
    spread_out, refs = take(refs, spreads)
    tail_refs, refs = take(refs, 7 * tail)
    head_refs, refs = take(refs, 14 * head)
    last_refs, refs = take(refs, 8 * last)
    spot = Spot()
    spot.enter(head or last, tail or spreads)
    moving = [Spread(spot, *refs) for refs in zip(spread_in, spread_out, refs)]
    for spread in moving:
        spread.begin()
    if last:
        out_blocks, gains = last_in
        out_target, qkv_target, gain_sum = last_out
        new_qkv, own_gain, all_dp, dp_sum, all_mp, ship_sems, gain_sems, gain_spread_sems = last_refs
        ship_out = Ship(spot, out_blocks, out_target, ship_sems.at[0])
        ship_out.start()
    if head:
        rows_ref, out_weight_ref, qkv, ids_ref, cos_ref, sin_ref, mix_ref = head_in
        head_proj_ref, new_out = head_out
        part, got, part_send, part_recv = head_refs[:4]
        made_q, got_q, q_send, q_recv, made_kv, got_kv, kv_send, kv_recv, dq, mix_turned = head_refs[4:]
        pairs = part.shape[0]
        owner_rows = toks * (pairs // heads)
        total = rows_ref.shape[0]
        step = min(512, total)

        @pl.loop(0, total // step)
        def _(i):
            rows = pl.ds(pl.multiple_of(i * step, step), step)
            made = dot_nt(rows_ref[rows, :], out_weight_ref[...]).astype(BF16)
            for j in range(step // owner_rows):
                to = pl.ds(pl.multiple_of((i * (step // owner_rows) + j) * toks, toks), toks)
                for p in range(pairs):
                    s, h = p // heads, p % heads
                    start = j * owner_rows + s * toks
                    part[p, to, :] = made[start : start + toks, h * HEAD : (h + 1) * HEAD]

        swap = Swap(spot, part, got, part_send, part_recv)
        swap.start()

    if tail:
        proj_ref, weight_ref, rows_one_ref, x_ref, grad_ref, gain_ref = tail_in
        result_ref = tail_out[0]
        sum_refs, (turned, gain_acc) = take(tail_refs, 5)
        if not last:
            new_qkv, gain_acc = tail_out[1:]
        owner_rows = x_ref.shape[0]
        summed = Sum(spot, *sum_refs)
        chip_rows = 2 * owner_rows
        gain_acc[...] = jnp.zeros_like(gain_acc)

        @pl.loop(0, spot.places)
        def _(s):
            t = summed.term(s)
            rows = pl.ds(pl.multiple_of(t * chip_rows, chip_rows), chip_rows)
            value = dot_nt(proj_ref[rows, :], weight_ref[...])
            gain_acc[...] += jnp.sum(
                value * rows_one_ref[rows, :].astype(F32), axis=0, keepdims=True
            )
            keep, send = split_cores(spot.core, value.astype(BF16), owner_rows)
            summed.mine[t] = keep[0]
            summed.out[t] = send[0]
            summed.sibling(t).start()
            pl.when(s > 0)(lambda: summed.begin(s - 1))

        if last:
            own_gain[...] = gains[...]
            own_gain[1:2, :] += gain_acc[...]
            gain_dp = Gather(spot, own_gain, lambda index: all_dp.at[index], gain_sems)
            gain_dp.start()
        before = old_qkv[0] if old_tail else None

    if last:
        add_grads(spot.dp_size, rows_one_ref, proj_ref, turned, before, new_qkv)
        ship_qkv = Ship(spot, new_qkv, qkv_target, ship_sems.at[1])
        ship_qkv.start()
        gain_dp.wait()
        dp_sum[...] = jnp.sum(all_dp[...], axis=0)
        gain_mp = Spread(spot, dp_sum, all_mp, gain_spread_sems)
        gain_mp.begin()
        gain_mp.go_on(1)
    if head:
        add_grads(
            spot.dp_size, mix_ref, rows_ref, mix_turned, old_out[0] if old_head else None, new_out
        )
        swap.wait()
    for spread in moving:
        spread.go_on(1)
    if tail and spot.places > 2:
        summed.go_on(1)
    if head:
        swap_kv = Swap(spot, made_kv, got_kv, kv_send, kv_recv)
        attend_back_blocks(
            spot, qkv, got, ids_ref, cos_ref, sin_ref, made_q, made_kv, dq,
            lambda step: swap_kv.copy(step).start(), scale, shift,
        )
        swap_kv.keep()
        swap = Swap(spot, made_q, got_q, q_send, q_recv)
        swap.start()
    for hop in range(2, spot.places - 1):
        if last:
            gain_mp.go_on(hop)
        for spread in moving:
            spread.go_on(hop)
        if tail:
            summed.go_on(hop)
    if tail and not last:
        add_grads(spot.dp_size, rows_one_ref, proj_ref, turned, before, new_qkv)
    if head:
        swap_kv.wait()
        swap.wait()
        for o in range(total // owner_rows):
            for p in range(pairs):
                s, h = p // heads, p % heads
                here, there = pl.ds(o * owner_rows + s * toks, toks), pl.ds(o * toks, toks)
                for kind in range(3):
                    piece = (
                        got_kv[p, there, (kind - 1) * HEAD : kind * HEAD] if kind else got_q[p, there, :]
                    )
                    head_proj_ref[
                        here, (kind * heads + h) * HEAD : (kind * heads + h + 1) * HEAD
                    ] = piece
    if spot.places > 2:
        for spread in moving:
            spread.go_on(spot.places - 1)
        if last:
            gain_mp.go_on(spot.places - 1)
    if tail:
        incoming = summed.finish()
        x = x_ref[...].astype(F32)
        term, _ = norm_back(x, norm_factor(x), gain_ref[...], incoming)
        result_ref[...] = grad_ref[...] + term
    if last:
        gain_mp.finish()
        gain_sum[...] = jnp.sum(all_mp[...], axis=0)
        ship_out.wait()
        ship_qkv.wait()
    for spread in moving:
        spread.finish()


def ffn_kernel(
    rows_ref, cot_ref, gate_ref, up_ref, down_ref, y_ref, dh_ref, act_ref, dgate_ref, dup_ref
):
    hidden = gate_ref.shape[1]
    width = rows_ref.shape[1]
    tile = min(256, hidden)

    @pl.loop(0, hidden // tile)
    def _(t):
        cols = pl.ds(pl.multiple_of(t * tile, tile), tile)
        gate = dot(rows_ref[...], gate_ref[:, cols])
        up = dot(rows_ref[...], up_ref[:, cols])
        sig = jax.nn.sigmoid(gate)
        silu = gate * sig
        act_ref[:, cols] = (silu * up).astype(BF16)
        grad = dot_nt(cot_ref[...], down_ref[cols, :])
        dgate_ref[:, cols] = (grad * up * sig * (1.0 + gate * (1.0 - sig))).astype(BF16)
        dup_ref[:, cols] = (grad * silu).astype(BF16)

    @pl.loop(0, width // 256)
    def _(t):
        cols = pl.ds(pl.multiple_of(t * 256, 256), 256)
        y_ref[:, cols] = dot(act_ref[...], down_ref[:, cols]).astype(BF16)
        dh = dot_nt(dgate_ref[...], gate_ref[cols, :]) + dot_nt(dup_ref[...], up_ref[cols, :])
        dh_ref[:, cols] = dh.astype(BF16)


def grad_kernel(count, groups, left_blocked, *refs):
    lefts, refs = take(refs, count)
    rights, refs = take(refs, count * groups)
    out_refs, (turned,) = take(refs, groups)
    rows = lefts[0].shape[0]

    def turn():
        for m, left in enumerate(lefts):
            turned[:, m * rows : (m + 1) * rows] = left[...].T

    if left_blocked:
        turn()
    else:
        pl.when(pl.program_id(0) == 0)(turn)
    tile = math.gcd(out_refs[0].shape[2], 256)
    for g, out_ref in enumerate(out_refs):
        own = rights[g * count : (g + 1) * count]

        @pl.loop(0, out_ref.shape[2] // tile)
        def _(t):
            cols = pl.ds(pl.multiple_of(t * tile, tile), tile)
            total = dot(turned[:, :rows], own[0][:, cols])
            for m in range(1, count):
                total += dot(turned[:, m * rows : (m + 1) * rows], own[m][:, cols])
            out_ref[0, :, cols] = total.astype(BF16)


VMEM = pl.BlockSpec(memory_space=pltpu.VMEM)
ANY = pl.BlockSpec(memory_space=pl.ANY)


def cost(flops, nbytes):
    return pl.CostEstimate(flops=flops, bytes_accessed=nbytes, transcendentals=0)


def limits(mebibytes):
    return pltpu.CompilerParams(vmem_limit_bytes=mebibytes * 2**20)


def shape(*dims, dtype=BF16):
    return jax.ShapeDtypeStruct(dims, dtype)


def comm_params(collective_id, mebibytes):
    return pltpu.CompilerParams(
        collective_id=collective_id, has_side_effects=True, vmem_limit_bytes=mebibytes * 2**20
    )


def begin(x, gain, query, key, value, out):
    size, mp_size = lax.axis_size("dp"), lax.axis_size("mp")
    rows, columns = query.shape
    return pl.pallas_call(
        begin_kernel,
        out_shape=[
            shape(rows * size, 3 * columns),
            shape(out.shape[0], out.shape[1] * size),
            shape(mp_size, *x.shape),
        ],
        in_specs=[VMEM] * 2 + [ANY] * 4,
        out_specs=[ANY] * 3,
        scratch_shapes=[
            pltpu.VMEM(x.shape, BF16),
            pltpu.SemaphoreType.DMA((4, 2, size + 1)),
            *spread_scratch(mp_size // 2),
        ],
        compiler_params=comm_params(0, 16),
        cost_estimate=cost(0, 60 * 2**20),
        name="begin",
    )(x, gain, query, key, value, out)


def forward_stage(collective_id, tail, head, norm, shard, gather, heads, toks, scale, shift):
    size, mp_size = lax.axis_size("dp"), lax.axis_size("mp")
    out_shape, scratch = [], []
    if tail:
        blocks, _, x, _ = tail
        owner_rows, width = x.shape
        total = blocks.shape[1] * blocks.shape[0] // heads
        out_shape += [
            shape(owner_rows, width, dtype=F32),
            shape(owner_rows, width),
            shape(total, heads * HEAD),
        ]
        scratch += sum_scratch(mp_size // 2, owner_rows, width)
    if head:
        total, slice_len = head[0].shape[0], head[2].shape[0]
        out_shape += [shape(size, slice_len, 3 * HEAD), shape(size, slice_len, HEAD)]
        scratch += [
            pltpu.VMEM((min(512, total), 3 * heads * HEAD), F32),
            *swap_scratch(size, slice_len, 3 * HEAD),
            *swap_scratch(size, slice_len, HEAD),
        ]
    if norm:
        scratch.append(pltpu.VMEM(norm[0].shape, BF16))
    here, spreads = len(out_shape), bool(norm) + len(shard)
    out_shape += [shape(mp_size, *array.shape) for array in (*norm[:1], *shard)]
    scratch += spread_scratch(mp_size // 2) * spreads
    axis = None
    if gather:
        weight, axis = gather
        dims = list(weight.shape)
        dims[axis] *= size
        out_shape.append(shape(*dims))
        scratch.append(pltpu.SemaphoreType.DMA((2, size + 1)))
    arrays = [*tail, *head, *norm]
    return pl.pallas_call(
        functools.partial(
            forward_kernel,
            bool(tail), bool(head), bool(norm), spreads, axis, heads, toks, scale, shift,
        ),
        out_shape=out_shape,
        in_specs=[VMEM] * len(arrays) + [ANY] * (len(shard) + bool(gather)),
        out_specs=[VMEM] * here + [ANY] * (spreads + bool(gather)),
        scratch_shapes=scratch,
        compiler_params=comm_params(collective_id, 52),
        cost_estimate=cost(10**10, 100 * 2**20),
        name="forward_stage",
    )(*arrays, *shard, *gather[:1])


def middle_part(
    collective_id, rows, cot, gate, up, down, middle, local_cot, gain, shards, before
):
    total, width = rows.shape
    hidden = gate.shape[1]
    size, mp_size = lax.axis_size("dp"), lax.axis_size("mp")
    owner_rows = middle.shape[0]
    block = width // size
    wide = [shape(size, block, hidden)] * 2 + [shape(size, hidden, block)]
    return pl.pallas_call(
        functools.partial(middle_kernel, not before, len(shards), owner_rows),
        out_shape=[
            shape(owner_rows, width),
            shape(owner_rows, width, dtype=F32),
            shape(owner_rows, width),
            shape(1, width, dtype=F32),
            *[shape(mp_size, *array.shape) for array in shards],
            *wide,
        ],
        in_specs=[VMEM] * 8 + [ANY] * (len(shards) + len(before)),
        out_specs=[VMEM] * 4 + [ANY] * (len(shards) + 3),
        scratch_shapes=[
            *[pltpu.VMEM((total, hidden), BF16)] * 3,
            pltpu.VMEM((max(block, hidden), total), BF16),
            pltpu.VMEM((2, block, hidden), BF16),
            pltpu.VMEM((hidden, block), BF16),
            pltpu.VMEM((2, block, hidden), BF16),
            pltpu.VMEM((hidden, block), BF16),
            pltpu.SemaphoreType.DMA((2, 3)),
            *sum_scratch(mp_size // 2, owner_rows, width) * 2,
            *spread_scratch(mp_size // 2) * len(shards),
        ],
        compiler_params=comm_params(collective_id, 61),
        cost_estimate=cost(18 * total * width * hidden, 60 * 2**20),
        name="middle_part",
    )(rows, cot, gate, up, down, middle, local_cot, gain, *shards, *before)


def backward_stage(collective_id, tail, old_qkv, head, old_out, last, shard, heads, toks, scale, shift):
    size, mp_size = lax.axis_size("dp"), lax.axis_size("mp")
    places = mp_size // 2
    out_shape, scratch = [], []
    if tail:
        owner_rows, width = tail[3].shape
        out_shape.append(shape(owner_rows, width, dtype=F32))
        total = tail[0].shape[0]
        wide = shape(size, width // size, 3 * heads * HEAD)
        if not last:
            out_shape += [wide, shape(1, width, dtype=F32)]
        scratch += [
            *sum_scratch(places, owner_rows, width),
            pltpu.VMEM((width // size, total), BF16),
            pltpu.VMEM((1, width), F32),
        ]
    if head:
        (total, width), slice_len = head[0].shape, head[2].shape[1]
        out_shape.append(shape(total, 3 * heads * HEAD))
        out_shape.append(shape(size, heads * HEAD, width // size))
        scratch += [
            *swap_scratch(size, slice_len, HEAD),
            *swap_scratch(size, slice_len, HEAD),
            *swap_scratch(size, slice_len, 2 * HEAD),
            pltpu.VMEM((size, HEAD, slice_len), F32),
            pltpu.VMEM((heads * HEAD, total), BF16),
        ]
    here = len(out_shape)
    if last:
        gains = last[1].shape
        out_shape += [shape(*last[0].shape), wide]
        scratch += [
            pltpu.VMEM(wide.shape, BF16),
            pltpu.VMEM(gains, F32),
            pltpu.VMEM((size, *gains), F32),
            pltpu.VMEM(gains, F32),
            pltpu.VMEM((mp_size, *gains), F32),
            pltpu.SemaphoreType.DMA((2, 2, size)),
            pltpu.SemaphoreType.DMA((2, size)),
            *spread_scratch(places),
        ]
        out_shape.append(shape(*gains, dtype=F32))
    scratch += spread_scratch(places) * len(shard)
    out_shape += [shape(mp_size, *array.shape) for array in shard]
    arrays = [*tail, *old_qkv, *head, *old_out]
    last_specs, last_outs = ([ANY, VMEM], [ANY, ANY, VMEM]) if last else ([], [])
    return pl.pallas_call(
        functools.partial(
            backward_kernel, bool(tail), bool(head), bool(last), len(old_qkv), len(old_out),
            len(shard), heads, toks, scale, shift,
        ),
        out_shape=out_shape,
        in_specs=[VMEM] * len(arrays) + last_specs + [ANY] * len(shard),
        out_specs=[VMEM] * here + last_outs + [ANY] * len(shard),
        scratch_shapes=scratch,
        compiler_params=comm_params(collective_id, 58),
        cost_estimate=cost(10**10, 100 * 2**20),
        name="backward_stage",
    )(*arrays, *last, *shard)


def ffn(rows, cot, gate, up, down):
    total, width = rows.shape
    hidden = gate.shape[1]
    step = min(512, total)
    by_rows = pl.BlockSpec((step, width), lambda i: (i, 0))
    by_hidden = pl.BlockSpec((step, hidden), lambda i: (i, 0))
    held = lambda array: pl.BlockSpec(array.shape, lambda i: (0, 0), pipeline_mode=pl.Buffered(1))
    return pl.pallas_call(
        ffn_kernel,
        grid=(total // step,),
        out_shape=[shape(total, width)] * 2 + [shape(total, hidden)] * 3,
        in_specs=[by_rows, by_rows, held(gate), held(up), held(down)],
        out_specs=[by_rows] * 2 + [by_hidden] * 3,
        compiler_params=limits(56),
        cost_estimate=cost(12 * total * width * hidden, 34 * 2**20),
        name="ffn",
    )(rows, cot, gate, up, down)


def weight_grad(lefts, groups, left_blocked):
    count = len(lefts)
    size = lax.axis_size("dp")
    rows = lefts[0].shape[0]
    m, n = lefts[0].shape[1], groups[0][0].shape[1]
    moving = lambda width: pl.BlockSpec((rows, width // size), lambda e: (0, e))
    fixed = lambda width: pl.BlockSpec(
        (rows, width), lambda e: (0, 0), pipeline_mode=pl.Buffered(1)
    )
    left_spec = moving(m) if left_blocked else fixed(m)
    right_spec = fixed(n) if left_blocked else moving(n)
    out = (m // size, n) if left_blocked else (m, n // size)
    return pl.pallas_call(
        functools.partial(grad_kernel, count, len(groups), left_blocked),
        grid=(size,),
        in_specs=[left_spec] * count + [right_spec] * (count * len(groups)),
        out_specs=[pl.BlockSpec((1, *out), lambda e: (e, 0, 0))] * len(groups),
        out_shape=[shape(size, *out)] * len(groups),
        scratch_shapes=[pltpu.VMEM((out[0], count * rows), BF16)],
        compiler_params=limits(52),
        cost_estimate=cost(2 * count * rows * m * n * len(groups), 24 * 2**20),
        name="weight_grad",
    )(*lefts, *(right for group in groups for right in group))


def first_visible(ids):
    at = jnp.arange(ids.shape[-1], dtype=jnp.int32)
    starts = jnp.concatenate([jnp.ones_like(ids[..., :1], jnp.bool_), ids[..., 1:] != ids[..., :-1]], axis=-1)
    return lax.cummax(jnp.where(starts, at, 0), axis=ids.ndim - 1)


def block_at(values, index):
    return lax.dynamic_index_in_dim(values, index, 0, keepdims=False)


def scatter_mp(values):
    return lax.psum_scatter(values, "mp", scatter_dimension=0, tiled=True).astype(F32)


def sliced_scores(qkv, kv_all, first, positions, scale, shift):
    raw = jnp.einsum("pqd,pkd->pqk", qkv[..., :HEAD], kv_all[..., :HEAD], preferred_element_type=F32)
    at = jnp.arange(kv_all.shape[1], dtype=jnp.int32)
    visible = (at >= first[..., None]) & (at <= positions[:, None])
    return jnp.where(visible, sigmoid_of(raw, scale, shift), 0.0)


def per_device(
    inputs,
    cotangent,
    doc_ids,
    gain_attn,
    w_query,
    w_key,
    w_value,
    w_out,
    gain_ffn,
    w_gate,
    w_up,
    w_down,
):
    dp_size = lax.axis_size("dp")
    mp_size = lax.axis_size("mp")
    micro_count, row_count, seq_count, width = inputs.shape
    slice_len = row_count * mp_size
    total_len = slice_len * dp_size
    rows_here = row_count * seq_count
    shift = math.log(total_len)
    scale = HEAD ** (-0.5)
    dp_at = lax.axis_index("dp")
    mp_at = lax.axis_index("mp")
    first_row = dp_at * slice_len
    positions = first_row + jnp.arange(slice_len, dtype=jnp.int32)
    head_width = w_query.shape[1]
    heads = head_width // HEAD
    hidden = w_gate.shape[1]
    pairs = seq_count * heads
    whole_pairs = pairs == dp_size
    cos_all, sin_all = full_tables(total_len)
    cos_slice, sin_slice = [
        lax.dynamic_slice_in_dim(table, first_row, slice_len, 0) for table in (cos_all, sin_all)
    ]

    def by_row(table):
        shaped = table.reshape(mp_size, 1, row_count, 1, HEAD)
        return jnp.broadcast_to(shaped, (mp_size, seq_count, row_count, 1, HEAD))

    def rotate(values, back=False):
        sine = -by_row(sin_slice) if back else by_row(sin_slice)
        return values * by_row(cos_slice) + swap_halves(values) * sine

    def to_pairs(values):
        shaped = values.reshape(mp_size, seq_count, row_count, heads, -1)
        return shaped.transpose(1, 3, 0, 2, 4).reshape(pairs, slice_len, -1)

    def from_pairs(values):
        shaped = values.reshape(seq_count, heads, mp_size, row_count, -1)
        return shaped.transpose(2, 0, 3, 1, 4).reshape(mp_size * rows_here, heads, -1)

    def to_rows(values):
        return jnp.swapaxes(values, 0, 1).reshape(rows_here, width)

    def from_rows(values):
        return jnp.swapaxes(values.reshape(seq_count, row_count, width), 0, 1)

    def gather_mp(values):
        return lax.all_gather(values, "mp", axis=0, tiled=True)

    gain_attn_grad = jnp.zeros((width,), F32)
    gain_ffn_grad = jnp.zeros((width,), F32)
    results = []
    input_grads = []
    kept = [[] for _ in range(9)]
    xs = [to_rows(inputs[m]) for m in range(micro_count)]
    cots = [to_rows(cotangent[m]) for m in range(micro_count)]
    micros = range(micro_count)
    if whole_pairs:
        stage = (heads, row_count, scale, shift)
        ids = [
            block_at(doc_ids[m], dp_at // heads).astype(F32).reshape(dp_size, 1, slice_len)
            for m in micros
        ]
        last = micro_count - 1

        def whole(blocks):
            return blocks.reshape(mp_size * rows_here, width)

        def scatter_dp(blocks):
            return lax.psum_scatter(blocks, "dp", scatter_dimension=0, tiled=True)[0].astype(F32)

        qkv_full, out_full, rows_one = begin(
            xs[0], gain_attn[None], w_query, w_key, w_value, w_out
        )
        gathers = {0: (w_gate, 0), last: (w_up, 0), micro_count: (w_down, 1)}
        wide = []
        ones, qkvs, got, middles, lows, twos, mixtures = [whole(rows_one)], [], [], [], [], [], []
        for m in range(micro_count + 1):
            tail, head, norm, shard = (), (), (), ()
            if m:
                tail = (got[m - 1], out_full, xs[m - 1], gain_ffn[None])
            if m < micro_count:
                head = (ones[m], qkv_full, cos_slice, sin_slice, ids[m])
            if m < last:
                norm = (xs[m + 1], gain_attn[None])
            elif lows:
                shard = (lows[m - last],)
            if m == 0:
                shard += (cots[0],)
            outs = forward_stage(10 + m, tail, head, norm, shard, gathers.get(m, ()), *stage)
            if tail:
                (middle, low, mixture), outs = take(outs, 3)
                middles.append(middle)
                lows.append(low)
                mixtures.append(mixture)
            if head:
                (qkv, block), outs = take(outs, 2)
                qkvs.append(qkv)
                got.append(block)
            if norm or shard:
                (ones if m < last else twos).append(whole(outs[0]))
            if m == 0:
                portions = [whole(outs[1])]
            if m in gathers:
                wide.append(outs[-1])
        grads, low_grads, attns, projs, sums, gain_parts = [], [], [], [], [], []
        for m in micros:
            shard = (lows[len(twos)] if len(twos) < micro_count else low_grads[len(attns)],)
            if m < last:
                shard += (cots[m + 1],)
            result, grad, low, gain_part, full, *others = middle_part(
                30 + m, twos[m], portions[m], *wide, middles[m], cots[m], gain_ffn[None], shard, sums
            )
            (twos if len(twos) < micro_count else attns).append(whole(full))
            if m < last:
                portions.append(whole(others[0]))
            sums = others[-3:]
            grads.append(grad)
            low_grads.append(low)
            gain_parts.append(gain_part)
            results.append(from_rows(result))
        sum_gate, sum_up, sum_down = [scatter_dp(blocks) for blocks in sums]
        old_qkv, old_out, attn_parts = (), (), []
        for m in range(micro_count + 1):
            tail, head, shard, final = (), (), (), ()
            if m:
                tail = (projs[m - 1], qkv_full, ones[m - 1], xs[m - 1], grads[m - 1], gain_attn[None])
            if m < micro_count:
                head = (attns[m], out_full, qkvs[m], ids[m], cos_all, sin_all, mixtures[m])
            else:
                rows = [sum(gain_parts), sum(attn_parts), jnp.zeros((6, width), F32)]
                final = (*old_out, jnp.concatenate(rows, axis=0))
            if len(attns) < micro_count:
                shard = (low_grads[len(attns)],)
            outs = backward_stage(
                20 + m, tail, old_qkv, head, () if final else old_out, final, shard, *stage
            )
            if tail:
                (input_grad,), outs = take(outs, 1)
                input_grads.append(from_rows(input_grad))
            if tail and head:
                (new_qkv, gain_part), outs = take(outs, 2)
                old_qkv = (new_qkv,)
                attn_parts.append(gain_part)
            if head:
                (proj, new_out), outs = take(outs, 2)
                projs.append(proj)
                old_out = (new_out,)
            if shard:
                attns.append(whole(outs[-1]))
        sum_out, sum_qkv = (jnp.sum(blocks.astype(F32), axis=0) for blocks in outs[:2])
        gain_sums = (outs[2][1] / gain_attn, outs[2][0])
    else:
        qkv_full = lax.all_gather(
            jnp.concatenate([w_query, w_key, w_value], axis=1), "dp", axis=0, tiled=True
        )
        out_full = lax.all_gather(w_out, "dp", axis=1, tiled=True)
        gate_full = lax.all_gather(w_gate, "dp", axis=0, tiled=True)
        up_full = lax.all_gather(w_up, "dp", axis=0, tiled=True)
        down_full = lax.all_gather(w_down, "dp", axis=1, tiled=True)
        first_all = first_visible(doc_ids)
        normed = [
            (x.astype(F32) * norm_factor(x.astype(F32)) * gain_attn).astype(BF16) for x in xs
        ]
        for micro in micros:
            local_rows = xs[micro].astype(F32)
            local_cot = cots[micro]
            factor_one = norm_factor(local_rows)
            rows_one = gather_mp(normed[micro])
            portion = gather_mp(local_cot)
            projected = dot(rows_one, qkv_full).reshape(
                mp_size, seq_count, row_count, 3, heads, HEAD
            )
            packed = to_pairs(
                jnp.concatenate(
                    [
                        rotate(projected[:, :, :, 0]).astype(BF16),
                        rotate(projected[:, :, :, 1]).astype(BF16),
                        projected[:, :, :, 2].astype(BF16),
                    ],
                    axis=-1,
                )
            )
            kv_all = lax.all_gather(packed[..., HEAD:], "dp", axis=1, tiled=True)
            first = lax.dynamic_slice_in_dim(first_all[micro], first_row, slice_len, 1)
            first = jnp.repeat(first, heads, axis=0)
            weights = sliced_scores(packed, kv_all, first, positions, scale, shift)
            attended = jnp.einsum(
                "pqk,pkd->pqd", weights.astype(BF16), kv_all[..., HEAD:], preferred_element_type=F32
            ).astype(BF16)
            mixture = from_pairs(attended).reshape(mp_size * rows_here, head_width)
            middle = local_rows + scatter_mp(dot(mixture, out_full).astype(BF16))
            factor_two = norm_factor(middle)
            rows_two = gather_mp((middle * factor_two * gain_ffn).astype(BF16))
            y, dh, activated, gate_grad, up_grad = ffn(
                rows_two, portion, gate_full, up_full, down_full
            )
            results.append(from_rows((middle + scatter_mp(y)).astype(BF16)))
            middle_term, gain_part = norm_back(middle, factor_two, gain_ffn, scatter_mp(dh))
            gain_ffn_grad = gain_ffn_grad + gain_part
            middle_grad = local_cot.astype(F32) + middle_term
            attn_portion = gather_mp(middle_grad.astype(BF16))
            mix_grad = to_pairs(dot_nt(attn_portion, out_full).astype(BF16))
            sig = sliced_scores(packed, kv_all, first, positions, scale, shift)
            prob_grad = jnp.einsum(
                "pqd,pkd->pqk", mix_grad, kv_all[..., HEAD:], preferred_element_type=F32
            )
            score_grad = (prob_grad * sig * (1.0 - sig)).astype(BF16)
            dq = jnp.einsum("pqk,pkd->pqd", score_grad, kv_all[..., :HEAD], preferred_element_type=F32)
            dk = jnp.einsum("pqk,pqd->pkd", score_grad, packed[..., :HEAD], preferred_element_type=F32)
            dv = jnp.einsum("pqk,pqd->pkd", sig.astype(BF16), mix_grad, preferred_element_type=F32)
            dkv = lax.psum_scatter(
                jnp.concatenate([dk * scale, dv], axis=-1).astype(BF16), "dp", scatter_dimension=1, tiled=True
            ).astype(F32)
            back = from_pairs(jnp.concatenate([dq * scale, dkv], axis=-1))
            back = back.reshape(mp_size, seq_count, row_count, heads, 3 * HEAD)
            proj_grad = jnp.stack(
                [
                    rotate(back[..., :HEAD], True),
                    rotate(back[..., HEAD : 2 * HEAD], True),
                    back[..., 2 * HEAD :],
                ],
                axis=3,
            ).astype(BF16).reshape(mp_size * rows_here, 3 * head_width)
            partial_grad = dot_nt(proj_grad, qkv_full)
            gain_attn_grad = gain_attn_grad + jnp.sum(partial_grad * rows_one.astype(F32), axis=0)
            input_term, _ = norm_back(
                local_rows, factor_one, gain_attn, scatter_mp(partial_grad.astype(BF16))
            )
            input_grads.append(from_rows(middle_grad + input_term))
            for held, array in zip(
                kept,
                (rows_one, proj_grad, mixture, attn_portion, rows_two, gate_grad, up_grad, activated, portion),
            ):
                held.append(array)

        def scatter_dp(lefts, rights, left_blocked):
            (blocks,) = weight_grad(lefts, (rights,), left_blocked)
            return lax.psum_scatter(blocks, "dp", scatter_dimension=0, tiled=True)[0].astype(F32)

        ones, projs, mixtures, attns, twos, gates, ups, acts, portions = kept
        sum_gate = scatter_dp(twos, gates, True)
        sum_up = scatter_dp(twos, ups, True)
        sum_down = scatter_dp(acts, portions, False)
        sum_out = scatter_dp(mixtures, attns, False)
        sum_qkv = scatter_dp(ones, projs, True)
        gain_sums = lax.psum((gain_attn_grad / gain_attn, gain_ffn_grad), ("dp", "mp"))
    return (
        jnp.stack(results),
        jnp.stack(input_grads),
        gain_sums[0],
        sum_qkv[:, :head_width],
        sum_qkv[:, head_width : 2 * head_width],
        sum_qkv[:, 2 * head_width :],
        sum_out,
        gain_sums[1],
        sum_gate,
        sum_up,
        sum_down,
    )


def solution(mesh):
    tokens = P(None, ("dp", "mp"), None, None)
    column = P("dp", "mp")
    row = P("mp", "dp")
    return jax.shard_map(
        per_device,
        mesh=mesh,
        in_specs=(
            tokens, tokens, P(), P(), column, column, column, row, P(), column, column, row,
        ),
        out_specs=(
            tokens, tokens, P(), column, column, column, row, P(), column, column, row,
        ),
        check_vma=False,
    )
```

```python
import functools
import math

import jax
import jax.numpy as jnp
import numpy as np
from jax import lax
from jax.experimental import pallas as pl
from jax.experimental.pallas import tpu as pltpu
from jax.sharding import PartitionSpec as P

HEAD = 128
epsilon = 1e-05
rope_base = 10000.0
F32 = jnp.float32
BF16 = jnp.bfloat16


def full_tables(total):
    half_size = HEAD // 2
    exponents = -(np.arange(half_size, dtype=np.float32) * np.float32(2.0 / HEAD))
    inverse = np.power(np.float32(rope_base), exponents)
    angles = np.arange(total, dtype=np.float32)[:, None] * inverse[None, :]
    cosine, sine = np.cos(angles), np.sin(angles)
    return (
        jnp.asarray(np.concatenate([cosine, cosine], axis=-1)),
        jnp.asarray(np.concatenate([-sine, sine], axis=-1)),
    )


def swap_halves(values):
    half_size = HEAD // 2
    return jnp.concatenate([values[..., half_size:], values[..., :half_size]], axis=-1)


def dot(left, right):
    return jnp.dot(left, right, preferred_element_type=F32)


def dot_tn(left, right):
    return lax.dot_general(left, right, (((0,), (0,)), ((), ())), preferred_element_type=F32)


def dot_nt(left, right):
    return lax.dot_general(left, right, (((1,), (1,)), ((), ())), preferred_element_type=F32)


def norm_factor(values):
    return lax.rsqrt(jnp.mean(values * values, axis=-1, keepdims=True) + epsilon)


def norm_back(values, factor, gain, incoming):
    scaled = incoming * gain
    gain_term = jnp.sum(incoming * values * factor, axis=0)
    input_term = factor * scaled - values * factor**3 * jnp.mean(
        scaled * values, axis=-1, keepdims=True
    )
    return (input_term, gain_term)


def sigmoid_of(raw, scale, shift):
    return 1.0 / (1.0 + jnp.exp(shift - raw * scale))


def split_cores(core, values, rows_here):
    shaped = values.reshape(-1, 2, rows_here, values.shape[-1])
    first, second = shaped[:, 0], shaped[:, 1]
    is_first = core == 0
    return jnp.where(is_first, first, second), jnp.where(is_first, second, first)

MESH = pl.DeviceIdType.MESH


class Spot:
    def __init__(self):
        self.dp, self.mp = lax.axis_index("dp"), lax.axis_index("mp")
        self.dp_size, self.mp_size = lax.axis_size("dp"), lax.axis_size("mp")
        self.places = self.mp_size // 2
        self.place, self.core = lax.div(self.mp, 2), lax.rem(self.mp, 2)
        self.sibling = (self.dp, self.mp + 1 - 2 * self.core)
        self.right = (self.dp, self.mp + 2)
        self.left = (self.dp, self.mp - 2)
        self.has_right = self.place < self.places - 1
        self.has_left = self.place > 0

    def peer(self, step):
        return lax.rem(self.dp + step, self.dp_size)

    def enter(self, with_dp, with_mp):
        barrier = pltpu.get_barrier_semaphore()
        count = 0

        def greet(device):
            pl.semaphore_signal(barrier, inc=1, device_id=device, device_id_type=MESH)

        if with_mp:
            greet(self.sibling)
            pl.when(self.has_right)(lambda: greet(self.right))
            pl.when(self.has_left)(lambda: greet(self.left))
            count += 1 + self.has_right.astype(jnp.int32) + self.has_left.astype(jnp.int32)
        if with_dp:
            for step in range(1, self.dp_size):
                greet((self.peer(step), self.mp))
            count += self.dp_size - 1
        pl.semaphore_wait(barrier, count)


class Swap:
    def __init__(self, spot, source, target, send, receive):
        self.spot, self.source, self.target = spot, source, target
        self.send, self.receive = send, receive
        self.copies = [self.copy(step) for step in range(1, spot.dp_size)]

    def copy(self, step):
        spot = self.spot
        return pltpu.make_async_remote_copy(
            src_ref=self.source.at[spot.peer(step)],
            dst_ref=self.target.at[spot.dp],
            send_sem=self.send.at[step],
            recv_sem=self.receive.at[step],
            device_id=(spot.peer(step), spot.mp),
            device_id_type=MESH,
        )

    def start(self):
        for copy in self.copies:
            copy.start()
        self.keep()

    def keep(self):
        self.target[self.spot.dp] = self.source[self.spot.dp]

    def wait(self):
        for copy in self.copies:
            copy.wait()


class Gather:
    def __init__(self, spot, shard, window, sems):
        self.local = pltpu.make_async_copy(shard, window(spot.dp), sems.at[0, 0])
        self.copies = [
            pltpu.make_async_remote_copy(
                src_ref=shard,
                dst_ref=window(spot.dp),
                send_sem=sems.at[0, step],
                recv_sem=sems.at[1, step],
                device_id=(spot.peer(step), spot.mp),
                device_id_type=MESH,
            )
            for step in range(1, spot.dp_size)
        ]

    def start(self):
        for copy in self.copies:
            copy.start()
        self.local.start()

    def go_on(self):
        pass

    def wait(self):
        for copy in self.copies:
            copy.wait()
        self.local.wait()


def gather_of(spot, *arguments):
    return (RingGather if spot.dp_size == 4 else Gather)(spot, *arguments)


class RingGather:
    def __init__(self, spot, shard, window, sems):
        side = spot.dp + 1 - 2 * lax.rem(spot.dp, 2)
        across = spot.dp + 2 - 4 * lax.div(spot.dp, 2)

        def copy(source, index, kind, to, half=None):
            return pltpu.make_async_remote_copy(
                src_ref=source,
                dst_ref=window(index, half),
                send_sem=sems.at[0, kind],
                recv_sem=sems.at[1, kind],
                device_id=(to, spot.mp),
                device_id_type=MESH,
            )

        self.local = pltpu.make_async_copy(shard, window(spot.dp), sems.at[0, 4])
        self.to_side = copy(shard, spot.dp, 0, side)
        self.to_across = copy(shard, spot.dp, 1, across)
        self.on_across = copy(window(side, 0), side, 2, across, 0)
        self.on_side = copy(window(across, 1), across, 3, side, 1)

    def start(self):
        self.to_side.start()
        self.to_across.start()
        self.local.start()

    def go_on(self):
        self.to_side.wait_recv()
        self.on_across.start()
        self.to_across.wait_recv()
        self.on_side.start()

    def wait(self):
        self.to_side.wait_send()
        self.to_across.wait_send()
        self.on_across.wait()
        self.on_side.wait()
        self.local.wait()


class Spread:
    def __init__(self, spot, shard, full, sems):
        self.spot, self.shard, self.full, self.sems = spot, shard, full, sems
        self.local = pltpu.make_async_copy(shard, full.at[spot.mp], sems.at[6, 0])

    def copy(self, kind, device, p, source=None, core=None):
        at = 2 * p + (self.spot.core if core is None else core)
        return pltpu.make_async_remote_copy(
            src_ref=self.full.at[at] if source is None else source,
            dst_ref=self.full.at[at],
            send_sem=self.sems.at[kind, p],
            recv_sem=self.sems.at[kind + 1, p],
            device_id=device,
            device_id_type=MESH,
        )

    def rightward(self, p, source=None):
        return self.copy(0, self.spot.right, p, source)

    def leftward(self, p, source=None):
        return self.copy(2, self.spot.left, p, source)

    def across(self, p, source=None):
        return self.copy(4, self.spot.sibling, p, source)

    def begin(self):
        spot = self.spot
        pl.when(spot.has_right)(lambda: self.rightward(spot.place, self.shard).start())
        pl.when(spot.has_left)(lambda: self.leftward(spot.place, self.shard).start())
        self.across(spot.place, self.shard).start()
        self.local.start()

    def go_on(self, hop):
        spot = self.spot

        @pl.when(spot.place >= hop)
        def _():
            p = spot.place - hop
            self.rightward(p).wait_recv()
            pl.when(spot.has_right)(lambda: self.rightward(p).start())
            self.across(p).start()

        @pl.when(spot.place + hop < spot.places)
        def _():
            p = spot.place + hop
            self.leftward(p).wait_recv()
            pl.when(spot.has_left)(lambda: self.leftward(p).start())
            self.across(p).start()

    def finish(self):
        spot = self.spot
        for p in range(spot.places):
            self.copy(4, spot.sibling, p, core=1 - spot.core).wait_recv()
            self.across(p).wait_send()
            pl.when(spot.has_right & (spot.place >= p))(lambda: self.rightward(p).wait_send())
            pl.when(spot.has_left & (spot.place <= p))(lambda: self.leftward(p).wait_send())
        self.local.wait()


def spread_scratch(places):
    return [pltpu.SemaphoreType.DMA((7, places))]


class Ship(Swap):
    def __init__(self, spot, source, target, sems):
        super().__init__(spot, source, target, sems.at[0], sems.at[1])
        self.local = pltpu.make_async_copy(source.at[spot.dp], target.at[spot.dp], sems.at[0, 0])

    def start(self):
        for copy in self.copies:
            copy.start()
        self.local.start()

    def wait(self):
        super().wait()
        self.local.wait()


def window_of(full, axis, step, column=0, columns=None):
    def window(index, half=None):
        rows = step if axis == 0 else full.shape[0]
        first, count = (0, rows) if half is None else (half * (rows // 2), rows // 2)
        if axis == 1:
            return full.at[
                pl.ds(first, count), pl.ds(pl.multiple_of(index * step, step), step)
            ]
        along = pl.ds(pl.multiple_of(index * step + first, count), count)
        return full.at[along, pl.ds(column, full.shape[1] if columns is None else columns)]

    return window


def swap_scratch(size, *block):
    return [
        pltpu.VMEM((size, *block), BF16),
        pltpu.VMEM((size, *block), BF16),
        pltpu.SemaphoreType.DMA((size,)),
        pltpu.SemaphoreType.DMA((size,)),
    ]


def far_first(places):
    orders = []
    for place in range(places):
        right, left, order = list(range(places - 1, place, -1)), list(range(place)), []
        while right or left:
            order += right[:1] + left[:1]
            right, left = right[1:], left[1:]
        orders.append(order + [place])
    return orders


class Sum:
    def __init__(self, spot, mine, out, from_sibling, passed, sems):
        self.spot = spot
        self.mine, self.out = mine, out
        self.from_sibling, self.passed = from_sibling, passed
        self.sems = sems
        self.orders = far_first(spot.places)

    def copy(self, source, target, kind, t, device, to=None):
        return pltpu.make_async_remote_copy(
            src_ref=source.at[t],
            dst_ref=target.at[t if to is None else to],
            send_sem=self.sems.at[kind, t],
            recv_sem=self.sems.at[kind + 1, t],
            device_id=device,
            device_id_type=MESH,
        )

    def sibling(self, t):
        return self.copy(self.out, self.from_sibling, 0, t, self.spot.sibling)

    def rightward(self, t):
        return self.copy(self.mine, self.passed, 2, t, self.spot.right)

    def leftward(self, t, place):
        to = jnp.where(t == place, self.spot.places, t)
        return self.copy(self.mine, self.passed, 4, t, self.spot.left, to)

    def leftward_out(self, t):
        return self.leftward(t, self.spot.place - 1)

    def leftward_in(self, t):
        return self.leftward(t, self.spot.place)

    def term(self, s):
        chosen = 0
        for place, order in enumerate(self.orders):
            for at, t in enumerate(order):
                if t:
                    chosen = chosen + jnp.where((self.spot.place == place) & (s == at), t, 0)
        return chosen

    def add(self, t, arrived):
        self.mine[t] = (self.mine[t].astype(F32) + arrived.astype(F32)).astype(BF16)

    def absorb(self, t):
        self.sibling(t).wait_recv()
        self.add(t, self.from_sibling[t])

    def begin(self, s):
        spot = self.spot

        @pl.when((spot.place == 0) & (s < spot.places - 1))
        def _():
            t = spot.places - 1 - s
            self.absorb(t)
            self.rightward(t).start()

        @pl.when((spot.place == spot.places - 1) & (s < spot.places - 1))
        def _():
            self.absorb(s)
            self.leftward_out(s).start()

    def go_on(self, hop):
        spot = self.spot
        last = spot.places - 1

        @pl.when((spot.place > 0) & (spot.place <= hop))
        def _():
            t = last + spot.place - hop
            self.absorb(t)
            self.rightward(t).wait_recv()
            self.add(t, self.passed[t])
            self.rightward(t).start()

        @pl.when((spot.place < last) & (last - spot.place <= hop))
        def _():
            t = hop - last + spot.place
            self.absorb(t)
            self.leftward_in(t).wait_recv()
            self.add(t, self.passed[t])
            self.leftward_out(t).start()

    def finish(self):
        spot = self.spot
        t = spot.place
        self.absorb(t)

        @pl.when(spot.has_left)
        def _():
            self.rightward(t).wait_recv()
            self.add(t, self.passed[t])

        @pl.when(spot.has_right)
        def _():
            self.leftward_in(t).wait_recv()
            self.add(t, self.passed[spot.places])

        for t in range(spot.places):
            self.sibling(t).wait_send()
            pl.when(spot.place < t)(lambda: self.rightward(t).wait_send())
            pl.when(spot.place > t)(lambda: self.leftward_out(t).wait_send())
        return self.mine[spot.place].astype(F32)


def sum_scratch(places, rows_here, width):
    return [
        *[pltpu.VMEM((places, rows_here, width), BF16)] * 3,
        pltpu.VMEM((places + 1, rows_here, width), BF16),
        pltpu.SemaphoreType.DMA((6, places)),
    ]


def as_column(row):
    return jnp.broadcast_to(row, (HEAD, row.shape[1])).T[:, 0:1]


def attend_blocks(qkv, ids_ref, out, scale, shift):
    count, block = out.shape[:2]
    row_at = lax.broadcasted_iota(jnp.int32, (block, block), 0)
    col_at = lax.broadcasted_iota(jnp.int32, (block, block), 1)

    @pl.loop(0, count)
    def _(i):
        queries = qkv[i, :, 0:HEAD]
        ids = as_column(ids_ref[i])

        def add_block(j, acc, diagonal=False):
            sig = sigmoid_of(dot_nt(queries, qkv[j, :, HEAD : 2 * HEAD]), scale, shift)
            visible = ids == ids_ref[j]
            if diagonal:
                visible = visible & (col_at <= row_at)
            weights = jnp.where(visible, sig, 0.0).astype(BF16)
            return acc + dot(weights, qkv[j, :, 2 * HEAD :])

        acc = add_block(i, jnp.zeros((block, HEAD), F32), True)
        out[i] = lax.fori_loop(0, i, add_block, acc).astype(BF16)


def attend_back_blocks(
    spot, qkv, grad, ids_ref, cos_ref, sin_ref, out_q, out_kv, dq, made, scale, shift
):
    count, block = grad.shape[:2]
    col_at = lax.broadcasted_iota(jnp.int32, (block, block), 0)
    row_at = lax.broadcasted_iota(jnp.int32, (block, block), 1)
    dq[...] = jnp.zeros_like(dq)

    def unrotate(values, i):
        rows = pl.ds(pl.multiple_of(i * block, block), block)
        swapped = pltpu.roll(values, HEAD // 2, 1)
        return (values * cos_ref[rows, :] - swapped * sin_ref[rows, :]).astype(BF16)

    @pl.loop(0, count)
    def _(at):
        j = spot.peer(at + 1)
        keys = qkv[j, :, HEAD : 2 * HEAD]
        values = qkv[j, :, 2 * HEAD :]
        keys_t = keys.T
        ids = as_column(ids_ref[j])

        def add_block(i, sums, diagonal=False):
            dk, dv = sums
            queries, grads = qkv[i, :, 0:HEAD], grad[i]
            sig = sigmoid_of(dot_nt(keys, queries), scale, shift)
            visible = ids == ids_ref[i]
            if diagonal:
                visible = visible & (col_at <= row_at)
            sig = jnp.where(visible, sig, 0.0)
            prob_grad = dot_nt(values, grads)
            score_grad = (prob_grad * sig * (1.0 - sig)).astype(BF16)
            dq[i] += dot(keys_t, score_grad)
            return dk + dot(score_grad, queries), dv + dot(sig.astype(BF16), grads)

        zero = jnp.zeros((block, HEAD), F32)
        dk, dv = lax.fori_loop(j + 1, count, add_block, add_block(j, (zero, zero), True))
        out_kv[j, :, 0:HEAD] = unrotate(dk * scale, j)
        out_kv[j, :, HEAD:] = dv.astype(BF16)
        pl.when(at < count - 1)(lambda: made(at + 1))

    @pl.loop(0, count)
    def _(i):
        out_q[i] = unrotate(dq[i].T * scale, i)


def take(refs, count):
    return refs[:count], refs[count:]


class Loads:
    def __init__(self, pairs, sems):
        self.copies = [
            pltpu.make_async_copy(source, target, sems.at[i])
            for i, (source, target) in enumerate(pairs)
        ]
        for copy in self.copies:
            copy.start()

    def wait(self, *which):
        for i in which or range(len(self.copies)):
            self.copies[i].wait()


def lazy_scratch(*arrays):
    return [pltpu.VMEM(array.shape, array.dtype) for array in arrays] + [
        pltpu.SemaphoreType.DMA((len(arrays),))
    ]


def put_norm(x_ref, gain_ref, out_ref):
    x = x_ref[...].astype(F32)
    out_ref[...] = (x * norm_factor(x) * gain_ref[...]).astype(BF16)


def begin_kernel(
    x_ref, gain_ref, query, key, value, out, qkv_full, out_full, first_full,
    normed, sems, spread_sems,
):
    spot = Spot()
    spot.enter(True, True)
    rows, columns = query.shape
    jobs = [
        (shard, window_of(qkv_full, 0, rows, i * columns, columns))
        for i, shard in enumerate((query, key, value))
    ]
    jobs.append((out, window_of(out_full, 1, out.shape[1])))
    gathers = [
        gather_of(spot, shard, window, sems.at[i]) for i, (shard, window) in enumerate(jobs)
    ]
    for gather in gathers:
        gather.start()
    put_norm(x_ref, gain_ref, normed)
    spread = Spread(spot, normed, first_full, spread_sems)
    spread.begin()
    spread.go_on(1)
    for gather in gathers:
        gather.go_on()
    for hop in range(2, spot.places):
        spread.go_on(hop)
    for gather in gathers:
        gather.wait()
    spread.finish()


def forward_kernel(tail, head, norms, spreads, gather_axis, heads, toks, scale, shift, *refs):
    gathers = gather_axis is not None
    tail_in, refs = take(refs, 4 * tail)
    head_in, refs = take(refs, 5 * head)
    norm_in, refs = take(refs, 2 * norms)
    spread_in, refs = take(refs, spreads - norms)
    gather_in, refs = take(refs, gathers)
    tail_out, refs = take(refs, 3 * tail)
    head_out, refs = take(refs, 2 * head)
    spread_out, refs = take(refs, spreads)
    gather_out, refs = take(refs, gathers)
    sum_refs, refs = take(refs, 5 * tail)
    head_refs, refs = take(refs, 9 * head)
    normed, refs = take(refs, norms)
    lazy, refs = take(refs, 3 * head)
    if head:
        rows_ref, weight_ref, cos_ref, sin_ref, ids_ref = head_in
        loads = Loads(zip((rows_ref, weight_ref), lazy), lazy[2])
        rows_ref, weight_ref = lazy[:2]
    spot = Spot()
    spot.enter(head or gathers, tail or spreads)
    if norms:
        put_norm(*norm_in, *normed)
        spread_in = (*normed, *spread_in)
    moving = [Spread(spot, *refs) for refs in zip(spread_in, spread_out, refs)]
    for spread in moving:
        spread.begin()
    if gathers:
        window = window_of(gather_out[0], gather_axis, gather_in[0].shape[gather_axis])
        gather = gather_of(spot, gather_in[0], window, refs[-1])
        if not (tail and head):
            gather.start()

    if tail:
        got, out_weight, x_ref, gain_ref = tail_in
        middle_ref, normed_ref, mix_ref = tail_out
        pairs = got.shape[0]
        owner_rows = toks * (pairs // heads)
        for o in range(mix_ref.shape[0] // owner_rows):
            for p in range(pairs):
                s, h = p // heads, p % heads
                mix_ref[pl.ds(o * owner_rows + s * toks, toks), h * HEAD : (h + 1) * HEAD] = got[
                    p, pl.ds(o * toks, toks), :
                ]
        summed = Sum(spot, *sum_refs)
        chip_rows = 2 * owner_rows

        @pl.loop(0, spot.places)
        def _(s):
            t = summed.term(s)
            rows = pl.ds(pl.multiple_of(t * chip_rows, chip_rows), chip_rows)
            value = dot(mix_ref[rows, :], out_weight[...]).astype(BF16)
            keep, send = split_cores(spot.core, value, owner_rows)
            summed.mine[t] = keep[0]
            summed.out[t] = send[0]
            summed.sibling(t).start()

        @pl.loop(0, spot.places - 1)
        def _(s):
            summed.begin(s)

    if head:
        qkv_ref, got_ref = head_out
        made, paired, qkv, qkv_send, qkv_recv, part, got, part_send, part_recv = head_refs
        pairs = paired.shape[0]
        owner_rows = toks * (pairs // heads)
        step = made.shape[0]
        loads.wait()

        @pl.loop(0, rows_ref.shape[0] // step)
        def _(i):
            rows = pl.ds(pl.multiple_of(i * step, step), step)
            made[...] = dot(rows_ref[rows, :], weight_ref[...])
            for j in range(step // owner_rows):
                to = pl.ds(pl.multiple_of((i * (step // owner_rows) + j) * toks, toks), toks)
                cosine, sine = cos_ref[to, :], sin_ref[to, :]
                for p in range(pairs):
                    s, h = p // heads, p % heads
                    here = pl.ds(j * owner_rows + s * toks, toks)
                    for kind in range(3):
                        piece = made[here, pl.ds((kind * heads + h) * HEAD, HEAD)]
                        if kind < 2:
                            piece = piece * cosine + pltpu.roll(piece, HEAD // 2, 1) * sine
                        paired[p, to, kind * HEAD : (kind + 1) * HEAD] = piece.astype(BF16)

        swap = Swap(spot, paired, qkv, qkv_send, qkv_recv)
        swap.start()
    if gathers and tail and head:
        gather.start()
    for spread in moving:
        spread.go_on(1)
    if tail and spot.places > 2:
        summed.go_on(1)
    if head:
        swap.wait()
    for hop in range(2, spot.places - 1):
        for spread in moving:
            spread.go_on(hop)
        if tail:
            summed.go_on(hop)
    if gathers:
        gather.go_on()
    if head:
        attend_blocks(qkv, ids_ref, part, scale, shift)
        swap = Swap(spot, part, got, part_send, part_recv)
        swap.start()
        qkv_ref[...] = qkv[...]
        swap.wait()
        got_ref[...] = got[...]
    for spread in moving:
        if spot.places > 2:
            spread.go_on(spot.places - 1)
    if tail:
        middle = x_ref[...].astype(F32) + summed.finish()
        middle_ref[...] = middle
        normed_ref[...] = (middle * norm_factor(middle) * gain_ref[...]).astype(BF16)
    for spread in moving:
        spread.finish()
    if gathers:
        gather.wait()


def middle_kernel(
    first, defer, spreads, owner_rows,
    middle_ref, local_cot_ref, gain_ref, rows_in, cot_in, gate_in, up_low, up_high, down_in,
    *refs,
):
    shards, refs = take(refs, spreads)
    before, refs = take(refs, 0 if first else 3)
    (grad_ref, low_ref, gain_grad_ref), refs = take(refs, 3)
    y_out, refs = take(refs, 2 if defer else 1)
    fulls, refs = take(refs, spreads)
    after, refs = take(refs, 3)
    (act_ref, dgate_ref, dup_ref, turned, new_rows, new_cols, old_rows, old_cols), refs = take(refs, 8)
    (rows_ref, cot_ref, gate_ref, up_ref, down_ref, load_sems, wide_sems), refs = take(refs, 7)
    sum_refs, refs = take(refs, 5)
    y_refs, refs = take(refs, 3 if defer else 5)
    size, half = after[0].shape[0], up_low.shape[0] // after[0].shape[0]
    pairs = [(rows_in, rows_ref), (gate_in, gate_ref)]
    for e in range(size):
        for i, part in enumerate((up_low, up_high)):
            to = up_ref.at[pl.ds((2 * e + i) * half, half), :]
            pairs.append((part.at[pl.ds(e * half, half), :], to))
    pairs += [(cot_in, cot_ref), (down_in, down_ref)]
    loads = Loads(pairs, load_sems)
    spot = Spot()
    spot.enter(False, True)
    summed = Sum(spot, *sum_refs)
    if defer:
        y_mine, y_send, y_sems = y_refs
        stores = [
            pltpu.make_async_copy(source, target, y_sems.at[i])
            for i, (source, target) in enumerate(zip((y_mine, y_send), y_out))
        ]
        sums = [summed]
    else:
        summed_y = Sum(spot, *y_refs)
        y_mine, y_send = summed_y.mine, summed_y.out
        sums = [summed, summed_y]
    moving = [Spread(spot, *refs) for refs in zip(shards, fulls, refs)]
    for spread in moving:
        spread.begin()
    hidden, width = gate_ref.shape[1], rows_ref.shape[1]
    chip_rows = 2 * owner_rows
    tile = min(256, hidden)
    blocks = after[0].shape[0]
    block = width // blocks
    new = (new_rows.at[0], new_rows.at[1], new_cols)
    old = (old_rows.at[0], old_rows.at[1], old_cols)

    def load(g, e):
        return pltpu.make_async_copy(before[g].at[e], old[g], wide_sems.at[0, g])

    def store(g, e):
        return pltpu.make_async_copy(new[g], after[g].at[e], wide_sems.at[1, g])

    if not first:
        for g in range(3):
            load(g, 0).start()
    loads.wait()

    @pl.loop(0, spot.places)
    def _(s):
        place = summed.term(s)
        rows = pl.ds(pl.multiple_of(place * chip_rows, chip_rows), chip_rows)

        @pl.loop(0, hidden // tile)
        def _(t):
            cols = pl.ds(pl.multiple_of(t * tile, tile), tile)
            gate = dot(rows_ref[rows, :], gate_ref[:, cols])
            up = dot(rows_ref[rows, :], up_ref[:, cols])
            sig = jax.nn.sigmoid(gate)
            silu = gate * sig
            act_ref[rows, cols] = (silu * up).astype(BF16)
            grad = dot_nt(cot_ref[rows, :], down_ref[cols, :])
            dgate_ref[rows, cols] = (grad * up * sig * (1.0 + gate * (1.0 - sig))).astype(BF16)
            dup_ref[rows, cols] = (grad * silu).astype(BF16)

        @pl.when(s > 0)
        def _():
            for each in sums:
                each.begin(s - 1)

        for hop in range(1, spot.places - 1):

            @pl.when(s == hop + 1)
            def _():
                for spread in moving:
                    spread.go_on(hop)
                for each in sums:
                    each.go_on(hop)

        @pl.loop(0, width // 256)
        def _(t):
            cols = pl.ds(pl.multiple_of(t * 256, 256), 256)
            value = dot(act_ref[rows, :], down_ref[:, cols])
            keep, send = split_cores(spot.core, value.astype(BF16), owner_rows)
            y_mine[place, :, cols] = keep[0]
            y_send[place, :, cols] = send[0]
            value = dot_nt(dgate_ref[rows, :], gate_ref[cols, :])
            value += dot_nt(dup_ref[rows, :], up_ref[cols, :])
            keep, send = split_cores(spot.core, value.astype(BF16), owner_rows)
            summed.mine[place, :, cols] = keep[0]
            summed.out[place, :, cols] = send[0]

        for each in sums:
            each.sibling(place).start()

    if defer:
        for copy in stores:
            copy.start()

    def make(g, e, left, right, right_at, columns):
        pl.when(e > 0)(lambda: store(g, e - 1).wait())
        if not first:
            load(g, e).wait()
        step = math.gcd(columns, 256)

        @pl.loop(0, columns // step)
        def _(t):
            cols = pl.ds(pl.multiple_of(t * step, step), step)
            total = dot(left[...], right[:, pl.ds(pl.multiple_of(right_at + t * step, step), step)])
            if not first:
                total += old[g][:, cols].astype(F32)
            new[g][:, cols] = total.astype(BF16)

        if not first:
            pl.when(e < blocks - 1)(lambda: load(g, e + 1).start())
        store(g, e).start()

    @pl.loop(0, blocks)
    def _(e):
        left = turned.at[pl.ds(0, block), :]
        left[...] = rows_ref[:, pl.ds(pl.multiple_of(e * block, block), block)].T
        make(0, e, left, dgate_ref, 0, hidden)
        make(1, e, left, dup_ref, 0, hidden)

    for spread in moving:
        spread.go_on(spot.places - 1)
    left = turned.at[pl.ds(0, hidden), :]
    left[...] = act_ref[...].T

    @pl.loop(0, blocks)
    def _(e):
        make(2, e, left, cot_ref, e * block, block)

    incoming = summed.finish()
    middle = middle_ref[...]
    term, gain_grad = norm_back(middle, norm_factor(middle), gain_ref[...], incoming)
    gain_grad_ref[...] = gain_grad[None]
    grad = local_cot_ref[...].astype(F32) + term
    grad_ref[...] = grad
    low_ref[...] = grad.astype(BF16)
    if defer:
        for copy in stores:
            copy.wait()
    else:
        y_out[0][...] = (middle + summed_y.finish()).astype(BF16)
    for spread in moving:
        spread.finish()
    for g in range(3):
        store(g, blocks - 1).wait()


def add_grads(blocks, left, right, turned, before, after):
    size, rows, columns = after.shape

    @pl.loop(0, size)
    def _(e):
        if rows < left.shape[1]:
            turned[...] = left[:, pl.ds(pl.multiple_of(e * rows, rows), rows)].T
            total = dot(turned[...], right[...])
        else:

            @pl.when(e == 0)
            def _():
                turned[...] = left[...].T

            cut = pl.ds(pl.multiple_of(e * columns, columns), columns)
            total = dot(turned[...], right[:, cut])
        if before is not None:
            total += before[e].astype(F32)
        after[e] = total.astype(BF16)


def backward_kernel(
    tail, head, last, old_tail, old_head, extra, spreads, heads, toks, scale, shift, *refs
):
    tail_in, refs = take(refs, 6 * tail)
    old_qkv, refs = take(refs, old_tail)
    head_in, refs = take(refs, 7 * head)
    old_out, refs = take(refs, old_head)
    last_in, refs = take(refs, 2 * last)
    extra_in, refs = take(refs, 3 * extra)
    spread_in, refs = take(refs, spreads)
    tail_out, refs = take(refs, (1 if last else 3) * tail)
    head_out, refs = take(refs, 2 * head)
    last_out, refs = take(refs, 3 * last)
    extra_out, refs = take(refs, extra)
    spread_out, refs = take(refs, spreads)
    tail_refs, refs = take(refs, 7 * tail)
    head_refs, refs = take(refs, 14 * head)
    last_refs, refs = take(refs, 8 * last)
    extra_refs, refs = take(refs, 6 * extra)
    lazy_tail, refs = take(refs, 3 * tail)
    lazy_old, refs = take(refs, 2 * old_tail)
    lazy_head, refs = take(refs, 5 * head)
    if head:
        rows_ref, out_weight_ref, qkv, ids_ref, cos_ref, sin_ref, mix_ref = head_in
        loads_head = Loads(zip((rows_ref, qkv, cos_ref, sin_ref), lazy_head), lazy_head[4])
        rows_ref, qkv, cos_ref, sin_ref = lazy_head[:4]
    if tail:
        proj_ref, weight_ref, rows_one_ref, x_ref, grad_ref, gain_ref = tail_in
        loads_tail = Loads(zip((weight_ref, rows_one_ref), lazy_tail), lazy_tail[2])
        weight_ref, rows_one_ref = lazy_tail[:2]
    if extra:
        loads_extra = Loads(zip(extra_in[:2], extra_refs), extra_refs[5])
    before = None
    if old_tail:
        before = lazy_old[0]
        loads_old = Loads([(old_qkv[0], before)], lazy_old[1])
    spot = Spot()
    spot.enter(head or last, tail or spreads or extra)
    moving = [Spread(spot, *refs) for refs in zip(spread_in, spread_out, refs)]
    for spread in moving:
        spread.begin()
    if last:
        out_blocks, gains = last_in
        out_target, qkv_target, gain_sum = last_out
        new_qkv, own_gain, all_dp, dp_sum, all_mp, ship_sems, gain_sems, gain_spread_sems = last_refs
        ship_out = Ship(spot, out_blocks, out_target, ship_sems.at[0])
        ship_out.start()
    sums = []
    if extra:
        summed_y = Sum(spot, *extra_refs[:5])
        loads_extra.wait()
        for t in range(spot.places):
            summed_y.sibling(t).start()
        sums.append(summed_y)
    if head:
        head_proj_ref, new_out = head_out
        part, got, part_send, part_recv = head_refs[:4]
        made_q, got_q, q_send, q_recv, made_kv, got_kv, kv_send, kv_recv, dq, mix_turned = head_refs[4:]
        pairs = part.shape[0]
        owner_rows = toks * (pairs // heads)
        total = rows_ref.shape[0]
        step = min(512, total)
        loads_head.wait(0)

        @pl.loop(0, total // step)
        def _(i):
            rows = pl.ds(pl.multiple_of(i * step, step), step)
            made = dot_nt(rows_ref[rows, :], out_weight_ref[...]).astype(BF16)
            for j in range(step // owner_rows):
                to = pl.ds(pl.multiple_of((i * (step // owner_rows) + j) * toks, toks), toks)
                for p in range(pairs):
                    s, h = p // heads, p % heads
                    start = j * owner_rows + s * toks
                    part[p, to, :] = made[start : start + toks, h * HEAD : (h + 1) * HEAD]

        swap = Swap(spot, part, got, part_send, part_recv)
        swap.start()

    if tail:
        result_ref = tail_out[0]
        sum_refs, (turned, gain_acc) = take(tail_refs, 5)
        if not last:
            new_qkv, gain_acc = tail_out[1:]
        owner_rows = x_ref.shape[0]
        summed = Sum(spot, *sum_refs)
        sums.insert(0, summed)
        chip_rows = 2 * owner_rows
        gain_acc[...] = jnp.zeros_like(gain_acc)
        loads_tail.wait()

        @pl.loop(0, spot.places)
        def _(s):
            t = summed.term(s)
            rows = pl.ds(pl.multiple_of(t * chip_rows, chip_rows), chip_rows)
            value = dot_nt(proj_ref[rows, :], weight_ref[...])
            gain_acc[...] += jnp.sum(
                value * rows_one_ref[rows, :].astype(F32), axis=0, keepdims=True
            )
            keep, send = split_cores(spot.core, value.astype(BF16), owner_rows)
            summed.mine[t] = keep[0]
            summed.out[t] = send[0]
            summed.sibling(t).start()
            pl.when(s > 0)(lambda: summed.begin(s - 1))

        if last:
            own_gain[...] = gains[...]
            own_gain[1:2, :] += gain_acc[...]
            gain_dp = Gather(spot, own_gain, lambda index: all_dp.at[index], gain_sems)
            gain_dp.start()
    if extra:

        @pl.loop(0, spot.places - 1)
        def _(s):
            summed_y.begin(s)

    if last:
        if old_tail:
            loads_old.wait()
        add_grads(spot.dp_size, rows_one_ref, proj_ref, turned, before, new_qkv)
        ship_qkv = Ship(spot, new_qkv, qkv_target, ship_sems.at[1])
        ship_qkv.start()
        gain_dp.wait()
        dp_sum[...] = jnp.sum(all_dp[...], axis=0)
        gain_mp = Spread(spot, dp_sum, all_mp, gain_spread_sems)
        gain_mp.begin()
        gain_mp.go_on(1)
    if head:
        add_grads(
            spot.dp_size, mix_ref, rows_ref, mix_turned, old_out[0] if old_head else None, new_out
        )
        swap.wait()
    for spread in moving:
        spread.go_on(1)
    if spot.places > 2:
        for each in sums:
            each.go_on(1)
    if head:
        loads_head.wait(1, 2, 3)
        swap_kv = Swap(spot, made_kv, got_kv, kv_send, kv_recv)
        attend_back_blocks(
            spot, qkv, got, ids_ref, cos_ref, sin_ref, made_q, made_kv, dq,
            lambda step: swap_kv.copy(step).start(), scale, shift,
        )
        swap_kv.keep()
        swap = Swap(spot, made_q, got_q, q_send, q_recv)
        swap.start()
    for hop in range(2, spot.places - 1):
        if last:
            gain_mp.go_on(hop)
        for spread in moving:
            spread.go_on(hop)
        for each in sums:
            each.go_on(hop)
    if tail and not last:
        if old_tail:
            loads_old.wait()
        add_grads(spot.dp_size, rows_one_ref, proj_ref, turned, before, new_qkv)
    if head:
        swap_kv.wait()
        swap.wait()
        for o in range(total // owner_rows):
            for p in range(pairs):
                s, h = p // heads, p % heads
                here, there = pl.ds(o * owner_rows + s * toks, toks), pl.ds(o * toks, toks)
                for kind in range(3):
                    piece = (
                        got_kv[p, there, (kind - 1) * HEAD : kind * HEAD] if kind else got_q[p, there, :]
                    )
                    head_proj_ref[
                        here, (kind * heads + h) * HEAD : (kind * heads + h + 1) * HEAD
                    ] = piece
    if spot.places > 2:
        for spread in moving:
            spread.go_on(spot.places - 1)
        if last:
            gain_mp.go_on(spot.places - 1)
    if tail:
        incoming = summed.finish()
        x = x_ref[...].astype(F32)
        term, _ = norm_back(x, norm_factor(x), gain_ref[...], incoming)
        result_ref[...] = grad_ref[...] + term
    if extra:
        extra_out[0][...] = (extra_in[2][...] + summed_y.finish()).astype(BF16)
    if last:
        gain_mp.finish()
        gain_sum[...] = jnp.sum(all_mp[...], axis=0)
        ship_out.wait()
        ship_qkv.wait()
    for spread in moving:
        spread.finish()


def ffn_kernel(
    rows_ref, cot_ref, gate_ref, up_ref, down_ref, y_ref, dh_ref, act_ref, dgate_ref, dup_ref
):
    hidden = gate_ref.shape[1]
    width = rows_ref.shape[1]
    tile = min(256, hidden)

    @pl.loop(0, hidden // tile)
    def _(t):
        cols = pl.ds(pl.multiple_of(t * tile, tile), tile)
        gate = dot(rows_ref[...], gate_ref[:, cols])
        up = dot(rows_ref[...], up_ref[:, cols])
        sig = jax.nn.sigmoid(gate)
        silu = gate * sig
        act_ref[:, cols] = (silu * up).astype(BF16)
        grad = dot_nt(cot_ref[...], down_ref[cols, :])
        dgate_ref[:, cols] = (grad * up * sig * (1.0 + gate * (1.0 - sig))).astype(BF16)
        dup_ref[:, cols] = (grad * silu).astype(BF16)

    @pl.loop(0, width // 256)
    def _(t):
        cols = pl.ds(pl.multiple_of(t * 256, 256), 256)
        y_ref[:, cols] = dot(act_ref[...], down_ref[:, cols]).astype(BF16)
        dh = dot_nt(dgate_ref[...], gate_ref[cols, :]) + dot_nt(dup_ref[...], up_ref[cols, :])
        dh_ref[:, cols] = dh.astype(BF16)


def grad_kernel(count, groups, left_blocked, *refs):
    lefts, refs = take(refs, count)
    rights, refs = take(refs, count * groups)
    out_refs, (turned,) = take(refs, groups)
    rows = lefts[0].shape[0]

    def turn():
        for m, left in enumerate(lefts):
            turned[:, m * rows : (m + 1) * rows] = left[...].T

    if left_blocked:
        turn()
    else:
        pl.when(pl.program_id(0) == 0)(turn)
    tile = math.gcd(out_refs[0].shape[2], 256)
    for g, out_ref in enumerate(out_refs):
        own = rights[g * count : (g + 1) * count]

        @pl.loop(0, out_ref.shape[2] // tile)
        def _(t):
            cols = pl.ds(pl.multiple_of(t * tile, tile), tile)
            total = dot(turned[:, :rows], own[0][:, cols])
            for m in range(1, count):
                total += dot(turned[:, m * rows : (m + 1) * rows], own[m][:, cols])
            out_ref[0, :, cols] = total.astype(BF16)


VMEM = pl.BlockSpec(memory_space=pltpu.VMEM)
ANY = pl.BlockSpec(memory_space=pl.ANY)


def cost(flops, nbytes):
    return pl.CostEstimate(flops=flops, bytes_accessed=nbytes, transcendentals=0)


def limits(mebibytes):
    return pltpu.CompilerParams(vmem_limit_bytes=mebibytes * 2**20)


def shape(*dims, dtype=BF16):
    return jax.ShapeDtypeStruct(dims, dtype)


def comm_params(collective_id, mebibytes):
    return pltpu.CompilerParams(
        collective_id=collective_id, has_side_effects=True, vmem_limit_bytes=mebibytes * 2**20
    )


def begin(x, gain, query, key, value, out):
    size, mp_size = lax.axis_size("dp"), lax.axis_size("mp")
    rows, columns = query.shape
    return pl.pallas_call(
        begin_kernel,
        out_shape=[
            shape(rows * size, 3 * columns),
            shape(out.shape[0], out.shape[1] * size),
            shape(mp_size, *x.shape),
        ],
        in_specs=[VMEM] * 2 + [ANY] * 4,
        out_specs=[ANY] * 3,
        scratch_shapes=[
            pltpu.VMEM(x.shape, BF16),
            pltpu.SemaphoreType.DMA((4, 2, size + 1)),
            *spread_scratch(mp_size // 2),
        ],
        compiler_params=comm_params(0, 16),
        cost_estimate=cost(0, 60 * 2**20),
        name="begin",
    )(x, gain, query, key, value, out)


def forward_stage(collective_id, tail, head, norm, shard, gather, heads, toks, scale, shift):
    size, mp_size = lax.axis_size("dp"), lax.axis_size("mp")
    out_shape, scratch = [], []
    if tail:
        blocks, _, x, _ = tail
        owner_rows, width = x.shape
        total = blocks.shape[1] * blocks.shape[0] // heads
        out_shape += [
            shape(owner_rows, width, dtype=F32),
            shape(owner_rows, width),
            shape(total, heads * HEAD),
        ]
        scratch += sum_scratch(mp_size // 2, owner_rows, width)
    if head:
        total, slice_len = head[0].shape[0], head[2].shape[0]
        out_shape += [shape(size, slice_len, 3 * HEAD), shape(size, slice_len, HEAD)]
        scratch += [
            pltpu.VMEM((min(512, total), 3 * heads * HEAD), F32),
            *swap_scratch(size, slice_len, 3 * HEAD),
            *swap_scratch(size, slice_len, HEAD),
        ]
    if norm:
        scratch.append(pltpu.VMEM(norm[0].shape, BF16))
    if head:
        scratch += lazy_scratch(*head[:2])
    here, spreads = len(out_shape), bool(norm) + len(shard)
    out_shape += [shape(mp_size, *array.shape) for array in (*norm[:1], *shard)]
    scratch += spread_scratch(mp_size // 2) * spreads
    axis = None
    if gather:
        weight, axis = gather
        dims = list(weight.shape)
        dims[axis] *= size
        out_shape.append(shape(*dims))
        scratch.append(pltpu.SemaphoreType.DMA((2, size + 1)))
    arrays = [*tail, *head, *norm]
    specs = [VMEM] * len(arrays)
    if head:
        specs[len(tail) : len(tail) + 2] = [ANY] * 2
    return pl.pallas_call(
        functools.partial(
            forward_kernel,
            bool(tail), bool(head), bool(norm), spreads, axis, heads, toks, scale, shift,
        ),
        out_shape=out_shape,
        in_specs=specs + [ANY] * (len(shard) + bool(gather)),
        out_specs=[VMEM] * here + [ANY] * (spreads + bool(gather)),
        scratch_shapes=scratch,
        compiler_params=comm_params(collective_id, 52),
        cost_estimate=cost(10**10, 100 * 2**20),
        name="forward_stage",
    )(*arrays, *shard, *gather[:1])


def middle_part(
    collective_id, defer, rows, cot, weights, middle, local_cot, gain, shards, before
):
    total, width = rows.shape
    gate, _, _, down = weights
    hidden = gate.shape[1]
    size, mp_size = lax.axis_size("dp"), lax.axis_size("mp")
    places = mp_size // 2
    owner_rows = middle.shape[0]
    block = width // size
    wide = [shape(size, block, hidden)] * 2 + [shape(size, hidden, block)]
    half = shape(places, owner_rows, width)
    y_scratch = sum_scratch(places, owner_rows, width)
    if defer:
        y_scratch = [*[pltpu.VMEM(half.shape, BF16)] * 2, pltpu.SemaphoreType.DMA((2,))]
    return pl.pallas_call(
        functools.partial(middle_kernel, not before, defer, len(shards), owner_rows),
        out_shape=[
            shape(owner_rows, width, dtype=F32),
            shape(owner_rows, width),
            shape(1, width, dtype=F32),
            *([half, half] if defer else [shape(owner_rows, width)]),
            *[shape(mp_size, *array.shape) for array in shards],
            *wide,
        ],
        in_specs=[VMEM] * 3 + [ANY] * (6 + len(shards) + len(before)),
        out_specs=[VMEM] * 3 + ([ANY] * 2 if defer else [VMEM]) + [ANY] * (len(shards) + 3),
        scratch_shapes=[
            *[pltpu.VMEM((total, hidden), BF16)] * 3,
            pltpu.VMEM((max(block, hidden), total), BF16),
            pltpu.VMEM((2, block, hidden), BF16),
            pltpu.VMEM((hidden, block), BF16),
            pltpu.VMEM((2, block, hidden), BF16),
            pltpu.VMEM((hidden, block), BF16),
            *[pltpu.VMEM(array.shape, BF16) for array in (rows, cot, gate, gate, down)],
            pltpu.SemaphoreType.DMA((4 + 2 * size,)),
            pltpu.SemaphoreType.DMA((2, 3)),
            *sum_scratch(places, owner_rows, width),
            *y_scratch,
            *spread_scratch(places) * len(shards),
        ],
        compiler_params=comm_params(collective_id, 61),
        cost_estimate=cost(18 * total * width * hidden, 60 * 2**20),
        name="middle_part",
    )(middle, local_cot, gain, rows, cot, *weights, *shards, *before)


def backward_stage(
    collective_id, tail, old_qkv, head, old_out, last, extra, shard, heads, toks, scale, shift
):
    size, mp_size = lax.axis_size("dp"), lax.axis_size("mp")
    places = mp_size // 2
    out_shape, scratch = [], []
    if tail:
        owner_rows, width = tail[3].shape
        out_shape.append(shape(owner_rows, width, dtype=F32))
        total = tail[0].shape[0]
        wide = shape(size, width // size, 3 * heads * HEAD)
        if not last:
            out_shape += [wide, shape(1, width, dtype=F32)]
        scratch += [
            *sum_scratch(places, owner_rows, width),
            pltpu.VMEM((width // size, total), BF16),
            pltpu.VMEM((1, width), F32),
        ]
    if head:
        (total, width), slice_len = head[0].shape, head[2].shape[1]
        out_shape.append(shape(total, 3 * heads * HEAD))
        out_shape.append(shape(size, heads * HEAD, width // size))
        scratch += [
            *swap_scratch(size, slice_len, HEAD),
            *swap_scratch(size, slice_len, HEAD),
            *swap_scratch(size, slice_len, 2 * HEAD),
            pltpu.VMEM((size, HEAD, slice_len), F32),
            pltpu.VMEM((heads * HEAD, total), BF16),
        ]
    here = len(out_shape)
    if last:
        gains = last[1].shape
        out_shape += [shape(*last[0].shape), wide]
        scratch += [
            pltpu.VMEM(wide.shape, BF16),
            pltpu.VMEM(gains, F32),
            pltpu.VMEM((size, *gains), F32),
            pltpu.VMEM(gains, F32),
            pltpu.VMEM((mp_size, *gains), F32),
            pltpu.SemaphoreType.DMA((2, 2, size)),
            pltpu.SemaphoreType.DMA((2, size)),
            *spread_scratch(places),
        ]
        out_shape.append(shape(*gains, dtype=F32))
    if extra:
        out_shape.append(shape(*extra[2].shape))
        scratch += sum_scratch(places, *extra[2].shape)
        scratch.append(pltpu.SemaphoreType.DMA((2,)))
    if tail:
        scratch += lazy_scratch(tail[1], tail[2])
    scratch += lazy_scratch(*old_qkv) if old_qkv else []
    if head:
        scratch += lazy_scratch(head[0], head[2], head[4], head[5])
    scratch += spread_scratch(places) * len(shard)
    out_shape += [shape(mp_size, *array.shape) for array in shard]
    arrays = [*tail, *old_qkv, *head, *old_out]
    tail_specs = [VMEM, ANY, ANY, VMEM, VMEM, VMEM] if tail else []
    head_specs = [ANY, VMEM, ANY, VMEM, ANY, ANY, VMEM] if head else []
    specs = [*tail_specs, *[ANY] * len(old_qkv), *head_specs, *[VMEM] * len(old_out)]
    last_specs, last_outs = ([ANY, VMEM], [ANY, ANY, VMEM]) if last else ([], [])
    extra_specs, extra_outs = ([ANY, ANY, VMEM], [VMEM]) if extra else ([], [])
    return pl.pallas_call(
        functools.partial(
            backward_kernel, bool(tail), bool(head), bool(last), len(old_qkv), len(old_out),
            bool(extra), len(shard), heads, toks, scale, shift,
        ),
        out_shape=out_shape,
        in_specs=specs + last_specs + extra_specs + [ANY] * len(shard),
        out_specs=[VMEM] * here + last_outs + extra_outs + [ANY] * len(shard),
        scratch_shapes=scratch,
        compiler_params=comm_params(collective_id, 58),
        cost_estimate=cost(10**10, 100 * 2**20),
        name="backward_stage",
    )(*arrays, *last, *extra, *shard)


def ffn(rows, cot, gate, up, down):
    total, width = rows.shape
    hidden = gate.shape[1]
    step = min(512, total)
    by_rows = pl.BlockSpec((step, width), lambda i: (i, 0))
    by_hidden = pl.BlockSpec((step, hidden), lambda i: (i, 0))
    held = lambda array: pl.BlockSpec(array.shape, lambda i: (0, 0), pipeline_mode=pl.Buffered(1))
    return pl.pallas_call(
        ffn_kernel,
        grid=(total // step,),
        out_shape=[shape(total, width)] * 2 + [shape(total, hidden)] * 3,
        in_specs=[by_rows, by_rows, held(gate), held(up), held(down)],
        out_specs=[by_rows] * 2 + [by_hidden] * 3,
        compiler_params=limits(56),
        cost_estimate=cost(12 * total * width * hidden, 34 * 2**20),
        name="ffn",
    )(rows, cot, gate, up, down)


def weight_grad(lefts, groups, left_blocked):
    count = len(lefts)
    size = lax.axis_size("dp")
    rows = lefts[0].shape[0]
    m, n = lefts[0].shape[1], groups[0][0].shape[1]
    moving = lambda width: pl.BlockSpec((rows, width // size), lambda e: (0, e))
    fixed = lambda width: pl.BlockSpec(
        (rows, width), lambda e: (0, 0), pipeline_mode=pl.Buffered(1)
    )
    left_spec = moving(m) if left_blocked else fixed(m)
    right_spec = fixed(n) if left_blocked else moving(n)
    out = (m // size, n) if left_blocked else (m, n // size)
    return pl.pallas_call(
        functools.partial(grad_kernel, count, len(groups), left_blocked),
        grid=(size,),
        in_specs=[left_spec] * count + [right_spec] * (count * len(groups)),
        out_specs=[pl.BlockSpec((1, *out), lambda e: (e, 0, 0))] * len(groups),
        out_shape=[shape(size, *out)] * len(groups),
        scratch_shapes=[pltpu.VMEM((out[0], count * rows), BF16)],
        compiler_params=limits(52),
        cost_estimate=cost(2 * count * rows * m * n * len(groups), 24 * 2**20),
        name="weight_grad",
    )(*lefts, *(right for group in groups for right in group))


def first_visible(ids):
    at = jnp.arange(ids.shape[-1], dtype=jnp.int32)
    starts = jnp.concatenate([jnp.ones_like(ids[..., :1], jnp.bool_), ids[..., 1:] != ids[..., :-1]], axis=-1)
    return lax.cummax(jnp.where(starts, at, 0), axis=ids.ndim - 1)


def block_at(values, index):
    return lax.dynamic_index_in_dim(values, index, 0, keepdims=False)


def scatter_mp(values):
    return lax.psum_scatter(values, "mp", scatter_dimension=0, tiled=True).astype(F32)


def sliced_scores(qkv, kv_all, first, positions, scale, shift):
    raw = jnp.einsum("pqd,pkd->pqk", qkv[..., :HEAD], kv_all[..., :HEAD], preferred_element_type=F32)
    at = jnp.arange(kv_all.shape[1], dtype=jnp.int32)
    visible = (at >= first[..., None]) & (at <= positions[:, None])
    return jnp.where(visible, sigmoid_of(raw, scale, shift), 0.0)


def per_device(
    inputs,
    cotangent,
    doc_ids,
    gain_attn,
    w_query,
    w_key,
    w_value,
    w_out,
    gain_ffn,
    w_gate,
    w_up,
    w_down,
):
    dp_size = lax.axis_size("dp")
    mp_size = lax.axis_size("mp")
    micro_count, row_count, seq_count, width = inputs.shape
    slice_len = row_count * mp_size
    total_len = slice_len * dp_size
    rows_here = row_count * seq_count
    shift = math.log(total_len)
    scale = HEAD ** (-0.5)
    dp_at = lax.axis_index("dp")
    mp_at = lax.axis_index("mp")
    first_row = dp_at * slice_len
    positions = first_row + jnp.arange(slice_len, dtype=jnp.int32)
    head_width = w_query.shape[1]
    heads = head_width // HEAD
    hidden = w_gate.shape[1]
    pairs = seq_count * heads
    whole_pairs = pairs == dp_size
    cos_all, sin_all = full_tables(total_len)
    cos_slice, sin_slice = [
        lax.dynamic_slice_in_dim(table, first_row, slice_len, 0) for table in (cos_all, sin_all)
    ]

    def by_row(table):
        shaped = table.reshape(mp_size, 1, row_count, 1, HEAD)
        return jnp.broadcast_to(shaped, (mp_size, seq_count, row_count, 1, HEAD))

    def rotate(values, back=False):
        sine = -by_row(sin_slice) if back else by_row(sin_slice)
        return values * by_row(cos_slice) + swap_halves(values) * sine

    def to_pairs(values):
        shaped = values.reshape(mp_size, seq_count, row_count, heads, -1)
        return shaped.transpose(1, 3, 0, 2, 4).reshape(pairs, slice_len, -1)

    def from_pairs(values):
        shaped = values.reshape(seq_count, heads, mp_size, row_count, -1)
        return shaped.transpose(2, 0, 3, 1, 4).reshape(mp_size * rows_here, heads, -1)

    def to_rows(values):
        return jnp.swapaxes(values, 0, 1).reshape(rows_here, width)

    def from_rows(values):
        return jnp.swapaxes(values.reshape(seq_count, row_count, width), 0, 1)

    def gather_mp(values):
        return lax.all_gather(values, "mp", axis=0, tiled=True)

    gain_attn_grad = jnp.zeros((width,), F32)
    gain_ffn_grad = jnp.zeros((width,), F32)
    results = []
    input_grads = []
    kept = [[] for _ in range(9)]
    xs = [to_rows(inputs[m]) for m in range(micro_count)]
    cots = [to_rows(cotangent[m]) for m in range(micro_count)]
    micros = range(micro_count)
    if whole_pairs:
        stage = (heads, row_count, scale, shift)
        ids = [
            block_at(doc_ids[m], dp_at // heads).astype(F32).reshape(dp_size, 1, slice_len)
            for m in micros
        ]
        last = micro_count - 1

        def whole(blocks):
            return blocks.reshape(mp_size * rows_here, width)

        def scatter_dp(blocks):
            return lax.psum_scatter(blocks, "dp", scatter_dimension=0, tiled=True)[0].astype(F32)

        qkv_full, out_full, rows_one = begin(
            xs[0], gain_attn[None], w_query, w_key, w_value, w_out
        )
        cut = w_up.shape[0] // 2
        gathers = {
            0: (w_gate, 0), 1: (w_up[:cut], 0), 2: (w_up[cut:], 0), micro_count: (w_down, 1)
        }
        wide = []
        ones, qkvs, got, middles, lows, twos, mixtures = [whole(rows_one)], [], [], [], [], [], []
        for m in range(micro_count + 1):
            tail, head, norm, shard = (), (), (), ()
            if m:
                tail = (got[m - 1], out_full, xs[m - 1], gain_ffn[None])
            if m < micro_count:
                head = (ones[m], qkv_full, cos_slice, sin_slice, ids[m])
            if m < last:
                norm = (xs[m + 1], gain_attn[None])
            elif lows:
                shard = (lows[m - last],)
            if m == 0:
                shard += (cots[0],)
            outs = forward_stage(10 + m, tail, head, norm, shard, gathers.get(m, ()), *stage)
            if tail:
                (middle, low, mixture), outs = take(outs, 3)
                middles.append(middle)
                lows.append(low)
                mixtures.append(mixture)
            if head:
                (qkv, block), outs = take(outs, 2)
                qkvs.append(qkv)
                got.append(block)
            if norm or shard:
                (ones if m < last else twos).append(whole(outs[0]))
            if m == 0:
                portions = [whole(outs[1])]
            if m in gathers:
                wide.append(outs[-1])
        grads, low_grads, attns, projs, sums, gain_parts, later = [], [], [], [], [], [], []
        for m in micros:
            shard = (lows[len(twos)] if len(twos) < micro_count else low_grads[len(attns)],)
            if m < last:
                shard += (cots[m + 1],)
            defer = m < last
            grad, low, gain_part, *others = middle_part(
                30 + m, defer, twos[m], portions[m], wide, middles[m], cots[m], gain_ffn[None],
                shard, sums,
            )
            ys, (full, *others) = take(others, 2 if defer else 1)
            later.append((*ys, middles[m]) if defer else ys)
            (twos if len(twos) < micro_count else attns).append(whole(full))
            if m < last:
                portions.append(whole(others[0]))
            sums = others[-3:]
            grads.append(grad)
            low_grads.append(low)
            gain_parts.append(gain_part)
        sum_gate, sum_up, sum_down = [scatter_dp(blocks) for blocks in sums]
        old_qkv, old_out, attn_parts, finished = (), (), [], list(later)
        for m in range(micro_count + 1):
            tail, head, shard, final = (), (), (), ()
            if m:
                tail = (projs[m - 1], qkv_full, ones[m - 1], xs[m - 1], grads[m - 1], gain_attn[None])
            if m < micro_count:
                head = (attns[m], out_full, qkvs[m], ids[m], cos_all, sin_all, mixtures[m])
            else:
                rows = [sum(gain_parts), sum(attn_parts), jnp.zeros((6, width), F32)]
                final = (*old_out, jnp.concatenate(rows, axis=0))
            if len(attns) < micro_count:
                shard = (low_grads[len(attns)],)
            which = {0: 0, micro_count: 1}.get(m)
            extra = () if which is None else later[which]
            outs = backward_stage(
                20 + m, tail, old_qkv, head, () if final else old_out, final, extra, shard, *stage
            )
            if tail:
                (input_grad,), outs = take(outs, 1)
                input_grads.append(from_rows(input_grad))
            if tail and head:
                (new_qkv, gain_part), outs = take(outs, 2)
                old_qkv = (new_qkv,)
                attn_parts.append(gain_part)
            if head:
                (proj, new_out), outs = take(outs, 2)
                projs.append(proj)
                old_out = (new_out,)
            if extra:
                finished[which] = outs[3 * bool(final) : 3 * bool(final) + 1]
            if shard:
                attns.append(whole(outs[-1]))
        results = [from_rows(result[0]) for result in finished]
        sum_out, sum_qkv = (jnp.sum(blocks.astype(F32), axis=0) for blocks in outs[:2])
        gain_sums = (outs[2][1] / gain_attn, outs[2][0])
    else:
        qkv_full = lax.all_gather(
            jnp.concatenate([w_query, w_key, w_value], axis=1), "dp", axis=0, tiled=True
        )
        out_full = lax.all_gather(w_out, "dp", axis=1, tiled=True)
        gate_full = lax.all_gather(w_gate, "dp", axis=0, tiled=True)
        up_full = lax.all_gather(w_up, "dp", axis=0, tiled=True)
        down_full = lax.all_gather(w_down, "dp", axis=1, tiled=True)
        first_all = first_visible(doc_ids)
        normed = [
            (x.astype(F32) * norm_factor(x.astype(F32)) * gain_attn).astype(BF16) for x in xs
        ]
        for micro in micros:
            local_rows = xs[micro].astype(F32)
            local_cot = cots[micro]
            factor_one = norm_factor(local_rows)
            rows_one = gather_mp(normed[micro])
            portion = gather_mp(local_cot)
            projected = dot(rows_one, qkv_full).reshape(
                mp_size, seq_count, row_count, 3, heads, HEAD
            )
            packed = to_pairs(
                jnp.concatenate(
                    [
                        rotate(projected[:, :, :, 0]).astype(BF16),
                        rotate(projected[:, :, :, 1]).astype(BF16),
                        projected[:, :, :, 2].astype(BF16),
                    ],
                    axis=-1,
                )
            )
            kv_all = lax.all_gather(packed[..., HEAD:], "dp", axis=1, tiled=True)
            first = lax.dynamic_slice_in_dim(first_all[micro], first_row, slice_len, 1)
            first = jnp.repeat(first, heads, axis=0)
            weights = sliced_scores(packed, kv_all, first, positions, scale, shift)
            attended = jnp.einsum(
                "pqk,pkd->pqd", weights.astype(BF16), kv_all[..., HEAD:], preferred_element_type=F32
            ).astype(BF16)
            mixture = from_pairs(attended).reshape(mp_size * rows_here, head_width)
            middle = local_rows + scatter_mp(dot(mixture, out_full).astype(BF16))
            factor_two = norm_factor(middle)
            rows_two = gather_mp((middle * factor_two * gain_ffn).astype(BF16))
            y, dh, activated, gate_grad, up_grad = ffn(
                rows_two, portion, gate_full, up_full, down_full
            )
            results.append(from_rows((middle + scatter_mp(y)).astype(BF16)))
            middle_term, gain_part = norm_back(middle, factor_two, gain_ffn, scatter_mp(dh))
            gain_ffn_grad = gain_ffn_grad + gain_part
            middle_grad = local_cot.astype(F32) + middle_term
            attn_portion = gather_mp(middle_grad.astype(BF16))
            mix_grad = to_pairs(dot_nt(attn_portion, out_full).astype(BF16))
            sig = sliced_scores(packed, kv_all, first, positions, scale, shift)
            prob_grad = jnp.einsum(
                "pqd,pkd->pqk", mix_grad, kv_all[..., HEAD:], preferred_element_type=F32
            )
            score_grad = (prob_grad * sig * (1.0 - sig)).astype(BF16)
            dq = jnp.einsum("pqk,pkd->pqd", score_grad, kv_all[..., :HEAD], preferred_element_type=F32)
            dk = jnp.einsum("pqk,pqd->pkd", score_grad, packed[..., :HEAD], preferred_element_type=F32)
            dv = jnp.einsum("pqk,pqd->pkd", sig.astype(BF16), mix_grad, preferred_element_type=F32)
            dkv = lax.psum_scatter(
                jnp.concatenate([dk * scale, dv], axis=-1).astype(BF16), "dp", scatter_dimension=1, tiled=True
            ).astype(F32)
            back = from_pairs(jnp.concatenate([dq * scale, dkv], axis=-1))
            back = back.reshape(mp_size, seq_count, row_count, heads, 3 * HEAD)
            proj_grad = jnp.stack(
                [
                    rotate(back[..., :HEAD], True),
                    rotate(back[..., HEAD : 2 * HEAD], True),
                    back[..., 2 * HEAD :],
                ],
                axis=3,
            ).astype(BF16).reshape(mp_size * rows_here, 3 * head_width)
            partial_grad = dot_nt(proj_grad, qkv_full)
            gain_attn_grad = gain_attn_grad + jnp.sum(partial_grad * rows_one.astype(F32), axis=0)
            input_term, _ = norm_back(
                local_rows, factor_one, gain_attn, scatter_mp(partial_grad.astype(BF16))
            )
            input_grads.append(from_rows(middle_grad + input_term))
            for held, array in zip(
                kept,
                (rows_one, proj_grad, mixture, attn_portion, rows_two, gate_grad, up_grad, activated, portion),
            ):
                held.append(array)

        def scatter_dp(lefts, rights, left_blocked):
            (blocks,) = weight_grad(lefts, (rights,), left_blocked)
            return lax.psum_scatter(blocks, "dp", scatter_dimension=0, tiled=True)[0].astype(F32)

        ones, projs, mixtures, attns, twos, gates, ups, acts, portions = kept
        sum_gate = scatter_dp(twos, gates, True)
        sum_up = scatter_dp(twos, ups, True)
        sum_down = scatter_dp(acts, portions, False)
        sum_out = scatter_dp(mixtures, attns, False)
        sum_qkv = scatter_dp(ones, projs, True)
        gain_sums = lax.psum((gain_attn_grad / gain_attn, gain_ffn_grad), ("dp", "mp"))
    return (
        jnp.stack(results),
        jnp.stack(input_grads),
        gain_sums[0],
        sum_qkv[:, :head_width],
        sum_qkv[:, head_width : 2 * head_width],
        sum_qkv[:, 2 * head_width :],
        sum_out,
        gain_sums[1],
        sum_gate,
        sum_up,
        sum_down,
    )


def solution(mesh):
    tokens = P(None, ("dp", "mp"), None, None)
    column = P("dp", "mp")
    row = P("mp", "dp")
    return jax.shard_map(
        per_device,
        mesh=mesh,
        in_specs=(
            tokens, tokens, P(), P(), column, column, column, row, P(), column, column, row,
        ),
        out_specs=(
            tokens, tokens, P(), column, column, column, row, P(), column, column, row,
        ),
        check_vma=False,
    )
```

```python
import functools
import math

import jax
import jax.numpy as jnp
import numpy as np
from jax import lax
from jax.experimental import pallas as pl
from jax.experimental.pallas import tpu as pltpu
from jax.sharding import PartitionSpec as P

HEAD = 128
epsilon = 1e-05
rope_base = 10000.0
F32 = jnp.float32
BF16 = jnp.bfloat16


def full_tables(total):
    half_size = HEAD // 2
    exponents = -(np.arange(half_size, dtype=np.float32) * np.float32(2.0 / HEAD))
    inverse = np.power(np.float32(rope_base), exponents)
    angles = np.arange(total, dtype=np.float32)[:, None] * inverse[None, :]
    cosine, sine = np.cos(angles), np.sin(angles)
    return (
        jnp.asarray(np.concatenate([cosine, cosine], axis=-1)),
        jnp.asarray(np.concatenate([-sine, sine], axis=-1)),
    )


def swap_halves(values):
    half_size = HEAD // 2
    return jnp.concatenate([values[..., half_size:], values[..., :half_size]], axis=-1)


def dot(left, right):
    return jnp.dot(left, right, preferred_element_type=F32)


def dot_tn(left, right):
    return lax.dot_general(left, right, (((0,), (0,)), ((), ())), preferred_element_type=F32)


def dot_nt(left, right):
    return lax.dot_general(left, right, (((1,), (1,)), ((), ())), preferred_element_type=F32)


def norm_factor(values):
    return lax.rsqrt(jnp.mean(values * values, axis=-1, keepdims=True) + epsilon)


def norm_back(values, factor, gain, incoming):
    scaled = incoming * gain
    gain_term = jnp.sum(incoming * values * factor, axis=0)
    input_term = factor * scaled - values * factor**3 * jnp.mean(
        scaled * values, axis=-1, keepdims=True
    )
    return (input_term, gain_term)


def sigmoid_of(raw, scale, shift):
    return 1.0 / (1.0 + jnp.exp(shift - raw * scale))


def split_cores(core, values, rows_here):
    shaped = values.reshape(-1, 2, rows_here, values.shape[-1])
    first, second = shaped[:, 0], shaped[:, 1]
    is_first = core == 0
    return jnp.where(is_first, first, second), jnp.where(is_first, second, first)

MESH = pl.DeviceIdType.MESH


class Spot:
    def __init__(self):
        self.dp, self.mp = lax.axis_index("dp"), lax.axis_index("mp")
        self.dp_size, self.mp_size = lax.axis_size("dp"), lax.axis_size("mp")
        self.places = self.mp_size // 2
        self.place, self.core = lax.div(self.mp, 2), lax.rem(self.mp, 2)
        self.sibling = (self.dp, self.mp + 1 - 2 * self.core)
        self.right = (self.dp, self.mp + 2)
        self.left = (self.dp, self.mp - 2)
        self.has_right = self.place < self.places - 1
        self.has_left = self.place > 0

    def peer(self, step):
        return lax.rem(self.dp + step, self.dp_size)

    def enter(self, with_dp, with_mp):
        barrier = pltpu.get_barrier_semaphore()
        count = 0

        def greet(device):
            pl.semaphore_signal(barrier, inc=1, device_id=device, device_id_type=MESH)

        if with_mp:
            greet(self.sibling)
            pl.when(self.has_right)(lambda: greet(self.right))
            pl.when(self.has_left)(lambda: greet(self.left))
            count += 1 + self.has_right.astype(jnp.int32) + self.has_left.astype(jnp.int32)
        if with_dp:
            for step in range(1, self.dp_size):
                greet((self.peer(step), self.mp))
            count += self.dp_size - 1
        pl.semaphore_wait(barrier, count)


class Swap:
    def __init__(self, spot, source, target, send, receive):
        self.spot, self.source, self.target = spot, source, target
        self.send, self.receive = send, receive
        self.copies = [self.copy(step) for step in range(1, spot.dp_size)]

    def copy(self, step):
        spot = self.spot
        return pltpu.make_async_remote_copy(
            src_ref=self.source.at[spot.peer(step)],
            dst_ref=self.target.at[spot.dp],
            send_sem=self.send.at[step],
            recv_sem=self.receive.at[step],
            device_id=(spot.peer(step), spot.mp),
            device_id_type=MESH,
        )

    def start(self):
        for copy in self.copies:
            copy.start()
        self.keep()

    def keep(self):
        self.target[self.spot.dp] = self.source[self.spot.dp]

    def wait(self):
        for copy in self.copies:
            copy.wait()


class Gather:
    def __init__(self, spot, shard, window, sems):
        self.local = pltpu.make_async_copy(shard, window(spot.dp), sems.at[0, 0])
        self.copies = [
            pltpu.make_async_remote_copy(
                src_ref=shard,
                dst_ref=window(spot.dp),
                send_sem=sems.at[0, step],
                recv_sem=sems.at[1, step],
                device_id=(spot.peer(step), spot.mp),
                device_id_type=MESH,
            )
            for step in range(1, spot.dp_size)
        ]

    def start(self):
        for copy in self.copies:
            copy.start()
        self.local.start()

    def go_on(self):
        pass

    def wait(self):
        for copy in self.copies:
            copy.wait()
        self.local.wait()


def gather_of(spot, *arguments):
    return (RingGather if spot.dp_size == 4 else Gather)(spot, *arguments)


class RingGather:
    def __init__(self, spot, shard, window, sems):
        side = spot.dp + 1 - 2 * lax.rem(spot.dp, 2)
        across = spot.dp + 2 - 4 * lax.div(spot.dp, 2)

        def copy(source, index, kind, to, half=None):
            return pltpu.make_async_remote_copy(
                src_ref=source,
                dst_ref=window(index, half),
                send_sem=sems.at[0, kind],
                recv_sem=sems.at[1, kind],
                device_id=(to, spot.mp),
                device_id_type=MESH,
            )

        self.local = pltpu.make_async_copy(shard, window(spot.dp), sems.at[0, 4])
        self.to_side = copy(shard, spot.dp, 0, side)
        self.to_across = copy(shard, spot.dp, 1, across)
        self.on_across = copy(window(side, 0), side, 2, across, 0)
        self.on_side = copy(window(across, 1), across, 3, side, 1)

    def start(self):
        self.to_side.start()
        self.to_across.start()
        self.local.start()

    def go_on(self):
        self.to_side.wait_recv()
        self.on_across.start()
        self.to_across.wait_recv()
        self.on_side.start()

    def wait(self):
        self.to_side.wait_send()
        self.to_across.wait_send()
        self.on_across.wait()
        self.on_side.wait()
        self.local.wait()


class Spread:
    def __init__(self, spot, shard, full, sems):
        self.spot, self.shard, self.full, self.sems = spot, shard, full, sems
        self.local = pltpu.make_async_copy(shard, full.at[spot.mp], sems.at[6, 0])

    def copy(self, kind, device, p, source=None, core=None):
        at = 2 * p + (self.spot.core if core is None else core)
        return pltpu.make_async_remote_copy(
            src_ref=self.full.at[at] if source is None else source,
            dst_ref=self.full.at[at],
            send_sem=self.sems.at[kind, p],
            recv_sem=self.sems.at[kind + 1, p],
            device_id=device,
            device_id_type=MESH,
        )

    def rightward(self, p, source=None):
        return self.copy(0, self.spot.right, p, source)

    def leftward(self, p, source=None):
        return self.copy(2, self.spot.left, p, source)

    def across(self, p, source=None):
        return self.copy(4, self.spot.sibling, p, source)

    def begin(self):
        spot = self.spot
        pl.when(spot.has_right)(lambda: self.rightward(spot.place, self.shard).start())
        pl.when(spot.has_left)(lambda: self.leftward(spot.place, self.shard).start())
        self.across(spot.place, self.shard).start()
        self.local.start()

    def go_on(self, hop):
        spot = self.spot

        @pl.when(spot.place >= hop)
        def _():
            p = spot.place - hop
            self.rightward(p).wait_recv()
            pl.when(spot.has_right)(lambda: self.rightward(p).start())
            self.across(p).start()

        @pl.when(spot.place + hop < spot.places)
        def _():
            p = spot.place + hop
            self.leftward(p).wait_recv()
            pl.when(spot.has_left)(lambda: self.leftward(p).start())
            self.across(p).start()

    def finish(self):
        spot = self.spot
        for p in range(spot.places):
            self.copy(4, spot.sibling, p, core=1 - spot.core).wait_recv()
            self.across(p).wait_send()
            pl.when(spot.has_right & (spot.place >= p))(lambda: self.rightward(p).wait_send())
            pl.when(spot.has_left & (spot.place <= p))(lambda: self.leftward(p).wait_send())
        self.local.wait()


def spread_scratch(places):
    return [pltpu.SemaphoreType.DMA((7, places))]


class Ship(Swap):
    def __init__(self, spot, source, target, sems):
        super().__init__(spot, source, target, sems.at[0], sems.at[1])
        self.local = pltpu.make_async_copy(source.at[spot.dp], target.at[spot.dp], sems.at[0, 0])

    def start(self):
        for copy in self.copies:
            copy.start()
        self.local.start()

    def wait(self):
        super().wait()
        self.local.wait()


def window_of(full, axis, step, column=0, columns=None):
    def window(index, half=None):
        rows = step if axis == 0 else full.shape[0]
        first, count = (0, rows) if half is None else (half * (rows // 2), rows // 2)
        if axis == 1:
            return full.at[
                pl.ds(first, count), pl.ds(pl.multiple_of(index * step, step), step)
            ]
        along = pl.ds(pl.multiple_of(index * step + first, count), count)
        return full.at[along, pl.ds(column, full.shape[1] if columns is None else columns)]

    return window


def swap_scratch(size, *block):
    return [
        pltpu.VMEM((size, *block), BF16),
        pltpu.VMEM((size, *block), BF16),
        pltpu.SemaphoreType.DMA((size,)),
        pltpu.SemaphoreType.DMA((size,)),
    ]


def far_first(places):
    orders = []
    for place in range(places):
        right, left, order = list(range(places - 1, place, -1)), list(range(place)), []
        while right or left:
            order += right[:1] + left[:1]
            right, left = right[1:], left[1:]
        orders.append(order + [place])
    return orders


class Sum:
    def __init__(self, spot, mine, out, from_sibling, passed, sems):
        self.spot = spot
        self.mine, self.out = mine, out
        self.from_sibling, self.passed = from_sibling, passed
        self.sems = sems
        self.orders = far_first(spot.places)

    def copy(self, source, target, kind, t, device, to=None):
        return pltpu.make_async_remote_copy(
            src_ref=source.at[t],
            dst_ref=target.at[t if to is None else to],
            send_sem=self.sems.at[kind, t],
            recv_sem=self.sems.at[kind + 1, t],
            device_id=device,
            device_id_type=MESH,
        )

    def sibling(self, t):
        return self.copy(self.out, self.from_sibling, 0, t, self.spot.sibling)

    def rightward(self, t):
        return self.copy(self.mine, self.passed, 2, t, self.spot.right)

    def leftward(self, t, place):
        to = jnp.where(t == place, self.spot.places, t)
        return self.copy(self.mine, self.passed, 4, t, self.spot.left, to)

    def leftward_out(self, t):
        return self.leftward(t, self.spot.place - 1)

    def leftward_in(self, t):
        return self.leftward(t, self.spot.place)

    def term(self, s):
        chosen = 0
        for place, order in enumerate(self.orders):
            for at, t in enumerate(order):
                if t:
                    chosen = chosen + jnp.where((self.spot.place == place) & (s == at), t, 0)
        return chosen

    def add(self, t, arrived):
        self.mine[t] = (self.mine[t].astype(F32) + arrived.astype(F32)).astype(BF16)

    def absorb(self, t):
        self.sibling(t).wait_recv()
        self.add(t, self.from_sibling[t])

    def begin(self, s):
        spot = self.spot

        @pl.when((spot.place == 0) & (s < spot.places - 1))
        def _():
            t = spot.places - 1 - s
            self.absorb(t)
            self.rightward(t).start()

        @pl.when((spot.place == spot.places - 1) & (s < spot.places - 1))
        def _():
            self.absorb(s)
            self.leftward_out(s).start()

    def go_on(self, hop):
        spot = self.spot
        last = spot.places - 1

        @pl.when((spot.place > 0) & (spot.place <= hop))
        def _():
            t = last + spot.place - hop
            self.absorb(t)
            self.rightward(t).wait_recv()
            self.add(t, self.passed[t])
            self.rightward(t).start()

        @pl.when((spot.place < last) & (last - spot.place <= hop))
        def _():
            t = hop - last + spot.place
            self.absorb(t)
            self.leftward_in(t).wait_recv()
            self.add(t, self.passed[t])
            self.leftward_out(t).start()

    def finish(self):
        spot = self.spot
        t = spot.place
        self.absorb(t)

        @pl.when(spot.has_left)
        def _():
            self.rightward(t).wait_recv()
            self.add(t, self.passed[t])

        @pl.when(spot.has_right)
        def _():
            self.leftward_in(t).wait_recv()
            self.add(t, self.passed[spot.places])

        for t in range(spot.places):
            self.sibling(t).wait_send()
            pl.when(spot.place < t)(lambda: self.rightward(t).wait_send())
            pl.when(spot.place > t)(lambda: self.leftward_out(t).wait_send())
        return self.mine[spot.place].astype(F32)


def sum_scratch(places, rows_here, width):
    return [
        *[pltpu.VMEM((places, rows_here, width), BF16)] * 3,
        pltpu.VMEM((places + 1, rows_here, width), BF16),
        pltpu.SemaphoreType.DMA((6, places)),
    ]


def as_column(row):
    return jnp.broadcast_to(row, (HEAD, row.shape[1])).T[:, 0:1]


def attend_blocks(qkv, ids_ref, out, scale, shift):
    count, block = out.shape[:2]
    row_at = lax.broadcasted_iota(jnp.int32, (block, block), 0)
    col_at = lax.broadcasted_iota(jnp.int32, (block, block), 1)

    @pl.loop(0, count)
    def _(i):
        queries = qkv[i, :, 0:HEAD]
        ids = as_column(ids_ref[i])

        def add_block(j, acc, diagonal=False):
            sig = sigmoid_of(dot_nt(queries, qkv[j, :, HEAD : 2 * HEAD]), scale, shift)
            visible = ids == ids_ref[j]
            if diagonal:
                visible = visible & (col_at <= row_at)
            weights = jnp.where(visible, sig, 0.0).astype(BF16)
            return acc + dot(weights, qkv[j, :, 2 * HEAD :])

        acc = add_block(i, jnp.zeros((block, HEAD), F32), True)
        out[i] = lax.fori_loop(0, i, add_block, acc).astype(BF16)


def attend_back_blocks(
    spot, qkv, grad, ids_ref, cos_ref, sin_ref, out_q, out_kv, dq, made, scale, shift
):
    count, block = grad.shape[:2]
    col_at = lax.broadcasted_iota(jnp.int32, (block, block), 0)
    row_at = lax.broadcasted_iota(jnp.int32, (block, block), 1)
    dq[...] = jnp.zeros_like(dq)

    def unrotate(values, i):
        rows = pl.ds(pl.multiple_of(i * block, block), block)
        swapped = pltpu.roll(values, HEAD // 2, 1)
        return (values * cos_ref[rows, :] - swapped * sin_ref[rows, :]).astype(BF16)

    @pl.loop(0, count)
    def _(at):
        j = spot.peer(at + 1)
        keys = qkv[j, :, HEAD : 2 * HEAD]
        values = qkv[j, :, 2 * HEAD :]
        keys_t = keys.T
        ids = as_column(ids_ref[j])

        def add_block(i, sums, diagonal=False):
            dk, dv = sums
            queries, grads = qkv[i, :, 0:HEAD], grad[i]
            sig = sigmoid_of(dot_nt(keys, queries), scale, shift)
            visible = ids == ids_ref[i]
            if diagonal:
                visible = visible & (col_at <= row_at)
            sig = jnp.where(visible, sig, 0.0)
            prob_grad = dot_nt(values, grads)
            score_grad = (prob_grad * sig * (1.0 - sig)).astype(BF16)
            dq[i] += dot(keys_t, score_grad)
            return dk + dot(score_grad, queries), dv + dot(sig.astype(BF16), grads)

        zero = jnp.zeros((block, HEAD), F32)
        dk, dv = lax.fori_loop(j + 1, count, add_block, add_block(j, (zero, zero), True))
        out_kv[j, :, 0:HEAD] = unrotate(dk * scale, j)
        out_kv[j, :, HEAD:] = dv.astype(BF16)
        pl.when(at < count - 1)(lambda: made(at + 1))

    @pl.loop(0, count)
    def _(i):
        out_q[i] = unrotate(dq[i].T * scale, i)


def take(refs, count):
    return refs[:count], refs[count:]


class Loads:
    def __init__(self, pairs, sems):
        self.copies = [
            pltpu.make_async_copy(source, target, sems.at[i])
            for i, (source, target) in enumerate(pairs)
        ]
        for copy in self.copies:
            copy.start()

    def wait(self, *which):
        for i in which or range(len(self.copies)):
            self.copies[i].wait()


def lazy_scratch(*arrays):
    return [pltpu.VMEM(array.shape, array.dtype) for array in arrays] + [
        pltpu.SemaphoreType.DMA((len(arrays),))
    ]


def put_norm(x_ref, gain_ref, out_ref):
    x = x_ref[...].astype(F32)
    out_ref[...] = (x * norm_factor(x) * gain_ref[...]).astype(BF16)


def begin_kernel(
    x_ref, gain_ref, query, key, value, out, qkv_full, out_full, first_full,
    normed, sems, spread_sems,
):
    spot = Spot()
    spot.enter(True, True)
    rows, columns = query.shape
    jobs = [
        (shard, window_of(qkv_full, 0, rows, i * columns, columns))
        for i, shard in enumerate((query, key, value))
    ]
    jobs.append((out, window_of(out_full, 1, out.shape[1])))
    gathers = [
        gather_of(spot, shard, window, sems.at[i]) for i, (shard, window) in enumerate(jobs)
    ]
    for gather in gathers:
        gather.start()
    put_norm(x_ref, gain_ref, normed)
    spread = Spread(spot, normed, first_full, spread_sems)
    spread.begin()
    spread.go_on(1)
    for gather in gathers:
        gather.go_on()
    for hop in range(2, spot.places):
        spread.go_on(hop)
    for gather in gathers:
        gather.wait()
    spread.finish()


def forward_kernel(tail, head, norms, spreads, gather_axis, heads, toks, scale, shift, *refs):
    gathers = gather_axis is not None
    tail_in, refs = take(refs, 4 * tail)
    head_in, refs = take(refs, 5 * head)
    norm_in, refs = take(refs, 2 * norms)
    spread_in, refs = take(refs, spreads - norms)
    gather_in, refs = take(refs, gathers)
    tail_out, refs = take(refs, 3 * tail)
    head_out, refs = take(refs, 2 * head)
    spread_out, refs = take(refs, spreads)
    gather_out, refs = take(refs, gathers)
    sum_refs, refs = take(refs, 5 * tail)
    head_refs, refs = take(refs, 9 * head)
    normed, refs = take(refs, norms)
    lazy, refs = take(refs, 3 * head)
    if head:
        rows_ref, weight_ref, cos_ref, sin_ref, ids_ref = head_in
        loads = Loads(zip((rows_ref, weight_ref), lazy), lazy[2])
        rows_ref, weight_ref = lazy[:2]
    spot = Spot()
    spot.enter(head or gathers, tail or spreads)
    if norms:
        put_norm(*norm_in, *normed)
        spread_in = (*normed, *spread_in)
    moving = [Spread(spot, *refs) for refs in zip(spread_in, spread_out, refs)]
    for spread in moving:
        spread.begin()
    if gathers:
        window = window_of(gather_out[0], gather_axis, gather_in[0].shape[gather_axis])
        gather = gather_of(spot, gather_in[0], window, refs[-1])
        if not (tail and head):
            gather.start()

    if tail:
        got, out_weight, x_ref, gain_ref = tail_in
        middle_ref, normed_ref, mix_ref = tail_out
        pairs = got.shape[0]
        owner_rows = toks * (pairs // heads)
        for o in range(mix_ref.shape[0] // owner_rows):
            for p in range(pairs):
                s, h = p // heads, p % heads
                mix_ref[pl.ds(o * owner_rows + s * toks, toks), h * HEAD : (h + 1) * HEAD] = got[
                    p, pl.ds(o * toks, toks), :
                ]
        summed = Sum(spot, *sum_refs)
        chip_rows = 2 * owner_rows

        @pl.loop(0, spot.places)
        def _(s):
            t = summed.term(s)
            rows = pl.ds(pl.multiple_of(t * chip_rows, chip_rows), chip_rows)
            value = dot(mix_ref[rows, :], out_weight[...]).astype(BF16)
            keep, send = split_cores(spot.core, value, owner_rows)
            summed.mine[t] = keep[0]
            summed.out[t] = send[0]
            summed.sibling(t).start()

        @pl.loop(0, spot.places - 1)
        def _(s):
            summed.begin(s)

    if head:
        qkv_ref, got_ref = head_out
        made, paired, qkv, qkv_send, qkv_recv, part, got, part_send, part_recv = head_refs
        pairs = paired.shape[0]
        owner_rows = toks * (pairs // heads)
        step = made.shape[0]
        loads.wait()

        @pl.loop(0, rows_ref.shape[0] // step)
        def _(i):
            rows = pl.ds(pl.multiple_of(i * step, step), step)
            made[...] = dot(rows_ref[rows, :], weight_ref[...])
            for j in range(step // owner_rows):
                to = pl.ds(pl.multiple_of((i * (step // owner_rows) + j) * toks, toks), toks)
                cosine, sine = cos_ref[to, :], sin_ref[to, :]
                for p in range(pairs):
                    s, h = p // heads, p % heads
                    here = pl.ds(j * owner_rows + s * toks, toks)
                    for kind in range(3):
                        piece = made[here, pl.ds((kind * heads + h) * HEAD, HEAD)]
                        if kind < 2:
                            piece = piece * cosine + pltpu.roll(piece, HEAD // 2, 1) * sine
                        paired[p, to, kind * HEAD : (kind + 1) * HEAD] = piece.astype(BF16)

        swap = Swap(spot, paired, qkv, qkv_send, qkv_recv)
        swap.start()
    if gathers and tail and head:
        gather.start()
    for spread in moving:
        spread.go_on(1)
    if tail and spot.places > 2:
        summed.go_on(1)
    if head:
        swap.wait()
        attend_blocks(qkv, ids_ref, part, scale, shift)
        swap = Swap(spot, part, got, part_send, part_recv)
        swap.start()
    for hop in range(2, spot.places - 1):
        for spread in moving:
            spread.go_on(hop)
        if tail:
            summed.go_on(hop)
    if gathers:
        gather.go_on()
    if head:
        qkv_ref[...] = qkv[...]
        swap.wait()
        got_ref[...] = got[...]
    for spread in moving:
        if spot.places > 2:
            spread.go_on(spot.places - 1)
    if tail:
        middle = x_ref[...].astype(F32) + summed.finish()
        middle_ref[...] = middle
        normed_ref[...] = (middle * norm_factor(middle) * gain_ref[...]).astype(BF16)
    for spread in moving:
        spread.finish()
    if gathers:
        gather.wait()


def middle_kernel(
    first, defer, ships, spreads, owner_rows,
    middle_ref, local_cot_ref, gain_ref, rows_in, cot_in, gate_in, up_low, up_high, down_in,
    *refs,
):
    shards, refs = take(refs, spreads)
    before, refs = take(refs, 0 if first else 3)
    (grad_ref, low_ref, gain_grad_ref), refs = take(refs, 3)
    y_out, refs = take(refs, 2 if defer else 1)
    fulls, refs = take(refs, spreads)
    after, refs = take(refs, 3)
    ship_out, refs = take(refs, ships)
    (act_ref, dgate_ref, dup_ref, turned, new_rows, new_cols, old_rows, old_cols), refs = take(refs, 8)
    (rows_ref, cot_ref, gate_ref, up_ref, down_ref, load_sems, wide_sems), refs = take(refs, 7)
    sum_refs, refs = take(refs, 5)
    y_refs, refs = take(refs, 3 if defer else 5)
    ship_sems, refs = take(refs, ships)
    size, half = after[0].shape[0], up_low.shape[0] // after[0].shape[0]
    pairs = [(rows_in, rows_ref), (gate_in, gate_ref)]
    for e in range(size):
        for i, part in enumerate((up_low, up_high)):
            to = up_ref.at[pl.ds((2 * e + i) * half, half), :]
            pairs.append((part.at[pl.ds(e * half, half), :], to))
    pairs += [(cot_in, cot_ref), (down_in, down_ref)]
    loads = Loads(pairs, load_sems)
    spot = Spot()
    spot.enter(bool(ships), True)
    if ships:
        ship = Ship(spot, after[0], ship_out[0], ship_sems[0])
    summed = Sum(spot, *sum_refs)
    if defer:
        y_mine, y_send, y_sems = y_refs
        stores = [
            pltpu.make_async_copy(source, target, y_sems.at[i])
            for i, (source, target) in enumerate(zip((y_mine, y_send), y_out))
        ]
        sums = [summed]
    else:
        summed_y = Sum(spot, *y_refs)
        y_mine, y_send = summed_y.mine, summed_y.out
        sums = [summed, summed_y]
    moving = [Spread(spot, *refs) for refs in zip(shards, fulls, refs)]
    for spread in moving:
        spread.begin()
    hidden, width = gate_ref.shape[1], rows_ref.shape[1]
    chip_rows = 2 * owner_rows
    tile = min(256, hidden)
    blocks = after[0].shape[0]
    block = width // blocks
    new = (new_rows.at[0], new_rows.at[1], new_cols)
    old = (old_rows.at[0], old_rows.at[1], old_cols)

    def load(g, e):
        return pltpu.make_async_copy(before[g].at[e], old[g], wide_sems.at[0, g])

    def store(g, e):
        return pltpu.make_async_copy(new[g], after[g].at[e], wide_sems.at[1, g])

    if not first:
        for g in range(3):
            load(g, spot.peer(1)).start()
    loads.wait()

    @pl.loop(0, spot.places)
    def _(s):
        place = summed.term(s)
        rows = pl.ds(pl.multiple_of(place * chip_rows, chip_rows), chip_rows)

        @pl.loop(0, hidden // tile)
        def _(t):
            cols = pl.ds(pl.multiple_of(t * tile, tile), tile)
            gate = dot(rows_ref[rows, :], gate_ref[:, cols])
            up = dot(rows_ref[rows, :], up_ref[:, cols])
            sig = jax.nn.sigmoid(gate)
            silu = gate * sig
            act_ref[rows, cols] = (silu * up).astype(BF16)
            grad = dot_nt(cot_ref[rows, :], down_ref[cols, :])
            dgate_ref[rows, cols] = (grad * up * sig * (1.0 + gate * (1.0 - sig))).astype(BF16)
            dup_ref[rows, cols] = (grad * silu).astype(BF16)

        @pl.when(s > 0)
        def _():
            for each in sums:
                each.begin(s - 1)

        for hop in range(1, spot.places - 1):

            @pl.when(s == hop + 1)
            def _():
                for spread in moving:
                    spread.go_on(hop)
                for each in sums:
                    each.go_on(hop)

        @pl.loop(0, width // 256)
        def _(t):
            cols = pl.ds(pl.multiple_of(t * 256, 256), 256)
            value = dot(act_ref[rows, :], down_ref[:, cols])
            keep, send = split_cores(spot.core, value.astype(BF16), owner_rows)
            y_mine[place, :, cols] = keep[0]
            y_send[place, :, cols] = send[0]
            value = dot_nt(dgate_ref[rows, :], gate_ref[cols, :])
            value += dot_nt(dup_ref[rows, :], up_ref[cols, :])
            keep, send = split_cores(spot.core, value.astype(BF16), owner_rows)
            summed.mine[place, :, cols] = keep[0]
            summed.out[place, :, cols] = send[0]

        for each in sums:
            each.sibling(place).start()

    if defer:
        for copy in stores:
            copy.start()

    def send(i):
        if ships:
            pl.when(i < blocks - 1)(lambda: ship.copy(i + 1).start())
            pl.when(i == blocks - 1)(lambda: ship.local.start())

    def make(g, i, left, right, right_at, columns):
        e = spot.peer(i + 1)

        @pl.when(i > 0)
        def _():
            store(g, spot.peer(i)).wait()
            if g == 0:
                send(i - 1)

        if not first:
            load(g, e).wait()
        step = math.gcd(columns, 256)

        @pl.loop(0, columns // step)
        def _(t):
            cols = pl.ds(pl.multiple_of(t * step, step), step)
            total = dot(left[...], right[:, pl.ds(pl.multiple_of(right_at + t * step, step), step)])
            if not first:
                total += old[g][:, cols].astype(F32)
            new[g][:, cols] = total.astype(BF16)

        if not first:
            pl.when(i < blocks - 1)(lambda: load(g, spot.peer(i + 2)).start())
        store(g, e).start()

    @pl.loop(0, blocks)
    def _(i):
        left = turned.at[pl.ds(0, block), :]
        at = spot.peer(i + 1) * block
        left[...] = rows_ref[:, pl.ds(pl.multiple_of(at, block), block)].T
        make(0, i, left, dgate_ref, 0, hidden)
        make(1, i, left, dup_ref, 0, hidden)

    if ships:
        store(0, spot.dp).wait()
        send(blocks - 1)
    for spread in moving:
        spread.go_on(spot.places - 1)
    left = turned.at[pl.ds(0, hidden), :]
    left[...] = act_ref[...].T

    @pl.loop(0, blocks)
    def _(i):
        make(2, i, left, cot_ref, spot.peer(i + 1) * block, block)

    incoming = summed.finish()
    middle = middle_ref[...]
    term, gain_grad = norm_back(middle, norm_factor(middle), gain_ref[...], incoming)
    gain_grad_ref[...] = gain_grad[None]
    grad = local_cot_ref[...].astype(F32) + term
    grad_ref[...] = grad
    low_ref[...] = grad.astype(BF16)
    if defer:
        for copy in stores:
            copy.wait()
    else:
        y_out[0][...] = (middle + summed_y.finish()).astype(BF16)
    for spread in moving:
        spread.finish()
    for g in range(ships, 3):
        store(g, spot.dp).wait()
    if ships:
        ship.wait()


def add_grads(blocks, left, right, turned, before, after):
    size, rows, columns = after.shape

    @pl.loop(0, size)
    def _(e):
        if rows < left.shape[1]:
            turned[...] = left[:, pl.ds(pl.multiple_of(e * rows, rows), rows)].T
            total = dot(turned[...], right[...])
        else:

            @pl.when(e == 0)
            def _():
                turned[...] = left[...].T

            cut = pl.ds(pl.multiple_of(e * columns, columns), columns)
            total = dot(turned[...], right[:, cut])
        if before is not None:
            total += before[e].astype(F32)
        after[e] = total.astype(BF16)


def backward_kernel(
    tail, head, last, old_tail, old_head, extra, spreads, heads, toks, scale, shift, *refs
):
    tail_in, refs = take(refs, 6 * tail)
    old_qkv, refs = take(refs, old_tail)
    head_in, refs = take(refs, 7 * head)
    old_out, refs = take(refs, old_head)
    last_in, refs = take(refs, 2 * last)
    extra_in, refs = take(refs, 3 * extra)
    spread_in, refs = take(refs, spreads)
    tail_out, refs = take(refs, (1 if last else 3) * tail)
    head_out, refs = take(refs, 2 * head)
    last_out, refs = take(refs, 3 * last)
    extra_out, refs = take(refs, extra)
    spread_out, refs = take(refs, spreads)
    tail_refs, refs = take(refs, 7 * tail)
    head_refs, refs = take(refs, 14 * head)
    last_refs, refs = take(refs, 8 * last)
    extra_refs, refs = take(refs, 6 * extra)
    lazy_tail, refs = take(refs, 3 * tail)
    lazy_old, refs = take(refs, 2 * old_tail)
    lazy_head, refs = take(refs, 5 * head)
    if head:
        rows_ref, out_weight_ref, qkv, ids_ref, cos_ref, sin_ref, mix_ref = head_in
        loads_head = Loads(zip((rows_ref, qkv, cos_ref, sin_ref), lazy_head), lazy_head[4])
        rows_ref, qkv, cos_ref, sin_ref = lazy_head[:4]
    if tail:
        proj_ref, weight_ref, rows_one_ref, x_ref, grad_ref, gain_ref = tail_in
        loads_tail = Loads(zip((weight_ref, rows_one_ref), lazy_tail), lazy_tail[2])
        weight_ref, rows_one_ref = lazy_tail[:2]
    if extra:
        loads_extra = Loads(zip(extra_in[:2], extra_refs), extra_refs[5])
    before = None
    if old_tail:
        before = lazy_old[0]
        loads_old = Loads([(old_qkv[0], before)], lazy_old[1])
    spot = Spot()
    spot.enter(head or last, tail or spreads or extra)
    moving = [Spread(spot, *refs) for refs in zip(spread_in, spread_out, refs)]
    for spread in moving:
        spread.begin()
    if last:
        out_blocks, gains = last_in
        out_target, qkv_target, gain_sum = last_out
        new_qkv, own_gain, all_dp, dp_sum, all_mp, ship_sems, gain_sems, gain_spread_sems = last_refs
        ship_out = Ship(spot, out_blocks, out_target, ship_sems.at[0])
        ship_out.start()
    early, late = [], []
    if extra:
        summed_y = Sum(spot, *extra_refs[:5])
        loads_extra.wait()
        for t in range(spot.places):
            summed_y.sibling(t).start()
        late.append(summed_y)
    if head:
        head_proj_ref, new_out = head_out
        part, got, part_send, part_recv = head_refs[:4]
        made_q, got_q, q_send, q_recv, made_kv, got_kv, kv_send, kv_recv, dq, mix_turned = head_refs[4:]
        pairs = part.shape[0]
        owner_rows = toks * (pairs // heads)
        total = rows_ref.shape[0]
        step = min(512, total)
        loads_head.wait(0)

        @pl.loop(0, total // step)
        def _(i):
            rows = pl.ds(pl.multiple_of(i * step, step), step)
            made = dot_nt(rows_ref[rows, :], out_weight_ref[...]).astype(BF16)
            for j in range(step // owner_rows):
                to = pl.ds(pl.multiple_of((i * (step // owner_rows) + j) * toks, toks), toks)
                for p in range(pairs):
                    s, h = p // heads, p % heads
                    start = j * owner_rows + s * toks
                    part[p, to, :] = made[start : start + toks, h * HEAD : (h + 1) * HEAD]

        swap = Swap(spot, part, got, part_send, part_recv)
        swap.start()

    if extra:

        @pl.loop(0, spot.places - 1)
        def _(s):
            summed_y.begin(s)

    if tail:
        result_ref = tail_out[0]
        sum_refs, (turned, gain_acc) = take(tail_refs, 5)
        if not last:
            new_qkv, gain_acc = tail_out[1:]
        owner_rows = x_ref.shape[0]
        summed = Sum(spot, *sum_refs)
        early.append(summed)
        chip_rows = 2 * owner_rows
        gain_acc[...] = jnp.zeros_like(gain_acc)
        loads_tail.wait()

        @pl.loop(0, spot.places)
        def _(s):
            t = summed.term(s)
            rows = pl.ds(pl.multiple_of(t * chip_rows, chip_rows), chip_rows)
            value = dot_nt(proj_ref[rows, :], weight_ref[...])
            gain_acc[...] += jnp.sum(
                value * rows_one_ref[rows, :].astype(F32), axis=0, keepdims=True
            )
            keep, send = split_cores(spot.core, value.astype(BF16), owner_rows)
            summed.mine[t] = keep[0]
            summed.out[t] = send[0]
            summed.sibling(t).start()
            pl.when(s > 0)(lambda: summed.begin(s - 1))

        if last:
            own_gain[...] = gains[...]
            own_gain[1:2, :] += gain_acc[...]
            gain_dp = Gather(spot, own_gain, lambda index: all_dp.at[index], gain_sems)
            gain_dp.start()
    if last:
        if extra and spot.places > 2:
            late.remove(summed_y)
            summed_y.go_on(1)
        if old_tail:
            loads_old.wait()
        add_grads(spot.dp_size, rows_one_ref, proj_ref, turned, before, new_qkv)
        ship_qkv = Ship(spot, new_qkv, qkv_target, ship_sems.at[1])
        ship_qkv.start()
        if extra:
            for hop in range(2, spot.places - 1):
                summed_y.go_on(hop)
        gain_dp.wait()
        dp_sum[...] = jnp.sum(all_dp[...], axis=0)
        gain_mp = Spread(spot, dp_sum, all_mp, gain_spread_sems)
        gain_mp.begin()
        gain_mp.go_on(1)
    if head:
        add_grads(
            spot.dp_size, mix_ref, rows_ref, mix_turned, old_out[0] if old_head else None, new_out
        )
        swap.wait()
    for spread in moving:
        spread.go_on(1)
    if spot.places > 2:
        for each in early:
            each.go_on(1)
    if head:
        loads_head.wait(1, 2, 3)
        swap_kv = Swap(spot, made_kv, got_kv, kv_send, kv_recv)
        attend_back_blocks(
            spot, qkv, got, ids_ref, cos_ref, sin_ref, made_q, made_kv, dq,
            lambda step: swap_kv.copy(step).start(), scale, shift,
        )
        swap_kv.keep()
        swap = Swap(spot, made_q, got_q, q_send, q_recv)
        swap.start()
    if spot.places > 2:
        for each in late:
            each.go_on(1)
    for hop in range(2, spot.places - 1):
        if last:
            gain_mp.go_on(hop)
        for spread in moving:
            spread.go_on(hop)
        for each in early + late:
            each.go_on(hop)
    if tail and not last:
        if old_tail:
            loads_old.wait()
        add_grads(spot.dp_size, rows_one_ref, proj_ref, turned, before, new_qkv)
    if head:
        swap_kv.wait()
        swap.wait()
        for o in range(total // owner_rows):
            for p in range(pairs):
                s, h = p // heads, p % heads
                here, there = pl.ds(o * owner_rows + s * toks, toks), pl.ds(o * toks, toks)
                for kind in range(3):
                    piece = (
                        got_kv[p, there, (kind - 1) * HEAD : kind * HEAD] if kind else got_q[p, there, :]
                    )
                    head_proj_ref[
                        here, (kind * heads + h) * HEAD : (kind * heads + h + 1) * HEAD
                    ] = piece
    if spot.places > 2:
        for spread in moving:
            spread.go_on(spot.places - 1)
        if last:
            gain_mp.go_on(spot.places - 1)
    if tail:
        incoming = summed.finish()
        x = x_ref[...].astype(F32)
        term, _ = norm_back(x, norm_factor(x), gain_ref[...], incoming)
        result_ref[...] = grad_ref[...] + term
    if extra:
        extra_out[0][...] = (extra_in[2][...] + summed_y.finish()).astype(BF16)
    if last:
        gain_mp.finish()
        gain_sum[...] = jnp.sum(all_mp[...], axis=0)
        ship_out.wait()
        ship_qkv.wait()
    for spread in moving:
        spread.finish()


def ffn_kernel(
    rows_ref, cot_ref, gate_ref, up_ref, down_ref, y_ref, dh_ref, act_ref, dgate_ref, dup_ref
):
    hidden = gate_ref.shape[1]
    width = rows_ref.shape[1]
    tile = min(256, hidden)

    @pl.loop(0, hidden // tile)
    def _(t):
        cols = pl.ds(pl.multiple_of(t * tile, tile), tile)
        gate = dot(rows_ref[...], gate_ref[:, cols])
        up = dot(rows_ref[...], up_ref[:, cols])
        sig = jax.nn.sigmoid(gate)
        silu = gate * sig
        act_ref[:, cols] = (silu * up).astype(BF16)
        grad = dot_nt(cot_ref[...], down_ref[cols, :])
        dgate_ref[:, cols] = (grad * up * sig * (1.0 + gate * (1.0 - sig))).astype(BF16)
        dup_ref[:, cols] = (grad * silu).astype(BF16)

    @pl.loop(0, width // 256)
    def _(t):
        cols = pl.ds(pl.multiple_of(t * 256, 256), 256)
        y_ref[:, cols] = dot(act_ref[...], down_ref[:, cols]).astype(BF16)
        dh = dot_nt(dgate_ref[...], gate_ref[cols, :]) + dot_nt(dup_ref[...], up_ref[cols, :])
        dh_ref[:, cols] = dh.astype(BF16)


def grad_kernel(count, groups, left_blocked, *refs):
    lefts, refs = take(refs, count)
    rights, refs = take(refs, count * groups)
    out_refs, (turned,) = take(refs, groups)
    rows = lefts[0].shape[0]

    def turn():
        for m, left in enumerate(lefts):
            turned[:, m * rows : (m + 1) * rows] = left[...].T

    if left_blocked:
        turn()
    else:
        pl.when(pl.program_id(0) == 0)(turn)
    tile = math.gcd(out_refs[0].shape[2], 256)
    for g, out_ref in enumerate(out_refs):
        own = rights[g * count : (g + 1) * count]

        @pl.loop(0, out_ref.shape[2] // tile)
        def _(t):
            cols = pl.ds(pl.multiple_of(t * tile, tile), tile)
            total = dot(turned[:, :rows], own[0][:, cols])
            for m in range(1, count):
                total += dot(turned[:, m * rows : (m + 1) * rows], own[m][:, cols])
            out_ref[0, :, cols] = total.astype(BF16)


VMEM = pl.BlockSpec(memory_space=pltpu.VMEM)
ANY = pl.BlockSpec(memory_space=pl.ANY)


def cost(flops, nbytes):
    return pl.CostEstimate(flops=flops, bytes_accessed=nbytes, transcendentals=0)


def limits(mebibytes):
    return pltpu.CompilerParams(vmem_limit_bytes=mebibytes * 2**20)


def shape(*dims, dtype=BF16):
    return jax.ShapeDtypeStruct(dims, dtype)


def comm_params(collective_id, mebibytes):
    return pltpu.CompilerParams(
        collective_id=collective_id, has_side_effects=True, vmem_limit_bytes=mebibytes * 2**20
    )


def begin(x, gain, query, key, value, out):
    size, mp_size = lax.axis_size("dp"), lax.axis_size("mp")
    rows, columns = query.shape
    return pl.pallas_call(
        begin_kernel,
        out_shape=[
            shape(rows * size, 3 * columns),
            shape(out.shape[0], out.shape[1] * size),
            shape(mp_size, *x.shape),
        ],
        in_specs=[VMEM] * 2 + [ANY] * 4,
        out_specs=[ANY] * 3,
        scratch_shapes=[
            pltpu.VMEM(x.shape, BF16),
            pltpu.SemaphoreType.DMA((4, 2, size + 1)),
            *spread_scratch(mp_size // 2),
        ],
        compiler_params=comm_params(0, 16),
        cost_estimate=cost(0, 60 * 2**20),
        name="begin",
    )(x, gain, query, key, value, out)


def forward_stage(collective_id, tail, head, norm, shard, gather, heads, toks, scale, shift):
    size, mp_size = lax.axis_size("dp"), lax.axis_size("mp")
    out_shape, scratch = [], []
    if tail:
        blocks, _, x, _ = tail
        owner_rows, width = x.shape
        total = blocks.shape[1] * blocks.shape[0] // heads
        out_shape += [
            shape(owner_rows, width, dtype=F32),
            shape(owner_rows, width),
            shape(total, heads * HEAD),
        ]
        scratch += sum_scratch(mp_size // 2, owner_rows, width)
    if head:
        total, slice_len = head[0].shape[0], head[2].shape[0]
        out_shape += [shape(size, slice_len, 3 * HEAD), shape(size, slice_len, HEAD)]
        scratch += [
            pltpu.VMEM((min(512, total), 3 * heads * HEAD), F32),
            *swap_scratch(size, slice_len, 3 * HEAD),
            *swap_scratch(size, slice_len, HEAD),
        ]
    if norm:
        scratch.append(pltpu.VMEM(norm[0].shape, BF16))
    if head:
        scratch += lazy_scratch(*head[:2])
    here, spreads = len(out_shape), bool(norm) + len(shard)
    out_shape += [shape(mp_size, *array.shape) for array in (*norm[:1], *shard)]
    scratch += spread_scratch(mp_size // 2) * spreads
    axis = None
    if gather:
        weight, axis = gather
        dims = list(weight.shape)
        dims[axis] *= size
        out_shape.append(shape(*dims))
        scratch.append(pltpu.SemaphoreType.DMA((2, size + 1)))
    arrays = [*tail, *head, *norm]
    specs = [VMEM] * len(arrays)
    if head:
        specs[len(tail) : len(tail) + 2] = [ANY] * 2
    return pl.pallas_call(
        functools.partial(
            forward_kernel,
            bool(tail), bool(head), bool(norm), spreads, axis, heads, toks, scale, shift,
        ),
        out_shape=out_shape,
        in_specs=specs + [ANY] * (len(shard) + bool(gather)),
        out_specs=[VMEM] * here + [ANY] * (spreads + bool(gather)),
        scratch_shapes=scratch,
        compiler_params=comm_params(collective_id, 52),
        cost_estimate=cost(10**10, 100 * 2**20),
        name="forward_stage",
    )(*arrays, *shard, *gather[:1])


def middle_part(
    collective_id, defer, ships, rows, cot, weights, middle, local_cot, gain, shards, before
):
    total, width = rows.shape
    gate, _, _, down = weights
    hidden = gate.shape[1]
    size, mp_size = lax.axis_size("dp"), lax.axis_size("mp")
    places = mp_size // 2
    owner_rows = middle.shape[0]
    block = width // size
    wide = [shape(size, block, hidden)] * 2 + [shape(size, hidden, block)]
    half = shape(places, owner_rows, width)
    y_scratch = sum_scratch(places, owner_rows, width)
    if defer:
        y_scratch = [*[pltpu.VMEM(half.shape, BF16)] * 2, pltpu.SemaphoreType.DMA((2,))]
    return pl.pallas_call(
        functools.partial(middle_kernel, not before, defer, ships, len(shards), owner_rows),
        out_shape=[
            shape(owner_rows, width, dtype=F32),
            shape(owner_rows, width),
            shape(1, width, dtype=F32),
            *([half, half] if defer else [shape(owner_rows, width)]),
            *[shape(mp_size, *array.shape) for array in shards],
            *wide,
            *wide[:ships],
        ],
        in_specs=[VMEM] * 3 + [ANY] * (6 + len(shards) + len(before)),
        out_specs=[VMEM] * 3 + ([ANY] * 2 if defer else [VMEM]) + [ANY] * (len(shards) + 3 + ships),
        scratch_shapes=[
            *[pltpu.VMEM((total, hidden), BF16)] * 3,
            pltpu.VMEM((max(block, hidden), total), BF16),
            pltpu.VMEM((2, block, hidden), BF16),
            pltpu.VMEM((hidden, block), BF16),
            pltpu.VMEM((2, block, hidden), BF16),
            pltpu.VMEM((hidden, block), BF16),
            *[pltpu.VMEM(array.shape, BF16) for array in (rows, cot, gate, gate, down)],
            pltpu.SemaphoreType.DMA((4 + 2 * size,)),
            pltpu.SemaphoreType.DMA((2, 3)),
            *sum_scratch(places, owner_rows, width),
            *y_scratch,
            *[pltpu.SemaphoreType.DMA((2, size))] * ships,
            *spread_scratch(places) * len(shards),
        ],
        compiler_params=comm_params(collective_id, 61),
        cost_estimate=cost(18 * total * width * hidden, 60 * 2**20),
        name="middle_part",
    )(middle, local_cot, gain, rows, cot, *weights, *shards, *before)


def backward_stage(
    collective_id, tail, old_qkv, head, old_out, last, extra, shard, heads, toks, scale, shift
):
    size, mp_size = lax.axis_size("dp"), lax.axis_size("mp")
    places = mp_size // 2
    out_shape, scratch = [], []
    if tail:
        owner_rows, width = tail[3].shape
        out_shape.append(shape(owner_rows, width, dtype=F32))
        total = tail[0].shape[0]
        wide = shape(size, width // size, 3 * heads * HEAD)
        if not last:
            out_shape += [wide, shape(1, width, dtype=F32)]
        scratch += [
            *sum_scratch(places, owner_rows, width),
            pltpu.VMEM((width // size, total), BF16),
            pltpu.VMEM((1, width), F32),
        ]
    if head:
        (total, width), slice_len = head[0].shape, head[2].shape[1]
        out_shape.append(shape(total, 3 * heads * HEAD))
        out_shape.append(shape(size, heads * HEAD, width // size))
        scratch += [
            *swap_scratch(size, slice_len, HEAD),
            *swap_scratch(size, slice_len, HEAD),
            *swap_scratch(size, slice_len, 2 * HEAD),
            pltpu.VMEM((size, HEAD, slice_len), F32),
            pltpu.VMEM((heads * HEAD, total), BF16),
        ]
    here = len(out_shape)
    if last:
        gains = last[1].shape
        out_shape += [shape(*last[0].shape), wide]
        scratch += [
            pltpu.VMEM(wide.shape, BF16),
            pltpu.VMEM(gains, F32),
            pltpu.VMEM((size, *gains), F32),
            pltpu.VMEM(gains, F32),
            pltpu.VMEM((mp_size, *gains), F32),
            pltpu.SemaphoreType.DMA((2, 2, size)),
            pltpu.SemaphoreType.DMA((2, size)),
            *spread_scratch(places),
        ]
        out_shape.append(shape(*gains, dtype=F32))
    if extra:
        out_shape.append(shape(*extra[2].shape))
        scratch += sum_scratch(places, *extra[2].shape)
        scratch.append(pltpu.SemaphoreType.DMA((2,)))
    if tail:
        scratch += lazy_scratch(tail[1], tail[2])
    scratch += lazy_scratch(*old_qkv) if old_qkv else []
    if head:
        scratch += lazy_scratch(head[0], head[2], head[4], head[5])
    scratch += spread_scratch(places) * len(shard)
    out_shape += [shape(mp_size, *array.shape) for array in shard]
    arrays = [*tail, *old_qkv, *head, *old_out]
    tail_specs = [VMEM, ANY, ANY, VMEM, VMEM, VMEM] if tail else []
    head_specs = [ANY, VMEM, ANY, VMEM, ANY, ANY, VMEM] if head else []
    specs = [*tail_specs, *[ANY] * len(old_qkv), *head_specs, *[VMEM] * len(old_out)]
    last_specs, last_outs = ([ANY, VMEM], [ANY, ANY, VMEM]) if last else ([], [])
    extra_specs, extra_outs = ([ANY, ANY, VMEM], [VMEM]) if extra else ([], [])
    return pl.pallas_call(
        functools.partial(
            backward_kernel, bool(tail), bool(head), bool(last), len(old_qkv), len(old_out),
            bool(extra), len(shard), heads, toks, scale, shift,
        ),
        out_shape=out_shape,
        in_specs=specs + last_specs + extra_specs + [ANY] * len(shard),
        out_specs=[VMEM] * here + last_outs + extra_outs + [ANY] * len(shard),
        scratch_shapes=scratch,
        compiler_params=comm_params(collective_id, 58),
        cost_estimate=cost(10**10, 100 * 2**20),
        name="backward_stage",
    )(*arrays, *last, *extra, *shard)


def ffn(rows, cot, gate, up, down):
    total, width = rows.shape
    hidden = gate.shape[1]
    step = min(512, total)
    by_rows = pl.BlockSpec((step, width), lambda i: (i, 0))
    by_hidden = pl.BlockSpec((step, hidden), lambda i: (i, 0))
    held = lambda array: pl.BlockSpec(array.shape, lambda i: (0, 0), pipeline_mode=pl.Buffered(1))
    return pl.pallas_call(
        ffn_kernel,
        grid=(total // step,),
        out_shape=[shape(total, width)] * 2 + [shape(total, hidden)] * 3,
        in_specs=[by_rows, by_rows, held(gate), held(up), held(down)],
        out_specs=[by_rows] * 2 + [by_hidden] * 3,
        compiler_params=limits(56),
        cost_estimate=cost(12 * total * width * hidden, 34 * 2**20),
        name="ffn",
    )(rows, cot, gate, up, down)


def weight_grad(lefts, groups, left_blocked):
    count = len(lefts)
    size = lax.axis_size("dp")
    rows = lefts[0].shape[0]
    m, n = lefts[0].shape[1], groups[0][0].shape[1]
    moving = lambda width: pl.BlockSpec((rows, width // size), lambda e: (0, e))
    fixed = lambda width: pl.BlockSpec(
        (rows, width), lambda e: (0, 0), pipeline_mode=pl.Buffered(1)
    )
    left_spec = moving(m) if left_blocked else fixed(m)
    right_spec = fixed(n) if left_blocked else moving(n)
    out = (m // size, n) if left_blocked else (m, n // size)
    return pl.pallas_call(
        functools.partial(grad_kernel, count, len(groups), left_blocked),
        grid=(size,),
        in_specs=[left_spec] * count + [right_spec] * (count * len(groups)),
        out_specs=[pl.BlockSpec((1, *out), lambda e: (e, 0, 0))] * len(groups),
        out_shape=[shape(size, *out)] * len(groups),
        scratch_shapes=[pltpu.VMEM((out[0], count * rows), BF16)],
        compiler_params=limits(52),
        cost_estimate=cost(2 * count * rows * m * n * len(groups), 24 * 2**20),
        name="weight_grad",
    )(*lefts, *(right for group in groups for right in group))


def first_visible(ids):
    at = jnp.arange(ids.shape[-1], dtype=jnp.int32)
    starts = jnp.concatenate([jnp.ones_like(ids[..., :1], jnp.bool_), ids[..., 1:] != ids[..., :-1]], axis=-1)
    return lax.cummax(jnp.where(starts, at, 0), axis=ids.ndim - 1)


def block_at(values, index):
    return lax.dynamic_index_in_dim(values, index, 0, keepdims=False)


def scatter_mp(values):
    return lax.psum_scatter(values, "mp", scatter_dimension=0, tiled=True).astype(F32)


def sliced_scores(qkv, kv_all, first, positions, scale, shift):
    raw = jnp.einsum("pqd,pkd->pqk", qkv[..., :HEAD], kv_all[..., :HEAD], preferred_element_type=F32)
    at = jnp.arange(kv_all.shape[1], dtype=jnp.int32)
    visible = (at >= first[..., None]) & (at <= positions[:, None])
    return jnp.where(visible, sigmoid_of(raw, scale, shift), 0.0)


def per_device(
    inputs,
    cotangent,
    doc_ids,
    gain_attn,
    w_query,
    w_key,
    w_value,
    w_out,
    gain_ffn,
    w_gate,
    w_up,
    w_down,
):
    dp_size = lax.axis_size("dp")
    mp_size = lax.axis_size("mp")
    micro_count, row_count, seq_count, width = inputs.shape
    slice_len = row_count * mp_size
    total_len = slice_len * dp_size
    rows_here = row_count * seq_count
    shift = math.log(total_len)
    scale = HEAD ** (-0.5)
    dp_at = lax.axis_index("dp")
    mp_at = lax.axis_index("mp")
    first_row = dp_at * slice_len
    positions = first_row + jnp.arange(slice_len, dtype=jnp.int32)
    head_width = w_query.shape[1]
    heads = head_width // HEAD
    hidden = w_gate.shape[1]
    pairs = seq_count * heads
    whole_pairs = pairs == dp_size
    cos_all, sin_all = full_tables(total_len)
    cos_slice, sin_slice = [
        lax.dynamic_slice_in_dim(table, first_row, slice_len, 0) for table in (cos_all, sin_all)
    ]

    def by_row(table):
        shaped = table.reshape(mp_size, 1, row_count, 1, HEAD)
        return jnp.broadcast_to(shaped, (mp_size, seq_count, row_count, 1, HEAD))

    def rotate(values, back=False):
        sine = -by_row(sin_slice) if back else by_row(sin_slice)
        return values * by_row(cos_slice) + swap_halves(values) * sine

    def to_pairs(values):
        shaped = values.reshape(mp_size, seq_count, row_count, heads, -1)
        return shaped.transpose(1, 3, 0, 2, 4).reshape(pairs, slice_len, -1)

    def from_pairs(values):
        shaped = values.reshape(seq_count, heads, mp_size, row_count, -1)
        return shaped.transpose(2, 0, 3, 1, 4).reshape(mp_size * rows_here, heads, -1)

    def to_rows(values):
        return jnp.swapaxes(values, 0, 1).reshape(rows_here, width)

    def from_rows(values):
        return jnp.swapaxes(values.reshape(seq_count, row_count, width), 0, 1)

    def gather_mp(values):
        return lax.all_gather(values, "mp", axis=0, tiled=True)

    gain_attn_grad = jnp.zeros((width,), F32)
    gain_ffn_grad = jnp.zeros((width,), F32)
    results = []
    input_grads = []
    kept = [[] for _ in range(9)]
    xs = [to_rows(inputs[m]) for m in range(micro_count)]
    cots = [to_rows(cotangent[m]) for m in range(micro_count)]
    micros = range(micro_count)
    if whole_pairs:
        stage = (heads, row_count, scale, shift)
        ids = [
            block_at(doc_ids[m], dp_at // heads).astype(F32).reshape(dp_size, 1, slice_len)
            for m in micros
        ]
        last = micro_count - 1

        def whole(blocks):
            return blocks.reshape(mp_size * rows_here, width)

        def scatter_dp(blocks):
            return lax.psum_scatter(blocks, "dp", scatter_dimension=0, tiled=True)[0].astype(F32)

        qkv_full, out_full, rows_one = begin(
            xs[0], gain_attn[None], w_query, w_key, w_value, w_out
        )
        cut = w_up.shape[0] // 2
        gathers = {
            0: (w_gate, 0), 1: (w_up[:cut], 0), 2: (w_up[cut:], 0), micro_count: (w_down, 1)
        }
        wide = []
        ones, qkvs, got, middles, lows, twos, mixtures = [whole(rows_one)], [], [], [], [], [], []
        for m in range(micro_count + 1):
            tail, head, norm, shard = (), (), (), ()
            if m:
                tail = (got[m - 1], out_full, xs[m - 1], gain_ffn[None])
            if m < micro_count:
                head = (ones[m], qkv_full, cos_slice, sin_slice, ids[m])
            if m < last:
                norm = (xs[m + 1], gain_attn[None])
            elif lows:
                shard = (lows[m - last],)
            if m == 0:
                shard += (cots[0],)
            outs = forward_stage(10 + m, tail, head, norm, shard, gathers.get(m, ()), *stage)
            if tail:
                (middle, low, mixture), outs = take(outs, 3)
                middles.append(middle)
                lows.append(low)
                mixtures.append(mixture)
            if head:
                (qkv, block), outs = take(outs, 2)
                qkvs.append(qkv)
                got.append(block)
            if norm or shard:
                (ones if m < last else twos).append(whole(outs[0]))
            if m == 0:
                portions = [whole(outs[1])]
            if m in gathers:
                wide.append(outs[-1])
        grads, low_grads, attns, projs, sums, gain_parts, later = [], [], [], [], [], [], []
        for m in micros:
            shard = (lows[len(twos)] if len(twos) < micro_count else low_grads[len(attns)],)
            if m < last:
                shard += (cots[m + 1],)
            defer = m < last
            grad, low, gain_part, *others = middle_part(
                30 + m, defer, int(m == last), twos[m], portions[m], wide, middles[m], cots[m], gain_ffn[None],
                shard, sums,
            )
            ys, (full, *others) = take(others, 2 if defer else 1)
            later.append((*ys, middles[m]) if defer else ys)
            (twos if len(twos) < micro_count else attns).append(whole(full))
            if m < last:
                portions.append(whole(others[0]))
            sums, gate_blocks = take(others[m < last :], 3)
            grads.append(grad)
            low_grads.append(low)
            gain_parts.append(gain_part)
        sum_up, sum_down = [scatter_dp(blocks) for blocks in sums[1:]]
        sum_gate = jnp.sum(gate_blocks[0].astype(F32), axis=0)
        old_qkv, old_out, attn_parts, finished = (), (), [], list(later)
        for m in range(micro_count + 1):
            tail, head, shard, final = (), (), (), ()
            if m:
                tail = (projs[m - 1], qkv_full, ones[m - 1], xs[m - 1], grads[m - 1], gain_attn[None])
            if m < micro_count:
                head = (attns[m], out_full, qkvs[m], ids[m], cos_all, sin_all, mixtures[m])
            else:
                rows = [sum(gain_parts), sum(attn_parts), jnp.zeros((6, width), F32)]
                final = (*old_out, jnp.concatenate(rows, axis=0))
            if len(attns) < micro_count:
                shard = (low_grads[len(attns)],)
            which = {0: 0, micro_count: 1}.get(m)
            extra = () if which is None else later[which]
            outs = backward_stage(
                20 + m, tail, old_qkv, head, () if final else old_out, final, extra, shard, *stage
            )
            if tail:
                (input_grad,), outs = take(outs, 1)
                input_grads.append(from_rows(input_grad))
            if tail and head:
                (new_qkv, gain_part), outs = take(outs, 2)
                old_qkv = (new_qkv,)
                attn_parts.append(gain_part)
            if head:
                (proj, new_out), outs = take(outs, 2)
                projs.append(proj)
                old_out = (new_out,)
            if extra:
                finished[which] = outs[3 * bool(final) : 3 * bool(final) + 1]
            if shard:
                attns.append(whole(outs[-1]))
        results = [from_rows(result[0]) for result in finished]
        sum_out, sum_qkv = (jnp.sum(blocks.astype(F32), axis=0) for blocks in outs[:2])
        gain_sums = (outs[2][1] / gain_attn, outs[2][0])
    else:
        qkv_full = lax.all_gather(
            jnp.concatenate([w_query, w_key, w_value], axis=1), "dp", axis=0, tiled=True
        )
        out_full = lax.all_gather(w_out, "dp", axis=1, tiled=True)
        gate_full = lax.all_gather(w_gate, "dp", axis=0, tiled=True)
        up_full = lax.all_gather(w_up, "dp", axis=0, tiled=True)
        down_full = lax.all_gather(w_down, "dp", axis=1, tiled=True)
        first_all = first_visible(doc_ids)
        normed = [
            (x.astype(F32) * norm_factor(x.astype(F32)) * gain_attn).astype(BF16) for x in xs
        ]
        for micro in micros:
            local_rows = xs[micro].astype(F32)
            local_cot = cots[micro]
            factor_one = norm_factor(local_rows)
            rows_one = gather_mp(normed[micro])
            portion = gather_mp(local_cot)
            projected = dot(rows_one, qkv_full).reshape(
                mp_size, seq_count, row_count, 3, heads, HEAD
            )
            packed = to_pairs(
                jnp.concatenate(
                    [
                        rotate(projected[:, :, :, 0]).astype(BF16),
                        rotate(projected[:, :, :, 1]).astype(BF16),
                        projected[:, :, :, 2].astype(BF16),
                    ],
                    axis=-1,
                )
            )
            kv_all = lax.all_gather(packed[..., HEAD:], "dp", axis=1, tiled=True)
            first = lax.dynamic_slice_in_dim(first_all[micro], first_row, slice_len, 1)
            first = jnp.repeat(first, heads, axis=0)
            weights = sliced_scores(packed, kv_all, first, positions, scale, shift)
            attended = jnp.einsum(
                "pqk,pkd->pqd", weights.astype(BF16), kv_all[..., HEAD:], preferred_element_type=F32
            ).astype(BF16)
            mixture = from_pairs(attended).reshape(mp_size * rows_here, head_width)
            middle = local_rows + scatter_mp(dot(mixture, out_full).astype(BF16))
            factor_two = norm_factor(middle)
            rows_two = gather_mp((middle * factor_two * gain_ffn).astype(BF16))
            y, dh, activated, gate_grad, up_grad = ffn(
                rows_two, portion, gate_full, up_full, down_full
            )
            results.append(from_rows((middle + scatter_mp(y)).astype(BF16)))
            middle_term, gain_part = norm_back(middle, factor_two, gain_ffn, scatter_mp(dh))
            gain_ffn_grad = gain_ffn_grad + gain_part
            middle_grad = local_cot.astype(F32) + middle_term
            attn_portion = gather_mp(middle_grad.astype(BF16))
            mix_grad = to_pairs(dot_nt(attn_portion, out_full).astype(BF16))
            sig = sliced_scores(packed, kv_all, first, positions, scale, shift)
            prob_grad = jnp.einsum(
                "pqd,pkd->pqk", mix_grad, kv_all[..., HEAD:], preferred_element_type=F32
            )
            score_grad = (prob_grad * sig * (1.0 - sig)).astype(BF16)
            dq = jnp.einsum("pqk,pkd->pqd", score_grad, kv_all[..., :HEAD], preferred_element_type=F32)
            dk = jnp.einsum("pqk,pqd->pkd", score_grad, packed[..., :HEAD], preferred_element_type=F32)
            dv = jnp.einsum("pqk,pqd->pkd", sig.astype(BF16), mix_grad, preferred_element_type=F32)
            dkv = lax.psum_scatter(
                jnp.concatenate([dk * scale, dv], axis=-1).astype(BF16), "dp", scatter_dimension=1, tiled=True
            ).astype(F32)
            back = from_pairs(jnp.concatenate([dq * scale, dkv], axis=-1))
            back = back.reshape(mp_size, seq_count, row_count, heads, 3 * HEAD)
            proj_grad = jnp.stack(
                [
                    rotate(back[..., :HEAD], True),
                    rotate(back[..., HEAD : 2 * HEAD], True),
                    back[..., 2 * HEAD :],
                ],
                axis=3,
            ).astype(BF16).reshape(mp_size * rows_here, 3 * head_width)
            partial_grad = dot_nt(proj_grad, qkv_full)
            gain_attn_grad = gain_attn_grad + jnp.sum(partial_grad * rows_one.astype(F32), axis=0)
            input_term, _ = norm_back(
                local_rows, factor_one, gain_attn, scatter_mp(partial_grad.astype(BF16))
            )
            input_grads.append(from_rows(middle_grad + input_term))
            for held, array in zip(
                kept,
                (rows_one, proj_grad, mixture, attn_portion, rows_two, gate_grad, up_grad, activated, portion),
            ):
                held.append(array)

        def scatter_dp(lefts, rights, left_blocked):
            (blocks,) = weight_grad(lefts, (rights,), left_blocked)
            return lax.psum_scatter(blocks, "dp", scatter_dimension=0, tiled=True)[0].astype(F32)

        ones, projs, mixtures, attns, twos, gates, ups, acts, portions = kept
        sum_gate = scatter_dp(twos, gates, True)
        sum_up = scatter_dp(twos, ups, True)
        sum_down = scatter_dp(acts, portions, False)
        sum_out = scatter_dp(mixtures, attns, False)
        sum_qkv = scatter_dp(ones, projs, True)
        gain_sums = lax.psum((gain_attn_grad / gain_attn, gain_ffn_grad), ("dp", "mp"))
    return (
        jnp.stack(results),
        jnp.stack(input_grads),
        gain_sums[0],
        sum_qkv[:, :head_width],
        sum_qkv[:, head_width : 2 * head_width],
        sum_qkv[:, 2 * head_width :],
        sum_out,
        gain_sums[1],
        sum_gate,
        sum_up,
        sum_down,
    )


def solution(mesh):
    tokens = P(None, ("dp", "mp"), None, None)
    column = P("dp", "mp")
    row = P("mp", "dp")
    return jax.shard_map(
        per_device,
        mesh=mesh,
        in_specs=(
            tokens, tokens, P(), P(), column, column, column, row, P(), column, column, row,
        ),
        out_specs=(
            tokens, tokens, P(), column, column, column, row, P(), column, column, row,
        ),
        check_vma=False,
    )
```

```python
import functools
import math

import jax
import jax.numpy as jnp
import numpy as np
from jax import lax
from jax.experimental import pallas as pl
from jax.experimental.pallas import tpu as pltpu
from jax.sharding import PartitionSpec as P

HEAD = 128
epsilon = 1e-05
rope_base = 10000.0
F32 = jnp.float32
BF16 = jnp.bfloat16


def full_tables(total):
    half_size = HEAD // 2
    exponents = -(np.arange(half_size, dtype=np.float32) * np.float32(2.0 / HEAD))
    inverse = np.power(np.float32(rope_base), exponents)
    angles = np.arange(total, dtype=np.float32)[:, None] * inverse[None, :]
    cosine, sine = np.cos(angles), np.sin(angles)
    return (
        jnp.asarray(np.concatenate([cosine, cosine], axis=-1)),
        jnp.asarray(np.concatenate([-sine, sine], axis=-1)),
    )


def swap_halves(values):
    half_size = HEAD // 2
    return jnp.concatenate([values[..., half_size:], values[..., :half_size]], axis=-1)


def dot(left, right):
    return jnp.dot(left, right, preferred_element_type=F32)


def dot_tn(left, right):
    return lax.dot_general(left, right, (((0,), (0,)), ((), ())), preferred_element_type=F32)


def dot_nt(left, right):
    return lax.dot_general(left, right, (((1,), (1,)), ((), ())), preferred_element_type=F32)


def norm_factor(values):
    return lax.rsqrt(jnp.mean(values * values, axis=-1, keepdims=True) + epsilon)


def norm_back(values, factor, gain, incoming):
    scaled = incoming * gain
    gain_term = jnp.sum(incoming * values * factor, axis=0)
    input_term = factor * scaled - values * factor**3 * jnp.mean(
        scaled * values, axis=-1, keepdims=True
    )
    return (input_term, gain_term)


def sigmoid_of(raw, scale, shift):
    return 1.0 / (1.0 + jnp.exp(shift - raw * scale))


def split_cores(core, values, rows_here):
    shaped = values.reshape(-1, 2, rows_here, values.shape[-1])
    first, second = shaped[:, 0], shaped[:, 1]
    is_first = core == 0
    return jnp.where(is_first, first, second), jnp.where(is_first, second, first)

MESH = pl.DeviceIdType.MESH


class Spot:
    def __init__(self):
        self.dp, self.mp = lax.axis_index("dp"), lax.axis_index("mp")
        self.dp_size, self.mp_size = lax.axis_size("dp"), lax.axis_size("mp")
        self.places = self.mp_size // 2
        self.place, self.core = lax.div(self.mp, 2), lax.rem(self.mp, 2)
        self.sibling = (self.dp, self.mp + 1 - 2 * self.core)
        self.right = (self.dp, self.mp + 2)
        self.left = (self.dp, self.mp - 2)
        self.has_right = self.place < self.places - 1
        self.has_left = self.place > 0

    def peer(self, step):
        return lax.rem(self.dp + step, self.dp_size)

    def enter(self, with_dp, with_mp):
        barrier = pltpu.get_barrier_semaphore()
        count = 0

        def greet(device):
            pl.semaphore_signal(barrier, inc=1, device_id=device, device_id_type=MESH)

        if with_mp:
            greet(self.sibling)
            pl.when(self.has_right)(lambda: greet(self.right))
            pl.when(self.has_left)(lambda: greet(self.left))
            count += 1 + self.has_right.astype(jnp.int32) + self.has_left.astype(jnp.int32)
        if with_dp:
            for step in range(1, self.dp_size):
                greet((self.peer(step), self.mp))
            count += self.dp_size - 1
        pl.semaphore_wait(barrier, count)


class Swap:
    def __init__(self, spot, source, target, send, receive):
        self.spot, self.source, self.target = spot, source, target
        self.send, self.receive = send, receive
        self.copies = [self.copy(step) for step in range(1, spot.dp_size)]

    def copy(self, step):
        spot = self.spot
        return pltpu.make_async_remote_copy(
            src_ref=self.source.at[spot.peer(step)],
            dst_ref=self.target.at[spot.dp],
            send_sem=self.send.at[step],
            recv_sem=self.receive.at[step],
            device_id=(spot.peer(step), spot.mp),
            device_id_type=MESH,
        )

    def start(self):
        for copy in self.copies:
            copy.start()
        self.keep()

    def keep(self):
        self.target[self.spot.dp] = self.source[self.spot.dp]

    def wait(self):
        for copy in self.copies:
            copy.wait()


class Gather:
    def __init__(self, spot, shard, window, sems):
        self.local = pltpu.make_async_copy(shard, window(spot.dp), sems.at[0, 0])
        self.copies = [
            pltpu.make_async_remote_copy(
                src_ref=shard,
                dst_ref=window(spot.dp),
                send_sem=sems.at[0, step],
                recv_sem=sems.at[1, step],
                device_id=(spot.peer(step), spot.mp),
                device_id_type=MESH,
            )
            for step in range(1, spot.dp_size)
        ]

    def start(self):
        for copy in self.copies:
            copy.start()
        self.local.start()

    def go_on(self):
        pass

    def wait(self):
        for copy in self.copies:
            copy.wait()
        self.local.wait()


def gather_of(spot, *arguments):
    return (RingGather if spot.dp_size == 4 else Gather)(spot, *arguments)


class RingGather:
    def __init__(self, spot, shard, window, sems):
        side = spot.dp + 1 - 2 * lax.rem(spot.dp, 2)
        across = spot.dp + 2 - 4 * lax.div(spot.dp, 2)

        def copy(source, index, kind, to, half=None):
            return pltpu.make_async_remote_copy(
                src_ref=source,
                dst_ref=window(index, half),
                send_sem=sems.at[0, kind],
                recv_sem=sems.at[1, kind],
                device_id=(to, spot.mp),
                device_id_type=MESH,
            )

        self.local = pltpu.make_async_copy(shard, window(spot.dp), sems.at[0, 4])
        self.to_side = copy(shard, spot.dp, 0, side)
        self.to_across = copy(shard, spot.dp, 1, across)
        self.on_across = copy(window(side, 0), side, 2, across, 0)
        self.on_side = copy(window(across, 1), across, 3, side, 1)

    def start(self):
        self.to_side.start()
        self.to_across.start()
        self.local.start()

    def go_on(self):
        self.to_side.wait_recv()
        self.on_across.start()
        self.to_across.wait_recv()
        self.on_side.start()

    def wait(self):
        self.to_side.wait_send()
        self.to_across.wait_send()
        self.on_across.wait()
        self.on_side.wait()
        self.local.wait()


class Spread:
    def __init__(self, spot, shard, full, sems):
        self.spot, self.shard, self.full, self.sems = spot, shard, full, sems
        self.local = pltpu.make_async_copy(shard, full.at[spot.mp], sems.at[6, 0])

    def copy(self, kind, device, p, source=None, core=None):
        at = 2 * p + (self.spot.core if core is None else core)
        return pltpu.make_async_remote_copy(
            src_ref=self.full.at[at] if source is None else source,
            dst_ref=self.full.at[at],
            send_sem=self.sems.at[kind, p],
            recv_sem=self.sems.at[kind + 1, p],
            device_id=device,
            device_id_type=MESH,
        )

    def rightward(self, p, source=None):
        return self.copy(0, self.spot.right, p, source)

    def leftward(self, p, source=None):
        return self.copy(2, self.spot.left, p, source)

    def across(self, p, source=None):
        return self.copy(4, self.spot.sibling, p, source)

    def begin(self):
        spot = self.spot
        pl.when(spot.has_right)(lambda: self.rightward(spot.place, self.shard).start())
        pl.when(spot.has_left)(lambda: self.leftward(spot.place, self.shard).start())
        self.across(spot.place, self.shard).start()
        self.local.start()

    def go_on(self, hop):
        spot = self.spot

        @pl.when(spot.place >= hop)
        def _():
            p = spot.place - hop
            self.rightward(p).wait_recv()
            pl.when(spot.has_right)(lambda: self.rightward(p).start())
            self.across(p).start()

        @pl.when(spot.place + hop < spot.places)
        def _():
            p = spot.place + hop
            self.leftward(p).wait_recv()
            pl.when(spot.has_left)(lambda: self.leftward(p).start())
            self.across(p).start()

    def finish(self):
        spot = self.spot
        for p in range(spot.places):
            self.copy(4, spot.sibling, p, core=1 - spot.core).wait_recv()
            self.across(p).wait_send()
            pl.when(spot.has_right & (spot.place >= p))(lambda: self.rightward(p).wait_send())
            pl.when(spot.has_left & (spot.place <= p))(lambda: self.leftward(p).wait_send())
        self.local.wait()


def spread_scratch(places):
    return [pltpu.SemaphoreType.DMA((7, places))]


class Ship(Swap):
    def __init__(self, spot, source, target, sems):
        super().__init__(spot, source, target, sems.at[0], sems.at[1])
        self.local = pltpu.make_async_copy(source.at[spot.dp], target.at[spot.dp], sems.at[0, 0])

    def start(self):
        for copy in self.copies:
            copy.start()
        self.local.start()

    def wait(self):
        super().wait()
        self.local.wait()


def window_of(full, axis, step, column=0, columns=None):
    def window(index, half=None):
        rows = step if axis == 0 else full.shape[0]
        first, count = (0, rows) if half is None else (half * (rows // 2), rows // 2)
        if axis == 1:
            return full.at[
                pl.ds(first, count), pl.ds(pl.multiple_of(index * step, step), step)
            ]
        along = pl.ds(pl.multiple_of(index * step + first, count), count)
        return full.at[along, pl.ds(column, full.shape[1] if columns is None else columns)]

    return window


def swap_scratch(size, *block):
    return [
        pltpu.VMEM((size, *block), BF16),
        pltpu.VMEM((size, *block), BF16),
        pltpu.SemaphoreType.DMA((size,)),
        pltpu.SemaphoreType.DMA((size,)),
    ]


def far_first(places):
    orders = []
    for place in range(places):
        right, left, order = list(range(places - 1, place, -1)), list(range(place)), []
        while right or left:
            order += right[:1] + left[:1]
            right, left = right[1:], left[1:]
        orders.append(order + [place])
    return orders


class Sum:
    def __init__(self, spot, mine, out, from_sibling, passed, sems):
        self.spot = spot
        self.mine, self.out = mine, out
        self.from_sibling, self.passed = from_sibling, passed
        self.sems = sems
        self.orders = far_first(spot.places)

    def copy(self, source, target, kind, t, device, to=None):
        return pltpu.make_async_remote_copy(
            src_ref=source.at[t],
            dst_ref=target.at[t if to is None else to],
            send_sem=self.sems.at[kind, t],
            recv_sem=self.sems.at[kind + 1, t],
            device_id=device,
            device_id_type=MESH,
        )

    def sibling(self, t):
        return self.copy(self.out, self.from_sibling, 0, t, self.spot.sibling)

    def rightward(self, t):
        return self.copy(self.mine, self.passed, 2, t, self.spot.right)

    def leftward(self, t, place):
        to = jnp.where(t == place, self.spot.places, t)
        return self.copy(self.mine, self.passed, 4, t, self.spot.left, to)

    def leftward_out(self, t):
        return self.leftward(t, self.spot.place - 1)

    def leftward_in(self, t):
        return self.leftward(t, self.spot.place)

    def term(self, s):
        chosen = 0
        for place, order in enumerate(self.orders):
            for at, t in enumerate(order):
                if t:
                    chosen = chosen + jnp.where((self.spot.place == place) & (s == at), t, 0)
        return chosen

    def add(self, t, arrived):
        self.mine[t] = (self.mine[t].astype(F32) + arrived.astype(F32)).astype(BF16)

    def absorb(self, t):
        self.sibling(t).wait_recv()
        self.add(t, self.from_sibling[t])

    def begin(self, s):
        spot = self.spot

        @pl.when((spot.place == 0) & (s < spot.places - 1))
        def _():
            t = spot.places - 1 - s
            self.absorb(t)
            self.rightward(t).start()

        @pl.when((spot.place == spot.places - 1) & (s < spot.places - 1))
        def _():
            self.absorb(s)
            self.leftward_out(s).start()

    def go_on(self, hop):
        spot = self.spot
        last = spot.places - 1

        @pl.when((spot.place > 0) & (spot.place <= hop))
        def _():
            t = last + spot.place - hop
            self.absorb(t)
            self.rightward(t).wait_recv()
            self.add(t, self.passed[t])
            self.rightward(t).start()

        @pl.when((spot.place < last) & (last - spot.place <= hop))
        def _():
            t = hop - last + spot.place
            self.absorb(t)
            self.leftward_in(t).wait_recv()
            self.add(t, self.passed[t])
            self.leftward_out(t).start()

    def finish(self):
        spot = self.spot
        t = spot.place
        self.absorb(t)

        @pl.when(spot.has_left)
        def _():
            self.rightward(t).wait_recv()
            self.add(t, self.passed[t])

        @pl.when(spot.has_right)
        def _():
            self.leftward_in(t).wait_recv()
            self.add(t, self.passed[spot.places])

        for t in range(spot.places):
            self.sibling(t).wait_send()
            pl.when(spot.place < t)(lambda: self.rightward(t).wait_send())
            pl.when(spot.place > t)(lambda: self.leftward_out(t).wait_send())
        return self.mine[spot.place].astype(F32)


def sum_scratch(places, rows_here, width):
    return [
        *[pltpu.VMEM((places, rows_here, width), BF16)] * 3,
        pltpu.VMEM((places + 1, rows_here, width), BF16),
        pltpu.SemaphoreType.DMA((6, places)),
    ]


def as_column(row):
    return jnp.broadcast_to(row, (HEAD, row.shape[1])).T[:, 0:1]


def attend_blocks(qkv, ids_ref, out, scale, shift):
    count, block = out.shape[:2]
    row_at = lax.broadcasted_iota(jnp.int32, (block, block), 0)
    col_at = lax.broadcasted_iota(jnp.int32, (block, block), 1)

    @pl.loop(0, count)
    def _(i):
        queries = qkv[i, :, 0:HEAD]
        ids = as_column(ids_ref[i])

        def add_block(j, acc, diagonal=False):
            sig = sigmoid_of(dot_nt(queries, qkv[j, :, HEAD : 2 * HEAD]), scale, shift)
            visible = ids == ids_ref[j]
            if diagonal:
                visible = visible & (col_at <= row_at)
            weights = jnp.where(visible, sig, 0.0).astype(BF16)
            return acc + dot(weights, qkv[j, :, 2 * HEAD :])

        acc = add_block(i, jnp.zeros((block, HEAD), F32), True)
        out[i] = lax.fori_loop(0, i, add_block, acc).astype(BF16)


def attend_back_blocks(
    spot, qkv, grad, ids_ref, cos_ref, sin_ref, out_q, out_kv, dq, made, midway, scale, shift
):
    count, block = grad.shape[:2]
    col_at = lax.broadcasted_iota(jnp.int32, (block, block), 0)
    row_at = lax.broadcasted_iota(jnp.int32, (block, block), 1)
    dq[...] = jnp.zeros_like(dq)

    def unrotate(values, i):
        rows = pl.ds(pl.multiple_of(i * block, block), block)
        swapped = pltpu.roll(values, HEAD // 2, 1)
        return (values * cos_ref[rows, :] - swapped * sin_ref[rows, :]).astype(BF16)

    @pl.loop(0, count)
    def _(at):
        j = spot.peer(at + 1)
        keys = qkv[j, :, HEAD : 2 * HEAD]
        values = qkv[j, :, 2 * HEAD :]
        keys_t = keys.T
        ids = as_column(ids_ref[j])

        def add_block(i, sums, diagonal=False):
            dk, dv = sums
            queries, grads = qkv[i, :, 0:HEAD], grad[i]
            sig = sigmoid_of(dot_nt(keys, queries), scale, shift)
            visible = ids == ids_ref[i]
            if diagonal:
                visible = visible & (col_at <= row_at)
            sig = jnp.where(visible, sig, 0.0)
            prob_grad = dot_nt(values, grads)
            score_grad = (prob_grad * sig * (1.0 - sig)).astype(BF16)
            dq[i] += dot(keys_t, score_grad)
            return dk + dot(score_grad, queries), dv + dot(sig.astype(BF16), grads)

        zero = jnp.zeros((block, HEAD), F32)
        dk, dv = lax.fori_loop(j + 1, count, add_block, add_block(j, (zero, zero), True))
        out_kv[j, :, 0:HEAD] = unrotate(dk * scale, j)
        out_kv[j, :, HEAD:] = dv.astype(BF16)
        pl.when(at < count - 1)(lambda: made(at + 1))
        pl.when(at == 1)(midway)

    @pl.loop(0, count)
    def _(i):
        out_q[i] = unrotate(dq[i].T * scale, i)


def take(refs, count):
    return refs[:count], refs[count:]


class Loads:
    def __init__(self, pairs, sems):
        self.copies = [
            pltpu.make_async_copy(source, target, sems.at[i])
            for i, (source, target) in enumerate(pairs)
        ]
        for copy in self.copies:
            copy.start()

    def wait(self, *which):
        for i in which or range(len(self.copies)):
            self.copies[i].wait()


def lazy_scratch(*arrays):
    return [pltpu.VMEM(array.shape, array.dtype) for array in arrays] + [
        pltpu.SemaphoreType.DMA((len(arrays),))
    ]


def put_norm(x_ref, gain_ref, out_ref):
    x = x_ref[...].astype(F32)
    out_ref[...] = (x * norm_factor(x) * gain_ref[...]).astype(BF16)


def begin_kernel(
    x_ref, gain_ref, query, key, value, out, qkv_full, out_full, first_full,
    normed, sems, spread_sems,
):
    spot = Spot()
    spot.enter(True, True)
    rows, columns = query.shape
    jobs = [
        (shard, window_of(qkv_full, 0, rows, i * columns, columns))
        for i, shard in enumerate((query, key, value))
    ]
    jobs.append((out, window_of(out_full, 1, out.shape[1])))
    gathers = [
        gather_of(spot, shard, window, sems.at[i]) for i, (shard, window) in enumerate(jobs)
    ]
    for gather in gathers:
        gather.start()
    put_norm(x_ref, gain_ref, normed)
    spread = Spread(spot, normed, first_full, spread_sems)
    spread.begin()
    spread.go_on(1)
    for gather in gathers:
        gather.go_on()
    for hop in range(2, spot.places):
        spread.go_on(hop)
    for gather in gathers:
        gather.wait()
    spread.finish()


def forward_kernel(tail, head, norms, spreads, gather_axis, heads, toks, scale, shift, *refs):
    gathers = gather_axis is not None
    tail_in, refs = take(refs, 4 * tail)
    head_in, refs = take(refs, 5 * head)
    norm_in, refs = take(refs, 2 * norms)
    spread_in, refs = take(refs, spreads - norms)
    gather_in, refs = take(refs, gathers)
    tail_out, refs = take(refs, 3 * tail)
    head_out, refs = take(refs, 2 * head)
    spread_out, refs = take(refs, spreads)
    gather_out, refs = take(refs, gathers)
    sum_refs, refs = take(refs, 5 * tail)
    head_refs, refs = take(refs, 9 * head)
    normed, refs = take(refs, norms)
    lazy, refs = take(refs, 3 * head)
    if head:
        rows_ref, weight_ref, cos_ref, sin_ref, ids_ref = head_in
        loads = Loads(zip((rows_ref, weight_ref), lazy), lazy[2])
        rows_ref, weight_ref = lazy[:2]
    spot = Spot()
    spot.enter(head or gathers, tail or spreads)
    if norms:
        put_norm(*norm_in, *normed)
        spread_in = (*normed, *spread_in)
    moving = [Spread(spot, *refs) for refs in zip(spread_in, spread_out, refs)]
    for spread in moving:
        spread.begin()
    if gathers:
        window = window_of(gather_out[0], gather_axis, gather_in[0].shape[gather_axis])
        gather = gather_of(spot, gather_in[0], window, refs[-1])
        if not (tail and head):
            gather.start()

    if tail:
        got, out_weight, x_ref, gain_ref = tail_in
        middle_ref, normed_ref, mix_ref = tail_out
        pairs = got.shape[0]
        owner_rows = toks * (pairs // heads)
        for o in range(mix_ref.shape[0] // owner_rows):
            for p in range(pairs):
                s, h = p // heads, p % heads
                mix_ref[pl.ds(o * owner_rows + s * toks, toks), h * HEAD : (h + 1) * HEAD] = got[
                    p, pl.ds(o * toks, toks), :
                ]
        summed = Sum(spot, *sum_refs)
        chip_rows = 2 * owner_rows

        @pl.loop(0, spot.places)
        def _(s):
            t = summed.term(s)
            rows = pl.ds(pl.multiple_of(t * chip_rows, chip_rows), chip_rows)
            value = dot(mix_ref[rows, :], out_weight[...]).astype(BF16)
            keep, send = split_cores(spot.core, value, owner_rows)
            summed.mine[t] = keep[0]
            summed.out[t] = send[0]
            summed.sibling(t).start()

        @pl.loop(0, spot.places - 1)
        def _(s):
            summed.begin(s)

    if head:
        qkv_ref, got_ref = head_out
        made, paired, qkv, qkv_send, qkv_recv, part, got, part_send, part_recv = head_refs
        pairs = paired.shape[0]
        owner_rows = toks * (pairs // heads)
        step = made.shape[0]
        loads.wait()

        @pl.loop(0, rows_ref.shape[0] // step)
        def _(i):
            rows = pl.ds(pl.multiple_of(i * step, step), step)
            made[...] = dot(rows_ref[rows, :], weight_ref[...])
            for j in range(step // owner_rows):
                to = pl.ds(pl.multiple_of((i * (step // owner_rows) + j) * toks, toks), toks)
                cosine, sine = cos_ref[to, :], sin_ref[to, :]
                for p in range(pairs):
                    s, h = p // heads, p % heads
                    here = pl.ds(j * owner_rows + s * toks, toks)
                    for kind in range(3):
                        piece = made[here, pl.ds((kind * heads + h) * HEAD, HEAD)]
                        if kind < 2:
                            piece = piece * cosine + pltpu.roll(piece, HEAD // 2, 1) * sine
                        paired[p, to, kind * HEAD : (kind + 1) * HEAD] = piece.astype(BF16)

        swap = Swap(spot, paired, qkv, qkv_send, qkv_recv)
        swap.start()
    if gathers and tail and head:
        gather.start()
    for spread in moving:
        spread.go_on(1)
    if tail and spot.places > 2:
        summed.go_on(1)
    if head:
        swap.wait()
        attend_blocks(qkv, ids_ref, part, scale, shift)
        swap = Swap(spot, part, got, part_send, part_recv)
        swap.start()
    for hop in range(2, spot.places - 1):
        for spread in moving:
            spread.go_on(hop)
        if tail:
            summed.go_on(hop)
    if gathers:
        gather.go_on()
    if head:
        qkv_ref[...] = qkv[...]
        swap.wait()
        got_ref[...] = got[...]
    for spread in moving:
        if spot.places > 2:
            spread.go_on(spot.places - 1)
    if tail:
        middle = x_ref[...].astype(F32) + summed.finish()
        middle_ref[...] = middle
        normed_ref[...] = (middle * norm_factor(middle) * gain_ref[...]).astype(BF16)
    for spread in moving:
        spread.finish()
    if gathers:
        gather.wait()


def middle_kernel(
    first, defer, ships, spreads, owner_rows,
    middle_ref, local_cot_ref, gain_ref, rows_in, cot_in, gate_in, up_low, up_high, down_in,
    *refs,
):
    shards, refs = take(refs, spreads)
    before, refs = take(refs, 0 if first else 3)
    (grad_ref, low_ref, gain_grad_ref), refs = take(refs, 3)
    y_out, refs = take(refs, 2 if defer else 1)
    fulls, refs = take(refs, spreads)
    after, refs = take(refs, 3)
    ship_out, refs = take(refs, ships)
    (act_ref, dgate_ref, dup_ref, turned, new_rows, new_cols, old_rows, old_cols), refs = take(refs, 8)
    (rows_ref, cot_ref, gate_ref, up_ref, down_ref, load_sems, wide_sems), refs = take(refs, 7)
    sum_refs, refs = take(refs, 5)
    y_refs, refs = take(refs, 3 if defer else 5)
    ship_sems, refs = take(refs, ships)
    size, half = after[0].shape[0], up_low.shape[0] // after[0].shape[0]
    pairs = [(rows_in, rows_ref), (gate_in, gate_ref)]
    for e in range(size):
        for i, part in enumerate((up_low, up_high)):
            to = up_ref.at[pl.ds((2 * e + i) * half, half), :]
            pairs.append((part.at[pl.ds(e * half, half), :], to))
    pairs += [(cot_in, cot_ref), (down_in, down_ref)]
    loads = Loads(pairs, load_sems)
    spot = Spot()
    spot.enter(bool(ships), True)
    if ships:
        ship = Ship(spot, after[0], ship_out[0], ship_sems[0])
    summed = Sum(spot, *sum_refs)
    if defer:
        y_mine, y_send, y_sems = y_refs
        stores = [
            pltpu.make_async_copy(source, target, y_sems.at[i])
            for i, (source, target) in enumerate(zip((y_mine, y_send), y_out))
        ]
        sums = [summed]
    else:
        summed_y = Sum(spot, *y_refs)
        y_mine, y_send = summed_y.mine, summed_y.out
        sums = [summed, summed_y]
    moving = [Spread(spot, *refs) for refs in zip(shards, fulls, refs)]
    for spread in moving:
        spread.begin()
    hidden, width = gate_ref.shape[1], rows_ref.shape[1]
    chip_rows = 2 * owner_rows
    tile = min(256, hidden)
    blocks = after[0].shape[0]
    block = width // blocks
    new = (new_rows.at[0], new_rows.at[1], new_cols)
    old = (old_rows.at[0], old_rows.at[1], old_cols)

    def load(g, e):
        return pltpu.make_async_copy(before[g].at[e], old[g], wide_sems.at[0, g])

    def store(g, e):
        return pltpu.make_async_copy(new[g], after[g].at[e], wide_sems.at[1, g])

    if not first:
        for g in range(3):
            load(g, spot.peer(1)).start()
    loads.wait()

    @pl.loop(0, spot.places)
    def _(s):
        place = summed.term(s)
        rows = pl.ds(pl.multiple_of(place * chip_rows, chip_rows), chip_rows)

        @pl.loop(0, hidden // tile)
        def _(t):
            cols = pl.ds(pl.multiple_of(t * tile, tile), tile)
            gate = dot(rows_ref[rows, :], gate_ref[:, cols])
            up = dot(rows_ref[rows, :], up_ref[:, cols])
            sig = jax.nn.sigmoid(gate)
            silu = gate * sig
            act_ref[rows, cols] = (silu * up).astype(BF16)
            grad = dot_nt(cot_ref[rows, :], down_ref[cols, :])
            dgate_ref[rows, cols] = (grad * up * sig * (1.0 + gate * (1.0 - sig))).astype(BF16)
            dup_ref[rows, cols] = (grad * silu).astype(BF16)

        @pl.when(s > 0)
        def _():
            for each in sums:
                each.begin(s - 1)

        for hop in range(1, spot.places - 1):

            @pl.when(s == hop + 1)
            def _():
                for spread in moving:
                    spread.go_on(hop)
                for each in sums:
                    each.go_on(hop)

        @pl.loop(0, width // 256)
        def _(t):
            cols = pl.ds(pl.multiple_of(t * 256, 256), 256)
            value = dot(act_ref[rows, :], down_ref[:, cols])
            keep, send = split_cores(spot.core, value.astype(BF16), owner_rows)
            y_mine[place, :, cols] = keep[0]
            y_send[place, :, cols] = send[0]
            value = dot_nt(dgate_ref[rows, :], gate_ref[cols, :])
            value += dot_nt(dup_ref[rows, :], up_ref[cols, :])
            keep, send = split_cores(spot.core, value.astype(BF16), owner_rows)
            summed.mine[place, :, cols] = keep[0]
            summed.out[place, :, cols] = send[0]

        for each in sums:
            each.sibling(place).start()

    if defer:
        for copy in stores:
            copy.start()

    def send(i):
        if ships:
            pl.when(i < blocks - 1)(lambda: ship.copy(i + 1).start())
            pl.when(i == blocks - 1)(lambda: ship.local.start())

    def make(g, i, left, right, right_at, columns):
        e = spot.peer(i + 1)

        @pl.when(i > 0)
        def _():
            store(g, spot.peer(i)).wait()
            if g == 0:
                send(i - 1)

        if not first:
            load(g, e).wait()
        step = math.gcd(columns, 256)

        @pl.loop(0, columns // step)
        def _(t):
            cols = pl.ds(pl.multiple_of(t * step, step), step)
            total = dot(left[...], right[:, pl.ds(pl.multiple_of(right_at + t * step, step), step)])
            if not first:
                total += old[g][:, cols].astype(F32)
            new[g][:, cols] = total.astype(BF16)

        if not first:
            pl.when(i < blocks - 1)(lambda: load(g, spot.peer(i + 2)).start())
        store(g, e).start()

    @pl.loop(0, blocks)
    def _(i):
        left = turned.at[pl.ds(0, block), :]
        at = spot.peer(i + 1) * block
        left[...] = rows_ref[:, pl.ds(pl.multiple_of(at, block), block)].T
        make(0, i, left, dgate_ref, 0, hidden)
        make(1, i, left, dup_ref, 0, hidden)

    if ships:
        store(0, spot.dp).wait()
        send(blocks - 1)
    for spread in moving:
        spread.go_on(spot.places - 1)
    left = turned.at[pl.ds(0, hidden), :]
    left[...] = act_ref[...].T

    @pl.loop(0, blocks)
    def _(i):
        make(2, i, left, cot_ref, spot.peer(i + 1) * block, block)

    incoming = summed.finish()
    middle = middle_ref[...]
    term, gain_grad = norm_back(middle, norm_factor(middle), gain_ref[...], incoming)
    gain_grad_ref[...] = gain_grad[None]
    grad = local_cot_ref[...].astype(F32) + term
    grad_ref[...] = grad
    low_ref[...] = grad.astype(BF16)
    if defer:
        for copy in stores:
            copy.wait()
    else:
        y_out[0][...] = (middle + summed_y.finish()).astype(BF16)
    for spread in moving:
        spread.finish()
    for g in range(ships, 3):
        store(g, spot.dp).wait()
    if ships:
        ship.wait()


def add_grads(spot, left, right, turned, before, after, made=None):
    size, rows, columns = after.shape

    @pl.loop(0, size)
    def _(i):
        e = spot.peer(i + 1)
        if rows < left.shape[1]:
            turned[...] = left[:, pl.ds(pl.multiple_of(e * rows, rows), rows)].T
            total = dot(turned[...], right[...])
        else:

            @pl.when(i == 0)
            def _():
                turned[...] = left[...].T

            cut = pl.ds(pl.multiple_of(e * columns, columns), columns)
            total = dot(turned[...], right[:, cut])
        if before is not None:
            total += before[e].astype(F32)
        after[e] = total.astype(BF16)
        if made is not None:
            made(i)


def backward_kernel(
    tail, head, last, old_tail, old_head, extra, spreads, heads, toks, scale, shift, *refs
):
    tail_in, refs = take(refs, 6 * tail)
    old_qkv, refs = take(refs, old_tail)
    head_in, refs = take(refs, 7 * head)
    old_out, refs = take(refs, old_head)
    last_in, refs = take(refs, 2 * last)
    extra_in, refs = take(refs, 3 * extra)
    spread_in, refs = take(refs, spreads)
    tail_out, refs = take(refs, (1 if last else 3) * tail)
    head_out, refs = take(refs, 2 * head)
    last_out, refs = take(refs, 3 * last)
    extra_out, refs = take(refs, extra)
    spread_out, refs = take(refs, spreads)
    tail_refs, refs = take(refs, 7 * tail)
    head_refs, refs = take(refs, 14 * head)
    last_refs, refs = take(refs, 8 * last)
    extra_refs, refs = take(refs, 6 * extra)
    lazy_tail, refs = take(refs, 3 * tail)
    lazy_old, refs = take(refs, 2 * old_tail)
    lazy_head, refs = take(refs, 5 * head)
    if head:
        rows_ref, out_weight_ref, qkv, ids_ref, cos_ref, sin_ref, mix_ref = head_in
        loads_head = Loads(zip((rows_ref, qkv, cos_ref, sin_ref), lazy_head), lazy_head[4])
        rows_ref, qkv, cos_ref, sin_ref = lazy_head[:4]
    if tail:
        proj_ref, weight_ref, rows_one_ref, x_ref, grad_ref, gain_ref = tail_in
        loads_tail = Loads(zip((weight_ref, rows_one_ref), lazy_tail), lazy_tail[2])
        weight_ref, rows_one_ref = lazy_tail[:2]
    if extra:
        loads_extra = Loads(zip(extra_in[:2], extra_refs), extra_refs[5])
    before = None
    if old_tail:
        before = lazy_old[0]
        loads_old = Loads([(old_qkv[0], before)], lazy_old[1])
    spot = Spot()
    spot.enter(head or last, tail or spreads or extra)
    moving = [Spread(spot, *refs) for refs in zip(spread_in, spread_out, refs)]
    for spread in moving:
        spread.begin()
    if last:
        out_blocks, gains = last_in
        out_target, qkv_target, gain_sum = last_out
        new_qkv, own_gain, all_dp, dp_sum, all_mp, ship_sems, gain_sems, gain_spread_sems = last_refs
        ship_out = Ship(spot, out_blocks, out_target, ship_sems.at[0])
        ship_out.start()
    early, late = [], []
    if extra:
        summed_y = Sum(spot, *extra_refs[:5])
        loads_extra.wait()
        for t in range(spot.places):
            summed_y.sibling(t).start()
        late.append(summed_y)
    if head:
        head_proj_ref, new_out = head_out
        part, got, part_send, part_recv = head_refs[:4]
        made_q, got_q, q_send, q_recv, made_kv, got_kv, kv_send, kv_recv, dq, mix_turned = head_refs[4:]
        pairs = part.shape[0]
        owner_rows = toks * (pairs // heads)
        total = rows_ref.shape[0]
        step = min(512, total)
        loads_head.wait(0)

        @pl.loop(0, total // step)
        def _(i):
            rows = pl.ds(pl.multiple_of(i * step, step), step)
            made = dot_nt(rows_ref[rows, :], out_weight_ref[...]).astype(BF16)
            for j in range(step // owner_rows):
                to = pl.ds(pl.multiple_of((i * (step // owner_rows) + j) * toks, toks), toks)
                for p in range(pairs):
                    s, h = p // heads, p % heads
                    start = j * owner_rows + s * toks
                    part[p, to, :] = made[start : start + toks, h * HEAD : (h + 1) * HEAD]

        swap = Swap(spot, part, got, part_send, part_recv)
        swap.start()

    if extra:

        @pl.loop(0, spot.places - 1)
        def _(s):
            summed_y.begin(s)

    if tail:
        result_ref = tail_out[0]
        sum_refs, (turned, gain_acc) = take(tail_refs, 5)
        if not last:
            new_qkv, gain_acc = tail_out[1:]
        owner_rows = x_ref.shape[0]
        summed = Sum(spot, *sum_refs)
        early.append(summed)
        chip_rows = 2 * owner_rows
        gain_acc[...] = jnp.zeros_like(gain_acc)
        loads_tail.wait()

        @pl.loop(0, spot.places)
        def _(s):
            t = summed.term(s)
            rows = pl.ds(pl.multiple_of(t * chip_rows, chip_rows), chip_rows)
            value = dot_nt(proj_ref[rows, :], weight_ref[...])
            gain_acc[...] += jnp.sum(
                value * rows_one_ref[rows, :].astype(F32), axis=0, keepdims=True
            )
            keep, send = split_cores(spot.core, value.astype(BF16), owner_rows)
            summed.mine[t] = keep[0]
            summed.out[t] = send[0]
            summed.sibling(t).start()
            pl.when(s > 0)(lambda: summed.begin(s - 1))

        if last:
            own_gain[...] = gains[...]
            own_gain[1:2, :] += gain_acc[...]
            gain_dp = Gather(spot, own_gain, lambda index: all_dp.at[index], gain_sems)
            gain_dp.start()
    if last:
        if old_tail:
            loads_old.wait()
        ship_qkv = Ship(spot, new_qkv, qkv_target, ship_sems.at[1])

        def send(i):
            pl.when(i < spot.dp_size - 1)(lambda: ship_qkv.copy(i + 1).start())
            pl.when(i == spot.dp_size - 1)(lambda: ship_qkv.local.start())

        add_grads(spot, rows_one_ref, proj_ref, turned, before, new_qkv, send)
        gain_dp.wait()
        dp_sum[...] = jnp.sum(all_dp[...], axis=0)
        gain_mp = Spread(spot, dp_sum, all_mp, gain_spread_sems)
        gain_mp.begin()
        gain_mp.go_on(1)
    if head:
        add_grads(
            spot, mix_ref, rows_ref, mix_turned, old_out[0] if old_head else None, new_out
        )
        swap.wait()
    for spread in moving:
        spread.go_on(1)

    def go_on():
        if spot.places > 2:
            for each in early + late:
                each.go_on(1)

    if not head:
        go_on()
    if head:
        loads_head.wait(1, 2, 3)
        swap_kv = Swap(spot, made_kv, got_kv, kv_send, kv_recv)
        attend_back_blocks(
            spot, qkv, got, ids_ref, cos_ref, sin_ref, made_q, made_kv, dq,
            lambda step: swap_kv.copy(step).start(), go_on, scale, shift,
        )
        swap_kv.keep()
        swap = Swap(spot, made_q, got_q, q_send, q_recv)
        swap.start()
    for hop in range(2, spot.places - 1):
        if last:
            gain_mp.go_on(hop)
        for spread in moving:
            spread.go_on(hop)
        for each in early + late:
            each.go_on(hop)
    if tail and not last:
        if old_tail:
            loads_old.wait()
        add_grads(spot, rows_one_ref, proj_ref, turned, before, new_qkv)
    if head:
        swap_kv.wait()
        swap.wait()
        for o in range(total // owner_rows):
            for p in range(pairs):
                s, h = p // heads, p % heads
                here, there = pl.ds(o * owner_rows + s * toks, toks), pl.ds(o * toks, toks)
                for kind in range(3):
                    piece = (
                        got_kv[p, there, (kind - 1) * HEAD : kind * HEAD] if kind else got_q[p, there, :]
                    )
                    head_proj_ref[
                        here, (kind * heads + h) * HEAD : (kind * heads + h + 1) * HEAD
                    ] = piece
    if spot.places > 2:
        for spread in moving:
            spread.go_on(spot.places - 1)
        if last:
            gain_mp.go_on(spot.places - 1)
    if tail:
        incoming = summed.finish()
        x = x_ref[...].astype(F32)
        term, _ = norm_back(x, norm_factor(x), gain_ref[...], incoming)
        result_ref[...] = grad_ref[...] + term
    if extra:
        extra_out[0][...] = (extra_in[2][...] + summed_y.finish()).astype(BF16)
    if last:
        gain_mp.finish()
        gain_sum[...] = jnp.sum(all_mp[...], axis=0)
        ship_out.wait()
        ship_qkv.wait()
    for spread in moving:
        spread.finish()


def ffn_kernel(
    rows_ref, cot_ref, gate_ref, up_ref, down_ref, y_ref, dh_ref, act_ref, dgate_ref, dup_ref
):
    hidden = gate_ref.shape[1]
    width = rows_ref.shape[1]
    tile = min(256, hidden)

    @pl.loop(0, hidden // tile)
    def _(t):
        cols = pl.ds(pl.multiple_of(t * tile, tile), tile)
        gate = dot(rows_ref[...], gate_ref[:, cols])
        up = dot(rows_ref[...], up_ref[:, cols])
        sig = jax.nn.sigmoid(gate)
        silu = gate * sig
        act_ref[:, cols] = (silu * up).astype(BF16)
        grad = dot_nt(cot_ref[...], down_ref[cols, :])
        dgate_ref[:, cols] = (grad * up * sig * (1.0 + gate * (1.0 - sig))).astype(BF16)
        dup_ref[:, cols] = (grad * silu).astype(BF16)

    @pl.loop(0, width // 256)
    def _(t):
        cols = pl.ds(pl.multiple_of(t * 256, 256), 256)
        y_ref[:, cols] = dot(act_ref[...], down_ref[:, cols]).astype(BF16)
        dh = dot_nt(dgate_ref[...], gate_ref[cols, :]) + dot_nt(dup_ref[...], up_ref[cols, :])
        dh_ref[:, cols] = dh.astype(BF16)


def grad_kernel(count, groups, left_blocked, *refs):
    lefts, refs = take(refs, count)
    rights, refs = take(refs, count * groups)
    out_refs, (turned,) = take(refs, groups)
    rows = lefts[0].shape[0]

    def turn():
        for m, left in enumerate(lefts):
            turned[:, m * rows : (m + 1) * rows] = left[...].T

    if left_blocked:
        turn()
    else:
        pl.when(pl.program_id(0) == 0)(turn)
    tile = math.gcd(out_refs[0].shape[2], 256)
    for g, out_ref in enumerate(out_refs):
        own = rights[g * count : (g + 1) * count]

        @pl.loop(0, out_ref.shape[2] // tile)
        def _(t):
            cols = pl.ds(pl.multiple_of(t * tile, tile), tile)
            total = dot(turned[:, :rows], own[0][:, cols])
            for m in range(1, count):
                total += dot(turned[:, m * rows : (m + 1) * rows], own[m][:, cols])
            out_ref[0, :, cols] = total.astype(BF16)


VMEM = pl.BlockSpec(memory_space=pltpu.VMEM)
ANY = pl.BlockSpec(memory_space=pl.ANY)


def cost(flops, nbytes):
    return pl.CostEstimate(flops=flops, bytes_accessed=nbytes, transcendentals=0)


def limits(mebibytes):
    return pltpu.CompilerParams(vmem_limit_bytes=mebibytes * 2**20)


def shape(*dims, dtype=BF16):
    return jax.ShapeDtypeStruct(dims, dtype)


def comm_params(collective_id, mebibytes):
    return pltpu.CompilerParams(
        collective_id=collective_id, has_side_effects=True, vmem_limit_bytes=mebibytes * 2**20
    )


def begin(x, gain, query, key, value, out):
    size, mp_size = lax.axis_size("dp"), lax.axis_size("mp")
    rows, columns = query.shape
    return pl.pallas_call(
        begin_kernel,
        out_shape=[
            shape(rows * size, 3 * columns),
            shape(out.shape[0], out.shape[1] * size),
            shape(mp_size, *x.shape),
        ],
        in_specs=[VMEM] * 2 + [ANY] * 4,
        out_specs=[ANY] * 3,
        scratch_shapes=[
            pltpu.VMEM(x.shape, BF16),
            pltpu.SemaphoreType.DMA((4, 2, size + 1)),
            *spread_scratch(mp_size // 2),
        ],
        compiler_params=comm_params(0, 16),
        cost_estimate=cost(0, 60 * 2**20),
        name="begin",
    )(x, gain, query, key, value, out)


def forward_stage(collective_id, tail, head, norm, shard, gather, heads, toks, scale, shift):
    size, mp_size = lax.axis_size("dp"), lax.axis_size("mp")
    out_shape, scratch = [], []
    if tail:
        blocks, _, x, _ = tail
        owner_rows, width = x.shape
        total = blocks.shape[1] * blocks.shape[0] // heads
        out_shape += [
            shape(owner_rows, width, dtype=F32),
            shape(owner_rows, width),
            shape(total, heads * HEAD),
        ]
        scratch += sum_scratch(mp_size // 2, owner_rows, width)
    if head:
        total, slice_len = head[0].shape[0], head[2].shape[0]
        out_shape += [shape(size, slice_len, 3 * HEAD), shape(size, slice_len, HEAD)]
        scratch += [
            pltpu.VMEM((min(512, total), 3 * heads * HEAD), F32),
            *swap_scratch(size, slice_len, 3 * HEAD),
            *swap_scratch(size, slice_len, HEAD),
        ]
    if norm:
        scratch.append(pltpu.VMEM(norm[0].shape, BF16))
    if head:
        scratch += lazy_scratch(*head[:2])
    here, spreads = len(out_shape), bool(norm) + len(shard)
    out_shape += [shape(mp_size, *array.shape) for array in (*norm[:1], *shard)]
    scratch += spread_scratch(mp_size // 2) * spreads
    axis = None
    if gather:
        weight, axis = gather
        dims = list(weight.shape)
        dims[axis] *= size
        out_shape.append(shape(*dims))
        scratch.append(pltpu.SemaphoreType.DMA((2, size + 1)))
    arrays = [*tail, *head, *norm]
    specs = [VMEM] * len(arrays)
    if head:
        specs[len(tail) : len(tail) + 2] = [ANY] * 2
    return pl.pallas_call(
        functools.partial(
            forward_kernel,
            bool(tail), bool(head), bool(norm), spreads, axis, heads, toks, scale, shift,
        ),
        out_shape=out_shape,
        in_specs=specs + [ANY] * (len(shard) + bool(gather)),
        out_specs=[VMEM] * here + [ANY] * (spreads + bool(gather)),
        scratch_shapes=scratch,
        compiler_params=comm_params(collective_id, 52),
        cost_estimate=cost(10**10, 100 * 2**20),
        name="forward_stage",
    )(*arrays, *shard, *gather[:1])


def middle_part(
    collective_id, defer, ships, rows, cot, weights, middle, local_cot, gain, shards, before
):
    total, width = rows.shape
    gate, _, _, down = weights
    hidden = gate.shape[1]
    size, mp_size = lax.axis_size("dp"), lax.axis_size("mp")
    places = mp_size // 2
    owner_rows = middle.shape[0]
    block = width // size
    wide = [shape(size, block, hidden)] * 2 + [shape(size, hidden, block)]
    half = shape(places, owner_rows, width)
    y_scratch = sum_scratch(places, owner_rows, width)
    if defer:
        y_scratch = [*[pltpu.VMEM(half.shape, BF16)] * 2, pltpu.SemaphoreType.DMA((2,))]
    return pl.pallas_call(
        functools.partial(middle_kernel, not before, defer, ships, len(shards), owner_rows),
        out_shape=[
            shape(owner_rows, width, dtype=F32),
            shape(owner_rows, width),
            shape(1, width, dtype=F32),
            *([half, half] if defer else [shape(owner_rows, width)]),
            *[shape(mp_size, *array.shape) for array in shards],
            *wide,
            *wide[:ships],
        ],
        in_specs=[VMEM] * 3 + [ANY] * (6 + len(shards) + len(before)),
        out_specs=[VMEM] * 3 + ([ANY] * 2 if defer else [VMEM]) + [ANY] * (len(shards) + 3 + ships),
        scratch_shapes=[
            *[pltpu.VMEM((total, hidden), BF16)] * 3,
            pltpu.VMEM((max(block, hidden), total), BF16),
            pltpu.VMEM((2, block, hidden), BF16),
            pltpu.VMEM((hidden, block), BF16),
            pltpu.VMEM((2, block, hidden), BF16),
            pltpu.VMEM((hidden, block), BF16),
            *[pltpu.VMEM(array.shape, BF16) for array in (rows, cot, gate, gate, down)],
            pltpu.SemaphoreType.DMA((4 + 2 * size,)),
            pltpu.SemaphoreType.DMA((2, 3)),
            *sum_scratch(places, owner_rows, width),
            *y_scratch,
            *[pltpu.SemaphoreType.DMA((2, size))] * ships,
            *spread_scratch(places) * len(shards),
        ],
        compiler_params=comm_params(collective_id, 61),
        cost_estimate=cost(18 * total * width * hidden, 60 * 2**20),
        name="middle_part",
    )(middle, local_cot, gain, rows, cot, *weights, *shards, *before)


def backward_stage(
    collective_id, tail, old_qkv, head, old_out, last, extra, shard, heads, toks, scale, shift
):
    size, mp_size = lax.axis_size("dp"), lax.axis_size("mp")
    places = mp_size // 2
    out_shape, scratch = [], []
    if tail:
        owner_rows, width = tail[3].shape
        out_shape.append(shape(owner_rows, width, dtype=F32))
        total = tail[0].shape[0]
        wide = shape(size, width // size, 3 * heads * HEAD)
        if not last:
            out_shape += [wide, shape(1, width, dtype=F32)]
        scratch += [
            *sum_scratch(places, owner_rows, width),
            pltpu.VMEM((width // size, total), BF16),
            pltpu.VMEM((1, width), F32),
        ]
    if head:
        (total, width), slice_len = head[0].shape, head[2].shape[1]
        out_shape.append(shape(total, 3 * heads * HEAD))
        out_shape.append(shape(size, heads * HEAD, width // size))
        scratch += [
            *swap_scratch(size, slice_len, HEAD),
            *swap_scratch(size, slice_len, HEAD),
            *swap_scratch(size, slice_len, 2 * HEAD),
            pltpu.VMEM((size, HEAD, slice_len), F32),
            pltpu.VMEM((heads * HEAD, total), BF16),
        ]
    here = len(out_shape)
    if last:
        gains = last[1].shape
        out_shape += [shape(*last[0].shape), wide]
        scratch += [
            pltpu.VMEM(wide.shape, BF16),
            pltpu.VMEM(gains, F32),
            pltpu.VMEM((size, *gains), F32),
            pltpu.VMEM(gains, F32),
            pltpu.VMEM((mp_size, *gains), F32),
            pltpu.SemaphoreType.DMA((2, 2, size)),
            pltpu.SemaphoreType.DMA((2, size)),
            *spread_scratch(places),
        ]
        out_shape.append(shape(*gains, dtype=F32))
    if extra:
        out_shape.append(shape(*extra[2].shape))
        scratch += sum_scratch(places, *extra[2].shape)
        scratch.append(pltpu.SemaphoreType.DMA((2,)))
    if tail:
        scratch += lazy_scratch(tail[1], tail[2])
    scratch += lazy_scratch(*old_qkv) if old_qkv else []
    if head:
        scratch += lazy_scratch(head[0], head[2], head[4], head[5])
    scratch += spread_scratch(places) * len(shard)
    out_shape += [shape(mp_size, *array.shape) for array in shard]
    arrays = [*tail, *old_qkv, *head, *old_out]
    tail_specs = [VMEM, ANY, ANY, VMEM, VMEM, VMEM] if tail else []
    head_specs = [ANY, VMEM, ANY, VMEM, ANY, ANY, VMEM] if head else []
    specs = [*tail_specs, *[ANY] * len(old_qkv), *head_specs, *[VMEM] * len(old_out)]
    last_specs, last_outs = ([ANY, VMEM], [ANY, ANY, VMEM]) if last else ([], [])
    extra_specs, extra_outs = ([ANY, ANY, VMEM], [VMEM]) if extra else ([], [])
    return pl.pallas_call(
        functools.partial(
            backward_kernel, bool(tail), bool(head), bool(last), len(old_qkv), len(old_out),
            bool(extra), len(shard), heads, toks, scale, shift,
        ),
        out_shape=out_shape,
        in_specs=specs + last_specs + extra_specs + [ANY] * len(shard),
        out_specs=[VMEM] * here + last_outs + extra_outs + [ANY] * len(shard),
        scratch_shapes=scratch,
        compiler_params=comm_params(collective_id, 58),
        cost_estimate=cost(10**10, 100 * 2**20),
        name="backward_stage",
    )(*arrays, *last, *extra, *shard)


def ffn(rows, cot, gate, up, down):
    total, width = rows.shape
    hidden = gate.shape[1]
    step = min(512, total)
    by_rows = pl.BlockSpec((step, width), lambda i: (i, 0))
    by_hidden = pl.BlockSpec((step, hidden), lambda i: (i, 0))
    held = lambda array: pl.BlockSpec(array.shape, lambda i: (0, 0), pipeline_mode=pl.Buffered(1))
    return pl.pallas_call(
        ffn_kernel,
        grid=(total // step,),
        out_shape=[shape(total, width)] * 2 + [shape(total, hidden)] * 3,
        in_specs=[by_rows, by_rows, held(gate), held(up), held(down)],
        out_specs=[by_rows] * 2 + [by_hidden] * 3,
        compiler_params=limits(56),
        cost_estimate=cost(12 * total * width * hidden, 34 * 2**20),
        name="ffn",
    )(rows, cot, gate, up, down)


def weight_grad(lefts, groups, left_blocked):
    count = len(lefts)
    size = lax.axis_size("dp")
    rows = lefts[0].shape[0]
    m, n = lefts[0].shape[1], groups[0][0].shape[1]
    moving = lambda width: pl.BlockSpec((rows, width // size), lambda e: (0, e))
    fixed = lambda width: pl.BlockSpec(
        (rows, width), lambda e: (0, 0), pipeline_mode=pl.Buffered(1)
    )
    left_spec = moving(m) if left_blocked else fixed(m)
    right_spec = fixed(n) if left_blocked else moving(n)
    out = (m // size, n) if left_blocked else (m, n // size)
    return pl.pallas_call(
        functools.partial(grad_kernel, count, len(groups), left_blocked),
        grid=(size,),
        in_specs=[left_spec] * count + [right_spec] * (count * len(groups)),
        out_specs=[pl.BlockSpec((1, *out), lambda e: (e, 0, 0))] * len(groups),
        out_shape=[shape(size, *out)] * len(groups),
        scratch_shapes=[pltpu.VMEM((out[0], count * rows), BF16)],
        compiler_params=limits(52),
        cost_estimate=cost(2 * count * rows * m * n * len(groups), 24 * 2**20),
        name="weight_grad",
    )(*lefts, *(right for group in groups for right in group))


def first_visible(ids):
    at = jnp.arange(ids.shape[-1], dtype=jnp.int32)
    starts = jnp.concatenate([jnp.ones_like(ids[..., :1], jnp.bool_), ids[..., 1:] != ids[..., :-1]], axis=-1)
    return lax.cummax(jnp.where(starts, at, 0), axis=ids.ndim - 1)


def block_at(values, index):
    return lax.dynamic_index_in_dim(values, index, 0, keepdims=False)


def scatter_mp(values):
    return lax.psum_scatter(values, "mp", scatter_dimension=0, tiled=True).astype(F32)


def sliced_scores(qkv, kv_all, first, positions, scale, shift):
    raw = jnp.einsum("pqd,pkd->pqk", qkv[..., :HEAD], kv_all[..., :HEAD], preferred_element_type=F32)
    at = jnp.arange(kv_all.shape[1], dtype=jnp.int32)
    visible = (at >= first[..., None]) & (at <= positions[:, None])
    return jnp.where(visible, sigmoid_of(raw, scale, shift), 0.0)


def per_device(
    inputs,
    cotangent,
    doc_ids,
    gain_attn,
    w_query,
    w_key,
    w_value,
    w_out,
    gain_ffn,
    w_gate,
    w_up,
    w_down,
):
    dp_size = lax.axis_size("dp")
    mp_size = lax.axis_size("mp")
    micro_count, row_count, seq_count, width = inputs.shape
    slice_len = row_count * mp_size
    total_len = slice_len * dp_size
    rows_here = row_count * seq_count
    shift = math.log(total_len)
    scale = HEAD ** (-0.5)
    dp_at = lax.axis_index("dp")
    mp_at = lax.axis_index("mp")
    first_row = dp_at * slice_len
    positions = first_row + jnp.arange(slice_len, dtype=jnp.int32)
    head_width = w_query.shape[1]
    heads = head_width // HEAD
    hidden = w_gate.shape[1]
    pairs = seq_count * heads
    whole_pairs = pairs == dp_size
    cos_all, sin_all = full_tables(total_len)
    cos_slice, sin_slice = [
        lax.dynamic_slice_in_dim(table, first_row, slice_len, 0) for table in (cos_all, sin_all)
    ]

    def by_row(table):
        shaped = table.reshape(mp_size, 1, row_count, 1, HEAD)
        return jnp.broadcast_to(shaped, (mp_size, seq_count, row_count, 1, HEAD))

    def rotate(values, back=False):
        sine = -by_row(sin_slice) if back else by_row(sin_slice)
        return values * by_row(cos_slice) + swap_halves(values) * sine

    def to_pairs(values):
        shaped = values.reshape(mp_size, seq_count, row_count, heads, -1)
        return shaped.transpose(1, 3, 0, 2, 4).reshape(pairs, slice_len, -1)

    def from_pairs(values):
        shaped = values.reshape(seq_count, heads, mp_size, row_count, -1)
        return shaped.transpose(2, 0, 3, 1, 4).reshape(mp_size * rows_here, heads, -1)

    def to_rows(values):
        return jnp.swapaxes(values, 0, 1).reshape(rows_here, width)

    def from_rows(values):
        return jnp.swapaxes(values.reshape(seq_count, row_count, width), 0, 1)

    def gather_mp(values):
        return lax.all_gather(values, "mp", axis=0, tiled=True)

    gain_attn_grad = jnp.zeros((width,), F32)
    gain_ffn_grad = jnp.zeros((width,), F32)
    results = []
    input_grads = []
    kept = [[] for _ in range(9)]
    xs = [to_rows(inputs[m]) for m in range(micro_count)]
    cots = [to_rows(cotangent[m]) for m in range(micro_count)]
    micros = range(micro_count)
    if whole_pairs:
        stage = (heads, row_count, scale, shift)
        ids = [
            block_at(doc_ids[m], dp_at // heads).astype(F32).reshape(dp_size, 1, slice_len)
            for m in micros
        ]
        last = micro_count - 1

        def whole(blocks):
            return blocks.reshape(mp_size * rows_here, width)

        def scatter_dp(blocks):
            return lax.psum_scatter(blocks, "dp", scatter_dimension=0, tiled=True)[0].astype(F32)

        qkv_full, out_full, rows_one = begin(
            xs[0], gain_attn[None], w_query, w_key, w_value, w_out
        )
        cut = w_up.shape[0] // 2
        gathers = {
            0: (w_gate, 0), 1: (w_up[:cut], 0), 2: (w_up[cut:], 0), micro_count: (w_down, 1)
        }
        wide = []
        ones, qkvs, got, middles, lows, twos, mixtures = [whole(rows_one)], [], [], [], [], [], []
        for m in range(micro_count + 1):
            tail, head, norm, shard = (), (), (), ()
            if m:
                tail = (got[m - 1], out_full, xs[m - 1], gain_ffn[None])
            if m < micro_count:
                head = (ones[m], qkv_full, cos_slice, sin_slice, ids[m])
            if m < last:
                norm = (xs[m + 1], gain_attn[None])
            elif lows:
                shard = (lows[m - last],)
            if m == 0:
                shard += (cots[0],)
            outs = forward_stage(10 + m, tail, head, norm, shard, gathers.get(m, ()), *stage)
            if tail:
                (middle, low, mixture), outs = take(outs, 3)
                middles.append(middle)
                lows.append(low)
                mixtures.append(mixture)
            if head:
                (qkv, block), outs = take(outs, 2)
                qkvs.append(qkv)
                got.append(block)
            if norm or shard:
                (ones if m < last else twos).append(whole(outs[0]))
            if m == 0:
                portions = [whole(outs[1])]
            if m in gathers:
                wide.append(outs[-1])
        grads, low_grads, attns, projs, sums, gain_parts, later = [], [], [], [], [], [], []
        for m in micros:
            shard = (lows[len(twos)] if len(twos) < micro_count else low_grads[len(attns)],)
            if m < last:
                shard += (cots[m + 1],)
            defer = m == 0
            grad, low, gain_part, *others = middle_part(
                30 + m, defer, int(m == last), twos[m], portions[m], wide, middles[m], cots[m], gain_ffn[None],
                shard, sums,
            )
            ys, (full, *others) = take(others, 2 if defer else 1)
            later.append((*ys, middles[m]) if defer else ys)
            (twos if len(twos) < micro_count else attns).append(whole(full))
            if m < last:
                portions.append(whole(others[0]))
            sums, gate_blocks = take(others[m < last :], 3)
            grads.append(grad)
            low_grads.append(low)
            gain_parts.append(gain_part)
        sum_up, sum_down = [scatter_dp(blocks) for blocks in sums[1:]]
        sum_gate = jnp.sum(gate_blocks[0].astype(F32), axis=0)
        old_qkv, old_out, attn_parts, finished = (), (), [], list(later)
        for m in range(micro_count + 1):
            tail, head, shard, final = (), (), (), ()
            if m:
                tail = (projs[m - 1], qkv_full, ones[m - 1], xs[m - 1], grads[m - 1], gain_attn[None])
            if m < micro_count:
                head = (attns[m], out_full, qkvs[m], ids[m], cos_all, sin_all, mixtures[m])
            else:
                rows = [sum(gain_parts), sum(attn_parts), jnp.zeros((6, width), F32)]
                final = (*old_out, jnp.concatenate(rows, axis=0))
            if len(attns) < micro_count:
                shard = (low_grads[len(attns)],)
            extra = later[0] if m == 0 else ()
            outs = backward_stage(
                20 + m, tail, old_qkv, head, () if final else old_out, final, extra, shard, *stage
            )
            if tail:
                (input_grad,), outs = take(outs, 1)
                input_grads.append(from_rows(input_grad))
            if tail and head:
                (new_qkv, gain_part), outs = take(outs, 2)
                old_qkv = (new_qkv,)
                attn_parts.append(gain_part)
            if head:
                (proj, new_out), outs = take(outs, 2)
                projs.append(proj)
                old_out = (new_out,)
            if extra:
                finished[0] = outs[:1]
            if shard:
                attns.append(whole(outs[-1]))
        results = [from_rows(result[0]) for result in finished]
        sum_out, sum_qkv = (jnp.sum(blocks.astype(F32), axis=0) for blocks in outs[:2])
        gain_sums = (outs[2][1] / gain_attn, outs[2][0])
    else:
        qkv_full = lax.all_gather(
            jnp.concatenate([w_query, w_key, w_value], axis=1), "dp", axis=0, tiled=True
        )
        out_full = lax.all_gather(w_out, "dp", axis=1, tiled=True)
        gate_full = lax.all_gather(w_gate, "dp", axis=0, tiled=True)
        up_full = lax.all_gather(w_up, "dp", axis=0, tiled=True)
        down_full = lax.all_gather(w_down, "dp", axis=1, tiled=True)
        first_all = first_visible(doc_ids)
        normed = [
            (x.astype(F32) * norm_factor(x.astype(F32)) * gain_attn).astype(BF16) for x in xs
        ]
        for micro in micros:
            local_rows = xs[micro].astype(F32)
            local_cot = cots[micro]
            factor_one = norm_factor(local_rows)
            rows_one = gather_mp(normed[micro])
            portion = gather_mp(local_cot)
            projected = dot(rows_one, qkv_full).reshape(
                mp_size, seq_count, row_count, 3, heads, HEAD
            )
            packed = to_pairs(
                jnp.concatenate(
                    [
                        rotate(projected[:, :, :, 0]).astype(BF16),
                        rotate(projected[:, :, :, 1]).astype(BF16),
                        projected[:, :, :, 2].astype(BF16),
                    ],
                    axis=-1,
                )
            )
            kv_all = lax.all_gather(packed[..., HEAD:], "dp", axis=1, tiled=True)
            first = lax.dynamic_slice_in_dim(first_all[micro], first_row, slice_len, 1)
            first = jnp.repeat(first, heads, axis=0)
            weights = sliced_scores(packed, kv_all, first, positions, scale, shift)
            attended = jnp.einsum(
                "pqk,pkd->pqd", weights.astype(BF16), kv_all[..., HEAD:], preferred_element_type=F32
            ).astype(BF16)
            mixture = from_pairs(attended).reshape(mp_size * rows_here, head_width)
            middle = local_rows + scatter_mp(dot(mixture, out_full).astype(BF16))
            factor_two = norm_factor(middle)
            rows_two = gather_mp((middle * factor_two * gain_ffn).astype(BF16))
            y, dh, activated, gate_grad, up_grad = ffn(
                rows_two, portion, gate_full, up_full, down_full
            )
            results.append(from_rows((middle + scatter_mp(y)).astype(BF16)))
            middle_term, gain_part = norm_back(middle, factor_two, gain_ffn, scatter_mp(dh))
            gain_ffn_grad = gain_ffn_grad + gain_part
            middle_grad = local_cot.astype(F32) + middle_term
            attn_portion = gather_mp(middle_grad.astype(BF16))
            mix_grad = to_pairs(dot_nt(attn_portion, out_full).astype(BF16))
            sig = sliced_scores(packed, kv_all, first, positions, scale, shift)
            prob_grad = jnp.einsum(
                "pqd,pkd->pqk", mix_grad, kv_all[..., HEAD:], preferred_element_type=F32
            )
            score_grad = (prob_grad * sig * (1.0 - sig)).astype(BF16)
            dq = jnp.einsum("pqk,pkd->pqd", score_grad, kv_all[..., :HEAD], preferred_element_type=F32)
            dk = jnp.einsum("pqk,pqd->pkd", score_grad, packed[..., :HEAD], preferred_element_type=F32)
            dv = jnp.einsum("pqk,pqd->pkd", sig.astype(BF16), mix_grad, preferred_element_type=F32)
            dkv = lax.psum_scatter(
                jnp.concatenate([dk * scale, dv], axis=-1).astype(BF16), "dp", scatter_dimension=1, tiled=True
            ).astype(F32)
            back = from_pairs(jnp.concatenate([dq * scale, dkv], axis=-1))
            back = back.reshape(mp_size, seq_count, row_count, heads, 3 * HEAD)
            proj_grad = jnp.stack(
                [
                    rotate(back[..., :HEAD], True),
                    rotate(back[..., HEAD : 2 * HEAD], True),
                    back[..., 2 * HEAD :],
                ],
                axis=3,
            ).astype(BF16).reshape(mp_size * rows_here, 3 * head_width)
            partial_grad = dot_nt(proj_grad, qkv_full)
            gain_attn_grad = gain_attn_grad + jnp.sum(partial_grad * rows_one.astype(F32), axis=0)
            input_term, _ = norm_back(
                local_rows, factor_one, gain_attn, scatter_mp(partial_grad.astype(BF16))
            )
            input_grads.append(from_rows(middle_grad + input_term))
            for held, array in zip(
                kept,
                (rows_one, proj_grad, mixture, attn_portion, rows_two, gate_grad, up_grad, activated, portion),
            ):
                held.append(array)

        def scatter_dp(lefts, rights, left_blocked):
            (blocks,) = weight_grad(lefts, (rights,), left_blocked)
            return lax.psum_scatter(blocks, "dp", scatter_dimension=0, tiled=True)[0].astype(F32)

        ones, projs, mixtures, attns, twos, gates, ups, acts, portions = kept
        sum_gate = scatter_dp(twos, gates, True)
        sum_up = scatter_dp(twos, ups, True)
        sum_down = scatter_dp(acts, portions, False)
        sum_out = scatter_dp(mixtures, attns, False)
        sum_qkv = scatter_dp(ones, projs, True)
        gain_sums = lax.psum((gain_attn_grad / gain_attn, gain_ffn_grad), ("dp", "mp"))
    return (
        jnp.stack(results),
        jnp.stack(input_grads),
        gain_sums[0],
        sum_qkv[:, :head_width],
        sum_qkv[:, head_width : 2 * head_width],
        sum_qkv[:, 2 * head_width :],
        sum_out,
        gain_sums[1],
        sum_gate,
        sum_up,
        sum_down,
    )


def solution(mesh):
    tokens = P(None, ("dp", "mp"), None, None)
    column = P("dp", "mp")
    row = P("mp", "dp")
    return jax.shard_map(
        per_device,
        mesh=mesh,
        in_specs=(
            tokens, tokens, P(), P(), column, column, column, row, P(), column, column, row,
        ),
        out_specs=(
            tokens, tokens, P(), column, column, column, row, P(), column, column, row,
        ),
        check_vma=False,
    )
```

```python
import functools
import math

import jax
import jax.numpy as jnp
import numpy as np
from jax import lax
from jax.experimental import pallas as pl
from jax.experimental.pallas import tpu as pltpu
from jax.sharding import PartitionSpec as P

HEAD = 128
epsilon = 1e-05
rope_base = 10000.0
F32 = jnp.float32
BF16 = jnp.bfloat16


def full_tables(total):
    half_size = HEAD // 2
    exponents = -(np.arange(half_size, dtype=np.float32) * np.float32(2.0 / HEAD))
    inverse = np.power(np.float32(rope_base), exponents)
    angles = np.arange(total, dtype=np.float32)[:, None] * inverse[None, :]
    cosine, sine = np.cos(angles), np.sin(angles)
    return (
        jnp.asarray(np.concatenate([cosine, cosine], axis=-1)),
        jnp.asarray(np.concatenate([-sine, sine], axis=-1)),
    )


def swap_halves(values):
    half_size = HEAD // 2
    return jnp.concatenate([values[..., half_size:], values[..., :half_size]], axis=-1)


def dot(left, right):
    return jnp.dot(left, right, preferred_element_type=F32)


def dot_tn(left, right):
    return lax.dot_general(left, right, (((0,), (0,)), ((), ())), preferred_element_type=F32)


def dot_nt(left, right):
    return lax.dot_general(left, right, (((1,), (1,)), ((), ())), preferred_element_type=F32)


def norm_factor(values):
    return lax.rsqrt(jnp.mean(values * values, axis=-1, keepdims=True) + epsilon)


def norm_back(values, factor, gain, incoming):
    scaled = incoming * gain
    gain_term = jnp.sum(incoming * values * factor, axis=0)
    input_term = factor * scaled - values * factor**3 * jnp.mean(
        scaled * values, axis=-1, keepdims=True
    )
    return (input_term, gain_term)


def sigmoid_of(raw, scale, shift):
    return 1.0 / (1.0 + jnp.exp(shift - raw * scale))


def split_cores(core, values, rows_here):
    shaped = values.reshape(-1, 2, rows_here, values.shape[-1])
    first, second = shaped[:, 0], shaped[:, 1]
    is_first = core == 0
    return jnp.where(is_first, first, second), jnp.where(is_first, second, first)

MESH = pl.DeviceIdType.MESH


class Spot:
    def __init__(self):
        self.dp, self.mp = lax.axis_index("dp"), lax.axis_index("mp")
        self.dp_size, self.mp_size = lax.axis_size("dp"), lax.axis_size("mp")
        self.places = self.mp_size // 2
        self.place, self.core = lax.div(self.mp, 2), lax.rem(self.mp, 2)
        self.sibling = (self.dp, self.mp + 1 - 2 * self.core)
        self.right = (self.dp, self.mp + 2)
        self.left = (self.dp, self.mp - 2)
        self.has_right = self.place < self.places - 1
        self.has_left = self.place > 0

    def peer(self, step):
        return lax.rem(self.dp + step, self.dp_size)

    def enter(self, with_dp, with_mp):
        barrier = pltpu.get_barrier_semaphore()
        count = 0

        def greet(device):
            pl.semaphore_signal(barrier, inc=1, device_id=device, device_id_type=MESH)

        if with_mp:
            greet(self.sibling)
            pl.when(self.has_right)(lambda: greet(self.right))
            pl.when(self.has_left)(lambda: greet(self.left))
            count += 1 + self.has_right.astype(jnp.int32) + self.has_left.astype(jnp.int32)
        if with_dp:
            for step in range(1, self.dp_size):
                greet((self.peer(step), self.mp))
            count += self.dp_size - 1
        pl.semaphore_wait(barrier, count)


class Swap:
    def __init__(self, spot, source, target, send, receive):
        self.spot, self.source, self.target = spot, source, target
        self.send, self.receive = send, receive
        self.copies = [self.copy(step) for step in range(1, spot.dp_size)]

    def copy(self, step):
        spot = self.spot
        return pltpu.make_async_remote_copy(
            src_ref=self.source.at[spot.peer(step)],
            dst_ref=self.target.at[spot.dp],
            send_sem=self.send.at[step],
            recv_sem=self.receive.at[step],
            device_id=(spot.peer(step), spot.mp),
            device_id_type=MESH,
        )

    def start(self):
        for copy in self.copies:
            copy.start()
        self.keep()

    def keep(self):
        self.target[self.spot.dp] = self.source[self.spot.dp]

    def wait(self):
        for copy in self.copies:
            copy.wait()


class Gather:
    def __init__(self, spot, shard, window, sems):
        self.local = pltpu.make_async_copy(shard, window(spot.dp), sems.at[0, 0])
        self.copies = [
            pltpu.make_async_remote_copy(
                src_ref=shard,
                dst_ref=window(spot.dp),
                send_sem=sems.at[0, step],
                recv_sem=sems.at[1, step],
                device_id=(spot.peer(step), spot.mp),
                device_id_type=MESH,
            )
            for step in range(1, spot.dp_size)
        ]

    def start(self):
        for copy in self.copies:
            copy.start()
        self.local.start()

    def go_on(self):
        pass

    def wait(self):
        for copy in self.copies:
            copy.wait()
        self.local.wait()


def gather_of(spot, *arguments):
    return (RingGather if spot.dp_size == 4 else Gather)(spot, *arguments)


class RingGather:
    def __init__(self, spot, shard, window, sems):
        side = spot.dp + 1 - 2 * lax.rem(spot.dp, 2)
        across = spot.dp + 2 - 4 * lax.div(spot.dp, 2)

        def copy(source, index, kind, to, half=None):
            return pltpu.make_async_remote_copy(
                src_ref=source,
                dst_ref=window(index, half),
                send_sem=sems.at[0, kind],
                recv_sem=sems.at[1, kind],
                device_id=(to, spot.mp),
                device_id_type=MESH,
            )

        self.local = pltpu.make_async_copy(shard, window(spot.dp), sems.at[0, 4])
        self.to_side = copy(shard, spot.dp, 0, side)
        self.to_across = copy(shard, spot.dp, 1, across)
        self.on_across = copy(window(side, 0), side, 2, across, 0)
        self.on_side = copy(window(across, 1), across, 3, side, 1)

    def start(self):
        self.to_side.start()
        self.to_across.start()
        self.local.start()

    def go_on(self):
        self.to_side.wait_recv()
        self.on_across.start()
        self.to_across.wait_recv()
        self.on_side.start()

    def wait(self):
        self.to_side.wait_send()
        self.to_across.wait_send()
        self.on_across.wait()
        self.on_side.wait()
        self.local.wait()


class Spread:
    def __init__(self, spot, shard, full, sems):
        self.spot, self.shard, self.full, self.sems = spot, shard, full, sems
        self.local = pltpu.make_async_copy(shard, full.at[spot.mp], sems.at[6, 0])

    def copy(self, kind, device, p, source=None, core=None):
        at = 2 * p + (self.spot.core if core is None else core)
        return pltpu.make_async_remote_copy(
            src_ref=self.full.at[at] if source is None else source,
            dst_ref=self.full.at[at],
            send_sem=self.sems.at[kind, p],
            recv_sem=self.sems.at[kind + 1, p],
            device_id=device,
            device_id_type=MESH,
        )

    def rightward(self, p, source=None):
        return self.copy(0, self.spot.right, p, source)

    def leftward(self, p, source=None):
        return self.copy(2, self.spot.left, p, source)

    def across(self, p, source=None):
        return self.copy(4, self.spot.sibling, p, source)

    def begin(self):
        spot = self.spot
        pl.when(spot.has_right)(lambda: self.rightward(spot.place, self.shard).start())
        pl.when(spot.has_left)(lambda: self.leftward(spot.place, self.shard).start())
        self.across(spot.place, self.shard).start()
        self.local.start()

    def go_on(self, hop):
        spot = self.spot

        @pl.when(spot.place >= hop)
        def _():
            p = spot.place - hop
            self.rightward(p).wait_recv()
            pl.when(spot.has_right)(lambda: self.rightward(p).start())
            self.across(p).start()

        @pl.when(spot.place + hop < spot.places)
        def _():
            p = spot.place + hop
            self.leftward(p).wait_recv()
            pl.when(spot.has_left)(lambda: self.leftward(p).start())
            self.across(p).start()

    def finish(self):
        spot = self.spot
        for p in range(spot.places):
            self.copy(4, spot.sibling, p, core=1 - spot.core).wait_recv()
            self.across(p).wait_send()
            pl.when(spot.has_right & (spot.place >= p))(lambda: self.rightward(p).wait_send())
            pl.when(spot.has_left & (spot.place <= p))(lambda: self.leftward(p).wait_send())
        self.local.wait()


def spread_scratch(places):
    return [pltpu.SemaphoreType.DMA((7, places))]


class Ship(Swap):
    def __init__(self, spot, source, target, sems):
        super().__init__(spot, source, target, sems.at[0], sems.at[1])
        self.local = pltpu.make_async_copy(source.at[spot.dp], target.at[spot.dp], sems.at[0, 0])

    def start(self):
        for copy in self.copies:
            copy.start()
        self.local.start()

    def wait(self):
        super().wait()
        self.local.wait()


def window_of(full, axis, step, column=0, columns=None):
    def window(index, half=None):
        rows = step if axis == 0 else full.shape[0]
        first, count = (0, rows) if half is None else (half * (rows // 2), rows // 2)
        if axis == 1:
            return full.at[
                pl.ds(first, count), pl.ds(pl.multiple_of(index * step, step), step)
            ]
        along = pl.ds(pl.multiple_of(index * step + first, count), count)
        return full.at[along, pl.ds(column, full.shape[1] if columns is None else columns)]

    return window


def swap_scratch(size, *block):
    return [
        pltpu.VMEM((size, *block), BF16),
        pltpu.VMEM((size, *block), BF16),
        pltpu.SemaphoreType.DMA((size,)),
        pltpu.SemaphoreType.DMA((size,)),
    ]


def far_first(places):
    orders = []
    for place in range(places):
        right, left, order = list(range(places - 1, place, -1)), list(range(place)), []
        while right or left:
            order += right[:1] + left[:1]
            right, left = right[1:], left[1:]
        orders.append(order + [place])
    return orders


class Sum:
    def __init__(self, spot, mine, out, from_sibling, passed, sems):
        self.spot = spot
        self.mine, self.out = mine, out
        self.from_sibling, self.passed = from_sibling, passed
        self.sems = sems
        self.orders = far_first(spot.places)

    def copy(self, source, target, kind, t, device, to=None):
        return pltpu.make_async_remote_copy(
            src_ref=source.at[t],
            dst_ref=target.at[t if to is None else to],
            send_sem=self.sems.at[kind, t],
            recv_sem=self.sems.at[kind + 1, t],
            device_id=device,
            device_id_type=MESH,
        )

    def sibling(self, t):
        return self.copy(self.out, self.from_sibling, 0, t, self.spot.sibling)

    def rightward(self, t):
        return self.copy(self.mine, self.passed, 2, t, self.spot.right)

    def leftward(self, t, place):
        to = jnp.where(t == place, self.spot.places, t)
        return self.copy(self.mine, self.passed, 4, t, self.spot.left, to)

    def leftward_out(self, t):
        return self.leftward(t, self.spot.place - 1)

    def leftward_in(self, t):
        return self.leftward(t, self.spot.place)

    def term(self, s):
        chosen = 0
        for place, order in enumerate(self.orders):
            for at, t in enumerate(order):
                if t:
                    chosen = chosen + jnp.where((self.spot.place == place) & (s == at), t, 0)
        return chosen

    def add(self, t, arrived):
        self.mine[t] = (self.mine[t].astype(F32) + arrived.astype(F32)).astype(BF16)

    def absorb(self, t):
        self.sibling(t).wait_recv()
        self.add(t, self.from_sibling[t])

    def begin(self, s):
        spot = self.spot

        @pl.when((spot.place == 0) & (s < spot.places - 1))
        def _():
            t = spot.places - 1 - s
            self.absorb(t)
            self.rightward(t).start()

        @pl.when((spot.place == spot.places - 1) & (s < spot.places - 1))
        def _():
            self.absorb(s)
            self.leftward_out(s).start()

    def go_on(self, hop):
        spot = self.spot
        last = spot.places - 1

        @pl.when((spot.place > 0) & (spot.place <= hop))
        def _():
            t = last + spot.place - hop
            self.absorb(t)
            self.rightward(t).wait_recv()
            self.add(t, self.passed[t])
            self.rightward(t).start()

        @pl.when((spot.place < last) & (last - spot.place <= hop))
        def _():
            t = hop - last + spot.place
            self.absorb(t)
            self.leftward_in(t).wait_recv()
            self.add(t, self.passed[t])
            self.leftward_out(t).start()

    def finish(self):
        spot = self.spot
        t = spot.place
        self.absorb(t)

        @pl.when(spot.has_left)
        def _():
            self.rightward(t).wait_recv()
            self.add(t, self.passed[t])

        @pl.when(spot.has_right)
        def _():
            self.leftward_in(t).wait_recv()
            self.add(t, self.passed[spot.places])

        for t in range(spot.places):
            self.sibling(t).wait_send()
            pl.when(spot.place < t)(lambda: self.rightward(t).wait_send())
            pl.when(spot.place > t)(lambda: self.leftward_out(t).wait_send())
        return self.mine[spot.place].astype(F32)


def sum_scratch(places, rows_here, width):
    return [
        *[pltpu.VMEM((places, rows_here, width), BF16)] * 3,
        pltpu.VMEM((places + 1, rows_here, width), BF16),
        pltpu.SemaphoreType.DMA((6, places)),
    ]


def as_column(row):
    return jnp.broadcast_to(row, (HEAD, row.shape[1])).T[:, 0:1]


def attend_blocks(qkv, ids_ref, out, scale, shift):
    count, block = out.shape[:2]
    row_at = lax.broadcasted_iota(jnp.int32, (block, block), 0)
    col_at = lax.broadcasted_iota(jnp.int32, (block, block), 1)

    @pl.loop(0, count)
    def _(i):
        queries = qkv[i, :, 0:HEAD]
        ids = as_column(ids_ref[i])

        def add_block(j, acc, diagonal=False):
            sig = sigmoid_of(dot_nt(queries, qkv[j, :, HEAD : 2 * HEAD]), scale, shift)
            visible = ids == ids_ref[j]
            if diagonal:
                visible = visible & (col_at <= row_at)
            weights = jnp.where(visible, sig, 0.0).astype(BF16)
            return acc + dot(weights, qkv[j, :, 2 * HEAD :])

        acc = add_block(i, jnp.zeros((block, HEAD), F32), True)
        out[i] = lax.fori_loop(0, i, add_block, acc).astype(BF16)


def attend_back_blocks(
    spot, qkv, grad, ids_ref, cos_ref, sin_ref, out_q, out_kv, dq, made, midway, scale, shift
):
    count, block = grad.shape[:2]
    col_at = lax.broadcasted_iota(jnp.int32, (block, block), 0)
    row_at = lax.broadcasted_iota(jnp.int32, (block, block), 1)
    dq[...] = jnp.zeros_like(dq)

    def unrotate(values, i):
        rows = pl.ds(pl.multiple_of(i * block, block), block)
        swapped = pltpu.roll(values, HEAD // 2, 1)
        return (values * cos_ref[rows, :] - swapped * sin_ref[rows, :]).astype(BF16)

    @pl.loop(0, count)
    def _(at):
        j = spot.peer(at + 1)
        keys = qkv[j, :, HEAD : 2 * HEAD]
        values = qkv[j, :, 2 * HEAD :]
        keys_t = keys.T
        ids = as_column(ids_ref[j])

        def add_block(i, sums, diagonal=False):
            dk, dv = sums
            queries, grads = qkv[i, :, 0:HEAD], grad[i]
            sig = sigmoid_of(dot_nt(keys, queries), scale, shift)
            visible = ids == ids_ref[i]
            if diagonal:
                visible = visible & (col_at <= row_at)
            sig = jnp.where(visible, sig, 0.0)
            prob_grad = dot_nt(values, grads)
            score_grad = (prob_grad * sig * (1.0 - sig)).astype(BF16)
            dq[i] += dot(keys_t, score_grad)
            return dk + dot(score_grad, queries), dv + dot(sig.astype(BF16), grads)

        zero = jnp.zeros((block, HEAD), F32)
        dk, dv = lax.fori_loop(j + 1, count, add_block, add_block(j, (zero, zero), True))
        out_kv[j, :, 0:HEAD] = unrotate(dk * scale, j)
        out_kv[j, :, HEAD:] = dv.astype(BF16)
        pl.when(at < count - 1)(lambda: made(at + 1))
        pl.when(at == 1)(midway)

    @pl.loop(0, count)
    def _(i):
        out_q[i] = unrotate(dq[i].T * scale, i)


def take(refs, count):
    return refs[:count], refs[count:]


class Loads:
    def __init__(self, pairs, sems):
        self.copies = [
            pltpu.make_async_copy(source, target, sems.at[i])
            for i, (source, target) in enumerate(pairs)
        ]
        for copy in self.copies:
            copy.start()

    def wait(self, *which):
        for i in which or range(len(self.copies)):
            self.copies[i].wait()


def lazy_scratch(*arrays):
    return [pltpu.VMEM(array.shape, array.dtype) for array in arrays] + [
        pltpu.SemaphoreType.DMA((len(arrays),))
    ]


def put_norm(x_ref, gain_ref, out_ref):
    x = x_ref[...].astype(F32)
    out_ref[...] = (x * norm_factor(x) * gain_ref[...]).astype(BF16)


def begin_kernel(
    x_ref, gain_ref, query, key, value, out, qkv_full, out_full, first_full,
    normed, sems, spread_sems,
):
    spot = Spot()
    spot.enter(True, True)
    rows, columns = query.shape
    jobs = [
        (shard, window_of(qkv_full, 0, rows, i * columns, columns))
        for i, shard in enumerate((query, key, value))
    ]
    jobs.append((out, window_of(out_full, 1, out.shape[1])))
    gathers = [
        gather_of(spot, shard, window, sems.at[i]) for i, (shard, window) in enumerate(jobs)
    ]
    for gather in gathers:
        gather.start()
    put_norm(x_ref, gain_ref, normed)
    spread = Spread(spot, normed, first_full, spread_sems)
    spread.begin()
    spread.go_on(1)
    for gather in gathers:
        gather.go_on()
    for hop in range(2, spot.places):
        spread.go_on(hop)
    for gather in gathers:
        gather.wait()
    spread.finish()


def forward_kernel(tail, head, norms, spreads, gather_axis, heads, toks, scale, shift, *refs):
    gathers = gather_axis is not None
    tail_in, refs = take(refs, 4 * tail)
    head_in, refs = take(refs, 5 * head)
    norm_in, refs = take(refs, 2 * norms)
    spread_in, refs = take(refs, spreads - norms)
    gather_in, refs = take(refs, gathers)
    tail_out, refs = take(refs, 3 * tail)
    head_out, refs = take(refs, 2 * head)
    spread_out, refs = take(refs, spreads)
    gather_out, refs = take(refs, gathers)
    sum_refs, refs = take(refs, 5 * tail)
    head_refs, refs = take(refs, 9 * head)
    normed, refs = take(refs, norms)
    lazy, refs = take(refs, 3 * head)
    if head:
        rows_ref, weight_ref, cos_ref, sin_ref, ids_ref = head_in
        loads = Loads(zip((rows_ref, weight_ref), lazy), lazy[2])
        rows_ref, weight_ref = lazy[:2]
    spot = Spot()
    spot.enter(head or gathers, tail or spreads)
    if norms:
        put_norm(*norm_in, *normed)
        spread_in = (*normed, *spread_in)
    moving = [Spread(spot, *refs) for refs in zip(spread_in, spread_out, refs)]
    for spread in moving:
        spread.begin()
    if gathers:
        window = window_of(gather_out[0], gather_axis, gather_in[0].shape[gather_axis])
        gather = gather_of(spot, gather_in[0], window, refs[-1])
        if not (tail and head):
            gather.start()

    if tail:
        got, out_weight, x_ref, gain_ref = tail_in
        middle_ref, normed_ref, mix_ref = tail_out
        pairs = got.shape[0]
        owner_rows = toks * (pairs // heads)
        for o in range(mix_ref.shape[0] // owner_rows):
            for p in range(pairs):
                s, h = p // heads, p % heads
                mix_ref[pl.ds(o * owner_rows + s * toks, toks), h * HEAD : (h + 1) * HEAD] = got[
                    p, pl.ds(o * toks, toks), :
                ]
        summed = Sum(spot, *sum_refs)
        chip_rows = 2 * owner_rows

        @pl.loop(0, spot.places)
        def _(s):
            t = summed.term(s)
            rows = pl.ds(pl.multiple_of(t * chip_rows, chip_rows), chip_rows)
            value = dot(mix_ref[rows, :], out_weight[...]).astype(BF16)
            keep, send = split_cores(spot.core, value, owner_rows)
            summed.mine[t] = keep[0]
            summed.out[t] = send[0]
            summed.sibling(t).start()

        @pl.loop(0, spot.places - 1)
        def _(s):
            summed.begin(s)

    if head:
        qkv_ref, got_ref = head_out
        made, paired, qkv, qkv_send, qkv_recv, part, got, part_send, part_recv = head_refs
        pairs = paired.shape[0]
        owner_rows = toks * (pairs // heads)
        step = made.shape[0]
        loads.wait()

        @pl.loop(0, rows_ref.shape[0] // step)
        def _(i):
            rows = pl.ds(pl.multiple_of(i * step, step), step)
            made[...] = dot(rows_ref[rows, :], weight_ref[...])
            for j in range(step // owner_rows):
                to = pl.ds(pl.multiple_of((i * (step // owner_rows) + j) * toks, toks), toks)
                cosine, sine = cos_ref[to, :], sin_ref[to, :]
                for p in range(pairs):
                    s, h = p // heads, p % heads
                    here = pl.ds(j * owner_rows + s * toks, toks)
                    for kind in range(3):
                        piece = made[here, pl.ds((kind * heads + h) * HEAD, HEAD)]
                        if kind < 2:
                            piece = piece * cosine + pltpu.roll(piece, HEAD // 2, 1) * sine
                        paired[p, to, kind * HEAD : (kind + 1) * HEAD] = piece.astype(BF16)

        swap = Swap(spot, paired, qkv, qkv_send, qkv_recv)
        swap.start()
    if gathers and tail and head:
        gather.start()
    for spread in moving:
        spread.go_on(1)
    if tail and spot.places > 2:
        summed.go_on(1)
    if head:
        swap.wait()
        attend_blocks(qkv, ids_ref, part, scale, shift)
        swap = Swap(spot, part, got, part_send, part_recv)
        swap.start()
    for hop in range(2, spot.places - 1):
        for spread in moving:
            spread.go_on(hop)
        if tail:
            summed.go_on(hop)
    if gathers:
        gather.go_on()
    if head:
        qkv_ref[...] = qkv[...]
        swap.wait()
        got_ref[...] = got[...]
    for spread in moving:
        if spot.places > 2:
            spread.go_on(spot.places - 1)
    if tail:
        middle = x_ref[...].astype(F32) + summed.finish()
        middle_ref[...] = middle
        normed_ref[...] = (middle * norm_factor(middle) * gain_ref[...]).astype(BF16)
    for spread in moving:
        spread.finish()
    if gathers:
        gather.wait()


def middle_kernel(
    first, defer, ships, spreads, owner_rows,
    middle_ref, local_cot_ref, gain_ref, rows_in, cot_in, gate_in, up_low, up_high, down_in,
    *refs,
):
    shards, refs = take(refs, spreads)
    before, refs = take(refs, 0 if first else 3)
    (grad_ref, low_ref, gain_grad_ref), refs = take(refs, 3)
    y_out, refs = take(refs, 2 if defer else 1)
    fulls, refs = take(refs, spreads)
    after, refs = take(refs, 3)
    ship_out, refs = take(refs, ships)
    (act_ref, dgate_ref, dup_ref, turned, new_rows, new_cols, old_rows, old_cols), refs = take(refs, 8)
    (rows_ref, cot_ref, gate_ref, up_ref, down_ref, load_sems, wide_sems), refs = take(refs, 7)
    sum_refs, refs = take(refs, 5)
    y_refs, refs = take(refs, 3 if defer else 5)
    ship_sems, refs = take(refs, ships)
    size, half = after[0].shape[0], up_low.shape[0] // after[0].shape[0]
    pairs = [(rows_in, rows_ref), (gate_in, gate_ref)]
    for e in range(size):
        for i, part in enumerate((up_low, up_high)):
            to = up_ref.at[pl.ds((2 * e + i) * half, half), :]
            pairs.append((part.at[pl.ds(e * half, half), :], to))
    pairs += [(cot_in, cot_ref), (down_in, down_ref)]
    loads = Loads(pairs, load_sems)
    spot = Spot()
    spot.enter(bool(ships), True)
    if ships:
        ship = Ship(spot, after[0], ship_out[0], ship_sems[0])
    summed = Sum(spot, *sum_refs)
    if defer:
        y_mine, y_send, y_sems = y_refs
        stores = [
            pltpu.make_async_copy(source, target, y_sems.at[i])
            for i, (source, target) in enumerate(zip((y_mine, y_send), y_out))
        ]
        sums = [summed]
    else:
        summed_y = Sum(spot, *y_refs)
        y_mine, y_send = summed_y.mine, summed_y.out
        sums = [summed, summed_y]
    moving = [Spread(spot, *refs) for refs in zip(shards, fulls, refs)]
    for spread in moving:
        spread.begin()
    hidden, width = gate_ref.shape[1], rows_ref.shape[1]
    chip_rows = 2 * owner_rows
    tile = min(256, hidden)
    blocks = after[0].shape[0]
    block = width // blocks
    new = (new_rows.at[0], new_rows.at[1], new_cols)
    old = (old_rows.at[0], old_rows.at[1], old_cols)

    def load(g, e):
        return pltpu.make_async_copy(before[g].at[e], old[g], wide_sems.at[0, g])

    def store(g, e):
        return pltpu.make_async_copy(new[g], after[g].at[e], wide_sems.at[1, g])

    if not first:
        for g in range(3):
            load(g, spot.peer(1)).start()
    loads.wait()

    @pl.loop(0, spot.places)
    def _(s):
        place = summed.term(s)
        rows = pl.ds(pl.multiple_of(place * chip_rows, chip_rows), chip_rows)

        @pl.loop(0, hidden // tile)
        def _(t):
            cols = pl.ds(pl.multiple_of(t * tile, tile), tile)
            gate = dot(rows_ref[rows, :], gate_ref[:, cols])
            up = dot(rows_ref[rows, :], up_ref[:, cols])
            sig = jax.nn.sigmoid(gate)
            silu = gate * sig
            act_ref[rows, cols] = (silu * up).astype(BF16)
            grad = dot_nt(cot_ref[rows, :], down_ref[cols, :])
            dgate_ref[rows, cols] = (grad * up * sig * (1.0 + gate * (1.0 - sig))).astype(BF16)
            dup_ref[rows, cols] = (grad * silu).astype(BF16)

            @pl.when((s > 0) & (t == min(1, hidden // tile - 1)))
            def _():
                for each in sums:
                    each.begin(s - 1)

        for hop in range(1, spot.places - 1):

            @pl.when(s == hop + 1)
            def _():
                for spread in moving:
                    spread.go_on(hop)
                for each in sums:
                    each.go_on(hop)

        @pl.loop(0, width // 256)
        def _(t):
            cols = pl.ds(pl.multiple_of(t * 256, 256), 256)
            value = dot(act_ref[rows, :], down_ref[:, cols])
            keep, send = split_cores(spot.core, value.astype(BF16), owner_rows)
            y_mine[place, :, cols] = keep[0]
            y_send[place, :, cols] = send[0]
            value = dot_nt(dgate_ref[rows, :], gate_ref[cols, :])
            value += dot_nt(dup_ref[rows, :], up_ref[cols, :])
            keep, send = split_cores(spot.core, value.astype(BF16), owner_rows)
            summed.mine[place, :, cols] = keep[0]
            summed.out[place, :, cols] = send[0]

        for each in sums:
            each.sibling(place).start()

    if defer:
        for copy in stores:
            copy.start()

    def send(i):
        if ships:
            pl.when(i < blocks - 1)(lambda: ship.copy(i + 1).start())
            pl.when(i == blocks - 1)(lambda: ship.local.start())

    def make(g, i, left, right, right_at, columns):
        e = spot.peer(i + 1)

        @pl.when(i > 0)
        def _():
            store(g, spot.peer(i)).wait()
            if g == 0:
                send(i - 1)

        if not first:
            load(g, e).wait()
        step = math.gcd(columns, 256)

        @pl.loop(0, columns // step)
        def _(t):
            cols = pl.ds(pl.multiple_of(t * step, step), step)
            total = dot(left[...], right[:, pl.ds(pl.multiple_of(right_at + t * step, step), step)])
            if not first:
                total += old[g][:, cols].astype(F32)
            new[g][:, cols] = total.astype(BF16)

        if not first:
            pl.when(i < blocks - 1)(lambda: load(g, spot.peer(i + 2)).start())
        store(g, e).start()

    @pl.loop(0, blocks)
    def _(i):
        left = turned.at[pl.ds(0, block), :]
        at = spot.peer(i + 1) * block
        left[...] = rows_ref[:, pl.ds(pl.multiple_of(at, block), block)].T
        make(0, i, left, dgate_ref, 0, hidden)
        make(1, i, left, dup_ref, 0, hidden)

    if ships:
        store(0, spot.dp).wait()
        send(blocks - 1)
    for spread in moving:
        spread.go_on(spot.places - 1)
    left = turned.at[pl.ds(0, hidden), :]
    left[...] = act_ref[...].T

    @pl.loop(0, blocks)
    def _(i):
        make(2, i, left, cot_ref, spot.peer(i + 1) * block, block)

    incoming = summed.finish()
    middle = middle_ref[...]
    term, gain_grad = norm_back(middle, norm_factor(middle), gain_ref[...], incoming)
    gain_grad_ref[...] = gain_grad[None]
    grad = local_cot_ref[...].astype(F32) + term
    grad_ref[...] = grad
    low_ref[...] = grad.astype(BF16)
    if defer:
        for copy in stores:
            copy.wait()
    else:
        y_out[0][...] = (middle + summed_y.finish()).astype(BF16)
    for spread in moving:
        spread.finish()
    for g in range(ships, 3):
        store(g, spot.dp).wait()
    if ships:
        ship.wait()


def add_grads(spot, left, right, turned, before, after, made=None):
    size, rows, columns = after.shape

    @pl.loop(0, size)
    def _(i):
        e = spot.peer(i + 1)
        if rows < left.shape[1]:
            turned[...] = left[:, pl.ds(pl.multiple_of(e * rows, rows), rows)].T
            total = dot(turned[...], right[...])
        else:

            @pl.when(i == 0)
            def _():
                turned[...] = left[...].T

            cut = pl.ds(pl.multiple_of(e * columns, columns), columns)
            total = dot(turned[...], right[:, cut])
        if before is not None:
            total += before[e].astype(F32)
        after[e] = total.astype(BF16)
        if made is not None:
            made(i)


def backward_kernel(
    tail, head, last, old_tail, old_head, extra, spreads, heads, toks, scale, shift, *refs
):
    tail_in, refs = take(refs, 6 * tail)
    old_qkv, refs = take(refs, old_tail)
    head_in, refs = take(refs, 7 * head)
    old_out, refs = take(refs, old_head)
    last_in, refs = take(refs, 2 * last)
    extra_in, refs = take(refs, 3 * extra)
    spread_in, refs = take(refs, spreads)
    tail_out, refs = take(refs, (1 if last else 3) * tail)
    head_out, refs = take(refs, 2 * head)
    last_out, refs = take(refs, 3 * last)
    extra_out, refs = take(refs, extra)
    spread_out, refs = take(refs, spreads)
    tail_refs, refs = take(refs, 7 * tail)
    head_refs, refs = take(refs, 14 * head)
    last_refs, refs = take(refs, 8 * last)
    extra_refs, refs = take(refs, 6 * extra)
    lazy_tail, refs = take(refs, 3 * tail)
    lazy_old, refs = take(refs, 2 * old_tail)
    lazy_head, refs = take(refs, 5 * head)
    if head:
        rows_ref, out_weight_ref, qkv, ids_ref, cos_ref, sin_ref, mix_ref = head_in
        loads_head = Loads(zip((rows_ref, qkv, cos_ref, sin_ref), lazy_head), lazy_head[4])
        rows_ref, qkv, cos_ref, sin_ref = lazy_head[:4]
    if tail:
        proj_ref, weight_ref, rows_one_ref, x_ref, grad_ref, gain_ref = tail_in
        loads_tail = Loads(zip((weight_ref, rows_one_ref), lazy_tail), lazy_tail[2])
        weight_ref, rows_one_ref = lazy_tail[:2]
    if extra:
        loads_extra = Loads(zip(extra_in[:2], extra_refs), extra_refs[5])
    before = None
    if old_tail:
        before = lazy_old[0]
        loads_old = Loads([(old_qkv[0], before)], lazy_old[1])
    spot = Spot()
    spot.enter(head or last, tail or spreads or extra)
    moving = [Spread(spot, *refs) for refs in zip(spread_in, spread_out, refs)]
    for spread in moving:
        spread.begin()
    if last:
        out_blocks, gains = last_in
        out_target, qkv_target, gain_sum = last_out
        new_qkv, own_gain, all_dp, dp_sum, all_mp, ship_sems, gain_sems, gain_spread_sems = last_refs
        ship_out = Ship(spot, out_blocks, out_target, ship_sems.at[0])
        ship_out.start()
    early, late = [], []
    if extra:
        summed_y = Sum(spot, *extra_refs[:5])
        loads_extra.wait()
        for t in range(spot.places):
            summed_y.sibling(t).start()
        late.append(summed_y)
    if head:
        head_proj_ref, new_out = head_out
        part, got, part_send, part_recv = head_refs[:4]
        made_q, got_q, q_send, q_recv, made_kv, got_kv, kv_send, kv_recv, dq, mix_turned = head_refs[4:]
        pairs = part.shape[0]
        owner_rows = toks * (pairs // heads)
        total = rows_ref.shape[0]
        step = min(512, total)
        loads_head.wait(0)

        @pl.loop(0, total // step)
        def _(i):
            rows = pl.ds(pl.multiple_of(i * step, step), step)
            made = dot_nt(rows_ref[rows, :], out_weight_ref[...]).astype(BF16)
            for j in range(step // owner_rows):
                to = pl.ds(pl.multiple_of((i * (step // owner_rows) + j) * toks, toks), toks)
                for p in range(pairs):
                    s, h = p // heads, p % heads
                    start = j * owner_rows + s * toks
                    part[p, to, :] = made[start : start + toks, h * HEAD : (h + 1) * HEAD]

        swap = Swap(spot, part, got, part_send, part_recv)
        swap.start()

    if extra:

        @pl.loop(0, spot.places - 1)
        def _(s):
            summed_y.begin(s)

    if tail:
        result_ref = tail_out[0]
        sum_refs, (turned, gain_acc) = take(tail_refs, 5)
        if not last:
            new_qkv, gain_acc = tail_out[1:]
        owner_rows = x_ref.shape[0]
        summed = Sum(spot, *sum_refs)
        early.append(summed)
        chip_rows = 2 * owner_rows
        gain_acc[...] = jnp.zeros_like(gain_acc)
        loads_tail.wait()

        @pl.loop(0, spot.places)
        def _(s):
            t = summed.term(s)
            rows = pl.ds(pl.multiple_of(t * chip_rows, chip_rows), chip_rows)
            value = dot_nt(proj_ref[rows, :], weight_ref[...])
            gain_acc[...] += jnp.sum(
                value * rows_one_ref[rows, :].astype(F32), axis=0, keepdims=True
            )
            keep, send = split_cores(spot.core, value.astype(BF16), owner_rows)
            summed.mine[t] = keep[0]
            summed.out[t] = send[0]
            summed.sibling(t).start()
            pl.when(s > 0)(lambda: summed.begin(s - 1))

        if last:
            own_gain[...] = gains[...]
            own_gain[1:2, :] += gain_acc[...]
            gain_dp = Gather(spot, own_gain, lambda index: all_dp.at[index], gain_sems)
            gain_dp.start()
    if last:
        if old_tail:
            loads_old.wait()
        ship_qkv = Ship(spot, new_qkv, qkv_target, ship_sems.at[1])

        def send(i):
            pl.when(i < spot.dp_size - 1)(lambda: ship_qkv.copy(i + 1).start())
            pl.when(i == spot.dp_size - 1)(lambda: ship_qkv.local.start())

        add_grads(spot, rows_one_ref, proj_ref, turned, before, new_qkv, send)
        gain_dp.wait()
        dp_sum[...] = jnp.sum(all_dp[...], axis=0)
        gain_mp = Spread(spot, dp_sum, all_mp, gain_spread_sems)
        gain_mp.begin()
        gain_mp.go_on(1)
    if head:
        add_grads(
            spot, mix_ref, rows_ref, mix_turned, old_out[0] if old_head else None, new_out
        )

    def go_on(hop):
        if hop < spot.places - 1:
            for each in moving + early + late:
                each.go_on(hop)

    if not (tail and head):
        go_on(1)
    if head:
        swap.wait()
        loads_head.wait(1, 2, 3)
        swap_kv = Swap(spot, made_kv, got_kv, kv_send, kv_recv)
        attend_back_blocks(
            spot, qkv, got, ids_ref, cos_ref, sin_ref, made_q, made_kv, dq,
            lambda step: swap_kv.copy(step).start(), lambda: go_on(1 if tail else 2), scale, shift,
        )
        swap_kv.keep()
        swap = Swap(spot, made_q, got_q, q_send, q_recv)
        swap.start()
    for hop in range(2 if tail else 3, spot.places - 1):
        if last:
            gain_mp.go_on(hop)
        go_on(hop)
    if tail and not last:
        if old_tail:
            loads_old.wait()
        add_grads(spot, rows_one_ref, proj_ref, turned, before, new_qkv)
    if head:
        swap_kv.wait()
        swap.wait()
        for o in range(total // owner_rows):
            for p in range(pairs):
                s, h = p // heads, p % heads
                here, there = pl.ds(o * owner_rows + s * toks, toks), pl.ds(o * toks, toks)
                for kind in range(3):
                    piece = (
                        got_kv[p, there, (kind - 1) * HEAD : kind * HEAD] if kind else got_q[p, there, :]
                    )
                    head_proj_ref[
                        here, (kind * heads + h) * HEAD : (kind * heads + h + 1) * HEAD
                    ] = piece
    for spread in moving:
        spread.go_on(spot.places - 1)
    if last and spot.places > 2:
        gain_mp.go_on(spot.places - 1)
    if tail:
        incoming = summed.finish()
        x = x_ref[...].astype(F32)
        term, _ = norm_back(x, norm_factor(x), gain_ref[...], incoming)
        result_ref[...] = grad_ref[...] + term
    if extra:
        extra_out[0][...] = (extra_in[2][...] + summed_y.finish()).astype(BF16)
    if last:
        gain_mp.finish()
        gain_sum[...] = jnp.sum(all_mp[...], axis=0)
        ship_out.wait()
        ship_qkv.wait()
    for spread in moving:
        spread.finish()


def ffn_kernel(
    rows_ref, cot_ref, gate_ref, up_ref, down_ref, y_ref, dh_ref, act_ref, dgate_ref, dup_ref
):
    hidden = gate_ref.shape[1]
    width = rows_ref.shape[1]
    tile = min(256, hidden)

    @pl.loop(0, hidden // tile)
    def _(t):
        cols = pl.ds(pl.multiple_of(t * tile, tile), tile)
        gate = dot(rows_ref[...], gate_ref[:, cols])
        up = dot(rows_ref[...], up_ref[:, cols])
        sig = jax.nn.sigmoid(gate)
        silu = gate * sig
        act_ref[:, cols] = (silu * up).astype(BF16)
        grad = dot_nt(cot_ref[...], down_ref[cols, :])
        dgate_ref[:, cols] = (grad * up * sig * (1.0 + gate * (1.0 - sig))).astype(BF16)
        dup_ref[:, cols] = (grad * silu).astype(BF16)

    @pl.loop(0, width // 256)
    def _(t):
        cols = pl.ds(pl.multiple_of(t * 256, 256), 256)
        y_ref[:, cols] = dot(act_ref[...], down_ref[:, cols]).astype(BF16)
        dh = dot_nt(dgate_ref[...], gate_ref[cols, :]) + dot_nt(dup_ref[...], up_ref[cols, :])
        dh_ref[:, cols] = dh.astype(BF16)


def grad_kernel(count, groups, left_blocked, *refs):
    lefts, refs = take(refs, count)
    rights, refs = take(refs, count * groups)
    out_refs, (turned,) = take(refs, groups)
    rows = lefts[0].shape[0]

    def turn():
        for m, left in enumerate(lefts):
            turned[:, m * rows : (m + 1) * rows] = left[...].T

    if left_blocked:
        turn()
    else:
        pl.when(pl.program_id(0) == 0)(turn)
    tile = math.gcd(out_refs[0].shape[2], 256)
    for g, out_ref in enumerate(out_refs):
        own = rights[g * count : (g + 1) * count]

        @pl.loop(0, out_ref.shape[2] // tile)
        def _(t):
            cols = pl.ds(pl.multiple_of(t * tile, tile), tile)
            total = dot(turned[:, :rows], own[0][:, cols])
            for m in range(1, count):
                total += dot(turned[:, m * rows : (m + 1) * rows], own[m][:, cols])
            out_ref[0, :, cols] = total.astype(BF16)


VMEM = pl.BlockSpec(memory_space=pltpu.VMEM)
ANY = pl.BlockSpec(memory_space=pltpu.HBM)


def cost(flops, nbytes):
    return pl.CostEstimate(flops=flops, bytes_accessed=nbytes, transcendentals=0)


def limits(mebibytes):
    return pltpu.CompilerParams(vmem_limit_bytes=mebibytes * 2**20)


def shape(*dims, dtype=BF16):
    return jax.ShapeDtypeStruct(dims, dtype)


def comm_params(collective_id, mebibytes):
    return pltpu.CompilerParams(
        collective_id=collective_id, has_side_effects=True, vmem_limit_bytes=mebibytes * 2**20
    )


def begin(x, gain, query, key, value, out):
    size, mp_size = lax.axis_size("dp"), lax.axis_size("mp")
    rows, columns = query.shape
    return pl.pallas_call(
        begin_kernel,
        out_shape=[
            shape(rows * size, 3 * columns),
            shape(out.shape[0], out.shape[1] * size),
            shape(mp_size, *x.shape),
        ],
        in_specs=[VMEM] * 2 + [ANY] * 4,
        out_specs=[ANY] * 3,
        scratch_shapes=[
            pltpu.VMEM(x.shape, BF16),
            pltpu.SemaphoreType.DMA((4, 2, size + 1)),
            *spread_scratch(mp_size // 2),
        ],
        compiler_params=comm_params(0, 16),
        cost_estimate=cost(0, 60 * 2**20),
        name="begin",
    )(x, gain, query, key, value, out)


def forward_stage(collective_id, tail, head, norm, shard, gather, heads, toks, scale, shift):
    size, mp_size = lax.axis_size("dp"), lax.axis_size("mp")
    out_shape, scratch = [], []
    if tail:
        blocks, _, x, _ = tail
        owner_rows, width = x.shape
        total = blocks.shape[1] * blocks.shape[0] // heads
        out_shape += [
            shape(owner_rows, width, dtype=F32),
            shape(owner_rows, width),
            shape(total, heads * HEAD),
        ]
        scratch += sum_scratch(mp_size // 2, owner_rows, width)
    if head:
        total, slice_len = head[0].shape[0], head[2].shape[0]
        out_shape += [shape(size, slice_len, 3 * HEAD), shape(size, slice_len, HEAD)]
        scratch += [
            pltpu.VMEM((min(512, total), 3 * heads * HEAD), F32),
            *swap_scratch(size, slice_len, 3 * HEAD),
            *swap_scratch(size, slice_len, HEAD),
        ]
    if norm:
        scratch.append(pltpu.VMEM(norm[0].shape, BF16))
    if head:
        scratch += lazy_scratch(*head[:2])
    here, spreads = len(out_shape), bool(norm) + len(shard)
    out_shape += [shape(mp_size, *array.shape) for array in (*norm[:1], *shard)]
    scratch += spread_scratch(mp_size // 2) * spreads
    axis = None
    if gather:
        weight, axis = gather
        dims = list(weight.shape)
        dims[axis] *= size
        out_shape.append(shape(*dims))
        scratch.append(pltpu.SemaphoreType.DMA((2, size + 1)))
    arrays = [*tail, *head, *norm]
    specs = [VMEM] * len(arrays)
    if head:
        specs[len(tail) : len(tail) + 2] = [ANY] * 2
    return pl.pallas_call(
        functools.partial(
            forward_kernel,
            bool(tail), bool(head), bool(norm), spreads, axis, heads, toks, scale, shift,
        ),
        out_shape=out_shape,
        in_specs=specs + [ANY] * (len(shard) + bool(gather)),
        out_specs=[VMEM] * here + [ANY] * (spreads + bool(gather)),
        scratch_shapes=scratch,
        compiler_params=comm_params(collective_id, 52),
        cost_estimate=cost(10**10, 100 * 2**20),
        name="forward_stage",
    )(*arrays, *shard, *gather[:1])


def middle_part(
    collective_id, defer, ships, rows, cot, weights, middle, local_cot, gain, shards, before
):
    total, width = rows.shape
    gate, _, _, down = weights
    hidden = gate.shape[1]
    size, mp_size = lax.axis_size("dp"), lax.axis_size("mp")
    places = mp_size // 2
    owner_rows = middle.shape[0]
    block = width // size
    wide = [shape(size, block, hidden)] * 2 + [shape(size, hidden, block)]
    half = shape(places, owner_rows, width)
    y_scratch = sum_scratch(places, owner_rows, width)
    if defer:
        y_scratch = [*[pltpu.VMEM(half.shape, BF16)] * 2, pltpu.SemaphoreType.DMA((2,))]
    return pl.pallas_call(
        functools.partial(middle_kernel, not before, defer, ships, len(shards), owner_rows),
        out_shape=[
            shape(owner_rows, width, dtype=F32),
            shape(owner_rows, width),
            shape(1, width, dtype=F32),
            *([half, half] if defer else [shape(owner_rows, width)]),
            *[shape(mp_size, *array.shape) for array in shards],
            *wide,
            *wide[:ships],
        ],
        in_specs=[VMEM] * 3 + [ANY] * (6 + len(shards) + len(before)),
        out_specs=[VMEM] * 3 + ([ANY] * 2 if defer else [VMEM]) + [ANY] * (len(shards) + 3 + ships),
        scratch_shapes=[
            *[pltpu.VMEM((total, hidden), BF16)] * 3,
            pltpu.VMEM((max(block, hidden), total), BF16),
            pltpu.VMEM((2, block, hidden), BF16),
            pltpu.VMEM((hidden, block), BF16),
            pltpu.VMEM((2, block, hidden), BF16),
            pltpu.VMEM((hidden, block), BF16),
            *[pltpu.VMEM(array.shape, BF16) for array in (rows, cot, gate, gate, down)],
            pltpu.SemaphoreType.DMA((4 + 2 * size,)),
            pltpu.SemaphoreType.DMA((2, 3)),
            *sum_scratch(places, owner_rows, width),
            *y_scratch,
            *[pltpu.SemaphoreType.DMA((2, size))] * ships,
            *spread_scratch(places) * len(shards),
        ],
        compiler_params=comm_params(collective_id, 61),
        cost_estimate=cost(18 * total * width * hidden, 60 * 2**20),
        name="middle_part",
    )(middle, local_cot, gain, rows, cot, *weights, *shards, *before)


def backward_stage(
    collective_id, tail, old_qkv, head, old_out, last, extra, shard, heads, toks, scale, shift
):
    size, mp_size = lax.axis_size("dp"), lax.axis_size("mp")
    places = mp_size // 2
    out_shape, scratch = [], []
    if tail:
        owner_rows, width = tail[3].shape
        out_shape.append(shape(owner_rows, width, dtype=F32))
        total = tail[0].shape[0]
        wide = shape(size, width // size, 3 * heads * HEAD)
        if not last:
            out_shape += [wide, shape(1, width, dtype=F32)]
        scratch += [
            *sum_scratch(places, owner_rows, width),
            pltpu.VMEM((width // size, total), BF16),
            pltpu.VMEM((1, width), F32),
        ]
    if head:
        (total, width), slice_len = head[0].shape, head[2].shape[1]
        out_shape.append(shape(total, 3 * heads * HEAD))
        out_shape.append(shape(size, heads * HEAD, width // size))
        scratch += [
            *swap_scratch(size, slice_len, HEAD),
            *swap_scratch(size, slice_len, HEAD),
            *swap_scratch(size, slice_len, 2 * HEAD),
            pltpu.VMEM((size, HEAD, slice_len), F32),
            pltpu.VMEM((heads * HEAD, total), BF16),
        ]
    here = len(out_shape)
    if last:
        gains = last[1].shape
        out_shape += [shape(*last[0].shape), wide]
        scratch += [
            pltpu.VMEM(wide.shape, BF16),
            pltpu.VMEM(gains, F32),
            pltpu.VMEM((size, *gains), F32),
            pltpu.VMEM(gains, F32),
            pltpu.VMEM((mp_size, *gains), F32),
            pltpu.SemaphoreType.DMA((2, 2, size)),
            pltpu.SemaphoreType.DMA((2, size)),
            *spread_scratch(places),
        ]
        out_shape.append(shape(*gains, dtype=F32))
    if extra:
        out_shape.append(shape(*extra[2].shape))
        scratch += sum_scratch(places, *extra[2].shape)
        scratch.append(pltpu.SemaphoreType.DMA((2,)))
    if tail:
        scratch += lazy_scratch(tail[1], tail[2])
    scratch += lazy_scratch(*old_qkv) if old_qkv else []
    if head:
        scratch += lazy_scratch(head[0], head[2], head[4], head[5])
    scratch += spread_scratch(places) * len(shard)
    out_shape += [shape(mp_size, *array.shape) for array in shard]
    arrays = [*tail, *old_qkv, *head, *old_out]
    tail_specs = [VMEM, ANY, ANY, VMEM, VMEM, VMEM] if tail else []
    head_specs = [ANY, VMEM, ANY, VMEM, ANY, ANY, VMEM] if head else []
    specs = [*tail_specs, *[ANY] * len(old_qkv), *head_specs, *[VMEM] * len(old_out)]
    last_specs, last_outs = ([ANY, VMEM], [ANY, ANY, VMEM]) if last else ([], [])
    extra_specs, extra_outs = ([ANY, ANY, VMEM], [VMEM]) if extra else ([], [])
    return pl.pallas_call(
        functools.partial(
            backward_kernel, bool(tail), bool(head), bool(last), len(old_qkv), len(old_out),
            bool(extra), len(shard), heads, toks, scale, shift,
        ),
        out_shape=out_shape,
        in_specs=specs + last_specs + extra_specs + [ANY] * len(shard),
        out_specs=[VMEM] * here + last_outs + extra_outs + [ANY] * len(shard),
        scratch_shapes=scratch,
        compiler_params=comm_params(collective_id, 58),
        cost_estimate=cost(10**10, 100 * 2**20),
        name="backward_stage",
    )(*arrays, *last, *extra, *shard)


def ffn(rows, cot, gate, up, down):
    total, width = rows.shape
    hidden = gate.shape[1]
    step = min(512, total)
    by_rows = pl.BlockSpec((step, width), lambda i: (i, 0))
    by_hidden = pl.BlockSpec((step, hidden), lambda i: (i, 0))
    held = lambda array: pl.BlockSpec(array.shape, lambda i: (0, 0), pipeline_mode=pl.Buffered(1))
    return pl.pallas_call(
        ffn_kernel,
        grid=(total // step,),
        out_shape=[shape(total, width)] * 2 + [shape(total, hidden)] * 3,
        in_specs=[by_rows, by_rows, held(gate), held(up), held(down)],
        out_specs=[by_rows] * 2 + [by_hidden] * 3,
        compiler_params=limits(56),
        cost_estimate=cost(12 * total * width * hidden, 34 * 2**20),
        name="ffn",
    )(rows, cot, gate, up, down)


def weight_grad(lefts, groups, left_blocked):
    count = len(lefts)
    size = lax.axis_size("dp")
    rows = lefts[0].shape[0]
    m, n = lefts[0].shape[1], groups[0][0].shape[1]
    moving = lambda width: pl.BlockSpec((rows, width // size), lambda e: (0, e))
    fixed = lambda width: pl.BlockSpec(
        (rows, width), lambda e: (0, 0), pipeline_mode=pl.Buffered(1)
    )
    left_spec = moving(m) if left_blocked else fixed(m)
    right_spec = fixed(n) if left_blocked else moving(n)
    out = (m // size, n) if left_blocked else (m, n // size)
    return pl.pallas_call(
        functools.partial(grad_kernel, count, len(groups), left_blocked),
        grid=(size,),
        in_specs=[left_spec] * count + [right_spec] * (count * len(groups)),
        out_specs=[pl.BlockSpec((1, *out), lambda e: (e, 0, 0))] * len(groups),
        out_shape=[shape(size, *out)] * len(groups),
        scratch_shapes=[pltpu.VMEM((out[0], count * rows), BF16)],
        compiler_params=limits(52),
        cost_estimate=cost(2 * count * rows * m * n * len(groups), 24 * 2**20),
        name="weight_grad",
    )(*lefts, *(right for group in groups for right in group))


def first_visible(ids):
    at = jnp.arange(ids.shape[-1], dtype=jnp.int32)
    starts = jnp.concatenate([jnp.ones_like(ids[..., :1], jnp.bool_), ids[..., 1:] != ids[..., :-1]], axis=-1)
    return lax.cummax(jnp.where(starts, at, 0), axis=ids.ndim - 1)


def block_at(values, index):
    return lax.dynamic_index_in_dim(values, index, 0, keepdims=False)


def stacked(blocks):
    full = jnp.zeros((len(blocks), *blocks[0].shape), blocks[0].dtype)
    for m, block in enumerate(blocks):
        full = lax.dynamic_update_index_in_dim(full, block, m, 0)
    return full


def scatter_mp(values):
    return lax.psum_scatter(values, "mp", scatter_dimension=0, tiled=True).astype(F32)


def sliced_scores(qkv, kv_all, first, positions, scale, shift):
    raw = jnp.einsum("pqd,pkd->pqk", qkv[..., :HEAD], kv_all[..., :HEAD], preferred_element_type=F32)
    at = jnp.arange(kv_all.shape[1], dtype=jnp.int32)
    visible = (at >= first[..., None]) & (at <= positions[:, None])
    return jnp.where(visible, sigmoid_of(raw, scale, shift), 0.0)


def per_device(
    inputs,
    cotangent,
    doc_ids,
    gain_attn,
    w_query,
    w_key,
    w_value,
    w_out,
    gain_ffn,
    w_gate,
    w_up,
    w_down,
):
    dp_size = lax.axis_size("dp")
    mp_size = lax.axis_size("mp")
    micro_count, row_count, seq_count, width = inputs.shape
    slice_len = row_count * mp_size
    total_len = slice_len * dp_size
    rows_here = row_count * seq_count
    shift = math.log(total_len)
    scale = HEAD ** (-0.5)
    dp_at = lax.axis_index("dp")
    mp_at = lax.axis_index("mp")
    first_row = dp_at * slice_len
    positions = first_row + jnp.arange(slice_len, dtype=jnp.int32)
    head_width = w_query.shape[1]
    heads = head_width // HEAD
    hidden = w_gate.shape[1]
    pairs = seq_count * heads
    whole_pairs = pairs == dp_size
    cos_all, sin_all = full_tables(total_len)
    cos_slice, sin_slice = [
        lax.dynamic_slice_in_dim(table, first_row, slice_len, 0) for table in (cos_all, sin_all)
    ]

    def by_row(table):
        shaped = table.reshape(mp_size, 1, row_count, 1, HEAD)
        return jnp.broadcast_to(shaped, (mp_size, seq_count, row_count, 1, HEAD))

    def rotate(values, back=False):
        sine = -by_row(sin_slice) if back else by_row(sin_slice)
        return values * by_row(cos_slice) + swap_halves(values) * sine

    def to_pairs(values):
        shaped = values.reshape(mp_size, seq_count, row_count, heads, -1)
        return shaped.transpose(1, 3, 0, 2, 4).reshape(pairs, slice_len, -1)

    def from_pairs(values):
        shaped = values.reshape(seq_count, heads, mp_size, row_count, -1)
        return shaped.transpose(2, 0, 3, 1, 4).reshape(mp_size * rows_here, heads, -1)

    def to_rows(values):
        return jnp.swapaxes(values, 0, 1).reshape(rows_here, width)

    def from_rows(values):
        return jnp.swapaxes(values.reshape(seq_count, row_count, width), 0, 1)

    def gather_mp(values):
        return lax.all_gather(values, "mp", axis=0, tiled=True)

    gain_attn_grad = jnp.zeros((width,), F32)
    gain_ffn_grad = jnp.zeros((width,), F32)
    results = []
    input_grads = []
    kept = [[] for _ in range(9)]
    xs = [to_rows(inputs[m]) for m in range(micro_count)]
    cots = [to_rows(cotangent[m]) for m in range(micro_count)]
    micros = range(micro_count)
    if whole_pairs:
        stage = (heads, row_count, scale, shift)
        ids = [
            block_at(doc_ids[m], dp_at // heads).astype(F32).reshape(dp_size, 1, slice_len)
            for m in micros
        ]
        last = micro_count - 1

        def whole(blocks):
            return blocks.reshape(mp_size * rows_here, width)

        def scatter_dp(blocks):
            flat = blocks.reshape(-1, blocks.shape[-1])
            return lax.psum_scatter(flat, "dp", scatter_dimension=0, tiled=True).astype(F32)

        qkv_full, out_full, rows_one = begin(
            xs[0], gain_attn[None], w_query, w_key, w_value, w_out
        )
        cut = w_up.shape[0] // 2
        gathers = {
            0: (w_gate, 0), 1: (w_up[:cut], 0), 2: (w_up[cut:], 0), micro_count: (w_down, 1)
        }
        wide = []
        ones, qkvs, got, middles, lows, twos, mixtures = [whole(rows_one)], [], [], [], [], [], []
        for m in range(micro_count + 1):
            tail, head, norm, shard = (), (), (), ()
            if m:
                tail = (got[m - 1], out_full, xs[m - 1], gain_ffn[None])
            if m < micro_count:
                head = (ones[m], qkv_full, cos_slice, sin_slice, ids[m])
            if m < last:
                norm = (xs[m + 1], gain_attn[None])
            elif lows:
                shard = (lows[m - last],)
            if m == 0:
                shard += (cots[0],)
            outs = forward_stage(10 + m, tail, head, norm, shard, gathers.get(m, ()), *stage)
            if tail:
                (middle, low, mixture), outs = take(outs, 3)
                middles.append(middle)
                lows.append(low)
                mixtures.append(mixture)
            if head:
                (qkv, block), outs = take(outs, 2)
                qkvs.append(qkv)
                got.append(block)
            if norm or shard:
                (ones if m < last else twos).append(whole(outs[0]))
            if m == 0:
                portions = [whole(outs[1])]
            if m in gathers:
                wide.append(outs[-1])
        grads, low_grads, attns, projs, sums, gain_parts, later = [], [], [], [], [], [], []
        for m in micros:
            shard = (lows[len(twos)] if len(twos) < micro_count else low_grads[len(attns)],)
            if m < last:
                shard += (cots[m + 1],)
            defer = m == 0
            grad, low, gain_part, *others = middle_part(
                30 + m, defer, int(m == last), twos[m], portions[m], wide, middles[m], cots[m], gain_ffn[None],
                shard, sums,
            )
            ys, (full, *others) = take(others, 2 if defer else 1)
            later.append((*ys, middles[m]) if defer else ys)
            (twos if len(twos) < micro_count else attns).append(whole(full))
            if m < last:
                portions.append(whole(others[0]))
            sums, gate_blocks = take(others[m < last :], 3)
            grads.append(grad)
            low_grads.append(low)
            gain_parts.append(gain_part)
        sum_up, sum_down = [scatter_dp(blocks) for blocks in sums[1:]]
        sum_gate = jnp.sum(gate_blocks[0].astype(F32), axis=0)
        old_qkv, old_out, attn_parts, finished = (), (), [], list(later)
        for m in range(micro_count + 1):
            tail, head, shard, final = (), (), (), ()
            if m:
                tail = (projs[m - 1], qkv_full, ones[m - 1], xs[m - 1], grads[m - 1], gain_attn[None])
            if m < micro_count:
                head = (attns[m], out_full, qkvs[m], ids[m], cos_all, sin_all, mixtures[m])
            else:
                rows = [sum(gain_parts), sum(attn_parts), jnp.zeros((6, width), F32)]
                final = (*old_out, jnp.concatenate(rows, axis=0))
            if len(attns) < micro_count:
                shard = (low_grads[len(attns)],)
            extra = later[0] if m == 0 else ()
            outs = backward_stage(
                20 + m, tail, old_qkv, head, () if final else old_out, final, extra, shard, *stage
            )
            if tail:
                (input_grad,), outs = take(outs, 1)
                input_grads.append(from_rows(input_grad))
            if tail and head:
                (new_qkv, gain_part), outs = take(outs, 2)
                old_qkv = (new_qkv,)
                attn_parts.append(gain_part)
            if head:
                (proj, new_out), outs = take(outs, 2)
                projs.append(proj)
                old_out = (new_out,)
            if extra:
                finished[0] = outs[:1]
            if shard:
                attns.append(whole(outs[-1]))
        results = [from_rows(result[0]) for result in finished]
        sum_out, sum_qkv = (jnp.sum(blocks.astype(F32), axis=0) for blocks in outs[:2])
        gain_sums = (outs[2][1] / gain_attn, outs[2][0])
    else:
        qkv_full = lax.all_gather(
            jnp.concatenate([w_query, w_key, w_value], axis=1), "dp", axis=0, tiled=True
        )
        out_full = lax.all_gather(w_out, "dp", axis=1, tiled=True)
        gate_full = lax.all_gather(w_gate, "dp", axis=0, tiled=True)
        up_full = lax.all_gather(w_up, "dp", axis=0, tiled=True)
        down_full = lax.all_gather(w_down, "dp", axis=1, tiled=True)
        first_all = first_visible(doc_ids)
        normed = [
            (x.astype(F32) * norm_factor(x.astype(F32)) * gain_attn).astype(BF16) for x in xs
        ]
        for micro in micros:
            local_rows = xs[micro].astype(F32)
            local_cot = cots[micro]
            factor_one = norm_factor(local_rows)
            rows_one = gather_mp(normed[micro])
            portion = gather_mp(local_cot)
            projected = dot(rows_one, qkv_full).reshape(
                mp_size, seq_count, row_count, 3, heads, HEAD
            )
            packed = to_pairs(
                jnp.concatenate(
                    [
                        rotate(projected[:, :, :, 0]).astype(BF16),
                        rotate(projected[:, :, :, 1]).astype(BF16),
                        projected[:, :, :, 2].astype(BF16),
                    ],
                    axis=-1,
                )
            )
            kv_all = lax.all_gather(packed[..., HEAD:], "dp", axis=1, tiled=True)
            first = lax.dynamic_slice_in_dim(first_all[micro], first_row, slice_len, 1)
            first = jnp.repeat(first, heads, axis=0)
            weights = sliced_scores(packed, kv_all, first, positions, scale, shift)
            attended = jnp.einsum(
                "pqk,pkd->pqd", weights.astype(BF16), kv_all[..., HEAD:], preferred_element_type=F32
            ).astype(BF16)
            mixture = from_pairs(attended).reshape(mp_size * rows_here, head_width)
            middle = local_rows + scatter_mp(dot(mixture, out_full).astype(BF16))
            factor_two = norm_factor(middle)
            rows_two = gather_mp((middle * factor_two * gain_ffn).astype(BF16))
            y, dh, activated, gate_grad, up_grad = ffn(
                rows_two, portion, gate_full, up_full, down_full
            )
            results.append(from_rows((middle + scatter_mp(y)).astype(BF16)))
            middle_term, gain_part = norm_back(middle, factor_two, gain_ffn, scatter_mp(dh))
            gain_ffn_grad = gain_ffn_grad + gain_part
            middle_grad = local_cot.astype(F32) + middle_term
            attn_portion = gather_mp(middle_grad.astype(BF16))
            mix_grad = to_pairs(dot_nt(attn_portion, out_full).astype(BF16))
            sig = sliced_scores(packed, kv_all, first, positions, scale, shift)
            prob_grad = jnp.einsum(
                "pqd,pkd->pqk", mix_grad, kv_all[..., HEAD:], preferred_element_type=F32
            )
            score_grad = (prob_grad * sig * (1.0 - sig)).astype(BF16)
            dq = jnp.einsum("pqk,pkd->pqd", score_grad, kv_all[..., :HEAD], preferred_element_type=F32)
            dk = jnp.einsum("pqk,pqd->pkd", score_grad, packed[..., :HEAD], preferred_element_type=F32)
            dv = jnp.einsum("pqk,pqd->pkd", sig.astype(BF16), mix_grad, preferred_element_type=F32)
            dkv = lax.psum_scatter(
                jnp.concatenate([dk * scale, dv], axis=-1).astype(BF16), "dp", scatter_dimension=1, tiled=True
            ).astype(F32)
            back = from_pairs(jnp.concatenate([dq * scale, dkv], axis=-1))
            back = back.reshape(mp_size, seq_count, row_count, heads, 3 * HEAD)
            proj_grad = jnp.stack(
                [
                    rotate(back[..., :HEAD], True),
                    rotate(back[..., HEAD : 2 * HEAD], True),
                    back[..., 2 * HEAD :],
                ],
                axis=3,
            ).astype(BF16).reshape(mp_size * rows_here, 3 * head_width)
            partial_grad = dot_nt(proj_grad, qkv_full)
            gain_attn_grad = gain_attn_grad + jnp.sum(partial_grad * rows_one.astype(F32), axis=0)
            input_term, _ = norm_back(
                local_rows, factor_one, gain_attn, scatter_mp(partial_grad.astype(BF16))
            )
            input_grads.append(from_rows(middle_grad + input_term))
            for held, array in zip(
                kept,
                (rows_one, proj_grad, mixture, attn_portion, rows_two, gate_grad, up_grad, activated, portion),
            ):
                held.append(array)

        def scatter_dp(lefts, rights, left_blocked):
            (blocks,) = weight_grad(lefts, (rights,), left_blocked)
            return lax.psum_scatter(blocks, "dp", scatter_dimension=0, tiled=True)[0].astype(F32)

        ones, projs, mixtures, attns, twos, gates, ups, acts, portions = kept
        sum_gate = scatter_dp(twos, gates, True)
        sum_up = scatter_dp(twos, ups, True)
        sum_down = scatter_dp(acts, portions, False)
        sum_out = scatter_dp(mixtures, attns, False)
        sum_qkv = scatter_dp(ones, projs, True)
        gain_sums = lax.psum((gain_attn_grad / gain_attn, gain_ffn_grad), ("dp", "mp"))
    return (
        stacked(results),
        stacked(input_grads),
        gain_sums[0],
        sum_qkv[:, :head_width],
        sum_qkv[:, head_width : 2 * head_width],
        sum_qkv[:, 2 * head_width :],
        sum_out,
        gain_sums[1],
        sum_gate,
        sum_up,
        sum_down,
    )


def solution(mesh):
    tokens = P(None, ("dp", "mp"), None, None)
    column = P("dp", "mp")
    row = P("mp", "dp")
    return jax.shard_map(
        per_device,
        mesh=mesh,
        in_specs=(
            tokens, tokens, P(), P(), column, column, column, row, P(), column, column, row,
        ),
        out_specs=(
            tokens, tokens, P(), column, column, column, row, P(), column, column, row,
        ),
        check_vma=False,
    )
```

```python
import functools
import math

import jax
import jax.numpy as jnp
import numpy as np
from jax import lax
from jax.experimental import pallas as pl
from jax.experimental.pallas import tpu as pltpu
from jax.sharding import PartitionSpec as P

HEAD = 128
epsilon = 1e-05
rope_base = 10000.0
F32 = jnp.float32
BF16 = jnp.bfloat16


def full_tables(total):
    half_size = HEAD // 2
    exponents = -(np.arange(half_size, dtype=np.float32) * np.float32(2.0 / HEAD))
    inverse = np.power(np.float32(rope_base), exponents)
    angles = np.arange(total, dtype=np.float32)[:, None] * inverse[None, :]
    cosine, sine = np.cos(angles), np.sin(angles)
    return (
        jnp.asarray(np.concatenate([cosine, cosine], axis=-1)),
        jnp.asarray(np.concatenate([-sine, sine], axis=-1)),
    )


def swap_halves(values):
    half_size = HEAD // 2
    return jnp.concatenate([values[..., half_size:], values[..., :half_size]], axis=-1)


def dot(left, right):
    return jnp.dot(left, right, preferred_element_type=F32)


def dot_tn(left, right):
    return lax.dot_general(left, right, (((0,), (0,)), ((), ())), preferred_element_type=F32)


def dot_nt(left, right):
    return lax.dot_general(left, right, (((1,), (1,)), ((), ())), preferred_element_type=F32)


def norm_factor(values):
    return lax.rsqrt(jnp.mean(values * values, axis=-1, keepdims=True) + epsilon)


def norm_back(values, factor, gain, incoming):
    scaled = incoming * gain
    gain_term = jnp.sum(incoming * values * factor, axis=0)
    input_term = factor * scaled - values * factor**3 * jnp.mean(
        scaled * values, axis=-1, keepdims=True
    )
    return (input_term, gain_term)


def sigmoid_of(raw, scale, shift):
    return 1.0 / (1.0 + jnp.exp(shift - raw * scale))


def split_cores(core, values, rows_here):
    shaped = values.reshape(-1, 2, rows_here, values.shape[-1])
    first, second = shaped[:, 0], shaped[:, 1]
    is_first = core == 0
    return jnp.where(is_first, first, second), jnp.where(is_first, second, first)

MESH = pl.DeviceIdType.MESH


class Spot:
    def __init__(self):
        self.dp, self.mp = lax.axis_index("dp"), lax.axis_index("mp")
        self.dp_size, self.mp_size = lax.axis_size("dp"), lax.axis_size("mp")
        self.places = self.mp_size // 2
        self.place, self.core = lax.div(self.mp, 2), lax.rem(self.mp, 2)
        self.sibling = (self.dp, self.mp + 1 - 2 * self.core)
        self.right = (self.dp, self.mp + 2)
        self.left = (self.dp, self.mp - 2)
        self.has_right = self.place < self.places - 1
        self.has_left = self.place > 0

    def peer(self, step):
        return lax.rem(self.dp + step, self.dp_size)

    def enter(self, with_dp, with_mp):
        barrier = pltpu.get_barrier_semaphore()
        count = 0

        def greet(device):
            pl.semaphore_signal(barrier, inc=1, device_id=device, device_id_type=MESH)

        if with_mp:
            greet(self.sibling)
            pl.when(self.has_right)(lambda: greet(self.right))
            pl.when(self.has_left)(lambda: greet(self.left))
            count += 1 + self.has_right.astype(jnp.int32) + self.has_left.astype(jnp.int32)
        if with_dp:
            for step in range(1, self.dp_size):
                greet((self.peer(step), self.mp))
            count += self.dp_size - 1
        pl.semaphore_wait(barrier, count)


class Swap:
    def __init__(self, spot, source, target, send, receive):
        self.spot, self.source, self.target = spot, source, target
        self.send, self.receive = send, receive
        self.copies = [self.copy(step) for step in range(1, spot.dp_size)]

    def copy(self, step):
        spot = self.spot
        return pltpu.make_async_remote_copy(
            src_ref=self.source.at[spot.peer(step)],
            dst_ref=self.target.at[spot.dp],
            send_sem=self.send.at[step],
            recv_sem=self.receive.at[step],
            device_id=(spot.peer(step), spot.mp),
            device_id_type=MESH,
        )

    def start(self):
        for copy in self.copies:
            copy.start()
        self.keep()

    def keep(self):
        self.target[self.spot.dp] = self.source[self.spot.dp]

    def wait(self):
        for copy in self.copies:
            copy.wait()


class Gather:
    def __init__(self, spot, shard, window, sems):
        self.local = pltpu.make_async_copy(shard, window(spot.dp), sems.at[0, 0])
        self.copies = [
            pltpu.make_async_remote_copy(
                src_ref=shard,
                dst_ref=window(spot.dp),
                send_sem=sems.at[0, step],
                recv_sem=sems.at[1, step],
                device_id=(spot.peer(step), spot.mp),
                device_id_type=MESH,
            )
            for step in range(1, spot.dp_size)
        ]

    def start(self):
        for copy in self.copies:
            copy.start()
        self.local.start()

    def go_on(self):
        pass

    def wait(self):
        for copy in self.copies:
            copy.wait()
        self.local.wait()


def gather_of(spot, *arguments):
    return (RingGather if spot.dp_size == 4 else Gather)(spot, *arguments)


class RingGather:
    def __init__(self, spot, shard, window, sems):
        side = spot.dp + 1 - 2 * lax.rem(spot.dp, 2)
        across = spot.dp + 2 - 4 * lax.div(spot.dp, 2)

        def copy(source, index, kind, to, half=None):
            return pltpu.make_async_remote_copy(
                src_ref=source,
                dst_ref=window(index, half),
                send_sem=sems.at[0, kind],
                recv_sem=sems.at[1, kind],
                device_id=(to, spot.mp),
                device_id_type=MESH,
            )

        self.local = pltpu.make_async_copy(shard, window(spot.dp), sems.at[0, 4])
        self.to_side = copy(shard, spot.dp, 0, side)
        self.to_across = copy(shard, spot.dp, 1, across)
        self.on_across = copy(window(side, 0), side, 2, across, 0)
        self.on_side = copy(window(across, 1), across, 3, side, 1)

    def start(self):
        self.to_side.start()
        self.to_across.start()
        self.local.start()

    def go_on(self):
        self.to_side.wait_recv()
        self.on_across.start()
        self.to_across.wait_recv()
        self.on_side.start()

    def wait(self):
        self.to_side.wait_send()
        self.to_across.wait_send()
        self.on_across.wait()
        self.on_side.wait()
        self.local.wait()


class Spread:
    def __init__(self, spot, shard, full, sems):
        self.spot, self.shard, self.full, self.sems = spot, shard, full, sems
        self.local = pltpu.make_async_copy(shard, full.at[spot.mp], sems.at[6, 0])

    def copy(self, kind, device, p, source=None, core=None):
        at = 2 * p + (self.spot.core if core is None else core)
        return pltpu.make_async_remote_copy(
            src_ref=self.full.at[at] if source is None else source,
            dst_ref=self.full.at[at],
            send_sem=self.sems.at[kind, p],
            recv_sem=self.sems.at[kind + 1, p],
            device_id=device,
            device_id_type=MESH,
        )

    def rightward(self, p, source=None):
        return self.copy(0, self.spot.right, p, source)

    def leftward(self, p, source=None):
        return self.copy(2, self.spot.left, p, source)

    def across(self, p, source=None):
        return self.copy(4, self.spot.sibling, p, source)

    def begin(self):
        spot = self.spot
        pl.when(spot.has_right)(lambda: self.rightward(spot.place, self.shard).start())
        pl.when(spot.has_left)(lambda: self.leftward(spot.place, self.shard).start())
        self.across(spot.place, self.shard).start()
        self.local.start()

    def go_on(self, hop):
        spot = self.spot

        @pl.when(spot.place >= hop)
        def _():
            p = spot.place - hop
            self.rightward(p).wait_recv()
            pl.when(spot.has_right)(lambda: self.rightward(p).start())
            self.across(p).start()

        @pl.when(spot.place + hop < spot.places)
        def _():
            p = spot.place + hop
            self.leftward(p).wait_recv()
            pl.when(spot.has_left)(lambda: self.leftward(p).start())
            self.across(p).start()

    def finish(self):
        spot = self.spot
        for p in range(spot.places):
            self.copy(4, spot.sibling, p, core=1 - spot.core).wait_recv()
            self.across(p).wait_send()
            pl.when(spot.has_right & (spot.place >= p))(lambda: self.rightward(p).wait_send())
            pl.when(spot.has_left & (spot.place <= p))(lambda: self.leftward(p).wait_send())
        self.local.wait()


def spread_scratch(places):
    return [pltpu.SemaphoreType.DMA((7, places))]


class Ship(Swap):
    def __init__(self, spot, source, target, sems):
        super().__init__(spot, source, target, sems.at[0], sems.at[1])
        self.local = pltpu.make_async_copy(source.at[spot.dp], target.at[spot.dp], sems.at[0, 0])

    def start(self):
        for copy in self.copies:
            copy.start()
        self.local.start()

    def wait(self):
        super().wait()
        self.local.wait()


def window_of(full, axis, step, column=0, columns=None):
    def window(index, half=None):
        rows = step if axis == 0 else full.shape[0]
        first, count = (0, rows) if half is None else (half * (rows // 2), rows // 2)
        if axis == 1:
            return full.at[
                pl.ds(first, count), pl.ds(pl.multiple_of(index * step, step), step)
            ]
        along = pl.ds(pl.multiple_of(index * step + first, count), count)
        return full.at[along, pl.ds(column, full.shape[1] if columns is None else columns)]

    return window


def swap_scratch(size, *block):
    return [
        pltpu.VMEM((size, *block), BF16),
        pltpu.VMEM((size, *block), BF16),
        pltpu.SemaphoreType.DMA((size,)),
        pltpu.SemaphoreType.DMA((size,)),
    ]


def far_first(places):
    orders = []
    for place in range(places):
        right, left, order = list(range(places - 1, place, -1)), list(range(place)), []
        while right or left:
            order += right[:1] + left[:1]
            right, left = right[1:], left[1:]
        orders.append(order + [place])
    return orders


class Sum:
    def __init__(self, spot, mine, out, from_sibling, passed, sems):
        self.spot = spot
        self.mine, self.out = mine, out
        self.from_sibling, self.passed = from_sibling, passed
        self.sems = sems
        self.orders = far_first(spot.places)

    def copy(self, source, target, kind, t, device, to=None):
        return pltpu.make_async_remote_copy(
            src_ref=source.at[t],
            dst_ref=target.at[t if to is None else to],
            send_sem=self.sems.at[kind, t],
            recv_sem=self.sems.at[kind + 1, t],
            device_id=device,
            device_id_type=MESH,
        )

    def sibling(self, t):
        return self.copy(self.out, self.from_sibling, 0, t, self.spot.sibling)

    def rightward(self, t):
        return self.copy(self.mine, self.passed, 2, t, self.spot.right)

    def leftward(self, t, place):
        to = jnp.where(t == place, self.spot.places, t)
        return self.copy(self.mine, self.passed, 4, t, self.spot.left, to)

    def leftward_out(self, t):
        return self.leftward(t, self.spot.place - 1)

    def leftward_in(self, t):
        return self.leftward(t, self.spot.place)

    def term(self, s):
        chosen = 0
        for place, order in enumerate(self.orders):
            for at, t in enumerate(order):
                if t:
                    chosen = chosen + jnp.where((self.spot.place == place) & (s == at), t, 0)
        return chosen

    def add(self, t, arrived):
        self.mine[t] = (self.mine[t].astype(F32) + arrived.astype(F32)).astype(BF16)

    def absorb(self, t):
        self.sibling(t).wait_recv()
        self.add(t, self.from_sibling[t])

    def begin(self, s):
        spot = self.spot

        @pl.when((spot.place == 0) & (s < spot.places - 1))
        def _():
            t = spot.places - 1 - s
            self.absorb(t)
            self.rightward(t).start()

        @pl.when((spot.place == spot.places - 1) & (s < spot.places - 1))
        def _():
            self.absorb(s)
            self.leftward_out(s).start()

    def go_on(self, hop):
        spot = self.spot
        last = spot.places - 1

        @pl.when((spot.place > 0) & (spot.place <= hop))
        def _():
            t = last + spot.place - hop
            self.absorb(t)
            self.rightward(t).wait_recv()
            self.add(t, self.passed[t])
            self.rightward(t).start()

        @pl.when((spot.place < last) & (last - spot.place <= hop))
        def _():
            t = hop - last + spot.place
            self.absorb(t)
            self.leftward_in(t).wait_recv()
            self.add(t, self.passed[t])
            self.leftward_out(t).start()

    def finish(self):
        spot = self.spot
        t = spot.place
        self.absorb(t)

        @pl.when(spot.has_left)
        def _():
            self.rightward(t).wait_recv()
            self.add(t, self.passed[t])

        @pl.when(spot.has_right)
        def _():
            self.leftward_in(t).wait_recv()
            self.add(t, self.passed[spot.places])

        for t in range(spot.places):
            self.sibling(t).wait_send()
            pl.when(spot.place < t)(lambda: self.rightward(t).wait_send())
            pl.when(spot.place > t)(lambda: self.leftward_out(t).wait_send())
        return self.mine[spot.place].astype(F32)


def sum_scratch(places, rows_here, width):
    return [
        *[pltpu.VMEM((places, rows_here, width), BF16)] * 3,
        pltpu.VMEM((places + 1, rows_here, width), BF16),
        pltpu.SemaphoreType.DMA((6, places)),
    ]


def as_column(row):
    return jnp.broadcast_to(row, (HEAD, row.shape[1])).T[:, 0:1]


def attend_blocks(qkv, ids_ref, out, scale, shift):
    count, block = out.shape[:2]
    row_at = lax.broadcasted_iota(jnp.int32, (block, block), 0)
    col_at = lax.broadcasted_iota(jnp.int32, (block, block), 1)

    @pl.loop(0, count)
    def _(i):
        queries = qkv[i, :, 0:HEAD]
        ids = as_column(ids_ref[i])

        def add_block(j, acc, diagonal=False):
            sig = sigmoid_of(dot_nt(queries, qkv[j, :, HEAD : 2 * HEAD]), scale, shift)
            visible = ids == ids_ref[j]
            if diagonal:
                visible = visible & (col_at <= row_at)
            weights = jnp.where(visible, sig, 0.0).astype(BF16)
            return acc + dot(weights, qkv[j, :, 2 * HEAD :])

        acc = add_block(i, jnp.zeros((block, HEAD), F32), True)
        out[i] = lax.fori_loop(0, i, add_block, acc).astype(BF16)


def attend_back_blocks(
    spot, qkv, grad, ids_ref, cos_ref, sin_ref, out_q, out_kv, dq, made, midway, scale, shift
):
    count, block = grad.shape[:2]
    col_at = lax.broadcasted_iota(jnp.int32, (block, block), 0)
    row_at = lax.broadcasted_iota(jnp.int32, (block, block), 1)
    dq[...] = jnp.zeros_like(dq)

    def unrotate(values, i):
        rows = pl.ds(pl.multiple_of(i * block, block), block)
        swapped = pltpu.roll(values, HEAD // 2, 1)
        return (values * cos_ref[rows, :] - swapped * sin_ref[rows, :]).astype(BF16)

    @pl.loop(0, count)
    def _(at):
        j = spot.peer(at + 1)
        keys = qkv[j, :, HEAD : 2 * HEAD]
        values = qkv[j, :, 2 * HEAD :]
        keys_t = keys.T
        ids = as_column(ids_ref[j])

        def add_block(i, sums, diagonal=False):
            dk, dv = sums
            queries, grads = qkv[i, :, 0:HEAD], grad[i]
            sig = sigmoid_of(dot_nt(keys, queries), scale, shift)
            visible = ids == ids_ref[i]
            if diagonal:
                visible = visible & (col_at <= row_at)
            sig = jnp.where(visible, sig, 0.0)
            prob_grad = dot_nt(values, grads)
            score_grad = (prob_grad * sig * (1.0 - sig)).astype(BF16)
            dq[i] += dot(keys_t, score_grad)
            return dk + dot(score_grad, queries), dv + dot(sig.astype(BF16), grads)

        zero = jnp.zeros((block, HEAD), F32)
        dk, dv = lax.fori_loop(j + 1, count, add_block, add_block(j, (zero, zero), True))
        out_kv[j, :, 0:HEAD] = unrotate(dk * scale, j)
        out_kv[j, :, HEAD:] = dv.astype(BF16)
        pl.when(at < count - 1)(lambda: made(at + 1))
        pl.when(at == 1)(midway)

    @pl.loop(0, count)
    def _(i):
        out_q[i] = unrotate(dq[i].T * scale, i)


def take(refs, count):
    return refs[:count], refs[count:]


class Loads:
    def __init__(self, pairs, sems):
        self.copies = [
            pltpu.make_async_copy(source, target, sems.at[i])
            for i, (source, target) in enumerate(pairs)
        ]
        for copy in self.copies:
            copy.start()

    def wait(self, *which):
        for i in which or range(len(self.copies)):
            self.copies[i].wait()


def lazy_scratch(*arrays):
    return [pltpu.VMEM(array.shape, array.dtype) for array in arrays] + [
        pltpu.SemaphoreType.DMA((len(arrays),))
    ]


def put_norm(x_ref, gain_ref, out_ref):
    x = x_ref[...].astype(F32)
    out_ref[...] = (x * norm_factor(x) * gain_ref[...]).astype(BF16)


def begin_kernel(
    x_ref, gain_ref, query, key, value, out, qkv_full, out_full, first_full,
    normed, sems, spread_sems,
):
    spot = Spot()
    spot.enter(True, True)
    rows, columns = query.shape
    jobs = [
        (shard, window_of(qkv_full, 0, rows, i * columns, columns))
        for i, shard in enumerate((query, key, value))
    ]
    jobs.append((out, window_of(out_full, 1, out.shape[1])))
    gathers = [
        gather_of(spot, shard, window, sems.at[i]) for i, (shard, window) in enumerate(jobs)
    ]
    for gather in gathers:
        gather.start()
    put_norm(x_ref, gain_ref, normed)
    spread = Spread(spot, normed, first_full, spread_sems)
    spread.begin()
    spread.go_on(1)
    for gather in gathers:
        gather.go_on()
    for hop in range(2, spot.places):
        spread.go_on(hop)
    for gather in gathers:
        gather.wait()
    spread.finish()


def forward_kernel(tail, head, norms, spreads, gather_axis, heads, toks, scale, shift, *refs):
    gathers = gather_axis is not None
    tail_in, refs = take(refs, 4 * tail)
    head_in, refs = take(refs, 5 * head)
    norm_in, refs = take(refs, 2 * norms)
    spread_in, refs = take(refs, spreads - norms)
    gather_in, refs = take(refs, gathers)
    tail_out, refs = take(refs, 3 * tail)
    head_out, refs = take(refs, 2 * head)
    spread_out, refs = take(refs, spreads)
    gather_out, refs = take(refs, gathers)
    sum_refs, refs = take(refs, 5 * tail)
    head_refs, refs = take(refs, 9 * head)
    normed, refs = take(refs, norms)
    lazy, refs = take(refs, 3 * head)
    if head:
        rows_ref, weight_ref, cos_ref, sin_ref, ids_ref = head_in
        loads = Loads(zip((rows_ref, weight_ref), lazy), lazy[2])
        rows_ref, weight_ref = lazy[:2]
    spot = Spot()
    spot.enter(head or gathers, tail or spreads)
    if norms:
        put_norm(*norm_in, *normed)
        spread_in = (*normed, *spread_in)
    moving = [Spread(spot, *refs) for refs in zip(spread_in, spread_out, refs)]
    for spread in moving:
        spread.begin()
    if gathers:
        window = window_of(gather_out[0], gather_axis, gather_in[0].shape[gather_axis])
        gather = gather_of(spot, gather_in[0], window, refs[-1])
        if not (tail and head):
            gather.start()

    if tail:
        got, out_weight, x_ref, gain_ref = tail_in
        middle_ref, normed_ref, mix_ref = tail_out
        pairs = got.shape[0]
        owner_rows = toks * (pairs // heads)
        for o in range(mix_ref.shape[0] // owner_rows):
            for p in range(pairs):
                s, h = p // heads, p % heads
                mix_ref[pl.ds(o * owner_rows + s * toks, toks), h * HEAD : (h + 1) * HEAD] = got[
                    p, pl.ds(o * toks, toks), :
                ]
        summed = Sum(spot, *sum_refs)
        chip_rows = 2 * owner_rows

        @pl.loop(0, spot.places)
        def _(s):
            t = summed.term(s)
            rows = pl.ds(pl.multiple_of(t * chip_rows, chip_rows), chip_rows)
            value = dot(mix_ref[rows, :], out_weight[...]).astype(BF16)
            keep, send = split_cores(spot.core, value, owner_rows)
            summed.mine[t] = keep[0]
            summed.out[t] = send[0]
            summed.sibling(t).start()

        @pl.loop(0, spot.places - 1)
        def _(s):
            summed.begin(s)

    if head:
        qkv_ref, got_ref = head_out
        made, paired, qkv, qkv_send, qkv_recv, part, got, part_send, part_recv = head_refs
        pairs = paired.shape[0]
        owner_rows = toks * (pairs // heads)
        step = made.shape[0]
        loads.wait()

        @pl.loop(0, rows_ref.shape[0] // step)
        def _(i):
            rows = pl.ds(pl.multiple_of(i * step, step), step)
            made[...] = dot(rows_ref[rows, :], weight_ref[...])
            for j in range(step // owner_rows):
                to = pl.ds(pl.multiple_of((i * (step // owner_rows) + j) * toks, toks), toks)
                cosine, sine = cos_ref[to, :], sin_ref[to, :]
                for p in range(pairs):
                    s, h = p // heads, p % heads
                    here = pl.ds(j * owner_rows + s * toks, toks)
                    for kind in range(3):
                        piece = made[here, pl.ds((kind * heads + h) * HEAD, HEAD)]
                        if kind < 2:
                            piece = piece * cosine + pltpu.roll(piece, HEAD // 2, 1) * sine
                        paired[p, to, kind * HEAD : (kind + 1) * HEAD] = piece.astype(BF16)

        swap = Swap(spot, paired, qkv, qkv_send, qkv_recv)
        swap.start()
    if gathers and tail and head:
        gather.start()
    for spread in moving:
        spread.go_on(1)
    if tail and spot.places > 2:
        summed.go_on(1)
    if head:
        swap.wait()
        attend_blocks(qkv, ids_ref, part, scale, shift)
        swap = Swap(spot, part, got, part_send, part_recv)
        swap.start()
    for hop in range(2, spot.places - 1):
        for spread in moving:
            spread.go_on(hop)
        if tail:
            summed.go_on(hop)
    if gathers:
        gather.go_on()
    if head:
        qkv_ref[...] = qkv[...]
        swap.wait()
        got_ref[...] = got[...]
    for spread in moving:
        if spot.places > 2:
            spread.go_on(spot.places - 1)
    if tail:
        middle = x_ref[...].astype(F32) + summed.finish()
        middle_ref[...] = middle
        normed_ref[...] = (middle * norm_factor(middle) * gain_ref[...]).astype(BF16)
    for spread in moving:
        spread.finish()
    if gathers:
        gather.wait()


def middle_kernel(
    first, defer, ships, spreads, owner_rows,
    middle_ref, local_cot_ref, gain_ref, rows_in, cot_in, gate_in, up_low, up_high, down_in,
    *refs,
):
    shards, refs = take(refs, spreads)
    before, refs = take(refs, 0 if first else 3)
    (grad_ref, low_ref, gain_grad_ref), refs = take(refs, 3)
    y_out, refs = take(refs, 2 if defer else 1)
    fulls, refs = take(refs, spreads)
    after, refs = take(refs, 3)
    ship_out, refs = take(refs, ships)
    (act_ref, dgate_ref, dup_ref, turned, new_rows, new_cols, old_rows, old_cols), refs = take(refs, 8)
    (rows_ref, cot_ref, gate_ref, up_ref, down_ref, load_sems, wide_sems), refs = take(refs, 7)
    sum_refs, refs = take(refs, 5)
    y_refs, refs = take(refs, 3 if defer else 5)
    ship_sems, refs = take(refs, ships)
    size, half = after[0].shape[0], up_low.shape[0] // after[0].shape[0]
    pairs = [(rows_in, rows_ref), (gate_in, gate_ref)]
    for e in range(size):
        for i, part in enumerate((up_low, up_high)):
            to = up_ref.at[pl.ds((2 * e + i) * half, half), :]
            pairs.append((part.at[pl.ds(e * half, half), :], to))
    pairs += [(cot_in, cot_ref), (down_in, down_ref)]
    loads = Loads(pairs, load_sems)
    spot = Spot()
    spot.enter(bool(ships), True)
    if ships:
        ship = Ship(spot, after[0], ship_out[0], ship_sems[0])
    summed = Sum(spot, *sum_refs)
    if defer:
        y_mine, y_send, y_sems = y_refs
        stores = [
            pltpu.make_async_copy(source, target, y_sems.at[i])
            for i, (source, target) in enumerate(zip((y_mine, y_send), y_out))
        ]
        sums = [summed]
    else:
        summed_y = Sum(spot, *y_refs)
        y_mine, y_send = summed_y.mine, summed_y.out
        sums = [summed, summed_y]
    moving = [Spread(spot, *refs) for refs in zip(shards, fulls, refs)]
    for spread in moving:
        spread.begin()
    hidden, width = gate_ref.shape[1], rows_ref.shape[1]
    chip_rows = 2 * owner_rows
    tile = min(256, hidden)
    blocks = after[0].shape[0]
    block = width // blocks
    new = (new_rows.at[0], new_rows.at[1], new_cols)
    old = (old_rows.at[0], old_rows.at[1], old_cols)

    def load(g, e):
        return pltpu.make_async_copy(before[g].at[e], old[g], wide_sems.at[0, g])

    def store(g, e):
        return pltpu.make_async_copy(new[g], after[g].at[e], wide_sems.at[1, g])

    if not first:
        for g in range(3):
            load(g, spot.peer(1)).start()
    loads.wait()

    def go_on(chains, hop):
        if hop < spot.places - 1:
            for each in chains:
                each.go_on(hop)

    @pl.loop(0, spot.places)
    def _(s):
        place = summed.term(s)
        rows = pl.ds(pl.multiple_of(place * chip_rows, chip_rows), chip_rows)

        @pl.loop(0, hidden // tile)
        def _(t):
            cols = pl.ds(pl.multiple_of(t * tile, tile), tile)
            gate = dot(rows_ref[rows, :], gate_ref[:, cols])
            up = dot(rows_ref[rows, :], up_ref[:, cols])
            sig = jax.nn.sigmoid(gate)
            silu = gate * sig
            act_ref[rows, cols] = (silu * up).astype(BF16)
            grad = dot_nt(cot_ref[rows, :], down_ref[cols, :])
            dgate_ref[rows, cols] = (grad * up * sig * (1.0 + gate * (1.0 - sig))).astype(BF16)
            dup_ref[rows, cols] = (grad * silu).astype(BF16)

            @pl.when((s > 0) & (t == min(1, hidden // tile - 1)))
            def _():
                for each in sums:
                    each.begin(s - 1)

        pl.when(s == 2)(lambda: go_on(moving, 1))
        pl.when(s == 3)(lambda: go_on(sums[:1], 1))

        @pl.loop(0, width // 256)
        def _(t):
            cols = pl.ds(pl.multiple_of(t * 256, 256), 256)
            value = dot(act_ref[rows, :], down_ref[:, cols])
            keep, send = split_cores(spot.core, value.astype(BF16), owner_rows)
            y_mine[place, :, cols] = keep[0]
            y_send[place, :, cols] = send[0]
            value = dot_nt(dgate_ref[rows, :], gate_ref[cols, :])
            value += dot_nt(dup_ref[rows, :], up_ref[cols, :])
            keep, send = split_cores(spot.core, value.astype(BF16), owner_rows)
            summed.mine[place, :, cols] = keep[0]
            summed.out[place, :, cols] = send[0]

        for each in sums:
            each.sibling(place).start()

    if defer:
        for copy in stores:
            copy.start()
    if spot.places == 3:
        go_on(sums[:1], 1)
    go_on(moving, 2)
    go_on(sums[1:], 1)

    def send(i):
        if ships:
            pl.when(i < blocks - 1)(lambda: ship.copy(i + 1).start())
            pl.when(i == blocks - 1)(lambda: ship.local.start())

    def make(g, i, left, right, right_at, columns):
        e = spot.peer(i + 1)

        @pl.when(i > 0)
        def _():
            store(g, spot.peer(i)).wait()
            if g == 0:
                send(i - 1)

        if not first:
            load(g, e).wait()
        step = math.gcd(columns, 256)

        @pl.loop(0, columns // step)
        def _(t):
            cols = pl.ds(pl.multiple_of(t * step, step), step)
            total = dot(left[...], right[:, pl.ds(pl.multiple_of(right_at + t * step, step), step)])
            if not first:
                total += old[g][:, cols].astype(F32)
            new[g][:, cols] = total.astype(BF16)

        if not first:
            pl.when(i < blocks - 1)(lambda: load(g, spot.peer(i + 2)).start())
        store(g, e).start()

    @pl.loop(0, blocks)
    def _(i):
        pl.when(i == 1)(lambda: go_on(sums[:1], 2))
        pl.when(i == blocks - 1)(lambda: go_on(sums[1:], 2))
        left = turned.at[pl.ds(0, block), :]
        at = spot.peer(i + 1) * block
        left[...] = rows_ref[:, pl.ds(pl.multiple_of(at, block), block)].T
        make(0, i, left, dgate_ref, 0, hidden)
        make(1, i, left, dup_ref, 0, hidden)

    if ships:
        store(0, spot.dp).wait()
        send(blocks - 1)
    for hop in range(3, spot.places - 1):
        go_on(moving + sums, hop)
    for spread in moving:
        spread.go_on(spot.places - 1)
    left = turned.at[pl.ds(0, hidden), :]
    left[...] = act_ref[...].T

    @pl.loop(0, blocks)
    def _(i):
        make(2, i, left, cot_ref, spot.peer(i + 1) * block, block)

    incoming = summed.finish()
    middle = middle_ref[...]
    term, gain_grad = norm_back(middle, norm_factor(middle), gain_ref[...], incoming)
    gain_grad_ref[...] = gain_grad[None]
    grad = local_cot_ref[...].astype(F32) + term
    grad_ref[...] = grad
    low_ref[...] = grad.astype(BF16)
    if defer:
        for copy in stores:
            copy.wait()
    else:
        y_out[0][...] = (middle + summed_y.finish()).astype(BF16)
    for spread in moving:
        spread.finish()
    for g in range(ships, 3):
        store(g, spot.dp).wait()
    if ships:
        ship.wait()


def add_grads(spot, left, right, turned, before, after, made=None):
    size, rows, columns = after.shape

    @pl.loop(0, size)
    def _(i):
        e = spot.peer(i + 1)
        if rows < left.shape[1]:
            turned[...] = left[:, pl.ds(pl.multiple_of(e * rows, rows), rows)].T
            total = dot(turned[...], right[...])
        else:

            @pl.when(i == 0)
            def _():
                turned[...] = left[...].T

            cut = pl.ds(pl.multiple_of(e * columns, columns), columns)
            total = dot(turned[...], right[:, cut])
        if before is not None:
            total += before[e].astype(F32)
        after[e] = total.astype(BF16)
        if made is not None:
            made(i)


def backward_kernel(
    tail, head, last, old_tail, old_head, extra, spreads, heads, toks, scale, shift, *refs
):
    tail_in, refs = take(refs, 6 * tail)
    old_qkv, refs = take(refs, old_tail)
    head_in, refs = take(refs, 7 * head)
    old_out, refs = take(refs, old_head)
    last_in, refs = take(refs, 2 * last)
    extra_in, refs = take(refs, 3 * extra)
    spread_in, refs = take(refs, spreads)
    tail_out, refs = take(refs, (1 if last else 3) * tail)
    head_out, refs = take(refs, 2 * head)
    last_out, refs = take(refs, 3 * last)
    extra_out, refs = take(refs, extra)
    spread_out, refs = take(refs, spreads)
    tail_refs, refs = take(refs, 7 * tail)
    head_refs, refs = take(refs, 14 * head)
    last_refs, refs = take(refs, 8 * last)
    extra_refs, refs = take(refs, 6 * extra)
    lazy_tail, refs = take(refs, 3 * tail)
    lazy_old, refs = take(refs, 2 * old_tail)
    lazy_head, refs = take(refs, 5 * head)
    if head:
        rows_ref, out_weight_ref, qkv, ids_ref, cos_ref, sin_ref, mix_ref = head_in
        loads_head = Loads(zip((rows_ref, qkv, cos_ref, sin_ref), lazy_head), lazy_head[4])
        rows_ref, qkv, cos_ref, sin_ref = lazy_head[:4]
    if tail:
        proj_ref, weight_ref, rows_one_ref, x_ref, grad_ref, gain_ref = tail_in
        loads_tail = Loads(zip((weight_ref, rows_one_ref), lazy_tail), lazy_tail[2])
        weight_ref, rows_one_ref = lazy_tail[:2]
    if extra:
        loads_extra = Loads(zip(extra_in[:2], extra_refs), extra_refs[5])
    before = None
    if old_tail:
        before = lazy_old[0]
        loads_old = Loads([(old_qkv[0], before)], lazy_old[1])
    spot = Spot()
    spot.enter(head or last, tail or spreads or extra)
    moving = [Spread(spot, *refs) for refs in zip(spread_in, spread_out, refs)]
    for spread in moving:
        spread.begin()
    if last:
        out_blocks, gains = last_in
        out_target, qkv_target, gain_sum = last_out
        new_qkv, own_gain, all_dp, dp_sum, all_mp, ship_sems, gain_sems, gain_spread_sems = last_refs
        ship_out = Ship(spot, out_blocks, out_target, ship_sems.at[0])
        ship_out.start()
    early, late = [], []
    if extra:
        summed_y = Sum(spot, *extra_refs[:5])
        loads_extra.wait()
        for t in range(spot.places):
            summed_y.sibling(t).start()
        late.append(summed_y)
    if head:
        head_proj_ref, new_out = head_out
        part, got, part_send, part_recv = head_refs[:4]
        made_q, got_q, q_send, q_recv, made_kv, got_kv, kv_send, kv_recv, dq, mix_turned = head_refs[4:]
        pairs = part.shape[0]
        owner_rows = toks * (pairs // heads)
        total = rows_ref.shape[0]
        step = min(512, total)
        loads_head.wait(0)

        @pl.loop(0, total // step)
        def _(i):
            rows = pl.ds(pl.multiple_of(i * step, step), step)
            made = dot_nt(rows_ref[rows, :], out_weight_ref[...]).astype(BF16)
            for j in range(step // owner_rows):
                to = pl.ds(pl.multiple_of((i * (step // owner_rows) + j) * toks, toks), toks)
                for p in range(pairs):
                    s, h = p // heads, p % heads
                    start = j * owner_rows + s * toks
                    part[p, to, :] = made[start : start + toks, h * HEAD : (h + 1) * HEAD]

        swap = Swap(spot, part, got, part_send, part_recv)
        swap.start()

    if extra:

        @pl.loop(0, spot.places - 1)
        def _(s):
            summed_y.begin(s)

    if tail:
        result_ref = tail_out[0]
        sum_refs, (turned, gain_acc) = take(tail_refs, 5)
        if not last:
            new_qkv, gain_acc = tail_out[1:]
        owner_rows = x_ref.shape[0]
        summed = Sum(spot, *sum_refs)
        early.append(summed)
        chip_rows = 2 * owner_rows
        gain_acc[...] = jnp.zeros_like(gain_acc)
        loads_tail.wait()

        @pl.loop(0, spot.places)
        def _(s):
            t = summed.term(s)
            rows = pl.ds(pl.multiple_of(t * chip_rows, chip_rows), chip_rows)
            value = dot_nt(proj_ref[rows, :], weight_ref[...])
            gain_acc[...] += jnp.sum(
                value * rows_one_ref[rows, :].astype(F32), axis=0, keepdims=True
            )
            keep, send = split_cores(spot.core, value.astype(BF16), owner_rows)
            summed.mine[t] = keep[0]
            summed.out[t] = send[0]
            summed.sibling(t).start()
            pl.when(s > 0)(lambda: summed.begin(s - 1))

        if last:
            own_gain[...] = gains[...]
            own_gain[1:2, :] += gain_acc[...]
            gain_dp = Gather(spot, own_gain, lambda index: all_dp.at[index], gain_sems)
            gain_dp.start()
    if last:
        if old_tail:
            loads_old.wait()
        ship_qkv = Ship(spot, new_qkv, qkv_target, ship_sems.at[1])

        def send(i):
            pl.when(i < spot.dp_size - 1)(lambda: ship_qkv.copy(i + 1).start())
            pl.when(i == spot.dp_size - 1)(lambda: ship_qkv.local.start())

        add_grads(spot, rows_one_ref, proj_ref, turned, before, new_qkv, send)
        gain_dp.wait()
        dp_sum[...] = jnp.sum(all_dp[...], axis=0)
        gain_mp = Spread(spot, dp_sum, all_mp, gain_spread_sems)
        gain_mp.begin()
        gain_mp.go_on(1)
    if head:
        add_grads(
            spot, mix_ref, rows_ref, mix_turned, old_out[0] if old_head else None, new_out
        )

    def go_on(hop):
        if hop < spot.places - 1:
            for each in moving + early + late:
                each.go_on(hop)

    if not (tail and head):
        go_on(1)
    if head:
        swap.wait()
        loads_head.wait(1, 2, 3)
        swap_kv = Swap(spot, made_kv, got_kv, kv_send, kv_recv)
        attend_back_blocks(
            spot, qkv, got, ids_ref, cos_ref, sin_ref, made_q, made_kv, dq,
            lambda step: swap_kv.copy(step).start(), lambda: go_on(1 if tail else 2), scale, shift,
        )
        swap_kv.keep()
        swap = Swap(spot, made_q, got_q, q_send, q_recv)
        swap.start()
    for hop in range(2 if tail else 3, spot.places - 1):
        if last:
            gain_mp.go_on(hop)
        go_on(hop)
    if tail and not last:
        if old_tail:
            loads_old.wait()
        add_grads(spot, rows_one_ref, proj_ref, turned, before, new_qkv)
    if head:
        swap_kv.wait()
        swap.wait()
        for o in range(total // owner_rows):
            for p in range(pairs):
                s, h = p // heads, p % heads
                here, there = pl.ds(o * owner_rows + s * toks, toks), pl.ds(o * toks, toks)
                for kind in range(3):
                    piece = (
                        got_kv[p, there, (kind - 1) * HEAD : kind * HEAD] if kind else got_q[p, there, :]
                    )
                    head_proj_ref[
                        here, (kind * heads + h) * HEAD : (kind * heads + h + 1) * HEAD
                    ] = piece
    for spread in moving:
        spread.go_on(spot.places - 1)
    if last and spot.places > 2:
        gain_mp.go_on(spot.places - 1)
    if tail:
        incoming = summed.finish()
        x = x_ref[...].astype(F32)
        term, _ = norm_back(x, norm_factor(x), gain_ref[...], incoming)
        result_ref[...] = grad_ref[...] + term
    if extra:
        extra_out[0][...] = (extra_in[2][...] + summed_y.finish()).astype(BF16)
    if last:
        gain_mp.finish()
        gain_sum[...] = jnp.sum(all_mp[...], axis=0)
        ship_out.wait()
        ship_qkv.wait()
    for spread in moving:
        spread.finish()


def ffn_kernel(
    rows_ref, cot_ref, gate_ref, up_ref, down_ref, y_ref, dh_ref, act_ref, dgate_ref, dup_ref
):
    hidden = gate_ref.shape[1]
    width = rows_ref.shape[1]
    tile = min(256, hidden)

    @pl.loop(0, hidden // tile)
    def _(t):
        cols = pl.ds(pl.multiple_of(t * tile, tile), tile)
        gate = dot(rows_ref[...], gate_ref[:, cols])
        up = dot(rows_ref[...], up_ref[:, cols])
        sig = jax.nn.sigmoid(gate)
        silu = gate * sig
        act_ref[:, cols] = (silu * up).astype(BF16)
        grad = dot_nt(cot_ref[...], down_ref[cols, :])
        dgate_ref[:, cols] = (grad * up * sig * (1.0 + gate * (1.0 - sig))).astype(BF16)
        dup_ref[:, cols] = (grad * silu).astype(BF16)

    @pl.loop(0, width // 256)
    def _(t):
        cols = pl.ds(pl.multiple_of(t * 256, 256), 256)
        y_ref[:, cols] = dot(act_ref[...], down_ref[:, cols]).astype(BF16)
        dh = dot_nt(dgate_ref[...], gate_ref[cols, :]) + dot_nt(dup_ref[...], up_ref[cols, :])
        dh_ref[:, cols] = dh.astype(BF16)


def grad_kernel(count, groups, left_blocked, *refs):
    lefts, refs = take(refs, count)
    rights, refs = take(refs, count * groups)
    out_refs, (turned,) = take(refs, groups)
    rows = lefts[0].shape[0]

    def turn():
        for m, left in enumerate(lefts):
            turned[:, m * rows : (m + 1) * rows] = left[...].T

    if left_blocked:
        turn()
    else:
        pl.when(pl.program_id(0) == 0)(turn)
    tile = math.gcd(out_refs[0].shape[2], 256)
    for g, out_ref in enumerate(out_refs):
        own = rights[g * count : (g + 1) * count]

        @pl.loop(0, out_ref.shape[2] // tile)
        def _(t):
            cols = pl.ds(pl.multiple_of(t * tile, tile), tile)
            total = dot(turned[:, :rows], own[0][:, cols])
            for m in range(1, count):
                total += dot(turned[:, m * rows : (m + 1) * rows], own[m][:, cols])
            out_ref[0, :, cols] = total.astype(BF16)


VMEM = pl.BlockSpec(memory_space=pltpu.VMEM)
ANY = pl.BlockSpec(memory_space=pltpu.HBM)


def cost(flops, nbytes):
    return pl.CostEstimate(flops=flops, bytes_accessed=nbytes, transcendentals=0)


def limits(mebibytes):
    return pltpu.CompilerParams(vmem_limit_bytes=mebibytes * 2**20)


def shape(*dims, dtype=BF16):
    return jax.ShapeDtypeStruct(dims, dtype)


def comm_params(collective_id, mebibytes):
    return pltpu.CompilerParams(
        collective_id=collective_id, has_side_effects=True, vmem_limit_bytes=mebibytes * 2**20
    )


def begin(x, gain, query, key, value, out):
    size, mp_size = lax.axis_size("dp"), lax.axis_size("mp")
    rows, columns = query.shape
    return pl.pallas_call(
        begin_kernel,
        out_shape=[
            shape(rows * size, 3 * columns),
            shape(out.shape[0], out.shape[1] * size),
            shape(mp_size, *x.shape),
        ],
        in_specs=[VMEM] * 2 + [ANY] * 4,
        out_specs=[ANY] * 3,
        scratch_shapes=[
            pltpu.VMEM(x.shape, BF16),
            pltpu.SemaphoreType.DMA((4, 2, size + 1)),
            *spread_scratch(mp_size // 2),
        ],
        compiler_params=comm_params(0, 16),
        cost_estimate=cost(0, 60 * 2**20),
        name="begin",
    )(x, gain, query, key, value, out)


def forward_stage(collective_id, tail, head, norm, shard, gather, heads, toks, scale, shift):
    size, mp_size = lax.axis_size("dp"), lax.axis_size("mp")
    out_shape, scratch = [], []
    if tail:
        blocks, _, x, _ = tail
        owner_rows, width = x.shape
        total = blocks.shape[1] * blocks.shape[0] // heads
        out_shape += [
            shape(owner_rows, width, dtype=F32),
            shape(owner_rows, width),
            shape(total, heads * HEAD),
        ]
        scratch += sum_scratch(mp_size // 2, owner_rows, width)
    if head:
        total, slice_len = head[0].shape[0], head[2].shape[0]
        out_shape += [shape(size, slice_len, 3 * HEAD), shape(size, slice_len, HEAD)]
        scratch += [
            pltpu.VMEM((min(512, total), 3 * heads * HEAD), F32),
            *swap_scratch(size, slice_len, 3 * HEAD),
            *swap_scratch(size, slice_len, HEAD),
        ]
    if norm:
        scratch.append(pltpu.VMEM(norm[0].shape, BF16))
    if head:
        scratch += lazy_scratch(*head[:2])
    here, spreads = len(out_shape), bool(norm) + len(shard)
    out_shape += [shape(mp_size, *array.shape) for array in (*norm[:1], *shard)]
    scratch += spread_scratch(mp_size // 2) * spreads
    axis = None
    if gather:
        weight, axis = gather
        dims = list(weight.shape)
        dims[axis] *= size
        out_shape.append(shape(*dims))
        scratch.append(pltpu.SemaphoreType.DMA((2, size + 1)))
    arrays = [*tail, *head, *norm]
    specs = [VMEM] * len(arrays)
    if head:
        specs[len(tail) : len(tail) + 2] = [ANY] * 2
    return pl.pallas_call(
        functools.partial(
            forward_kernel,
            bool(tail), bool(head), bool(norm), spreads, axis, heads, toks, scale, shift,
        ),
        out_shape=out_shape,
        in_specs=specs + [ANY] * (len(shard) + bool(gather)),
        out_specs=[VMEM] * here + [ANY] * (spreads + bool(gather)),
        scratch_shapes=scratch,
        compiler_params=comm_params(collective_id, 52),
        cost_estimate=cost(10**10, 100 * 2**20),
        name="forward_stage",
    )(*arrays, *shard, *gather[:1])


def middle_part(
    collective_id, defer, ships, rows, cot, weights, middle, local_cot, gain, shards, before
):
    total, width = rows.shape
    gate, _, _, down = weights
    hidden = gate.shape[1]
    size, mp_size = lax.axis_size("dp"), lax.axis_size("mp")
    places = mp_size // 2
    owner_rows = middle.shape[0]
    block = width // size
    wide = [shape(size, block, hidden)] * 2 + [shape(size, hidden, block)]
    half = shape(places, owner_rows, width)
    y_scratch = sum_scratch(places, owner_rows, width)
    if defer:
        y_scratch = [*[pltpu.VMEM(half.shape, BF16)] * 2, pltpu.SemaphoreType.DMA((2,))]
    return pl.pallas_call(
        functools.partial(middle_kernel, not before, defer, ships, len(shards), owner_rows),
        out_shape=[
            shape(owner_rows, width, dtype=F32),
            shape(owner_rows, width),
            shape(1, width, dtype=F32),
            *([half, half] if defer else [shape(owner_rows, width)]),
            *[shape(mp_size, *array.shape) for array in shards],
            *wide,
            *wide[:ships],
        ],
        in_specs=[VMEM] * 3 + [ANY] * (6 + len(shards) + len(before)),
        out_specs=[VMEM] * 3 + ([ANY] * 2 if defer else [VMEM]) + [ANY] * (len(shards) + 3 + ships),
        scratch_shapes=[
            *[pltpu.VMEM((total, hidden), BF16)] * 3,
            pltpu.VMEM((max(block, hidden), total), BF16),
            pltpu.VMEM((2, block, hidden), BF16),
            pltpu.VMEM((hidden, block), BF16),
            pltpu.VMEM((2, block, hidden), BF16),
            pltpu.VMEM((hidden, block), BF16),
            *[pltpu.VMEM(array.shape, BF16) for array in (rows, cot, gate, gate, down)],
            pltpu.SemaphoreType.DMA((4 + 2 * size,)),
            pltpu.SemaphoreType.DMA((2, 3)),
            *sum_scratch(places, owner_rows, width),
            *y_scratch,
            *[pltpu.SemaphoreType.DMA((2, size))] * ships,
            *spread_scratch(places) * len(shards),
        ],
        compiler_params=comm_params(collective_id, 61),
        cost_estimate=cost(18 * total * width * hidden, 60 * 2**20),
        name="middle_part",
    )(middle, local_cot, gain, rows, cot, *weights, *shards, *before)


def backward_stage(
    collective_id, tail, old_qkv, head, old_out, last, extra, shard, heads, toks, scale, shift
):
    size, mp_size = lax.axis_size("dp"), lax.axis_size("mp")
    places = mp_size // 2
    out_shape, scratch = [], []
    if tail:
        owner_rows, width = tail[3].shape
        out_shape.append(shape(owner_rows, width, dtype=F32))
        total = tail[0].shape[0]
        wide = shape(size, width // size, 3 * heads * HEAD)
        if not last:
            out_shape += [wide, shape(1, width, dtype=F32)]
        scratch += [
            *sum_scratch(places, owner_rows, width),
            pltpu.VMEM((width // size, total), BF16),
            pltpu.VMEM((1, width), F32),
        ]
    if head:
        (total, width), slice_len = head[0].shape, head[2].shape[1]
        out_shape.append(shape(total, 3 * heads * HEAD))
        out_shape.append(shape(size, heads * HEAD, width // size))
        scratch += [
            *swap_scratch(size, slice_len, HEAD),
            *swap_scratch(size, slice_len, HEAD),
            *swap_scratch(size, slice_len, 2 * HEAD),
            pltpu.VMEM((size, HEAD, slice_len), F32),
            pltpu.VMEM((heads * HEAD, total), BF16),
        ]
    here = len(out_shape)
    if last:
        gains = last[1].shape
        out_shape += [shape(*last[0].shape), wide]
        scratch += [
            pltpu.VMEM(wide.shape, BF16),
            pltpu.VMEM(gains, F32),
            pltpu.VMEM((size, *gains), F32),
            pltpu.VMEM(gains, F32),
            pltpu.VMEM((mp_size, *gains), F32),
            pltpu.SemaphoreType.DMA((2, 2, size)),
            pltpu.SemaphoreType.DMA((2, size)),
            *spread_scratch(places),
        ]
        out_shape.append(shape(*gains, dtype=F32))
    if extra:
        out_shape.append(shape(*extra[2].shape))
        scratch += sum_scratch(places, *extra[2].shape)
        scratch.append(pltpu.SemaphoreType.DMA((2,)))
    if tail:
        scratch += lazy_scratch(tail[1], tail[2])
    scratch += lazy_scratch(*old_qkv) if old_qkv else []
    if head:
        scratch += lazy_scratch(head[0], head[2], head[4], head[5])
    scratch += spread_scratch(places) * len(shard)
    out_shape += [shape(mp_size, *array.shape) for array in shard]
    arrays = [*tail, *old_qkv, *head, *old_out]
    tail_specs = [VMEM, ANY, ANY, VMEM, VMEM, VMEM] if tail else []
    head_specs = [ANY, VMEM, ANY, VMEM, ANY, ANY, VMEM] if head else []
    specs = [*tail_specs, *[ANY] * len(old_qkv), *head_specs, *[VMEM] * len(old_out)]
    last_specs, last_outs = ([ANY, VMEM], [ANY, ANY, VMEM]) if last else ([], [])
    extra_specs, extra_outs = ([ANY, ANY, VMEM], [VMEM]) if extra else ([], [])
    return pl.pallas_call(
        functools.partial(
            backward_kernel, bool(tail), bool(head), bool(last), len(old_qkv), len(old_out),
            bool(extra), len(shard), heads, toks, scale, shift,
        ),
        out_shape=out_shape,
        in_specs=specs + last_specs + extra_specs + [ANY] * len(shard),
        out_specs=[VMEM] * here + last_outs + extra_outs + [ANY] * len(shard),
        scratch_shapes=scratch,
        compiler_params=comm_params(collective_id, 58),
        cost_estimate=cost(10**10, 100 * 2**20),
        name="backward_stage",
    )(*arrays, *last, *extra, *shard)


def ffn(rows, cot, gate, up, down):
    total, width = rows.shape
    hidden = gate.shape[1]
    step = min(512, total)
    by_rows = pl.BlockSpec((step, width), lambda i: (i, 0))
    by_hidden = pl.BlockSpec((step, hidden), lambda i: (i, 0))
    held = lambda array: pl.BlockSpec(array.shape, lambda i: (0, 0), pipeline_mode=pl.Buffered(1))
    return pl.pallas_call(
        ffn_kernel,
        grid=(total // step,),
        out_shape=[shape(total, width)] * 2 + [shape(total, hidden)] * 3,
        in_specs=[by_rows, by_rows, held(gate), held(up), held(down)],
        out_specs=[by_rows] * 2 + [by_hidden] * 3,
        compiler_params=limits(56),
        cost_estimate=cost(12 * total * width * hidden, 34 * 2**20),
        name="ffn",
    )(rows, cot, gate, up, down)


def weight_grad(lefts, groups, left_blocked):
    count = len(lefts)
    size = lax.axis_size("dp")
    rows = lefts[0].shape[0]
    m, n = lefts[0].shape[1], groups[0][0].shape[1]
    moving = lambda width: pl.BlockSpec((rows, width // size), lambda e: (0, e))
    fixed = lambda width: pl.BlockSpec(
        (rows, width), lambda e: (0, 0), pipeline_mode=pl.Buffered(1)
    )
    left_spec = moving(m) if left_blocked else fixed(m)
    right_spec = fixed(n) if left_blocked else moving(n)
    out = (m // size, n) if left_blocked else (m, n // size)
    return pl.pallas_call(
        functools.partial(grad_kernel, count, len(groups), left_blocked),
        grid=(size,),
        in_specs=[left_spec] * count + [right_spec] * (count * len(groups)),
        out_specs=[pl.BlockSpec((1, *out), lambda e: (e, 0, 0))] * len(groups),
        out_shape=[shape(size, *out)] * len(groups),
        scratch_shapes=[pltpu.VMEM((out[0], count * rows), BF16)],
        compiler_params=limits(52),
        cost_estimate=cost(2 * count * rows * m * n * len(groups), 24 * 2**20),
        name="weight_grad",
    )(*lefts, *(right for group in groups for right in group))


def first_visible(ids):
    at = jnp.arange(ids.shape[-1], dtype=jnp.int32)
    starts = jnp.concatenate([jnp.ones_like(ids[..., :1], jnp.bool_), ids[..., 1:] != ids[..., :-1]], axis=-1)
    return lax.cummax(jnp.where(starts, at, 0), axis=ids.ndim - 1)


def block_at(values, index):
    return lax.dynamic_index_in_dim(values, index, 0, keepdims=False)


def stacked(blocks):
    full = jnp.zeros((len(blocks), *blocks[0].shape), blocks[0].dtype)
    for m, block in enumerate(blocks):
        full = lax.dynamic_update_index_in_dim(full, block, m, 0)
    return full


def scatter_mp(values):
    return lax.psum_scatter(values, "mp", scatter_dimension=0, tiled=True).astype(F32)


def sliced_scores(qkv, kv_all, first, positions, scale, shift):
    raw = jnp.einsum("pqd,pkd->pqk", qkv[..., :HEAD], kv_all[..., :HEAD], preferred_element_type=F32)
    at = jnp.arange(kv_all.shape[1], dtype=jnp.int32)
    visible = (at >= first[..., None]) & (at <= positions[:, None])
    return jnp.where(visible, sigmoid_of(raw, scale, shift), 0.0)


def per_device(
    inputs,
    cotangent,
    doc_ids,
    gain_attn,
    w_query,
    w_key,
    w_value,
    w_out,
    gain_ffn,
    w_gate,
    w_up,
    w_down,
):
    dp_size = lax.axis_size("dp")
    mp_size = lax.axis_size("mp")
    micro_count, row_count, seq_count, width = inputs.shape
    slice_len = row_count * mp_size
    total_len = slice_len * dp_size
    rows_here = row_count * seq_count
    shift = math.log(total_len)
    scale = HEAD ** (-0.5)
    dp_at = lax.axis_index("dp")
    mp_at = lax.axis_index("mp")
    first_row = dp_at * slice_len
    positions = first_row + jnp.arange(slice_len, dtype=jnp.int32)
    head_width = w_query.shape[1]
    heads = head_width // HEAD
    hidden = w_gate.shape[1]
    pairs = seq_count * heads
    whole_pairs = pairs == dp_size
    cos_all, sin_all = full_tables(total_len)
    cos_slice, sin_slice = [
        lax.dynamic_slice_in_dim(table, first_row, slice_len, 0) for table in (cos_all, sin_all)
    ]

    def by_row(table):
        shaped = table.reshape(mp_size, 1, row_count, 1, HEAD)
        return jnp.broadcast_to(shaped, (mp_size, seq_count, row_count, 1, HEAD))

    def rotate(values, back=False):
        sine = -by_row(sin_slice) if back else by_row(sin_slice)
        return values * by_row(cos_slice) + swap_halves(values) * sine

    def to_pairs(values):
        shaped = values.reshape(mp_size, seq_count, row_count, heads, -1)
        return shaped.transpose(1, 3, 0, 2, 4).reshape(pairs, slice_len, -1)

    def from_pairs(values):
        shaped = values.reshape(seq_count, heads, mp_size, row_count, -1)
        return shaped.transpose(2, 0, 3, 1, 4).reshape(mp_size * rows_here, heads, -1)

    def to_rows(values):
        return jnp.swapaxes(values, 0, 1).reshape(rows_here, width)

    def from_rows(values):
        return jnp.swapaxes(values.reshape(seq_count, row_count, width), 0, 1)

    def gather_mp(values):
        return lax.all_gather(values, "mp", axis=0, tiled=True)

    gain_attn_grad = jnp.zeros((width,), F32)
    gain_ffn_grad = jnp.zeros((width,), F32)
    results = []
    input_grads = []
    kept = [[] for _ in range(9)]
    xs = [to_rows(inputs[m]) for m in range(micro_count)]
    cots = [to_rows(cotangent[m]) for m in range(micro_count)]
    micros = range(micro_count)
    if whole_pairs:
        stage = (heads, row_count, scale, shift)
        ids = [
            block_at(doc_ids[m], dp_at // heads).astype(F32).reshape(dp_size, 1, slice_len)
            for m in micros
        ]
        last = micro_count - 1

        def whole(blocks):
            return blocks.reshape(mp_size * rows_here, width)

        def scatter_dp(blocks):
            flat = blocks.reshape(-1, blocks.shape[-1])
            return lax.psum_scatter(flat, "dp", scatter_dimension=0, tiled=True).astype(F32)

        qkv_full, out_full, rows_one = begin(
            xs[0], gain_attn[None], w_query, w_key, w_value, w_out
        )
        cut = w_up.shape[0] // 2
        gathers = {
            0: (w_gate, 0), 1: (w_up[:cut], 0), 2: (w_up[cut:], 0), micro_count: (w_down, 1)
        }
        wide = []
        ones, qkvs, got, middles, lows, twos, mixtures = [whole(rows_one)], [], [], [], [], [], []
        for m in range(micro_count + 1):
            tail, head, norm, shard = (), (), (), ()
            if m:
                tail = (got[m - 1], out_full, xs[m - 1], gain_ffn[None])
            if m < micro_count:
                head = (ones[m], qkv_full, cos_slice, sin_slice, ids[m])
            if m < last:
                norm = (xs[m + 1], gain_attn[None])
            elif lows:
                shard = (lows[m - last],)
            if m == 0:
                shard += (cots[0],)
            outs = forward_stage(10 + m, tail, head, norm, shard, gathers.get(m, ()), *stage)
            if tail:
                (middle, low, mixture), outs = take(outs, 3)
                middles.append(middle)
                lows.append(low)
                mixtures.append(mixture)
            if head:
                (qkv, block), outs = take(outs, 2)
                qkvs.append(qkv)
                got.append(block)
            if norm or shard:
                (ones if m < last else twos).append(whole(outs[0]))
            if m == 0:
                portions = [whole(outs[1])]
            if m in gathers:
                wide.append(outs[-1])
        grads, low_grads, attns, projs, sums, gain_parts, later = [], [], [], [], [], [], []
        for m in micros:
            shard = (lows[len(twos)] if len(twos) < micro_count else low_grads[len(attns)],)
            if m < last:
                shard += (cots[m + 1],)
            defer = m == 0
            grad, low, gain_part, *others = middle_part(
                30 + m, defer, int(m == last), twos[m], portions[m], wide, middles[m], cots[m], gain_ffn[None],
                shard, sums,
            )
            ys, (full, *others) = take(others, 2 if defer else 1)
            later.append((*ys, middles[m]) if defer else ys)
            (twos if len(twos) < micro_count else attns).append(whole(full))
            if m < last:
                portions.append(whole(others[0]))
            sums, gate_blocks = take(others[m < last :], 3)
            grads.append(grad)
            low_grads.append(low)
            gain_parts.append(gain_part)
        sum_up, sum_down = [scatter_dp(blocks) for blocks in sums[1:]]
        sum_gate = jnp.sum(gate_blocks[0].astype(F32), axis=0)
        old_qkv, old_out, attn_parts, finished = (), (), [], list(later)
        for m in range(micro_count + 1):
            tail, head, shard, final = (), (), (), ()
            if m:
                tail = (projs[m - 1], qkv_full, ones[m - 1], xs[m - 1], grads[m - 1], gain_attn[None])
            if m < micro_count:
                head = (attns[m], out_full, qkvs[m], ids[m], cos_all, sin_all, mixtures[m])
            else:
                rows = [sum(gain_parts), sum(attn_parts), jnp.zeros((6, width), F32)]
                final = (*old_out, jnp.concatenate(rows, axis=0))
            if len(attns) < micro_count:
                shard = (low_grads[len(attns)],)
            extra = later[0] if m == 0 else ()
            outs = backward_stage(
                20 + m, tail, old_qkv, head, () if final else old_out, final, extra, shard, *stage
            )
            if tail:
                (input_grad,), outs = take(outs, 1)
                input_grads.append(from_rows(input_grad))
            if tail and head:
                (new_qkv, gain_part), outs = take(outs, 2)
                old_qkv = (new_qkv,)
                attn_parts.append(gain_part)
            if head:
                (proj, new_out), outs = take(outs, 2)
                projs.append(proj)
                old_out = (new_out,)
            if extra:
                finished[0] = outs[:1]
            if shard:
                attns.append(whole(outs[-1]))
        results = [from_rows(result[0]) for result in finished]
        sum_out, sum_qkv = (jnp.sum(blocks.astype(F32), axis=0) for blocks in outs[:2])
        gain_sums = (outs[2][1] / gain_attn, outs[2][0])
    else:
        qkv_full = lax.all_gather(
            jnp.concatenate([w_query, w_key, w_value], axis=1), "dp", axis=0, tiled=True
        )
        out_full = lax.all_gather(w_out, "dp", axis=1, tiled=True)
        gate_full = lax.all_gather(w_gate, "dp", axis=0, tiled=True)
        up_full = lax.all_gather(w_up, "dp", axis=0, tiled=True)
        down_full = lax.all_gather(w_down, "dp", axis=1, tiled=True)
        first_all = first_visible(doc_ids)
        normed = [
            (x.astype(F32) * norm_factor(x.astype(F32)) * gain_attn).astype(BF16) for x in xs
        ]
        for micro in micros:
            local_rows = xs[micro].astype(F32)
            local_cot = cots[micro]
            factor_one = norm_factor(local_rows)
            rows_one = gather_mp(normed[micro])
            portion = gather_mp(local_cot)
            projected = dot(rows_one, qkv_full).reshape(
                mp_size, seq_count, row_count, 3, heads, HEAD
            )
            packed = to_pairs(
                jnp.concatenate(
                    [
                        rotate(projected[:, :, :, 0]).astype(BF16),
                        rotate(projected[:, :, :, 1]).astype(BF16),
                        projected[:, :, :, 2].astype(BF16),
                    ],
                    axis=-1,
                )
            )
            kv_all = lax.all_gather(packed[..., HEAD:], "dp", axis=1, tiled=True)
            first = lax.dynamic_slice_in_dim(first_all[micro], first_row, slice_len, 1)
            first = jnp.repeat(first, heads, axis=0)
            weights = sliced_scores(packed, kv_all, first, positions, scale, shift)
            attended = jnp.einsum(
                "pqk,pkd->pqd", weights.astype(BF16), kv_all[..., HEAD:], preferred_element_type=F32
            ).astype(BF16)
            mixture = from_pairs(attended).reshape(mp_size * rows_here, head_width)
            middle = local_rows + scatter_mp(dot(mixture, out_full).astype(BF16))
            factor_two = norm_factor(middle)
            rows_two = gather_mp((middle * factor_two * gain_ffn).astype(BF16))
            y, dh, activated, gate_grad, up_grad = ffn(
                rows_two, portion, gate_full, up_full, down_full
            )
            results.append(from_rows((middle + scatter_mp(y)).astype(BF16)))
            middle_term, gain_part = norm_back(middle, factor_two, gain_ffn, scatter_mp(dh))
            gain_ffn_grad = gain_ffn_grad + gain_part
            middle_grad = local_cot.astype(F32) + middle_term
            attn_portion = gather_mp(middle_grad.astype(BF16))
            mix_grad = to_pairs(dot_nt(attn_portion, out_full).astype(BF16))
            sig = sliced_scores(packed, kv_all, first, positions, scale, shift)
            prob_grad = jnp.einsum(
                "pqd,pkd->pqk", mix_grad, kv_all[..., HEAD:], preferred_element_type=F32
            )
            score_grad = (prob_grad * sig * (1.0 - sig)).astype(BF16)
            dq = jnp.einsum("pqk,pkd->pqd", score_grad, kv_all[..., :HEAD], preferred_element_type=F32)
            dk = jnp.einsum("pqk,pqd->pkd", score_grad, packed[..., :HEAD], preferred_element_type=F32)
            dv = jnp.einsum("pqk,pqd->pkd", sig.astype(BF16), mix_grad, preferred_element_type=F32)
            dkv = lax.psum_scatter(
                jnp.concatenate([dk * scale, dv], axis=-1).astype(BF16), "dp", scatter_dimension=1, tiled=True
            ).astype(F32)
            back = from_pairs(jnp.concatenate([dq * scale, dkv], axis=-1))
            back = back.reshape(mp_size, seq_count, row_count, heads, 3 * HEAD)
            proj_grad = jnp.stack(
                [
                    rotate(back[..., :HEAD], True),
                    rotate(back[..., HEAD : 2 * HEAD], True),
                    back[..., 2 * HEAD :],
                ],
                axis=3,
            ).astype(BF16).reshape(mp_size * rows_here, 3 * head_width)
            partial_grad = dot_nt(proj_grad, qkv_full)
            gain_attn_grad = gain_attn_grad + jnp.sum(partial_grad * rows_one.astype(F32), axis=0)
            input_term, _ = norm_back(
                local_rows, factor_one, gain_attn, scatter_mp(partial_grad.astype(BF16))
            )
            input_grads.append(from_rows(middle_grad + input_term))
            for held, array in zip(
                kept,
                (rows_one, proj_grad, mixture, attn_portion, rows_two, gate_grad, up_grad, activated, portion),
            ):
                held.append(array)

        def scatter_dp(lefts, rights, left_blocked):
            (blocks,) = weight_grad(lefts, (rights,), left_blocked)
            return lax.psum_scatter(blocks, "dp", scatter_dimension=0, tiled=True)[0].astype(F32)

        ones, projs, mixtures, attns, twos, gates, ups, acts, portions = kept
        sum_gate = scatter_dp(twos, gates, True)
        sum_up = scatter_dp(twos, ups, True)
        sum_down = scatter_dp(acts, portions, False)
        sum_out = scatter_dp(mixtures, attns, False)
        sum_qkv = scatter_dp(ones, projs, True)
        gain_sums = lax.psum((gain_attn_grad / gain_attn, gain_ffn_grad), ("dp", "mp"))
    return (
        stacked(results),
        stacked(input_grads),
        gain_sums[0],
        sum_qkv[:, :head_width],
        sum_qkv[:, head_width : 2 * head_width],
        sum_qkv[:, 2 * head_width :],
        sum_out,
        gain_sums[1],
        sum_gate,
        sum_up,
        sum_down,
    )


def solution(mesh):
    tokens = P(None, ("dp", "mp"), None, None)
    column = P("dp", "mp")
    row = P("mp", "dp")
    return jax.shard_map(
        per_device,
        mesh=mesh,
        in_specs=(
            tokens, tokens, P(), P(), column, column, column, row, P(), column, column, row,
        ),
        out_specs=(
            tokens, tokens, P(), column, column, column, row, P(), column, column, row,
        ),
        check_vma=False,
    )
```

```python
import functools
import math

import jax
import jax.numpy as jnp
import numpy as np
from jax import lax
from jax.experimental import pallas as pl
from jax.experimental.pallas import tpu as pltpu
from jax.sharding import PartitionSpec as P

HEAD = 128
epsilon = 1e-05
rope_base = 10000.0
F32 = jnp.float32
BF16 = jnp.bfloat16


def full_tables(total):
    half_size = HEAD // 2
    exponents = -(np.arange(half_size, dtype=np.float32) * np.float32(2.0 / HEAD))
    inverse = np.power(np.float32(rope_base), exponents)
    angles = np.arange(total, dtype=np.float32)[:, None] * inverse[None, :]
    cosine, sine = np.cos(angles), np.sin(angles)
    return (
        jnp.asarray(np.concatenate([cosine, cosine], axis=-1)),
        jnp.asarray(np.concatenate([-sine, sine], axis=-1)),
    )


def swap_halves(values):
    half_size = HEAD // 2
    return jnp.concatenate([values[..., half_size:], values[..., :half_size]], axis=-1)


def dot(left, right):
    return jnp.dot(left, right, preferred_element_type=F32)


def dot_tn(left, right):
    return lax.dot_general(left, right, (((0,), (0,)), ((), ())), preferred_element_type=F32)


def dot_nt(left, right):
    return lax.dot_general(left, right, (((1,), (1,)), ((), ())), preferred_element_type=F32)


def norm_factor(values):
    return lax.rsqrt(jnp.mean(values * values, axis=-1, keepdims=True) + epsilon)


def norm_back(values, factor, gain, incoming):
    scaled = incoming * gain
    gain_term = jnp.sum(incoming * values * factor, axis=0)
    input_term = factor * scaled - values * factor**3 * jnp.mean(
        scaled * values, axis=-1, keepdims=True
    )
    return (input_term, gain_term)


def sigmoid_of(raw, scale, shift):
    return 1.0 / (1.0 + jnp.exp(shift - raw * scale))


def split_cores(core, values, rows_here):
    shaped = values.reshape(-1, 2, rows_here, values.shape[-1])
    first, second = shaped[:, 0], shaped[:, 1]
    is_first = core == 0
    return jnp.where(is_first, first, second), jnp.where(is_first, second, first)

MESH = pl.DeviceIdType.MESH


class Spot:
    def __init__(self):
        self.dp, self.mp = lax.axis_index("dp"), lax.axis_index("mp")
        self.dp_size, self.mp_size = lax.axis_size("dp"), lax.axis_size("mp")
        self.places = self.mp_size // 2
        self.place, self.core = lax.div(self.mp, 2), lax.rem(self.mp, 2)
        self.sibling = (self.dp, self.mp + 1 - 2 * self.core)
        self.right = (self.dp, self.mp + 2)
        self.left = (self.dp, self.mp - 2)
        self.has_right = self.place < self.places - 1
        self.has_left = self.place > 0

    def peer(self, step):
        return lax.rem(self.dp + step, self.dp_size)

    def enter(self, with_dp, with_mp):
        barrier = pltpu.get_barrier_semaphore()
        count = 0

        def greet(device):
            pl.semaphore_signal(barrier, inc=1, device_id=device, device_id_type=MESH)

        if with_mp:
            greet(self.sibling)
            pl.when(self.has_right)(lambda: greet(self.right))
            pl.when(self.has_left)(lambda: greet(self.left))
            count += 1 + self.has_right.astype(jnp.int32) + self.has_left.astype(jnp.int32)
        if with_dp:
            for step in range(1, self.dp_size):
                greet((self.peer(step), self.mp))
            count += self.dp_size - 1
        pl.semaphore_wait(barrier, count)


class Swap:
    def __init__(self, spot, source, target, send, receive):
        self.spot, self.source, self.target = spot, source, target
        self.send, self.receive = send, receive
        self.copies = [self.copy(step) for step in range(1, spot.dp_size)]

    def copy(self, step):
        spot = self.spot
        return pltpu.make_async_remote_copy(
            src_ref=self.source.at[spot.peer(step)],
            dst_ref=self.target.at[spot.dp],
            send_sem=self.send.at[step],
            recv_sem=self.receive.at[step],
            device_id=(spot.peer(step), spot.mp),
            device_id_type=MESH,
        )

    def start(self):
        for copy in self.copies:
            copy.start()
        self.keep()

    def keep(self):
        self.target[self.spot.dp] = self.source[self.spot.dp]

    def wait(self):
        for copy in self.copies:
            copy.wait()


class Gather:
    def __init__(self, spot, shard, window, sems):
        self.local = pltpu.make_async_copy(shard, window(spot.dp), sems.at[0, 0])
        self.copies = [
            pltpu.make_async_remote_copy(
                src_ref=shard,
                dst_ref=window(spot.dp),
                send_sem=sems.at[0, step],
                recv_sem=sems.at[1, step],
                device_id=(spot.peer(step), spot.mp),
                device_id_type=MESH,
            )
            for step in range(1, spot.dp_size)
        ]

    def start(self):
        for copy in self.copies:
            copy.start()
        self.local.start()

    def go_on(self):
        pass

    def wait(self):
        for copy in self.copies:
            copy.wait()
        self.local.wait()


def gather_of(spot, *arguments):
    return (RingGather if spot.dp_size == 4 else Gather)(spot, *arguments)


class RingGather:
    def __init__(self, spot, shard, window, sems):
        side = spot.dp + 1 - 2 * lax.rem(spot.dp, 2)
        across = spot.dp + 2 - 4 * lax.div(spot.dp, 2)

        def copy(source, index, kind, to, half=None):
            return pltpu.make_async_remote_copy(
                src_ref=source,
                dst_ref=window(index, half),
                send_sem=sems.at[0, kind],
                recv_sem=sems.at[1, kind],
                device_id=(to, spot.mp),
                device_id_type=MESH,
            )

        self.local = pltpu.make_async_copy(shard, window(spot.dp), sems.at[0, 4])
        self.to_side = copy(shard, spot.dp, 0, side)
        self.to_across = copy(shard, spot.dp, 1, across)
        self.on_across = copy(window(side, 0), side, 2, across, 0)
        self.on_side = copy(window(across, 1), across, 3, side, 1)

    def start(self):
        self.to_side.start()
        self.to_across.start()
        self.local.start()

    def go_on(self):
        self.to_side.wait_recv()
        self.on_across.start()
        self.to_across.wait_recv()
        self.on_side.start()

    def wait(self):
        self.to_side.wait_send()
        self.to_across.wait_send()
        self.on_across.wait()
        self.on_side.wait()
        self.local.wait()


class Spread:
    def __init__(self, spot, shard, full, sems):
        self.spot, self.shard, self.full, self.sems = spot, shard, full, sems
        self.local = pltpu.make_async_copy(shard, full.at[spot.mp], sems.at[6, 0])

    def copy(self, kind, device, p, source=None, core=None):
        at = 2 * p + (self.spot.core if core is None else core)
        return pltpu.make_async_remote_copy(
            src_ref=self.full.at[at] if source is None else source,
            dst_ref=self.full.at[at],
            send_sem=self.sems.at[kind, p],
            recv_sem=self.sems.at[kind + 1, p],
            device_id=device,
            device_id_type=MESH,
        )

    def rightward(self, p, source=None):
        return self.copy(0, self.spot.right, p, source)

    def leftward(self, p, source=None):
        return self.copy(2, self.spot.left, p, source)

    def across(self, p, source=None):
        return self.copy(4, self.spot.sibling, p, source)

    def begin(self):
        spot = self.spot
        pl.when(spot.has_right)(lambda: self.rightward(spot.place, self.shard).start())
        pl.when(spot.has_left)(lambda: self.leftward(spot.place, self.shard).start())
        self.across(spot.place, self.shard).start()
        self.local.start()

    def go_on(self, hop):
        spot = self.spot

        @pl.when(spot.place >= hop)
        def _():
            p = spot.place - hop
            self.rightward(p).wait_recv()
            pl.when(spot.has_right)(lambda: self.rightward(p).start())
            self.across(p).start()

        @pl.when(spot.place + hop < spot.places)
        def _():
            p = spot.place + hop
            self.leftward(p).wait_recv()
            pl.when(spot.has_left)(lambda: self.leftward(p).start())
            self.across(p).start()

    def finish(self):
        spot = self.spot
        for p in range(spot.places):
            self.copy(4, spot.sibling, p, core=1 - spot.core).wait_recv()
            self.across(p).wait_send()
            pl.when(spot.has_right & (spot.place >= p))(lambda: self.rightward(p).wait_send())
            pl.when(spot.has_left & (spot.place <= p))(lambda: self.leftward(p).wait_send())
        self.local.wait()


def spread_scratch(places):
    return [pltpu.SemaphoreType.DMA((7, places))]


class Ship(Swap):
    def __init__(self, spot, source, target, sems):
        super().__init__(spot, source, target, sems.at[0], sems.at[1])
        self.local = pltpu.make_async_copy(source.at[spot.dp], target.at[spot.dp], sems.at[0, 0])

    def start(self):
        for copy in self.copies:
            copy.start()
        self.local.start()

    def wait(self):
        super().wait()
        self.local.wait()


def window_of(full, axis, step, column=0, columns=None):
    def window(index, half=None):
        rows = step if axis == 0 else full.shape[0]
        first, count = (0, rows) if half is None else (half * (rows // 2), rows // 2)
        if axis == 1:
            return full.at[
                pl.ds(first, count), pl.ds(pl.multiple_of(index * step, step), step)
            ]
        along = pl.ds(pl.multiple_of(index * step + first, count), count)
        return full.at[along, pl.ds(column, full.shape[1] if columns is None else columns)]

    return window


def swap_scratch(size, *block):
    return [
        pltpu.VMEM((size, *block), BF16),
        pltpu.VMEM((size, *block), BF16),
        pltpu.SemaphoreType.DMA((size,)),
        pltpu.SemaphoreType.DMA((size,)),
    ]


def far_first(places):
    orders = []
    for place in range(places):
        right, left, order = list(range(places - 1, place, -1)), list(range(place)), []
        while right or left:
            order += right[:1] + left[:1]
            right, left = right[1:], left[1:]
        orders.append(order + [place])
    return orders


class Sum:
    def __init__(self, spot, mine, out, from_sibling, passed, sems):
        self.spot = spot
        self.mine, self.out = mine, out
        self.from_sibling, self.passed = from_sibling, passed
        self.sems = sems
        self.orders = far_first(spot.places)

    def copy(self, source, target, kind, t, device, to=None):
        return pltpu.make_async_remote_copy(
            src_ref=source.at[t],
            dst_ref=target.at[t if to is None else to],
            send_sem=self.sems.at[kind, t],
            recv_sem=self.sems.at[kind + 1, t],
            device_id=device,
            device_id_type=MESH,
        )

    def sibling(self, t):
        return self.copy(self.out, self.from_sibling, 0, t, self.spot.sibling)

    def rightward(self, t):
        return self.copy(self.mine, self.passed, 2, t, self.spot.right)

    def leftward(self, t, place):
        to = jnp.where(t == place, self.spot.places, t)
        return self.copy(self.mine, self.passed, 4, t, self.spot.left, to)

    def leftward_out(self, t):
        return self.leftward(t, self.spot.place - 1)

    def leftward_in(self, t):
        return self.leftward(t, self.spot.place)

    def term(self, s):
        chosen = 0
        for place, order in enumerate(self.orders):
            for at, t in enumerate(order):
                if t:
                    chosen = chosen + jnp.where((self.spot.place == place) & (s == at), t, 0)
        return chosen

    def add(self, t, arrived):
        self.mine[t] = (self.mine[t].astype(F32) + arrived.astype(F32)).astype(BF16)

    def absorb(self, t):
        self.sibling(t).wait_recv()
        self.add(t, self.from_sibling[t])

    def begin(self, s):
        spot = self.spot

        @pl.when((spot.place == 0) & (s < spot.places - 1))
        def _():
            t = spot.places - 1 - s
            self.absorb(t)
            self.rightward(t).start()

        @pl.when((spot.place == spot.places - 1) & (s < spot.places - 1))
        def _():
            self.absorb(s)
            self.leftward_out(s).start()

    def go_on(self, hop):
        spot = self.spot
        last = spot.places - 1

        @pl.when((spot.place > 0) & (spot.place <= hop))
        def _():
            t = last + spot.place - hop
            self.absorb(t)
            self.rightward(t).wait_recv()
            self.add(t, self.passed[t])
            self.rightward(t).start()

        @pl.when((spot.place < last) & (last - spot.place <= hop))
        def _():
            t = hop - last + spot.place
            self.absorb(t)
            self.leftward_in(t).wait_recv()
            self.add(t, self.passed[t])
            self.leftward_out(t).start()

    def finish(self):
        spot = self.spot
        t = spot.place
        self.absorb(t)

        @pl.when(spot.has_left)
        def _():
            self.rightward(t).wait_recv()
            self.add(t, self.passed[t])

        @pl.when(spot.has_right)
        def _():
            self.leftward_in(t).wait_recv()
            self.add(t, self.passed[spot.places])

        for t in range(spot.places):
            self.sibling(t).wait_send()
            pl.when(spot.place < t)(lambda: self.rightward(t).wait_send())
            pl.when(spot.place > t)(lambda: self.leftward_out(t).wait_send())
        return self.mine[spot.place].astype(F32)


def sum_scratch(places, rows_here, width):
    return [
        *[pltpu.VMEM((places, rows_here, width), BF16)] * 3,
        pltpu.VMEM((places + 1, rows_here, width), BF16),
        pltpu.SemaphoreType.DMA((6, places)),
    ]


def as_column(row):
    return jnp.broadcast_to(row, (HEAD, row.shape[1])).T[:, 0:1]


def attend_blocks(qkv, ids_ref, out, scale, shift):
    count, block = out.shape[:2]
    row_at = lax.broadcasted_iota(jnp.int32, (block, block), 0)
    col_at = lax.broadcasted_iota(jnp.int32, (block, block), 1)

    @pl.loop(0, count)
    def _(i):
        queries = qkv[i, :, 0:HEAD]
        ids = as_column(ids_ref[i])

        def add_block(j, acc, diagonal=False):
            sig = sigmoid_of(dot_nt(queries, qkv[j, :, HEAD : 2 * HEAD]), scale, shift)
            visible = ids == ids_ref[j]
            if diagonal:
                visible = visible & (col_at <= row_at)
            weights = jnp.where(visible, sig, 0.0).astype(BF16)
            return acc + dot(weights, qkv[j, :, 2 * HEAD :])

        acc = add_block(i, jnp.zeros((block, HEAD), F32), True)
        out[i] = lax.fori_loop(0, i, add_block, acc).astype(BF16)


def attend_back_blocks(
    spot, qkv, grad, ids_ref, cos_ref, sin_ref, out_q, out_kv, dq, made, midway, scale, shift
):
    count, block = grad.shape[:2]
    col_at = lax.broadcasted_iota(jnp.int32, (block, block), 0)
    row_at = lax.broadcasted_iota(jnp.int32, (block, block), 1)
    dq[...] = jnp.zeros_like(dq)

    def unrotate(values, i):
        rows = pl.ds(pl.multiple_of(i * block, block), block)
        swapped = pltpu.roll(values, HEAD // 2, 1)
        return (values * cos_ref[rows, :] - swapped * sin_ref[rows, :]).astype(BF16)

    @pl.loop(0, count)
    def _(at):
        j = spot.peer(at + 1)
        keys = qkv[j, :, HEAD : 2 * HEAD]
        values = qkv[j, :, 2 * HEAD :]
        keys_t = keys.T
        ids = as_column(ids_ref[j])

        def add_block(i, sums, diagonal=False):
            dk, dv = sums
            queries, grads = qkv[i, :, 0:HEAD], grad[i]
            sig = sigmoid_of(dot_nt(keys, queries), scale, shift)
            visible = ids == ids_ref[i]
            if diagonal:
                visible = visible & (col_at <= row_at)
            sig = jnp.where(visible, sig, 0.0)
            prob_grad = dot_nt(values, grads)
            score_grad = (prob_grad * sig * (1.0 - sig)).astype(BF16)
            dq[i] += dot(keys_t, score_grad)
            return dk + dot(score_grad, queries), dv + dot(sig.astype(BF16), grads)

        zero = jnp.zeros((block, HEAD), F32)
        dk, dv = lax.fori_loop(j + 1, count, add_block, add_block(j, (zero, zero), True))
        out_kv[j, :, 0:HEAD] = unrotate(dk * scale, j)
        out_kv[j, :, HEAD:] = dv.astype(BF16)
        pl.when(at < count - 1)(lambda: made(at + 1))
        pl.when(at == 1)(midway)

    @pl.loop(0, count)
    def _(i):
        out_q[i] = unrotate(dq[i].T * scale, i)


def take(refs, count):
    return refs[:count], refs[count:]


class Loads:
    def __init__(self, pairs, sems):
        self.copies = [
            pltpu.make_async_copy(source, target, sems.at[i])
            for i, (source, target) in enumerate(pairs)
        ]
        for copy in self.copies:
            copy.start()

    def wait(self, *which):
        for i in which or range(len(self.copies)):
            self.copies[i].wait()


def lazy_scratch(*arrays):
    return [pltpu.VMEM(array.shape, array.dtype) for array in arrays] + [
        pltpu.SemaphoreType.DMA((len(arrays),))
    ]


def put_norm(x_ref, gain_ref, out_ref):
    x = x_ref[...].astype(F32)
    out_ref[...] = (x * norm_factor(x) * gain_ref[...]).astype(BF16)


def begin_kernel(
    x_ref, gain_ref, query, key, value, out, qkv_full, out_full, first_full,
    normed, sems, spread_sems,
):
    spot = Spot()
    spot.enter(True, True)
    rows, columns = query.shape
    jobs = [
        (shard, window_of(qkv_full, 0, rows, i * columns, columns))
        for i, shard in enumerate((query, key, value))
    ]
    jobs.append((out, window_of(out_full, 1, out.shape[1])))
    gathers = [
        gather_of(spot, shard, window, sems.at[i]) for i, (shard, window) in enumerate(jobs)
    ]
    for gather in gathers:
        gather.start()
    put_norm(x_ref, gain_ref, normed)
    spread = Spread(spot, normed, first_full, spread_sems)
    spread.begin()
    spread.go_on(1)
    for gather in gathers:
        gather.go_on()
    for hop in range(2, spot.places):
        spread.go_on(hop)
    for gather in gathers:
        gather.wait()
    spread.finish()


def forward_kernel(tail, head, norms, spreads, gather_axis, heads, toks, scale, shift, *refs):
    gathers = gather_axis is not None
    tail_in, refs = take(refs, 4 * tail)
    head_in, refs = take(refs, 5 * head)
    norm_in, refs = take(refs, 2 * norms)
    spread_in, refs = take(refs, spreads - norms)
    gather_in, refs = take(refs, gathers)
    tail_out, refs = take(refs, 3 * tail)
    head_out, refs = take(refs, 2 * head)
    spread_out, refs = take(refs, spreads)
    gather_out, refs = take(refs, gathers)
    sum_refs, refs = take(refs, 5 * tail)
    head_refs, refs = take(refs, 9 * head)
    normed, refs = take(refs, norms)
    lazy, refs = take(refs, 3 * head)
    if head:
        rows_ref, weight_ref, cos_ref, sin_ref, ids_ref = head_in
        loads = Loads(zip((rows_ref, weight_ref), lazy), lazy[2])
        rows_ref, weight_ref = lazy[:2]
    spot = Spot()
    spot.enter(head or gathers, tail or spreads)
    if norms:
        put_norm(*norm_in, *normed)
        spread_in = (*normed, *spread_in)
    moving = [Spread(spot, *refs) for refs in zip(spread_in, spread_out, refs)]
    for spread in moving:
        spread.begin()
    if gathers:
        window = window_of(gather_out[0], gather_axis, gather_in[0].shape[gather_axis])
        gather = gather_of(spot, gather_in[0], window, refs[-1])
        if not (tail and head):
            gather.start()

    if tail:
        got, out_weight, x_ref, gain_ref = tail_in
        middle_ref, normed_ref, mix_ref = tail_out
        pairs = got.shape[0]
        owner_rows = toks * (pairs // heads)
        for o in range(mix_ref.shape[0] // owner_rows):
            for p in range(pairs):
                s, h = p // heads, p % heads
                mix_ref[pl.ds(o * owner_rows + s * toks, toks), h * HEAD : (h + 1) * HEAD] = got[
                    p, pl.ds(o * toks, toks), :
                ]
        summed = Sum(spot, *sum_refs)
        chip_rows = 2 * owner_rows

        @pl.loop(0, spot.places)
        def _(s):
            t = summed.term(s)
            rows = pl.ds(pl.multiple_of(t * chip_rows, chip_rows), chip_rows)
            value = dot(mix_ref[rows, :], out_weight[...]).astype(BF16)
            keep, send = split_cores(spot.core, value, owner_rows)
            summed.mine[t] = keep[0]
            summed.out[t] = send[0]
            summed.sibling(t).start()

        @pl.loop(0, spot.places - 1)
        def _(s):
            summed.begin(s)

    if head:
        qkv_ref, got_ref = head_out
        made, paired, qkv, qkv_send, qkv_recv, part, got, part_send, part_recv = head_refs
        pairs = paired.shape[0]
        owner_rows = toks * (pairs // heads)
        step = made.shape[0]
        loads.wait()

        @pl.loop(0, rows_ref.shape[0] // step)
        def _(i):
            rows = pl.ds(pl.multiple_of(i * step, step), step)
            made[...] = dot(rows_ref[rows, :], weight_ref[...])
            for j in range(step // owner_rows):
                to = pl.ds(pl.multiple_of((i * (step // owner_rows) + j) * toks, toks), toks)
                cosine, sine = cos_ref[to, :], sin_ref[to, :]
                for p in range(pairs):
                    s, h = p // heads, p % heads
                    here = pl.ds(j * owner_rows + s * toks, toks)
                    for kind in range(3):
                        piece = made[here, pl.ds((kind * heads + h) * HEAD, HEAD)]
                        if kind < 2:
                            piece = piece * cosine + pltpu.roll(piece, HEAD // 2, 1) * sine
                        paired[p, to, kind * HEAD : (kind + 1) * HEAD] = piece.astype(BF16)

        swap = Swap(spot, paired, qkv, qkv_send, qkv_recv)
        swap.start()
    if gathers and tail and head:
        gather.start()
    for spread in moving:
        spread.go_on(1)
    if tail and spot.places > 2:
        summed.go_on(1)
    if head:
        swap.wait()
        attend_blocks(qkv, ids_ref, part, scale, shift)
        swap = Swap(spot, part, got, part_send, part_recv)
        swap.start()
    for hop in range(2, spot.places - 1):
        for spread in moving:
            spread.go_on(hop)
        if tail:
            summed.go_on(hop)
    if gathers:
        gather.go_on()
    if head:
        qkv_ref[...] = qkv[...]
        swap.wait()
        got_ref[...] = got[...]
    for spread in moving:
        if spot.places > 2:
            spread.go_on(spot.places - 1)
    if tail:
        middle = x_ref[...].astype(F32) + summed.finish()
        middle_ref[...] = middle
        normed_ref[...] = (middle * norm_factor(middle) * gain_ref[...]).astype(BF16)
    for spread in moving:
        spread.finish()
    if gathers:
        gather.wait()


def middle_kernel(
    first, defer, ships, spreads, owner_rows,
    middle_ref, local_cot_ref, gain_ref, rows_in, cot_in, gate_in, up_low, up_high, down_in,
    *refs,
):
    shards, refs = take(refs, spreads)
    before, refs = take(refs, 0 if first else 3)
    (grad_ref, low_ref, gain_grad_ref), refs = take(refs, 3)
    y_out, refs = take(refs, 2 if defer else 1)
    fulls, refs = take(refs, spreads)
    after, refs = take(refs, 3)
    ship_out, refs = take(refs, ships)
    (act_ref, dgate_ref, dup_ref, turned, new_rows, new_cols, old_rows, old_cols), refs = take(refs, 8)
    (rows_ref, cot_ref, gate_ref, up_ref, down_ref, load_sems, wide_sems), refs = take(refs, 7)
    sum_refs, refs = take(refs, 5)
    y_refs, refs = take(refs, 3 if defer else 5)
    ship_sems, refs = take(refs, ships)
    size, half = after[0].shape[0], up_low.shape[0] // after[0].shape[0]
    pairs = [(rows_in, rows_ref), (gate_in, gate_ref)]
    for e in range(size):
        for i, part in enumerate((up_low, up_high)):
            to = up_ref.at[pl.ds((2 * e + i) * half, half), :]
            pairs.append((part.at[pl.ds(e * half, half), :], to))
    pairs += [(cot_in, cot_ref), (down_in, down_ref)]
    loads = Loads(pairs, load_sems)
    spot = Spot()
    spot.enter(bool(ships), True)
    if ships:
        ship = Ship(spot, after[0], ship_out[0], ship_sems[0])
    summed = Sum(spot, *sum_refs)
    if defer:
        y_mine, y_send, y_sems = y_refs
        stores = [
            pltpu.make_async_copy(source, target, y_sems.at[i])
            for i, (source, target) in enumerate(zip((y_mine, y_send), y_out))
        ]
        sums = [summed]
    else:
        summed_y = Sum(spot, *y_refs)
        y_mine, y_send = summed_y.mine, summed_y.out
        sums = [summed, summed_y]
    moving = [Spread(spot, *refs) for refs in zip(shards, fulls, refs)]
    for spread in moving:
        spread.begin()
    hidden, width = gate_ref.shape[1], rows_ref.shape[1]
    chip_rows = 2 * owner_rows
    tile = min(256, hidden)
    blocks = after[0].shape[0]
    block = width // blocks
    new = (new_rows.at[0], new_rows.at[1], new_cols)
    old = (old_rows.at[0], old_rows.at[1], old_cols)

    def load(g, e):
        return pltpu.make_async_copy(before[g].at[e], old[g], wide_sems.at[0, g])

    def store(g, e):
        return pltpu.make_async_copy(new[g], after[g].at[e], wide_sems.at[1, g])

    if not first:
        for g in range(3):
            load(g, spot.peer(1)).start()
    loads.wait()

    def go_on(chains, hop):
        if hop < spot.places - 1:
            for each in chains:
                each.go_on(hop)

    @pl.loop(0, spot.places)
    def _(s):
        place = summed.term(s)
        rows = pl.ds(pl.multiple_of(place * chip_rows, chip_rows), chip_rows)

        @pl.loop(0, hidden // tile)
        def _(t):
            cols = pl.ds(pl.multiple_of(t * tile, tile), tile)
            gate = dot(rows_ref[rows, :], gate_ref[:, cols])
            up = dot(rows_ref[rows, :], up_ref[:, cols])
            sig = jax.nn.sigmoid(gate)
            silu = gate * sig
            act_ref[rows, cols] = (silu * up).astype(BF16)
            grad = dot_nt(cot_ref[rows, :], down_ref[cols, :])
            dgate_ref[rows, cols] = (grad * up * sig * (1.0 + gate * (1.0 - sig))).astype(BF16)
            dup_ref[rows, cols] = (grad * silu).astype(BF16)

            @pl.when((s > 0) & (t == min(1, hidden // tile - 1)))
            def _():
                for each in sums:
                    each.begin(s - 1)

        pl.when(s == 2)(lambda: go_on(moving, 1))
        pl.when(s == 3)(lambda: go_on(sums[:1], 1))

        wide = math.gcd(width, 512)

        @pl.loop(0, width // wide)
        def _(t):
            cols = pl.ds(pl.multiple_of(t * wide, wide), wide)
            value = dot(act_ref[rows, :], down_ref[:, cols])
            keep, send = split_cores(spot.core, value.astype(BF16), owner_rows)
            y_mine[place, :, cols] = keep[0]
            y_send[place, :, cols] = send[0]
            value = dot_nt(dgate_ref[rows, :], gate_ref[cols, :])
            value += dot_nt(dup_ref[rows, :], up_ref[cols, :])
            keep, send = split_cores(spot.core, value.astype(BF16), owner_rows)
            summed.mine[place, :, cols] = keep[0]
            summed.out[place, :, cols] = send[0]

        for each in sums:
            each.sibling(place).start()

    if defer:
        for copy in stores:
            copy.start()
    if spot.places == 3:
        go_on(sums[:1], 1)
    go_on(moving, 2)
    go_on(sums[1:], 1)

    def send(i):
        if ships:
            pl.when(i < blocks - 1)(lambda: ship.copy(i + 1).start())
            pl.when(i == blocks - 1)(lambda: ship.local.start())

    def make(g, i, left, right, right_at, columns):
        e = spot.peer(i + 1)

        @pl.when(i > 0)
        def _():
            store(g, spot.peer(i)).wait()
            if g == 0:
                send(i - 1)

        if not first:
            load(g, e).wait()
        step = math.gcd(columns, 256)

        @pl.loop(0, columns // step)
        def _(t):
            cols = pl.ds(pl.multiple_of(t * step, step), step)
            total = dot(left[...], right[:, pl.ds(pl.multiple_of(right_at + t * step, step), step)])
            if not first:
                total += old[g][:, cols].astype(F32)
            new[g][:, cols] = total.astype(BF16)

        if not first:
            pl.when(i < blocks - 1)(lambda: load(g, spot.peer(i + 2)).start())
        store(g, e).start()

    @pl.loop(0, blocks)
    def _(i):
        pl.when(i == 1)(lambda: go_on(sums[:1], 2))
        pl.when(i == blocks - 1)(lambda: go_on(sums[1:], 2))
        left = turned.at[pl.ds(0, block), :]
        at = spot.peer(i + 1) * block
        left[...] = rows_ref[:, pl.ds(pl.multiple_of(at, block), block)].T
        make(0, i, left, dgate_ref, 0, hidden)
        make(1, i, left, dup_ref, 0, hidden)

    if ships:
        store(0, spot.dp).wait()
        send(blocks - 1)
    for hop in range(3, spot.places - 1):
        go_on(moving + sums, hop)
    for spread in moving:
        spread.go_on(spot.places - 1)
    left = turned.at[pl.ds(0, hidden), :]
    left[...] = act_ref[...].T

    @pl.loop(0, blocks)
    def _(i):
        make(2, i, left, cot_ref, spot.peer(i + 1) * block, block)

    incoming = summed.finish()
    middle = middle_ref[...]
    term, gain_grad = norm_back(middle, norm_factor(middle), gain_ref[...], incoming)
    gain_grad_ref[...] = gain_grad[None]
    grad = local_cot_ref[...].astype(F32) + term
    grad_ref[...] = grad
    low_ref[...] = grad.astype(BF16)
    if defer:
        for copy in stores:
            copy.wait()
    else:
        y_out[0][...] = (middle + summed_y.finish()).astype(BF16)
    for spread in moving:
        spread.finish()
    for g in range(ships, 3):
        store(g, spot.dp).wait()
    if ships:
        ship.wait()


def add_grads(spot, left, right, turned, before, after, made=None):
    size, rows, columns = after.shape

    @pl.loop(0, size)
    def _(i):
        e = spot.peer(i + 1)
        if rows < left.shape[1]:
            turned[...] = left[:, pl.ds(pl.multiple_of(e * rows, rows), rows)].T
            total = dot(turned[...], right[...])
        else:

            @pl.when(i == 0)
            def _():
                turned[...] = left[...].T

            cut = pl.ds(pl.multiple_of(e * columns, columns), columns)
            total = dot(turned[...], right[:, cut])
        if before is not None:
            total += before[e].astype(F32)
        after[e] = total.astype(BF16)
        if made is not None:
            made(i)


def backward_kernel(
    tail, head, last, old_tail, old_head, extra, spreads, heads, toks, scale, shift, *refs
):
    tail_in, refs = take(refs, 6 * tail)
    old_qkv, refs = take(refs, old_tail)
    head_in, refs = take(refs, 7 * head)
    old_out, refs = take(refs, old_head)
    last_in, refs = take(refs, 2 * last)
    extra_in, refs = take(refs, 3 * extra)
    spread_in, refs = take(refs, spreads)
    tail_out, refs = take(refs, (1 if last else 3) * tail)
    head_out, refs = take(refs, 2 * head)
    last_out, refs = take(refs, 3 * last)
    extra_out, refs = take(refs, extra)
    spread_out, refs = take(refs, spreads)
    tail_refs, refs = take(refs, 7 * tail)
    head_refs, refs = take(refs, 14 * head)
    last_refs, refs = take(refs, 8 * last)
    extra_refs, refs = take(refs, 6 * extra)
    lazy_tail, refs = take(refs, 3 * tail)
    lazy_old, refs = take(refs, 2 * old_tail)
    lazy_head, refs = take(refs, 5 * head)
    if head:
        rows_ref, out_weight_ref, qkv, ids_ref, cos_ref, sin_ref, mix_ref = head_in
        loads_head = Loads(zip((rows_ref, qkv, cos_ref, sin_ref), lazy_head), lazy_head[4])
        rows_ref, qkv, cos_ref, sin_ref = lazy_head[:4]
    if tail:
        proj_ref, weight_ref, rows_one_ref, x_ref, grad_ref, gain_ref = tail_in
        loads_tail = Loads(zip((weight_ref, rows_one_ref), lazy_tail), lazy_tail[2])
        weight_ref, rows_one_ref = lazy_tail[:2]
    if extra:
        loads_extra = Loads(zip(extra_in[:2], extra_refs), extra_refs[5])
    before = None
    if old_tail:
        before = lazy_old[0]
        loads_old = Loads([(old_qkv[0], before)], lazy_old[1])
    spot = Spot()
    spot.enter(head or last, tail or spreads or extra)
    moving = [Spread(spot, *refs) for refs in zip(spread_in, spread_out, refs)]
    for spread in moving:
        spread.begin()
    if last:
        out_blocks, gains = last_in
        out_target, qkv_target, gain_sum = last_out
        new_qkv, own_gain, all_dp, dp_sum, all_mp, ship_sems, gain_sems, gain_spread_sems = last_refs
        ship_out = Ship(spot, out_blocks, out_target, ship_sems.at[0])
        ship_out.start()
    early, late = [], []
    if extra:
        summed_y = Sum(spot, *extra_refs[:5])
        loads_extra.wait()
        for t in range(spot.places):
            summed_y.sibling(t).start()
        late.append(summed_y)
    if head:
        head_proj_ref, new_out = head_out
        part, got, part_send, part_recv = head_refs[:4]
        made_q, got_q, q_send, q_recv, made_kv, got_kv, kv_send, kv_recv, dq, mix_turned = head_refs[4:]
        pairs = part.shape[0]
        owner_rows = toks * (pairs // heads)
        total = rows_ref.shape[0]
        step = min(512, total)
        loads_head.wait(0)

        @pl.loop(0, total // step)
        def _(i):
            rows = pl.ds(pl.multiple_of(i * step, step), step)
            made = dot_nt(rows_ref[rows, :], out_weight_ref[...]).astype(BF16)
            for j in range(step // owner_rows):
                to = pl.ds(pl.multiple_of((i * (step // owner_rows) + j) * toks, toks), toks)
                for p in range(pairs):
                    s, h = p // heads, p % heads
                    start = j * owner_rows + s * toks
                    part[p, to, :] = made[start : start + toks, h * HEAD : (h + 1) * HEAD]

        swap = Swap(spot, part, got, part_send, part_recv)
        swap.start()

    if extra:

        @pl.loop(0, spot.places - 1)
        def _(s):
            summed_y.begin(s)

    if tail:
        result_ref = tail_out[0]
        sum_refs, (turned, gain_acc) = take(tail_refs, 5)
        if not last:
            new_qkv, gain_acc = tail_out[1:]
        owner_rows = x_ref.shape[0]
        summed = Sum(spot, *sum_refs)
        early.append(summed)
        chip_rows = 2 * owner_rows
        gain_acc[...] = jnp.zeros_like(gain_acc)
        loads_tail.wait()

        @pl.loop(0, spot.places)
        def _(s):
            t = summed.term(s)
            rows = pl.ds(pl.multiple_of(t * chip_rows, chip_rows), chip_rows)
            value = dot_nt(proj_ref[rows, :], weight_ref[...])
            gain_acc[...] += jnp.sum(
                value * rows_one_ref[rows, :].astype(F32), axis=0, keepdims=True
            )
            keep, send = split_cores(spot.core, value.astype(BF16), owner_rows)
            summed.mine[t] = keep[0]
            summed.out[t] = send[0]
            summed.sibling(t).start()
            pl.when(s > 0)(lambda: summed.begin(s - 1))

        if last:
            own_gain[...] = gains[...]
            own_gain[1:2, :] += gain_acc[...]
            gain_dp = Gather(spot, own_gain, lambda index: all_dp.at[index], gain_sems)
            gain_dp.start()
    if last:
        if old_tail:
            loads_old.wait()
        ship_qkv = Ship(spot, new_qkv, qkv_target, ship_sems.at[1])

        def send(i):
            pl.when(i < spot.dp_size - 1)(lambda: ship_qkv.copy(i + 1).start())
            pl.when(i == spot.dp_size - 1)(lambda: ship_qkv.local.start())

        add_grads(spot, rows_one_ref, proj_ref, turned, before, new_qkv, send)
        gain_dp.wait()
        dp_sum[...] = jnp.sum(all_dp[...], axis=0)
        gain_mp = Spread(spot, dp_sum, all_mp, gain_spread_sems)
        gain_mp.begin()
        gain_mp.go_on(1)
    if head:
        add_grads(
            spot, mix_ref, rows_ref, mix_turned, old_out[0] if old_head else None, new_out
        )

    def go_on(hop):
        if hop < spot.places - 1:
            for each in moving + early + late:
                each.go_on(hop)

    if not (tail and head):
        go_on(1)
    if head:
        swap.wait()
        loads_head.wait(1, 2, 3)
        swap_kv = Swap(spot, made_kv, got_kv, kv_send, kv_recv)
        attend_back_blocks(
            spot, qkv, got, ids_ref, cos_ref, sin_ref, made_q, made_kv, dq,
            lambda step: swap_kv.copy(step).start(), lambda: go_on(1 if tail else 2), scale, shift,
        )
        swap_kv.keep()
        swap = Swap(spot, made_q, got_q, q_send, q_recv)
        swap.start()
    for hop in range(2 if tail else 3, spot.places - 1):
        if last:
            gain_mp.go_on(hop)
        go_on(hop)
    if tail and not last:
        if old_tail:
            loads_old.wait()
        add_grads(spot, rows_one_ref, proj_ref, turned, before, new_qkv)
    if head:
        swap_kv.wait()
        swap.wait()
        for o in range(total // owner_rows):
            for p in range(pairs):
                s, h = p // heads, p % heads
                here, there = pl.ds(o * owner_rows + s * toks, toks), pl.ds(o * toks, toks)
                for kind in range(3):
                    piece = (
                        got_kv[p, there, (kind - 1) * HEAD : kind * HEAD] if kind else got_q[p, there, :]
                    )
                    head_proj_ref[
                        here, (kind * heads + h) * HEAD : (kind * heads + h + 1) * HEAD
                    ] = piece
    for spread in moving:
        spread.go_on(spot.places - 1)
    if last and spot.places > 2:
        gain_mp.go_on(spot.places - 1)
    if tail:
        incoming = summed.finish()
        x = x_ref[...].astype(F32)
        term, _ = norm_back(x, norm_factor(x), gain_ref[...], incoming)
        result_ref[...] = grad_ref[...] + term
    if extra:
        extra_out[0][...] = (extra_in[2][...] + summed_y.finish()).astype(BF16)
    if last:
        gain_mp.finish()
        gain_sum[...] = jnp.sum(all_mp[...], axis=0)
        ship_out.wait()
        ship_qkv.wait()
    for spread in moving:
        spread.finish()


def ffn_kernel(
    rows_ref, cot_ref, gate_ref, up_ref, down_ref, y_ref, dh_ref, act_ref, dgate_ref, dup_ref
):
    hidden = gate_ref.shape[1]
    width = rows_ref.shape[1]
    tile = min(256, hidden)

    @pl.loop(0, hidden // tile)
    def _(t):
        cols = pl.ds(pl.multiple_of(t * tile, tile), tile)
        gate = dot(rows_ref[...], gate_ref[:, cols])
        up = dot(rows_ref[...], up_ref[:, cols])
        sig = jax.nn.sigmoid(gate)
        silu = gate * sig
        act_ref[:, cols] = (silu * up).astype(BF16)
        grad = dot_nt(cot_ref[...], down_ref[cols, :])
        dgate_ref[:, cols] = (grad * up * sig * (1.0 + gate * (1.0 - sig))).astype(BF16)
        dup_ref[:, cols] = (grad * silu).astype(BF16)

    @pl.loop(0, width // 256)
    def _(t):
        cols = pl.ds(pl.multiple_of(t * 256, 256), 256)
        y_ref[:, cols] = dot(act_ref[...], down_ref[:, cols]).astype(BF16)
        dh = dot_nt(dgate_ref[...], gate_ref[cols, :]) + dot_nt(dup_ref[...], up_ref[cols, :])
        dh_ref[:, cols] = dh.astype(BF16)


def grad_kernel(count, groups, left_blocked, *refs):
    lefts, refs = take(refs, count)
    rights, refs = take(refs, count * groups)
    out_refs, (turned,) = take(refs, groups)
    rows = lefts[0].shape[0]

    def turn():
        for m, left in enumerate(lefts):
            turned[:, m * rows : (m + 1) * rows] = left[...].T

    if left_blocked:
        turn()
    else:
        pl.when(pl.program_id(0) == 0)(turn)
    tile = math.gcd(out_refs[0].shape[2], 256)
    for g, out_ref in enumerate(out_refs):
        own = rights[g * count : (g + 1) * count]

        @pl.loop(0, out_ref.shape[2] // tile)
        def _(t):
            cols = pl.ds(pl.multiple_of(t * tile, tile), tile)
            total = dot(turned[:, :rows], own[0][:, cols])
            for m in range(1, count):
                total += dot(turned[:, m * rows : (m + 1) * rows], own[m][:, cols])
            out_ref[0, :, cols] = total.astype(BF16)


VMEM = pl.BlockSpec(memory_space=pltpu.VMEM)
ANY = pl.BlockSpec(memory_space=pltpu.HBM)


def cost(flops, nbytes):
    return pl.CostEstimate(flops=flops, bytes_accessed=nbytes, transcendentals=0)


def limits(mebibytes):
    return pltpu.CompilerParams(vmem_limit_bytes=mebibytes * 2**20)


def shape(*dims, dtype=BF16):
    return jax.ShapeDtypeStruct(dims, dtype)


def comm_params(collective_id, mebibytes):
    return pltpu.CompilerParams(
        collective_id=collective_id, has_side_effects=True, vmem_limit_bytes=mebibytes * 2**20
    )


def begin(x, gain, query, key, value, out):
    size, mp_size = lax.axis_size("dp"), lax.axis_size("mp")
    rows, columns = query.shape
    return pl.pallas_call(
        begin_kernel,
        out_shape=[
            shape(rows * size, 3 * columns),
            shape(out.shape[0], out.shape[1] * size),
            shape(mp_size, *x.shape),
        ],
        in_specs=[VMEM] * 2 + [ANY] * 4,
        out_specs=[ANY] * 3,
        scratch_shapes=[
            pltpu.VMEM(x.shape, BF16),
            pltpu.SemaphoreType.DMA((4, 2, size + 1)),
            *spread_scratch(mp_size // 2),
        ],
        compiler_params=comm_params(0, 16),
        cost_estimate=cost(0, 60 * 2**20),
        name="begin",
    )(x, gain, query, key, value, out)


def forward_stage(collective_id, tail, head, norm, shard, gather, heads, toks, scale, shift):
    size, mp_size = lax.axis_size("dp"), lax.axis_size("mp")
    out_shape, scratch = [], []
    if tail:
        blocks, _, x, _ = tail
        owner_rows, width = x.shape
        total = blocks.shape[1] * blocks.shape[0] // heads
        out_shape += [
            shape(owner_rows, width, dtype=F32),
            shape(owner_rows, width),
            shape(total, heads * HEAD),
        ]
        scratch += sum_scratch(mp_size // 2, owner_rows, width)
    if head:
        total, slice_len = head[0].shape[0], head[2].shape[0]
        out_shape += [shape(size, slice_len, 3 * HEAD), shape(size, slice_len, HEAD)]
        scratch += [
            pltpu.VMEM((min(512, total), 3 * heads * HEAD), F32),
            *swap_scratch(size, slice_len, 3 * HEAD),
            *swap_scratch(size, slice_len, HEAD),
        ]
    if norm:
        scratch.append(pltpu.VMEM(norm[0].shape, BF16))
    if head:
        scratch += lazy_scratch(*head[:2])
    here, spreads = len(out_shape), bool(norm) + len(shard)
    out_shape += [shape(mp_size, *array.shape) for array in (*norm[:1], *shard)]
    scratch += spread_scratch(mp_size // 2) * spreads
    axis = None
    if gather:
        weight, axis = gather
        dims = list(weight.shape)
        dims[axis] *= size
        out_shape.append(shape(*dims))
        scratch.append(pltpu.SemaphoreType.DMA((2, size + 1)))
    arrays = [*tail, *head, *norm]
    specs = [VMEM] * len(arrays)
    if head:
        specs[len(tail) : len(tail) + 2] = [ANY] * 2
    return pl.pallas_call(
        functools.partial(
            forward_kernel,
            bool(tail), bool(head), bool(norm), spreads, axis, heads, toks, scale, shift,
        ),
        out_shape=out_shape,
        in_specs=specs + [ANY] * (len(shard) + bool(gather)),
        out_specs=[VMEM] * here + [ANY] * (spreads + bool(gather)),
        scratch_shapes=scratch,
        compiler_params=comm_params(collective_id, 52),
        cost_estimate=cost(10**10, 100 * 2**20),
        name="forward_stage",
    )(*arrays, *shard, *gather[:1])


def middle_part(
    collective_id, defer, ships, rows, cot, weights, middle, local_cot, gain, shards, before
):
    total, width = rows.shape
    gate, _, _, down = weights
    hidden = gate.shape[1]
    size, mp_size = lax.axis_size("dp"), lax.axis_size("mp")
    places = mp_size // 2
    owner_rows = middle.shape[0]
    block = width // size
    wide = [shape(size, block, hidden)] * 2 + [shape(size, hidden, block)]
    half = shape(places, owner_rows, width)
    y_scratch = sum_scratch(places, owner_rows, width)
    if defer:
        y_scratch = [*[pltpu.VMEM(half.shape, BF16)] * 2, pltpu.SemaphoreType.DMA((2,))]
    return pl.pallas_call(
        functools.partial(middle_kernel, not before, defer, ships, len(shards), owner_rows),
        out_shape=[
            shape(owner_rows, width, dtype=F32),
            shape(owner_rows, width),
            shape(1, width, dtype=F32),
            *([half, half] if defer else [shape(owner_rows, width)]),
            *[shape(mp_size, *array.shape) for array in shards],
            *wide,
            *wide[:ships],
        ],
        in_specs=[VMEM] * 3 + [ANY] * (6 + len(shards) + len(before)),
        out_specs=[VMEM] * 3 + ([ANY] * 2 if defer else [VMEM]) + [ANY] * (len(shards) + 3 + ships),
        scratch_shapes=[
            *[pltpu.VMEM((total, hidden), BF16)] * 3,
            pltpu.VMEM((max(block, hidden), total), BF16),
            pltpu.VMEM((2, block, hidden), BF16),
            pltpu.VMEM((hidden, block), BF16),
            pltpu.VMEM((2, block, hidden), BF16),
            pltpu.VMEM((hidden, block), BF16),
            *[pltpu.VMEM(array.shape, BF16) for array in (rows, cot, gate, gate, down)],
            pltpu.SemaphoreType.DMA((4 + 2 * size,)),
            pltpu.SemaphoreType.DMA((2, 3)),
            *sum_scratch(places, owner_rows, width),
            *y_scratch,
            *[pltpu.SemaphoreType.DMA((2, size))] * ships,
            *spread_scratch(places) * len(shards),
        ],
        compiler_params=comm_params(collective_id, 61),
        cost_estimate=cost(18 * total * width * hidden, 60 * 2**20),
        name="middle_part",
    )(middle, local_cot, gain, rows, cot, *weights, *shards, *before)


def backward_stage(
    collective_id, tail, old_qkv, head, old_out, last, extra, shard, heads, toks, scale, shift
):
    size, mp_size = lax.axis_size("dp"), lax.axis_size("mp")
    places = mp_size // 2
    out_shape, scratch = [], []
    if tail:
        owner_rows, width = tail[3].shape
        out_shape.append(shape(owner_rows, width, dtype=F32))
        total = tail[0].shape[0]
        wide = shape(size, width // size, 3 * heads * HEAD)
        if not last:
            out_shape += [wide, shape(1, width, dtype=F32)]
        scratch += [
            *sum_scratch(places, owner_rows, width),
            pltpu.VMEM((width // size, total), BF16),
            pltpu.VMEM((1, width), F32),
        ]
    if head:
        (total, width), slice_len = head[0].shape, head[2].shape[1]
        out_shape.append(shape(total, 3 * heads * HEAD))
        out_shape.append(shape(size, heads * HEAD, width // size))
        scratch += [
            *swap_scratch(size, slice_len, HEAD),
            *swap_scratch(size, slice_len, HEAD),
            *swap_scratch(size, slice_len, 2 * HEAD),
            pltpu.VMEM((size, HEAD, slice_len), F32),
            pltpu.VMEM((heads * HEAD, total), BF16),
        ]
    here = len(out_shape)
    if last:
        gains = last[1].shape
        out_shape += [shape(*last[0].shape), wide]
        scratch += [
            pltpu.VMEM(wide.shape, BF16),
            pltpu.VMEM(gains, F32),
            pltpu.VMEM((size, *gains), F32),
            pltpu.VMEM(gains, F32),
            pltpu.VMEM((mp_size, *gains), F32),
            pltpu.SemaphoreType.DMA((2, 2, size)),
            pltpu.SemaphoreType.DMA((2, size)),
            *spread_scratch(places),
        ]
        out_shape.append(shape(*gains, dtype=F32))
    if extra:
        out_shape.append(shape(*extra[2].shape))
        scratch += sum_scratch(places, *extra[2].shape)
        scratch.append(pltpu.SemaphoreType.DMA((2,)))
    if tail:
        scratch += lazy_scratch(tail[1], tail[2])
    scratch += lazy_scratch(*old_qkv) if old_qkv else []
    if head:
        scratch += lazy_scratch(head[0], head[2], head[4], head[5])
    scratch += spread_scratch(places) * len(shard)
    out_shape += [shape(mp_size, *array.shape) for array in shard]
    arrays = [*tail, *old_qkv, *head, *old_out]
    tail_specs = [VMEM, ANY, ANY, VMEM, VMEM, VMEM] if tail else []
    head_specs = [ANY, VMEM, ANY, VMEM, ANY, ANY, VMEM] if head else []
    specs = [*tail_specs, *[ANY] * len(old_qkv), *head_specs, *[VMEM] * len(old_out)]
    last_specs, last_outs = ([ANY, VMEM], [ANY, ANY, VMEM]) if last else ([], [])
    extra_specs, extra_outs = ([ANY, ANY, VMEM], [VMEM]) if extra else ([], [])
    return pl.pallas_call(
        functools.partial(
            backward_kernel, bool(tail), bool(head), bool(last), len(old_qkv), len(old_out),
            bool(extra), len(shard), heads, toks, scale, shift,
        ),
        out_shape=out_shape,
        in_specs=specs + last_specs + extra_specs + [ANY] * len(shard),
        out_specs=[VMEM] * here + last_outs + extra_outs + [ANY] * len(shard),
        scratch_shapes=scratch,
        compiler_params=comm_params(collective_id, 58),
        cost_estimate=cost(10**10, 100 * 2**20),
        name="backward_stage",
    )(*arrays, *last, *extra, *shard)


def ffn(rows, cot, gate, up, down):
    total, width = rows.shape
    hidden = gate.shape[1]
    step = min(512, total)
    by_rows = pl.BlockSpec((step, width), lambda i: (i, 0))
    by_hidden = pl.BlockSpec((step, hidden), lambda i: (i, 0))
    held = lambda array: pl.BlockSpec(array.shape, lambda i: (0, 0), pipeline_mode=pl.Buffered(1))
    return pl.pallas_call(
        ffn_kernel,
        grid=(total // step,),
        out_shape=[shape(total, width)] * 2 + [shape(total, hidden)] * 3,
        in_specs=[by_rows, by_rows, held(gate), held(up), held(down)],
        out_specs=[by_rows] * 2 + [by_hidden] * 3,
        compiler_params=limits(56),
        cost_estimate=cost(12 * total * width * hidden, 34 * 2**20),
        name="ffn",
    )(rows, cot, gate, up, down)


def weight_grad(lefts, groups, left_blocked):
    count = len(lefts)
    size = lax.axis_size("dp")
    rows = lefts[0].shape[0]
    m, n = lefts[0].shape[1], groups[0][0].shape[1]
    moving = lambda width: pl.BlockSpec((rows, width // size), lambda e: (0, e))
    fixed = lambda width: pl.BlockSpec(
        (rows, width), lambda e: (0, 0), pipeline_mode=pl.Buffered(1)
    )
    left_spec = moving(m) if left_blocked else fixed(m)
    right_spec = fixed(n) if left_blocked else moving(n)
    out = (m // size, n) if left_blocked else (m, n // size)
    return pl.pallas_call(
        functools.partial(grad_kernel, count, len(groups), left_blocked),
        grid=(size,),
        in_specs=[left_spec] * count + [right_spec] * (count * len(groups)),
        out_specs=[pl.BlockSpec((1, *out), lambda e: (e, 0, 0))] * len(groups),
        out_shape=[shape(size, *out)] * len(groups),
        scratch_shapes=[pltpu.VMEM((out[0], count * rows), BF16)],
        compiler_params=limits(52),
        cost_estimate=cost(2 * count * rows * m * n * len(groups), 24 * 2**20),
        name="weight_grad",
    )(*lefts, *(right for group in groups for right in group))


def first_visible(ids):
    at = jnp.arange(ids.shape[-1], dtype=jnp.int32)
    starts = jnp.concatenate([jnp.ones_like(ids[..., :1], jnp.bool_), ids[..., 1:] != ids[..., :-1]], axis=-1)
    return lax.cummax(jnp.where(starts, at, 0), axis=ids.ndim - 1)


def block_at(values, index):
    return lax.dynamic_index_in_dim(values, index, 0, keepdims=False)


def stacked(blocks):
    full = jnp.zeros((len(blocks), *blocks[0].shape), blocks[0].dtype)
    for m, block in enumerate(blocks):
        full = lax.dynamic_update_index_in_dim(full, block, m, 0)
    return full


def scatter_mp(values):
    return lax.psum_scatter(values, "mp", scatter_dimension=0, tiled=True).astype(F32)


def sliced_scores(qkv, kv_all, first, positions, scale, shift):
    raw = jnp.einsum("pqd,pkd->pqk", qkv[..., :HEAD], kv_all[..., :HEAD], preferred_element_type=F32)
    at = jnp.arange(kv_all.shape[1], dtype=jnp.int32)
    visible = (at >= first[..., None]) & (at <= positions[:, None])
    return jnp.where(visible, sigmoid_of(raw, scale, shift), 0.0)


def per_device(
    inputs,
    cotangent,
    doc_ids,
    gain_attn,
    w_query,
    w_key,
    w_value,
    w_out,
    gain_ffn,
    w_gate,
    w_up,
    w_down,
):
    dp_size = lax.axis_size("dp")
    mp_size = lax.axis_size("mp")
    micro_count, row_count, seq_count, width = inputs.shape
    slice_len = row_count * mp_size
    total_len = slice_len * dp_size
    rows_here = row_count * seq_count
    shift = math.log(total_len)
    scale = HEAD ** (-0.5)
    dp_at = lax.axis_index("dp")
    mp_at = lax.axis_index("mp")
    first_row = dp_at * slice_len
    positions = first_row + jnp.arange(slice_len, dtype=jnp.int32)
    head_width = w_query.shape[1]
    heads = head_width // HEAD
    hidden = w_gate.shape[1]
    pairs = seq_count * heads
    whole_pairs = pairs == dp_size
    cos_all, sin_all = full_tables(total_len)
    cos_slice, sin_slice = [
        lax.dynamic_slice_in_dim(table, first_row, slice_len, 0) for table in (cos_all, sin_all)
    ]

    def by_row(table):
        shaped = table.reshape(mp_size, 1, row_count, 1, HEAD)
        return jnp.broadcast_to(shaped, (mp_size, seq_count, row_count, 1, HEAD))

    def rotate(values, back=False):
        sine = -by_row(sin_slice) if back else by_row(sin_slice)
        return values * by_row(cos_slice) + swap_halves(values) * sine

    def to_pairs(values):
        shaped = values.reshape(mp_size, seq_count, row_count, heads, -1)
        return shaped.transpose(1, 3, 0, 2, 4).reshape(pairs, slice_len, -1)

    def from_pairs(values):
        shaped = values.reshape(seq_count, heads, mp_size, row_count, -1)
        return shaped.transpose(2, 0, 3, 1, 4).reshape(mp_size * rows_here, heads, -1)

    def to_rows(values):
        return jnp.swapaxes(values, 0, 1).reshape(rows_here, width)

    def from_rows(values):
        return jnp.swapaxes(values.reshape(seq_count, row_count, width), 0, 1)

    def gather_mp(values):
        return lax.all_gather(values, "mp", axis=0, tiled=True)

    gain_attn_grad = jnp.zeros((width,), F32)
    gain_ffn_grad = jnp.zeros((width,), F32)
    results = []
    input_grads = []
    kept = [[] for _ in range(9)]
    xs = [to_rows(inputs[m]) for m in range(micro_count)]
    cots = [to_rows(cotangent[m]) for m in range(micro_count)]
    micros = range(micro_count)
    if whole_pairs:
        stage = (heads, row_count, scale, shift)
        ids = [
            block_at(doc_ids[m], dp_at // heads).astype(F32).reshape(dp_size, 1, slice_len)
            for m in micros
        ]
        last = micro_count - 1

        def whole(blocks):
            return blocks.reshape(mp_size * rows_here, width)

        def scatter_dp(blocks):
            flat = blocks.reshape(-1, blocks.shape[-1])
            return lax.psum_scatter(flat, "dp", scatter_dimension=0, tiled=True).astype(F32)

        qkv_full, out_full, rows_one = begin(
            xs[0], gain_attn[None], w_query, w_key, w_value, w_out
        )
        cut = w_up.shape[0] // 2
        gathers = {
            0: (w_gate, 0), 1: (w_up[:cut], 0), 2: (w_up[cut:], 0), micro_count: (w_down, 1)
        }
        wide = []
        ones, qkvs, got, middles, lows, twos, mixtures = [whole(rows_one)], [], [], [], [], [], []
        for m in range(micro_count + 1):
            tail, head, norm, shard = (), (), (), ()
            if m:
                tail = (got[m - 1], out_full, xs[m - 1], gain_ffn[None])
            if m < micro_count:
                head = (ones[m], qkv_full, cos_slice, sin_slice, ids[m])
            if m < last:
                norm = (xs[m + 1], gain_attn[None])
            elif lows:
                shard = (lows[m - last],)
            if m == 0:
                shard += (cots[0],)
            outs = forward_stage(10 + m, tail, head, norm, shard, gathers.get(m, ()), *stage)
            if tail:
                (middle, low, mixture), outs = take(outs, 3)
                middles.append(middle)
                lows.append(low)
                mixtures.append(mixture)
            if head:
                (qkv, block), outs = take(outs, 2)
                qkvs.append(qkv)
                got.append(block)
            if norm or shard:
                (ones if m < last else twos).append(whole(outs[0]))
            if m == 0:
                portions = [whole(outs[1])]
            if m in gathers:
                wide.append(outs[-1])
        grads, low_grads, attns, projs, sums, gain_parts, later = [], [], [], [], [], [], []
        for m in micros:
            shard = (lows[len(twos)] if len(twos) < micro_count else low_grads[len(attns)],)
            if m < last:
                shard += (cots[m + 1],)
            defer = m == 0
            grad, low, gain_part, *others = middle_part(
                30 + m, defer, int(m == last), twos[m], portions[m], wide, middles[m], cots[m], gain_ffn[None],
                shard, sums,
            )
            ys, (full, *others) = take(others, 2 if defer else 1)
            later.append((*ys, middles[m]) if defer else ys)
            (twos if len(twos) < micro_count else attns).append(whole(full))
            if m < last:
                portions.append(whole(others[0]))
            sums, gate_blocks = take(others[m < last :], 3)
            grads.append(grad)
            low_grads.append(low)
            gain_parts.append(gain_part)
        sum_up, sum_down = [scatter_dp(blocks) for blocks in sums[1:]]
        sum_gate = jnp.sum(gate_blocks[0].astype(F32), axis=0)
        old_qkv, old_out, attn_parts, finished = (), (), [], list(later)
        for m in range(micro_count + 1):
            tail, head, shard, final = (), (), (), ()
            if m:
                tail = (projs[m - 1], qkv_full, ones[m - 1], xs[m - 1], grads[m - 1], gain_attn[None])
            if m < micro_count:
                head = (attns[m], out_full, qkvs[m], ids[m], cos_all, sin_all, mixtures[m])
            else:
                rows = [sum(gain_parts), sum(attn_parts), jnp.zeros((6, width), F32)]
                final = (*old_out, jnp.concatenate(rows, axis=0))
            if len(attns) < micro_count:
                shard = (low_grads[len(attns)],)
            extra = later[0] if m == 0 else ()
            outs = backward_stage(
                20 + m, tail, old_qkv, head, () if final else old_out, final, extra, shard, *stage
            )
            if tail:
                (input_grad,), outs = take(outs, 1)
                input_grads.append(from_rows(input_grad))
            if tail and head:
                (new_qkv, gain_part), outs = take(outs, 2)
                old_qkv = (new_qkv,)
                attn_parts.append(gain_part)
            if head:
                (proj, new_out), outs = take(outs, 2)
                projs.append(proj)
                old_out = (new_out,)
            if extra:
                finished[0] = outs[:1]
            if shard:
                attns.append(whole(outs[-1]))
        results = [from_rows(result[0]) for result in finished]
        sum_out, sum_qkv = (jnp.sum(blocks.astype(F32), axis=0) for blocks in outs[:2])
        gain_sums = (outs[2][1] / gain_attn, outs[2][0])
    else:
        qkv_full = lax.all_gather(
            jnp.concatenate([w_query, w_key, w_value], axis=1), "dp", axis=0, tiled=True
        )
        out_full = lax.all_gather(w_out, "dp", axis=1, tiled=True)
        gate_full = lax.all_gather(w_gate, "dp", axis=0, tiled=True)
        up_full = lax.all_gather(w_up, "dp", axis=0, tiled=True)
        down_full = lax.all_gather(w_down, "dp", axis=1, tiled=True)
        first_all = first_visible(doc_ids)
        normed = [
            (x.astype(F32) * norm_factor(x.astype(F32)) * gain_attn).astype(BF16) for x in xs
        ]
        for micro in micros:
            local_rows = xs[micro].astype(F32)
            local_cot = cots[micro]
            factor_one = norm_factor(local_rows)
            rows_one = gather_mp(normed[micro])
            portion = gather_mp(local_cot)
            projected = dot(rows_one, qkv_full).reshape(
                mp_size, seq_count, row_count, 3, heads, HEAD
            )
            packed = to_pairs(
                jnp.concatenate(
                    [
                        rotate(projected[:, :, :, 0]).astype(BF16),
                        rotate(projected[:, :, :, 1]).astype(BF16),
                        projected[:, :, :, 2].astype(BF16),
                    ],
                    axis=-1,
                )
            )
            kv_all = lax.all_gather(packed[..., HEAD:], "dp", axis=1, tiled=True)
            first = lax.dynamic_slice_in_dim(first_all[micro], first_row, slice_len, 1)
            first = jnp.repeat(first, heads, axis=0)
            weights = sliced_scores(packed, kv_all, first, positions, scale, shift)
            attended = jnp.einsum(
                "pqk,pkd->pqd", weights.astype(BF16), kv_all[..., HEAD:], preferred_element_type=F32
            ).astype(BF16)
            mixture = from_pairs(attended).reshape(mp_size * rows_here, head_width)
            middle = local_rows + scatter_mp(dot(mixture, out_full).astype(BF16))
            factor_two = norm_factor(middle)
            rows_two = gather_mp((middle * factor_two * gain_ffn).astype(BF16))
            y, dh, activated, gate_grad, up_grad = ffn(
                rows_two, portion, gate_full, up_full, down_full
            )
            results.append(from_rows((middle + scatter_mp(y)).astype(BF16)))
            middle_term, gain_part = norm_back(middle, factor_two, gain_ffn, scatter_mp(dh))
            gain_ffn_grad = gain_ffn_grad + gain_part
            middle_grad = local_cot.astype(F32) + middle_term
            attn_portion = gather_mp(middle_grad.astype(BF16))
            mix_grad = to_pairs(dot_nt(attn_portion, out_full).astype(BF16))
            sig = sliced_scores(packed, kv_all, first, positions, scale, shift)
            prob_grad = jnp.einsum(
                "pqd,pkd->pqk", mix_grad, kv_all[..., HEAD:], preferred_element_type=F32
            )
            score_grad = (prob_grad * sig * (1.0 - sig)).astype(BF16)
            dq = jnp.einsum("pqk,pkd->pqd", score_grad, kv_all[..., :HEAD], preferred_element_type=F32)
            dk = jnp.einsum("pqk,pqd->pkd", score_grad, packed[..., :HEAD], preferred_element_type=F32)
            dv = jnp.einsum("pqk,pqd->pkd", sig.astype(BF16), mix_grad, preferred_element_type=F32)
            dkv = lax.psum_scatter(
                jnp.concatenate([dk * scale, dv], axis=-1).astype(BF16), "dp", scatter_dimension=1, tiled=True
            ).astype(F32)
            back = from_pairs(jnp.concatenate([dq * scale, dkv], axis=-1))
            back = back.reshape(mp_size, seq_count, row_count, heads, 3 * HEAD)
            proj_grad = jnp.stack(
                [
                    rotate(back[..., :HEAD], True),
                    rotate(back[..., HEAD : 2 * HEAD], True),
                    back[..., 2 * HEAD :],
                ],
                axis=3,
            ).astype(BF16).reshape(mp_size * rows_here, 3 * head_width)
            partial_grad = dot_nt(proj_grad, qkv_full)
            gain_attn_grad = gain_attn_grad + jnp.sum(partial_grad * rows_one.astype(F32), axis=0)
            input_term, _ = norm_back(
                local_rows, factor_one, gain_attn, scatter_mp(partial_grad.astype(BF16))
            )
            input_grads.append(from_rows(middle_grad + input_term))
            for held, array in zip(
                kept,
                (rows_one, proj_grad, mixture, attn_portion, rows_two, gate_grad, up_grad, activated, portion),
            ):
                held.append(array)

        def scatter_dp(lefts, rights, left_blocked):
            (blocks,) = weight_grad(lefts, (rights,), left_blocked)
            return lax.psum_scatter(blocks, "dp", scatter_dimension=0, tiled=True)[0].astype(F32)

        ones, projs, mixtures, attns, twos, gates, ups, acts, portions = kept
        sum_gate = scatter_dp(twos, gates, True)
        sum_up = scatter_dp(twos, ups, True)
        sum_down = scatter_dp(acts, portions, False)
        sum_out = scatter_dp(mixtures, attns, False)
        sum_qkv = scatter_dp(ones, projs, True)
        gain_sums = lax.psum((gain_attn_grad / gain_attn, gain_ffn_grad), ("dp", "mp"))
    return (
        stacked(results),
        stacked(input_grads),
        gain_sums[0],
        sum_qkv[:, :head_width],
        sum_qkv[:, head_width : 2 * head_width],
        sum_qkv[:, 2 * head_width :],
        sum_out,
        gain_sums[1],
        sum_gate,
        sum_up,
        sum_down,
    )


def solution(mesh):
    tokens = P(None, ("dp", "mp"), None, None)
    column = P("dp", "mp")
    row = P("mp", "dp")
    return jax.shard_map(
        per_device,
        mesh=mesh,
        in_specs=(
            tokens, tokens, P(), P(), column, column, column, row, P(), column, column, row,
        ),
        out_specs=(
            tokens, tokens, P(), column, column, column, row, P(), column, column, row,
        ),
        check_vma=False,
    )
```
